32 devices in a mesh: shard: 2 (over y), expert: 16 (over z, x, core).
Axes of the slice: x: 2, y: 2, z: 4, core: 2. Of those that a mesh axis runs over, the one named last changes fastest.
Arguments:
- tokens: bfloat16 [4096, 2048], P(('shard', 'expert')), may hold values from -6 to 6
- document_lengths: int32 [2, 4], replicated, may hold values from 1 to 1280, 2048 in all within a row
- routes: int32 [4096, 6], P(('shard', 'expert')), may hold values from 0 to 15, all different within a row; in each aligned block of 128 rows (0 to 127, 128 to 255, ...) at most 64 rows name the same one
- first_gain: float32 [2048], replicated, may hold values from 0.5 to 1.5
- query_weight: bfloat16 [2048, 3072], P('shard'), may hold values from -0.125 to 0.125
- latent_down: bfloat16 [2048, 576], P('shard'), may hold values from -0.125 to 0.125
- latent_gain: float32 [512], replicated, may hold values from 0.5 to 1.5
- latent_up: bfloat16 [512, 4096], P('shard'), may hold values from -0.25 to 0.25
- output_weight: bfloat16 [2048, 2048], P('shard'), may hold values from -1.5 to 1.5
- second_gain: float32 [2048], replicated, may hold values from 0.5 to 1.5
- router_weight: bfloat16 [2048, 16], replicated, may hold values from -0.0625 to 0.0625
- shared_gate: bfloat16 [2048, 2816], P('shard'), may hold values from -0.125 to 0.125
- shared_up: bfloat16 [2048, 2816], P('shard'), may hold values from -0.125 to 0.125
- shared_down: bfloat16 [2816, 2048], P('shard'), may hold values from -0.15625 to 0.15625
- expert_gate: bfloat16 [16, 2048, 1408], P('expert', 'shard'), may hold values from -0.125 to 0.125
- expert_up: bfloat16 [16, 2048, 1408], P('expert', 'shard'), may hold values from -0.125 to 0.125
- expert_down: bfloat16 [16, 1408, 2048], P('expert', 'shard'), may hold values from -0.4375 to 0.4375
- cotangent: bfloat16 [4096, 2048], P(('shard', 'expert')), may hold values from -6 to 6
Outputs:
- activations: bfloat16 [4096, 2048], P(('shard', 'expert'))
- input_grad: float32 [4096, 2048], P(('shard', 'expert'))
- first_gain_grad: float32 [2048], P(('shard', 'expert'))
- query_weight_grad: float32 [2048, 3072], P(('shard', 'expert'))
- latent_down_grad: float32 [2048, 576], P(('shard', 'expert'))
- latent_gain_grad: float32 [512], P(('shard', 'expert'))
- latent_up_grad: float32 [512, 4096], P(('shard', 'expert'))
- output_weight_grad: float32 [2048, 2048], P(('shard', 'expert'))
- second_gain_grad: float32 [2048], P(('shard', 'expert'))
- router_weight_grad: float32 [2048, 16], P(('shard', 'expert'))
- shared_gate_grad: float32 [2048, 2816], P(('shard', 'expert'))
- shared_up_grad: float32 [2048, 2816], P(('shard', 'expert'))
- shared_down_grad: float32 [2816, 2048], P(('shard', 'expert'))
- expert_gate_grad: float32 [16, 2048, 1408], P('expert', 'shard')
- expert_up_grad: float32 [16, 2048, 1408], P('expert', 'shard')
- expert_down_grad: float32 [16, 1408, 2048], P('expert', 'shard')
The draws below stay inside these ranges and needn't reach their ends.
Inputs may be any that keep to these rules, and one draw needn't show every extreme that they name: `routes`: each row names 6 different experts; among the rows of one device no expert is named more than 64 times, and in every draw some device names some expert exactly 64 times. `document_lengths`: each row lists the documents of one packed sequence in order and sums to 2048; its last entry is padding; the largest entry of every row is 1280.
All inputs are finite; a program needn't handle non-finite values.
Results may differ from the reference program's by a relative error of at most 0.02.
Values may be sent and summed in bfloat16 or wider, within the bound.
A program may use at most 512 MiB of HBM per device.

```python
import math
import jax
import jax.numpy as jnp
import numpy as np
from jax import lax

D = 2048
HEADS = 16
QK_NOPE = 128
QK_ROPE = 64
V_HEAD = 128
KV_RANK = 512
MOE_FF = 1408
TOP = 6
TOK_DEV = 128
SEQ = 2048
WINDOW = 1024
NDOC = 4
MOST = 1280
SFF = 2816
EXPERTS = 16
CAP = 64
TOKENS = 4096
SEQS = 2


def raised(values, rng, source, target, shards_of, factor):
    def block_of(axis_at):
        return (jnp.arange(values.shape[axis_at]) // (values.shape[axis_at] // shards_of)).reshape((-1,) + (1,) * (values.ndim - 1 - axis_at))

    first = jax.random.permutation(rng, shards_of)[block_of(target)]
    second = (block_of(target) + shards_of // 2) % shards_of
    return jnp.where((block_of(source) == first) | (block_of(source) == second), factor * values, values)


def shard_levels(rng, shape, cuts, smallest, top_value):
    loudness, own = 1.0, jax.random.fold_in(rng, 6)
    for axis_at, shards_of in cuts:
        steps = jnp.exp(jax.random.uniform(jax.random.fold_in(own, axis_at), (shards_of,), jnp.float32, smallest / len(cuts), top_value / len(cuts)))
        loudness = loudness * jnp.repeat(steps, shape[axis_at] // shards_of).reshape([-1 if axis == axis_at else 1 for axis in range(len(shape))])
    return loudness


def profile(count, total, most, lean):
    portions = [(1 << 20) // math.isqrt(grade ** lean) + 1 for grade in range(2, count + 1)]
    surplus, given = total - most - (count - 1), [1] * (count - 1)
    while surplus > 0:
        candidates = [i for i in range(count - 1) if given[i] < most]
        whole, budget = sum([portions[i] for i in candidates]), surplus
        for i in candidates:
            addition = min(most - given[i], max(1, budget * portions[i] // whole), surplus)
            given[i] = given[i] + addition
            surplus = surplus - addition
    return np.array([most] + given)


def ragged_sizes(rng, amount, total, most, lean):
    if amount == 2:
        one = jax.random.randint(rng, (), max(1, total - most), min(most, total - 1) + 1)
        return jnp.stack([one, total - one])
    lengths = jnp.asarray(profile(amount, total, most, lean), jnp.int32)
    twos = (amount - 1) // 2
    donor, receiver = lengths[1:1 + 2 * twos:2], lengths[2:2 + 2 * twos:2]
    margin = jnp.minimum(donor - 1, most - receiver)
    moved = jax.random.randint(jax.random.fold_in(rng, 1), (twos,), 0, 1 << 20) % (margin + 1)
    lengths = lengths.at[1:1 + 2 * twos:2].set(donor - moved).at[2:2 + 2 * twos:2].set(receiver + moved)
    return lengths[jax.random.permutation(jax.random.fold_in(rng, 2), amount)]


def routed_block(stream_key, own, number, rows, count, top, reach, skew):
    order = jax.random.permutation(stream_key, count)
    crowded, common = load_shares(count, rows * top, reach, skew, True), load_shares(count, rows * top, reach, skew, False)
    places = jnp.arange(count)

    def named(lengths, turn):
        used = int((lengths > 0).sum())
        fixed = max(1, used // 4)
        moved = fixed + (places - fixed + turn * (used - fixed)) % max(1, count - fixed)
        return jnp.zeros((count,), jnp.int32).at[order[jnp.where(places < fixed, places, moved)]].set(jnp.asarray(lengths, jnp.int32))

    lengths = jnp.where(number % 4 == 0, named(crowded, number // 4), named(common, number - number // 4 - 1))
    mixed = jax.random.permutation(jax.random.fold_in(own, 3), count)
    giver, taker = mixed[0:count // 2 * 2:2], mixed[1:count // 2 * 2:2]
    slack = jnp.minimum(lengths[giver] - 1, reach - lengths[taker]) // 2
    slack = jnp.where((giver == order[0]) | (taker == order[0]) | (lengths[taker] == 0), 0, jnp.maximum(slack, 0))
    moved = jax.random.randint(jax.random.fold_in(own, 4), (count // 2,), 0, 1 << 20) % (slack + 1)
    lengths = lengths.at[giver].add(-moved).at[taker].add(moved)
    labels = jnp.searchsorted(jnp.cumsum(lengths), jnp.arange(rows * top), side="right").astype(jnp.int32)
    listing = labels.reshape(top, rows).T
    listing = listing[jax.random.permutation(jax.random.fold_in(own, 1), rows)]
    turn = jax.random.randint(jax.random.fold_in(own, 2), (rows, 1), 0, top)
    return jnp.take_along_axis(listing, (jnp.arange(top)[None, :] + turn) % top, axis=1)


def load_shares(amount, total, bound, lean, full):
    weights = [(1 << 20) // math.isqrt(grade ** lean) + 1 for grade in range(1, amount + 1)]
    largest = bound if full else min(bound, max(-(-total // amount), total * weights[0] // sum(weights)))
    least = 1 if total - largest >= amount - 1 else 0
    counts, surplus = [largest] + [least] * (amount - 1), total - largest - least * (amount - 1)
    while surplus > 0:
        movable = [i for i in range(1, amount) if counts[i] < largest] or [i for i in range(1, amount) if counts[i] < bound]
        whole, left = sum([weights[i] for i in movable]), surplus
        for i in movable:
            addition = min(bound - counts[i], max(1, left * weights[i] // whole), surplus)
            counts[i] = counts[i] + addition
            surplus = surplus - addition
    return np.array(counts)


def noise(own_key, extent, deviation, limit, shards=(), kind=jnp.bfloat16):
    loudness = shard_levels(own_key, extent, shards, -0.22, 0.18) if shards else 1.0
    entries = jax.random.normal(own_key, extent, jnp.float32) * deviation * loudness
    return jnp.minimum(jnp.maximum(entries, -limit), limit).astype(kind)


def bell_draw_with(rng, dims, scale, most, shards, heavy, held_as=jnp.bfloat16):
    result = scale * jax.random.normal(rng, dims, jnp.float32)
    if shards:
        result = result * shard_levels(rng, dims, shards, -0.22, 0.18)
    return jnp.clip(raised(result, jax.random.fold_in(rng, 3), *heavy), -most, most).astype(held_as)


def setup_inputs(seed: int = 0) -> dict:
    arg_keys = jax.random.split(jax.random.key(seed), 19)
    tokens = bell_draw_with(arg_keys[0], (TOKENS, D), 1.0, 6.0, ((0, 32),), (0, 1, 32, 2.75))
    document_lengths = jax.vmap(lambda own: ragged_sizes(own, NDOC, SEQ, MOST, 1))(jax.random.split(arg_keys[1], SEQS)).reshape((SEQS, NDOC)).astype(jnp.int32)
    routes_keys = jax.random.split(jax.random.fold_in(arg_keys[2], 1), TOKENS // TOK_DEV)
    routes_turns = jax.random.permutation(jax.random.fold_in(arg_keys[2], 3), TOKENS // TOK_DEV)
    routes = jax.vmap(lambda own, number: routed_block(jax.random.fold_in(arg_keys[2], 2), own, number, TOK_DEV, EXPERTS, TOP, CAP, 2))(routes_keys, routes_turns).reshape((TOKENS, TOP))
    first_gain = jnp.clip(1.0 + 0.1 * jax.random.normal(arg_keys[3], (D,), jnp.float32), 0.5, 1.5)
    query_weight = noise(arg_keys[4], (D, HEADS * (QK_NOPE + QK_ROPE)), D ** -0.5, 0.125, ((0, 2),))
    latent_down = noise(arg_keys[5], (D, KV_RANK + QK_ROPE), D ** -0.5, 0.125, ((0, 2),))
    latent_gain = jnp.clip(1.0 + 0.1 * jax.random.normal(arg_keys[6], (KV_RANK,), jnp.float32), 0.5, 1.5)
    latent_up = noise(arg_keys[7], (KV_RANK, HEADS * (QK_NOPE + V_HEAD)), KV_RANK ** -0.5, 0.25, ((0, 2),))
    output_weight = noise(arg_keys[8], (HEADS * V_HEAD, D), 16 ** -0.5, 1.5, ((0, 2),))
    second_gain = jnp.clip(1.0 + 0.1 * jax.random.normal(arg_keys[9], (D,), jnp.float32), 0.5, 1.5)
    router_weight = noise(arg_keys[10], (D, EXPERTS), (4 * D) ** -0.5, 0.0625)
    shared_gate = noise(arg_keys[11], (D, SFF), D ** -0.5, 0.125, ((0, 2),))
    shared_up = noise(arg_keys[12], (D, SFF), D ** -0.5, 0.125, ((0, 2),))
    shared_down = noise(arg_keys[13], (SFF, D), (SFF // 2) ** -0.5, 0.15625, ((0, 2),))
    expert_gate = noise(arg_keys[14], (EXPERTS, D, MOE_FF), D ** -0.5, 0.125, ((0, 16), (1, 2)))
    expert_up = noise(arg_keys[15], (EXPERTS, D, MOE_FF), D ** -0.5, 0.125, ((0, 16), (1, 2)))
    expert_down = noise(arg_keys[16], (EXPERTS, MOE_FF, D), (MOE_FF // 8) ** -0.5, 0.4375, ((0, 16), (1, 2)))
    cotangent = noise(arg_keys[17], (TOKENS, D), 1.0, 6.0, ((0, 32),))
    return {"tokens": tokens, "document_lengths": document_lengths, "routes": routes, "first_gain": first_gain, "query_weight": query_weight, "latent_down": latent_down, "latent_gain": latent_gain, "latent_up": latent_up, "output_weight": output_weight, "second_gain": second_gain, "router_weight": router_weight, "shared_gate": shared_gate, "shared_up": shared_up, "shared_down": shared_down, "expert_gate": expert_gate, "expert_up": expert_up, "expert_down": expert_down, "cotangent": cotangent}


EPS = 1e-06
THETA = 10000.0
NEG = -1e+30
HIGH = lax.Precision.HIGHEST

@jax.custom_vjp
def low(v):
    return lax.optimization_barrier(v.astype(jnp.bfloat16)).astype(jnp.float32)

@jax.custom_vjp
def low_back(v):
    return v

def low_keep(v):
    return (low(v), None)

def low_pass(kept, grad):
    return (grad,)

def back_keep(v):
    return (v, None)

def back_low(kept, grad):
    return (low(grad),)
low.defvjp(low_keep, low_pass)
low_back.defvjp(back_keep, back_low)

def matmul(left, right):
    return jnp.dot(left, right, precision=HIGH, preferred_element_type=jnp.float32)

def norm_scale(values, gain):
    return values * lax.rsqrt(lax.optimization_barrier(jnp.mean(values * values, axis=-1, keepdims=True)) + EPS) * gain

def rotary_tables(positions, width):
    half = width // 2
    freqs = THETA ** (-jnp.arange(half, dtype=jnp.float32) / half)
    angles = positions.astype(jnp.float32)[:, None] * freqs[None, :]
    return (jnp.cos(angles), jnp.sin(angles))

def rotate(values, cosine_part, sine_part):
    half = values.shape[-1] // 2
    first = values[..., :half]
    second = values[..., half:]
    return jnp.concatenate([first * cosine_part - second * sine_part, second * cosine_part + first * sine_part], axis=-1)

def activate(values):
    return values * jax.nn.sigmoid(values)

def reference(tokens, document_lengths, routes, first_gain, query_weight, latent_down, latent_gain, latent_up, output_weight, second_gain, router_weight, shared_gate, shared_up, shared_down, expert_gate, expert_up, expert_down, cotangent):
    grand_total = tokens.shape[0]
    devices = grand_total // TOK_DEV
    sequences = grand_total // SEQ
    head_dim = QK_NOPE + QK_ROPE
    score_scale = 1.0 / math.sqrt(head_dim)
    positions = jnp.arange(grand_total, dtype=jnp.int32)
    seq_pos = positions % SEQ
    cosine_part, sine_part = rotary_tables(seq_pos, QK_ROPE)
    ends = jnp.cumsum(document_lengths, axis=1).astype(jnp.int32)
    row_ends = ends[positions // SEQ]
    documents = lax.optimization_barrier(jnp.sum((seq_pos[:, None] >= row_ends).astype(jnp.int32), axis=1)).astype(jnp.int32)
    query_mask = (documents < NDOC - 1).astype(jnp.float32)
    flat_routes = routes.reshape(-1).astype(jnp.int32)
    per_device = flat_routes.reshape(devices, TOK_DEV * TOP)
    route_marks = (per_device[:, :, None] == jnp.arange(EXPERTS, dtype=jnp.int32)[None, None, :]).astype(jnp.int32)
    running = jnp.cumsum(route_marks, axis=1).astype(jnp.int32) - 1
    slot_ranks = lax.optimization_barrier(jnp.sum(route_marks * running, axis=2)).astype(jnp.int32).reshape(-1)
    sender = jnp.arange(grand_total * TOP, dtype=jnp.int32) // (TOK_DEV * TOP)
    slot_index = flat_routes * (devices * CAP) + sender * CAP + slot_ranks
    source_indices = jnp.full((EXPERTS * devices * CAP,), grand_total * TOP, dtype=jnp.int32)
    source_indices = source_indices.at[slot_index].set(jnp.arange(grand_total * TOP, dtype=jnp.int32)).reshape(EXPERTS, devices * CAP)
    index_grid = jnp.arange(SEQ, dtype=jnp.int32)
    in_window = (index_grid[None, :] <= index_grid[:, None]) & (index_grid[None, :] > index_grid[:, None] - WINDOW)

    def layer_forward_pass(hidden_input_rows, attention_norm_gain, query_projection_weight, latent_down_weight, latent_norm_gain, latent_up_weight, attention_output_weight, feed_norm_gain, router_logit_weight, shared_gate_weight, shared_up_weight, shared_down_weight, expert_gate_weight, expert_up_weight, expert_down_weight):
        normed_one = low(norm_scale(hidden_input_rows, attention_norm_gain))
        query = low_back(matmul(normed_one, query_projection_weight)).reshape(grand_total, HEADS, head_dim)
        query_nope = low(query[..., :QK_NOPE])
        query_rope = low(rotate(query[..., QK_NOPE:], cosine_part[:, None, :], sine_part[:, None, :]))
        compressed = low_back(matmul(normed_one, latent_down_weight))
        key_latent = low(norm_scale(compressed[:, :KV_RANK], latent_norm_gain))
        key_rope = low(rotate(compressed[:, KV_RANK:], cosine_part, sine_part))
        up_heads = latent_up_weight.reshape(KV_RANK, HEADS, QK_NOPE + V_HEAD)
        key_up = up_heads[:, :, :QK_NOPE]
        value_up = up_heads[:, :, QK_NOPE:]

        def one_sequence(pieces):
            nope_part, rope_part, latent_part, key_part, doc_part, mask_part = pieces
            query_latent = low(low_back(jnp.einsum('thn,chn->thc', nope_part, key_up, precision=HIGH)))
            raw = jnp.einsum('thc,kc->htk', query_latent, latent_part, precision=HIGH)
            raw = low_back(raw + jnp.einsum('thr,kr->htk', rope_part, key_part, precision=HIGH))
            allowed = in_window & (doc_part[:, None] == doc_part[None, :])
            scores = jnp.where(allowed[None], raw * score_scale, NEG)
            top_score = lax.optimization_barrier(jnp.max(scores, axis=-1, keepdims=True))
            expo = jnp.exp(scores - top_score)
            probs = low(expo / lax.optimization_barrier(jnp.sum(expo, axis=-1, keepdims=True)))
            latent_out = low(low_back(jnp.einsum('htk,kc->thc', probs, latent_part, precision=HIGH)))
            heads_out = jnp.einsum('thc,chv->thv', latent_out, value_up, precision=HIGH) * mask_part[:, None, None]
            return low(low_back(heads_out)).reshape(SEQ, HEADS * V_HEAD)
        pieces = (query_nope.reshape(sequences, SEQ, HEADS, QK_NOPE), query_rope.reshape(sequences, SEQ, HEADS, QK_ROPE), key_latent.reshape(sequences, SEQ, KV_RANK), key_rope.reshape(sequences, SEQ, QK_ROPE), documents.reshape(sequences, SEQ), query_mask.reshape(sequences, SEQ))
        heads_all = lax.map(jax.checkpoint(one_sequence), pieces).reshape(grand_total, HEADS * V_HEAD)
        attention = low_back(matmul(heads_all, attention_output_weight))
        mid = hidden_input_rows + attention
        second_normed_rows = low(norm_scale(mid, feed_norm_gain))
        logits = matmul(second_normed_rows, router_logit_weight)
        chosen = jnp.take_along_axis(logits, routes, axis=1)
        chosen_top = lax.optimization_barrier(jnp.max(chosen, axis=1, keepdims=True))
        chosen_exp = jnp.exp(chosen - chosen_top)
        gate_values = chosen_exp / lax.optimization_barrier(jnp.sum(chosen_exp, axis=1, keepdims=True))
        shared_gate_pre = low_back(matmul(second_normed_rows, shared_gate_weight))
        shared_up_pre = low_back(matmul(second_normed_rows, shared_up_weight))
        shared_hidden = low(activate(shared_gate_pre) * shared_up_pre)
        shared_out = low_back(matmul(shared_hidden, shared_down_weight))
        normed_pad = jnp.concatenate([second_normed_rows, jnp.zeros((1, second_normed_rows.shape[1]), jnp.float32)], axis=0)
        gates_pad = jnp.concatenate([gate_values.reshape(-1), jnp.zeros((1,), jnp.float32)], axis=0)

        def single_expert_apply(routed_output, pieces_e):
            gate_w, up_w, down_w, source_e = pieces_e
            token_rows = source_e // TOP
            rows_in = low_back(normed_pad[token_rows])
            weights_e = gates_pad[source_e]
            gate_pre = low_back(matmul(rows_in, gate_w))
            up_pre = low_back(matmul(rows_in, up_w))
            hidden_e = low(activate(gate_pre) * up_pre)
            out_e = low(low_back(matmul(hidden_e, down_w)))
            return (routed_output.at[token_rows].add(weights_e[:, None] * out_e), None)
        routed_output, discarded_value = lax.scan(jax.checkpoint(single_expert_apply), jnp.zeros((grand_total + 1, second_normed_rows.shape[1]), jnp.float32), (expert_gate_weight, expert_up_weight, expert_down_weight, source_indices))
        return mid + shared_out + routed_output[:grand_total]
    primals = (tokens.astype(jnp.float32), first_gain.astype(jnp.float32), query_weight.astype(jnp.float32), latent_down.astype(jnp.float32), latent_gain.astype(jnp.float32), latent_up.astype(jnp.float32), output_weight.astype(jnp.float32), second_gain.astype(jnp.float32), router_weight.astype(jnp.float32), shared_gate.astype(jnp.float32), shared_up.astype(jnp.float32), shared_down.astype(jnp.float32), expert_gate.astype(jnp.float32), expert_up.astype(jnp.float32), expert_down.astype(jnp.float32))
    output, pullback = jax.vjp(layer_forward_pass, *primals)
    grads = pullback(cotangent.astype(jnp.float32))
    return (output.astype(jnp.bfloat16), grads[0], grads[1], grads[2], grads[3], grads[4], grads[5], grads[6], grads[7], grads[8], grads[9], grads[10], grads[11], grads[12], grads[13], grads[14])
```

```python
import math

import jax
import jax.numpy as jnp
from jax import lax
from jax.sharding import PartitionSpec as P

HEADS = 16
QK_NOPE = 128
QK_ROPE = 64
V_HEAD = 128
KV_RANK = 512
TOP = 6
SEQ = 2048
WINDOW = 1024
TOK_DEV = 128
SEQ_DEVICES = SEQ // TOK_DEV


EPS = 1e-06
THETA = 10000.0
NEG = -1e30
HIGH = lax.Precision.HIGHEST


def matmul(left, right):
    return jnp.dot(left, right, preferred_element_type=jnp.float32)


def matmul_tn(left, right):
    return lax.dot_general(
        left, right, (((0,), (0,)), ((), ())), preferred_element_type=jnp.float32
    )


def matmul_nt(left, right):
    return lax.dot_general(
        left, right, (((1,), (1,)), ((), ())), preferred_element_type=jnp.float32
    )


def norm_scale(values, gain):
    return values * lax.rsqrt(jnp.mean(values * values, axis=-1, keepdims=True) + EPS) * gain


def rotary_tables(positions, width):
    half = width // 2
    freqs = THETA ** (-jnp.arange(half, dtype=jnp.float32) / half)
    angles = positions.astype(jnp.float32)[:, None] * freqs[None, :]
    return (jnp.cos(angles), jnp.sin(angles))


def rotate(values, cosine_part, sine_part):
    half = values.shape[-1] // 2
    first = values[..., :half]
    second = values[..., half:]
    return jnp.concatenate(
        [first * cosine_part - second * sine_part, second * cosine_part + first * sine_part],
        axis=-1,
    )


def unrotate(values, cosine_part, sine_part):
    half = values.shape[-1] // 2
    first = values[..., :half]
    second = values[..., half:]
    return jnp.concatenate(
        [first * cosine_part + second * sine_part, second * cosine_part - first * sine_part],
        axis=-1,
    )


def swish_parts(values):
    sigmoid_part = jax.nn.sigmoid(values)
    return (values * sigmoid_part, sigmoid_part * (1.0 + values * (1.0 - sigmoid_part)))


def plane_groups(plane):
    members = SEQ_DEVICES
    if plane == members:
        return None
    return [list(range(low, low + members)) for low in range(0, plane, members)]


def shard_ring(block):
    count = lax.axis_size("shard")
    me = lax.axis_index("shard")
    whole = jnp.zeros((count,) + block.shape, block.dtype)
    whole = lax.dynamic_update_index_in_dim(whole, block, me, 0)
    for step in range(1, count):
        moved = lax.ppermute(
            block, "shard", [(source, (source + step) % count) for source in range(count)]
        )
        whole = lax.dynamic_update_index_in_dim(whole, moved, (me - step) % count, 0)
    return whole


def shard_rows(block):
    whole = shard_ring(block)
    return whole.reshape((-1,) + block.shape[1:])


def shard_sum(values):
    count = lax.axis_size("shard")
    me = lax.axis_index("shard")
    blocks = values.reshape((count, -1) + values.shape[1:])
    total = lax.dynamic_index_in_dim(blocks, me, 0, keepdims=False)
    for step in range(1, count):
        outgoing = lax.dynamic_index_in_dim(blocks, (me + step) % count, 0, keepdims=False)
        moved = lax.ppermute(
            outgoing.astype(jnp.bfloat16),
            "shard",
            [(source, (source + step) % count) for source in range(count)],
        )
        total = total + moved.astype(jnp.float32)
    return total


def shared_rows_plane(block):
    plane = lax.axis_size("expert")
    count = lax.axis_size("shard")
    rows = block.shape[0] // plane
    mine = lax.dynamic_slice_in_dim(block, lax.axis_index("expert") * rows, rows, 0)
    pieces = shard_ring(mine)
    gathered = lax.all_gather(pieces, "expert", axis=1, tiled=False)
    return gathered.reshape((count * block.shape[0],) + block.shape[1:])


def on_device(
    tokens,
    document_lengths,
    routes,
    first_gain,
    query_weight,
    latent_down,
    latent_gain,
    latent_up,
    output_weight,
    second_gain,
    router_weight,
    shared_gate,
    shared_up,
    shared_down,
    expert_gate,
    expert_up,
    expert_down,
    cotangent,
):
    local_rows, width = tokens.shape
    shards = lax.axis_size("shard")
    plane = lax.axis_size("expert")
    everyone = ("shard", "expert")
    all_devices = shards * plane
    shard_at = lax.axis_index("shard")
    plane_at = lax.axis_index("expert")
    groups = plane_groups(plane)
    head_at = plane_at % SEQ_DEVICES
    sequence_at = (shard_at * plane + plane_at) // SEQ_DEVICES
    capacity = local_rows * TOP * 4 // (3 * plane)
    head_dim = QK_NOPE + QK_ROPE
    scale = 1.0 / math.sqrt(head_dim)
    own_at = head_at * local_rows

    def own_rows(values):
        return lax.dynamic_slice_in_dim(values, own_at, local_rows, 0)

    query_head = shard_rows(
        lax.dynamic_slice_in_dim(query_weight, head_at * head_dim, head_dim, 1)
    )
    full_down = shard_rows(latent_down)
    up_head = shard_rows(
        lax.dynamic_slice_in_dim(latent_up, head_at * (QK_NOPE + V_HEAD), QK_NOPE + V_HEAD, 1)
    )
    full_out = shared_rows_plane(output_weight)
    full_query = shared_rows_plane(query_weight)
    units = shared_down.shape[0] // plane
    gate_columns, up_columns = (
        jnp.concatenate(
            [
                lax.dynamic_slice_in_dim(
                    weight, index * shared_down.shape[0] + plane_at * units, units, 1
                )
                for index in range(shards)
            ],
            axis=1,
        )
        for weight in (shared_gate, shared_up)
    )
    gate_shared = shard_rows(gate_columns)
    up_shared = shard_rows(up_columns)
    down_shared = shard_rows(lax.dynamic_slice_in_dim(shared_down, plane_at * units, units, 0))
    gate_single = shard_rows(expert_gate[0])
    up_single = shard_rows(expert_up[0])
    down_single = shard_rows(expert_down[0])

    all_tokens = lax.all_gather(
        tokens, "expert", axis=0, tiled=True, axis_index_groups=groups
    ).astype(jnp.float32)
    normed_one = norm_scale(all_tokens, first_gain).astype(jnp.bfloat16)
    positions = jnp.arange(SEQ, dtype=jnp.int32)
    cosine_part, sine_part = rotary_tables(positions, QK_ROPE)
    sequence_count, entry_count = document_lengths.shape
    ends = jnp.cumsum(document_lengths, axis=1)
    picked = jnp.arange(sequence_count, dtype=jnp.int32)[:, None] == sequence_at
    row_ends = jnp.sum(jnp.where(picked, ends, 0), axis=0)
    documents = jnp.sum((positions[:, None] >= row_ends[None, :]).astype(jnp.int32), axis=1)
    real = (documents < entry_count - 1).astype(jnp.float32)
    allowed = (
        (documents[:, None] == documents[None, :])
        & (positions[None, :] <= positions[:, None])
        & (positions[None, :] > positions[:, None] - WINDOW)
    )
    query = matmul(normed_one, query_head)
    query_nope = query[:, :QK_NOPE].astype(jnp.bfloat16)
    query_rope = rotate(query[:, QK_NOPE:], cosine_part, sine_part).astype(jnp.bfloat16)
    compressed = matmul(normed_one, full_down)
    key_latent = norm_scale(compressed[:, :KV_RANK], latent_gain).astype(jnp.bfloat16)
    key_rope = rotate(compressed[:, KV_RANK:], cosine_part, sine_part).astype(jnp.bfloat16)
    keys_values = matmul(key_latent, up_head).astype(jnp.bfloat16)
    key_nope = keys_values[:, :QK_NOPE]
    value = keys_values[:, QK_NOPE:]

    def scores_of():
        raw = matmul_nt(query_nope, key_nope) + matmul_nt(query_rope, key_rope)
        return jnp.where(allowed, raw * scale, NEG)

    scores = scores_of()
    top_score = jnp.max(scores, axis=1, keepdims=True)
    expo = jnp.exp(scores - top_score)
    expo_total = jnp.sum(expo, axis=1, keepdims=True)
    log_total = top_score + jnp.log(expo_total)
    probs = expo / expo_total
    head_out = (matmul(probs.astype(jnp.bfloat16), value) * real[:, None]).astype(jnp.bfloat16)
    heads_out = lax.all_to_all(
        head_out.reshape(SEQ_DEVICES, local_rows, V_HEAD),
        "expert",
        split_axis=0,
        concat_axis=0,
        tiled=True,
        axis_index_groups=groups,
    )
    heads_out = heads_out.transpose(1, 0, 2).reshape(local_rows, HEADS * V_HEAD)

    hidden_rows = tokens.astype(jnp.float32)
    middle = hidden_rows + matmul(heads_out, full_out)
    second_normed = norm_scale(middle, second_gain).astype(jnp.bfloat16)

    all_normed = lax.all_gather(second_normed, "expert", axis=0, tiled=True)
    all_grads = lax.all_gather(cotangent, "expert", axis=0, tiled=True)
    all_routes = lax.all_gather(routes, "expert", axis=0, tiled=True)
    plane_rows = plane * local_rows
    logits = matmul(all_normed, router_weight)
    expert_ids = jnp.arange(plane, dtype=jnp.int32)
    choose = all_routes[:, :, None] == expert_ids[None, None, :]
    chosen = jnp.sum(jnp.where(choose, logits[:, None, :], 0.0), axis=2)
    chosen_top = jnp.max(chosen, axis=1, keepdims=True)
    chosen_exp = jnp.exp(chosen - chosen_top)
    gate_values = chosen_exp / jnp.sum(chosen_exp, axis=1, keepdims=True)
    here = all_routes == plane_at
    gate_here = jnp.sum(jnp.where(here, gate_values, 0.0), axis=1).reshape(plane, local_rows)
    marks = jnp.any(here, axis=1).reshape(plane, local_rows)
    ranks = jnp.cumsum(marks.astype(jnp.int32), axis=1) - 1
    picks = marks[:, None, :] & (
        ranks[:, None, :] == jnp.arange(capacity, dtype=jnp.int32)[None, :, None]
    )
    select = picks.astype(jnp.bfloat16)

    def to_slots(values):
        return (
            jnp.einsum(
                "bct,btd->bcd",
                select,
                values.reshape(plane, local_rows, width),
                preferred_element_type=jnp.float32,
            )
            .astype(jnp.bfloat16)
            .reshape(plane * capacity, width)
        )

    def to_tokens(values):
        return jnp.einsum(
            "bct,bcd->btd",
            select,
            values.reshape(plane, capacity, width),
            preferred_element_type=jnp.float32,
        ).reshape(plane_rows, width)

    slot_rows = to_slots(all_normed)
    slot_cotangent = to_slots(all_grads).astype(jnp.float32)
    slot_gate = jnp.sum(jnp.where(picks, gate_here[:, None, :], 0.0), axis=2).reshape(-1, 1)
    gate_pre = matmul(slot_rows, gate_single)
    up_pre = matmul(slot_rows, up_single)
    swished, slope = swish_parts(gate_pre)
    hidden = (swished * up_pre).astype(jnp.bfloat16)
    expert_out = matmul(hidden, down_single).astype(jnp.bfloat16).astype(jnp.float32)
    slot_gate_grad = jnp.sum(slot_cotangent * expert_out, axis=1).reshape(plane, capacity)
    slot_grad = (slot_gate * slot_cotangent).astype(jnp.bfloat16)
    hidden_grad = matmul_nt(slot_grad, down_single)
    gate_pre_grad = (hidden_grad * up_pre * slope).astype(jnp.bfloat16)
    up_pre_grad = (hidden_grad * swished).astype(jnp.bfloat16)
    row_back = (
        matmul_nt(gate_pre_grad, gate_single) + matmul_nt(up_pre_grad, up_single)
    ).astype(jnp.bfloat16)

    shared_pre = matmul(all_normed, gate_shared)
    shared_up_pre = matmul(all_normed, up_shared)
    shared_swished, shared_slope = swish_parts(shared_pre)
    shared_hidden = (shared_swished * shared_up_pre).astype(jnp.bfloat16)
    shared_hidden_grad = matmul_nt(all_grads, down_shared)
    shared_gate_back = (shared_hidden_grad * shared_up_pre * shared_slope).astype(jnp.bfloat16)
    shared_up_back = (shared_hidden_grad * shared_swished).astype(jnp.bfloat16)

    normed_part = (
        to_tokens(row_back)
        + matmul_nt(shared_gate_back, gate_shared)
        + matmul_nt(shared_up_back, up_shared)
    ).astype(jnp.bfloat16)
    token_gate_grad = jnp.sum(
        jnp.where(picks, slot_gate_grad[:, :, None], 0.0), axis=1
    ).reshape(plane_rows, 1)
    gate_high = token_gate_grad.astype(jnp.bfloat16)
    gate_low = (token_gate_grad - gate_high.astype(jnp.float32)).astype(jnp.bfloat16)
    at_me = (expert_ids == plane_at).astype(jnp.bfloat16)[None, :]
    back = lax.psum_scatter(
        jnp.concatenate([normed_part, gate_high * at_me, gate_low * at_me], axis=1),
        "expert",
        scatter_dimension=0,
        tiled=True,
    ).astype(jnp.float32)
    output_part = (
        to_tokens((slot_gate * expert_out).astype(jnp.bfloat16))
        + matmul(shared_hidden, down_shared)
    ).astype(jnp.bfloat16)
    output_sum = lax.psum_scatter(output_part, "expert", scatter_dimension=0, tiled=True)
    activations = (middle + output_sum.astype(jnp.float32)).astype(jnp.bfloat16)

    expert_down_grad = shard_sum(matmul_tn(hidden, slot_grad))[None]
    expert_gate_grad = shard_sum(matmul_tn(slot_rows, gate_pre_grad))[None]
    expert_up_grad = shard_sum(matmul_tn(slot_rows, up_pre_grad))[None]
    shared_down_grad = shard_sum(matmul_tn(shared_hidden, all_grads))
    shared_term = jnp.concatenate(
        [matmul_tn(all_normed, shared_gate_back), matmul_tn(all_normed, shared_up_back)], axis=1
    )

    def to_owners(term):
        moved = lax.all_to_all(
            term.astype(jnp.bfloat16).reshape(all_devices, -1, term.shape[1]),
            everyone,
            split_axis=0,
            concat_axis=0,
            tiled=True,
        )
        moved = moved.reshape(shards, plane, -1, term.shape[1]).astype(jnp.float32)
        return jnp.sum(moved, axis=0)

    def by_head(moved):
        heads = moved.reshape((plane // SEQ_DEVICES, HEADS) + moved.shape[1:]).sum(axis=0)
        return heads.transpose(1, 0, 2).reshape(moved.shape[1], -1)

    shared_moved = to_owners(shared_term).reshape(plane, -1, 2, shards, units)
    shared_moved = shared_moved.transpose(2, 1, 3, 0, 4)
    shared_moved = shared_moved.reshape(2, shared_moved.shape[1], -1)
    shared_gate_grad = shared_moved[0]
    shared_up_grad = shared_moved[1]

    grad_out = cotangent.astype(jnp.float32)
    gate_dense = back[:, width : width + plane] + back[:, width + plane :]
    own_start = plane_at * local_rows
    own_gates = lax.dynamic_slice_in_dim(gate_values, own_start, local_rows, 0)
    own_choose = routes[:, :, None] == expert_ids[None, None, :]
    gate_grad = jnp.sum(jnp.where(own_choose, gate_dense[:, None, :], 0.0), axis=2)
    chosen_grad = own_gates * (
        gate_grad - jnp.sum(own_gates * gate_grad, axis=1, keepdims=True)
    )
    logit_grad = jnp.sum(jnp.where(own_choose, chosen_grad[:, :, None], 0.0), axis=1)
    router_term = lax.dot_general(
        second_normed.astype(jnp.float32),
        logit_grad,
        (((0,), (0,)), ((), ())),
        precision=HIGH,
        preferred_element_type=jnp.float32,
    )
    normed_grad = back[:, :width] + lax.dot_general(
        logit_grad,
        router_weight.astype(jnp.float32),
        (((1,), (1,)), ((), ())),
        precision=HIGH,
        preferred_element_type=jnp.float32,
    )
    unused_two, second_back = jax.vjp(norm_scale, middle, second_gain)
    middle_norm_grad, second_term = second_back(normed_grad)
    middle_grad = grad_out + middle_norm_grad
    middle_low = middle_grad.astype(jnp.bfloat16)
    small_sums = lax.psum_scatter(
        jnp.concatenate([router_term, second_term[:, None]], axis=1),
        everyone,
        scatter_dimension=0,
        tiled=True,
    )
    router_weight_grad = small_sums[:, :plane]
    second_gain_grad = small_sums[:, plane]

    output_weight_grad = lax.psum_scatter(
        matmul_tn(heads_out, middle_low).astype(jnp.bfloat16),
        everyone,
        scatter_dimension=0,
        tiled=True,
    ).astype(jnp.float32)
    heads_grad = (matmul_nt(middle_low, full_out)).astype(jnp.bfloat16)
    heads_grad = heads_grad.reshape(local_rows, HEADS, V_HEAD).transpose(1, 0, 2)
    head_grad = lax.all_to_all(
        heads_grad, "expert", split_axis=0, concat_axis=0, tiled=True, axis_index_groups=groups
    ).reshape(SEQ, V_HEAD)
    head_grad = (head_grad.astype(jnp.float32) * real[:, None]).astype(jnp.bfloat16)
    again = jnp.exp(scores_of() - log_total)
    prob_grad = matmul_nt(head_grad, value)
    raw_grad = (
        again * (prob_grad - jnp.sum(again * prob_grad, axis=1, keepdims=True)) * scale
    ).astype(jnp.bfloat16)
    value_grad = matmul_tn(again.astype(jnp.bfloat16), head_grad)
    key_nope_grad = matmul_tn(raw_grad, query_nope)
    key_rope_grad = matmul_tn(raw_grad, query_rope)
    query_grad = jnp.concatenate(
        [
            matmul(raw_grad, key_nope),
            unrotate(matmul(raw_grad, key_rope), cosine_part, sine_part),
        ],
        axis=1,
    ).astype(jnp.bfloat16)
    pair_grad = jnp.concatenate([key_nope_grad, value_grad], axis=1).astype(jnp.bfloat16)
    latent_up_term = matmul_tn(key_latent, pair_grad)
    latent_up_grad = by_head(to_owners(latent_up_term))
    key_grad_part = jnp.concatenate([matmul_nt(pair_grad, up_head), key_rope_grad], axis=1)
    own_key_grad = lax.psum_scatter(
        key_grad_part.astype(jnp.bfloat16),
        "expert",
        scatter_dimension=0,
        tiled=True,
        axis_index_groups=groups,
    ).astype(jnp.float32)
    own_query_grad = lax.all_to_all(
        query_grad.reshape(SEQ_DEVICES, local_rows, head_dim),
        "expert",
        split_axis=0,
        concat_axis=0,
        tiled=True,
        axis_index_groups=groups,
    )
    own_query_grad = own_query_grad.transpose(1, 0, 2).reshape(local_rows, HEADS * head_dim)
    own_compressed = own_rows(compressed)
    unused_latent, latent_back = jax.vjp(norm_scale, own_compressed[:, :KV_RANK], latent_gain)
    latent_in_grad, latent_gain_term = latent_back(own_key_grad[:, :KV_RANK])
    rope_in_grad = unrotate(
        own_key_grad[:, KV_RANK:], own_rows(cosine_part), own_rows(sine_part)
    )
    compressed_grad = jnp.concatenate([latent_in_grad, rope_in_grad], axis=1).astype(jnp.bfloat16)
    down_columns = (KV_RANK + QK_ROPE) // SEQ_DEVICES
    column_grad = lax.all_to_all(
        compressed_grad.reshape(local_rows, SEQ_DEVICES, down_columns).transpose(1, 0, 2),
        "expert",
        split_axis=0,
        concat_axis=0,
        tiled=True,
        axis_index_groups=groups,
    ).reshape(SEQ, down_columns)
    normed_one_grad = matmul_nt(own_query_grad, full_query) + matmul_nt(
        compressed_grad, full_down
    )
    unused_one, first_back = jax.vjp(norm_scale, hidden_rows, first_gain)
    input_norm_grad, first_term = first_back(normed_one_grad)
    input_grad = middle_grad + input_norm_grad
    weight_term = matmul_tn(normed_one, jnp.concatenate([query_grad, column_grad], axis=1))
    weight_moved = to_owners(weight_term)
    query_weight_grad = by_head(weight_moved[:, :, :head_dim])
    latent_down_grad = by_head(weight_moved[:, :, head_dim:])
    gain_sums = lax.psum_scatter(
        jnp.concatenate(
            [
                first_term.reshape(all_devices, -1),
                latent_gain_term.reshape(all_devices, -1),
            ],
            axis=1,
        ),
        everyone,
        scatter_dimension=0,
        tiled=True,
    )[0]
    first_gain_grad = gain_sums[: width // all_devices]
    latent_gain_grad = gain_sums[width // all_devices :]
    return (
        activations,
        input_grad,
        first_gain_grad,
        query_weight_grad,
        latent_down_grad,
        latent_gain_grad,
        latent_up_grad,
        output_weight_grad,
        second_gain_grad,
        router_weight_grad,
        shared_gate_grad,
        shared_up_grad,
        shared_down_grad,
        expert_gate_grad,
        expert_up_grad,
        expert_down_grad,
    )


def solution(mesh):
    return jax.shard_map(
        on_device,
        mesh=mesh,
        in_specs=(
            P(("shard", "expert"), None),
            P(),
            P(("shard", "expert"), None),
            P(),
            P("shard", None),
            P("shard", None),
            P(),
            P("shard", None),
            P("shard", None),
            P(),
            P(),
            P("shard", None),
            P("shard", None),
            P("shard", None),
            P("expert", "shard", None),
            P("expert", "shard", None),
            P("expert", "shard", None),
            P(("shard", "expert"), None),
        ),
        out_specs=(
            P(("shard", "expert"), None),
            P(("shard", "expert"), None),
            P(("shard", "expert")),
            P(("shard", "expert"), None),
            P(("shard", "expert"), None),
            P(("shard", "expert")),
            P(("shard", "expert"), None),
            P(("shard", "expert"), None),
            P(("shard", "expert")),
            P(("shard", "expert"), None),
            P(("shard", "expert"), None),
            P(("shard", "expert"), None),
            P(("shard", "expert"), None),
            P("expert", "shard", None),
            P("expert", "shard", None),
            P("expert", "shard", None),
        ),
        check_vma=False,
    )
```

```python
import functools
import math

import jax
import jax.numpy as jnp
from jax import lax
from jax.experimental import pallas as pl
from jax.experimental.pallas import tpu as pltpu
from jax.sharding import PartitionSpec as P

HEADS = 16
QK_NOPE = 128
QK_ROPE = 64
V_HEAD = 128
KV_RANK = 512
TOP = 6
SEQ = 2048
WINDOW = 1024
TOK_DEV = 128
SEQ_DEVICES = SEQ // TOK_DEV


EPS = 1e-06
THETA = 10000.0
NEG = -1e30
HIGH = lax.Precision.HIGHEST


def matmul(left, right):
    return jnp.dot(left, right, preferred_element_type=jnp.float32)


def matmul_tn(left, right):
    return lax.dot_general(
        left, right, (((0,), (0,)), ((), ())), preferred_element_type=jnp.float32
    )


def matmul_nt(left, right):
    return lax.dot_general(
        left, right, (((1,), (1,)), ((), ())), preferred_element_type=jnp.float32
    )


def norm_scale(values, gain):
    return values * lax.rsqrt(jnp.mean(values * values, axis=-1, keepdims=True) + EPS) * gain


def rotary_tables(positions, width):
    half = width // 2
    freqs = THETA ** (-jnp.arange(half, dtype=jnp.float32) / half)
    angles = positions.astype(jnp.float32)[:, None] * freqs[None, :]
    return (jnp.cos(angles), jnp.sin(angles))


def rotate(values, cosine_part, sine_part):
    half = values.shape[-1] // 2
    first = values[..., :half]
    second = values[..., half:]
    return jnp.concatenate(
        [first * cosine_part - second * sine_part, second * cosine_part + first * sine_part],
        axis=-1,
    )


def unrotate(values, cosine_part, sine_part):
    half = values.shape[-1] // 2
    first = values[..., :half]
    second = values[..., half:]
    return jnp.concatenate(
        [first * cosine_part + second * sine_part, second * cosine_part - first * sine_part],
        axis=-1,
    )


def swish_parts(values):
    sigmoid_part = jax.nn.sigmoid(values)
    return (values * sigmoid_part, sigmoid_part * (1.0 + values * (1.0 - sigmoid_part)))


def plane_groups(plane):
    members = SEQ_DEVICES
    if plane == members:
        return None
    return [list(range(low, low + members)) for low in range(0, plane, members)]


MESH = pl.DeviceIdType.MESH
INNER = 4
PIECES = 2


class Sender:
    def __init__(self):
        self.started = []

    def start(self, there, copy):
        @pl.when(there)
        def _():
            copy.start()

        self.started.append((there, copy))

    def finish(self):
        for there, copy in self.started:
            @pl.when(there)
            def _():
                copy.wait_send()


def remote(source, target, send_sem, recv_sem, place):
    return pltpu.make_async_remote_copy(
        src_ref=source,
        dst_ref=target,
        send_sem=send_sem,
        recv_sem=recv_sem,
        device_id=place,
        device_id_type=MESH,
    )


class Place:
    def __init__(self, group):
        self.me = lax.axis_index("expert")
        self.shard = lax.axis_index("shard")
        self.group = group
        self.outer = group // INNER
        self.local = lax.rem(self.me, group)
        self.base = self.me - self.local
        self.level = self.local // INNER
        inner = lax.rem(self.local, INNER)
        self.row_step = 2 - 4 * (inner // 2)
        self.twin_step = 1 - 2 * lax.rem(inner, 2)
        self.always = self.me >= 0
        self.upper = self.level < self.outer - 1
        self.lower = self.level > 0

    def neighbours(self):
        return [
            (self.upper, {"expert": self.me + INNER}),
            (self.lower, {"expert": self.me - INNER}),
            (self.always, {"expert": self.me + self.row_step}),
            (self.always, {"expert": self.me + self.twin_step}),
        ]

    def along(self, step):
        below = (self.level >= step, self.local - step * INNER, self.upper, self.me + INNER, 0)
        above = (self.level + step < self.outer, self.local + step * INNER, self.lower, self.me - INNER, 1)
        return (below, above)


def greet(peers):
    barrier = pltpu.get_barrier_semaphore()
    for there, peer in peers:
        @pl.when(there)
        def _():
            pl.semaphore_signal(barrier, inc=1, device_id=peer, device_id_type=MESH)
    pl.semaphore_wait(barrier, sum(there.astype(jnp.int32) for there, _ in peers))


def gather_steps(place, own_ref, out_ref, copy_sem, send_sem, recv_sem, sender):
    local = place.local
    row, twin = local + place.row_step, local + place.twin_step

    def push(kind, block, piece, target, source=None):
        spot = out_ref.at[block, piece]
        return remote(
            spot if source is None else source.at[piece],
            spot,
            send_sem.at[kind, block, piece],
            recv_sem.at[block, piece],
            {"expert": target},
        )

    def arrive(there, block, piece):
        @pl.when(there)
        def _():
            push(0, block, piece, place.me).wait_recv()

    pieces = own_ref.shape[0]
    row_at, twin_at = place.me + place.row_step, place.me + place.twin_step
    keep = pltpu.make_async_copy(own_ref, out_ref.at[local], copy_sem)
    keep.start()
    for piece in range(pieces):
        sender.start(place.upper, push(0, local, piece, place.me + INNER, own_ref))
        sender.start(place.lower, push(1, local, piece, place.me - INNER, own_ref))
        sender.start(place.always, push(2, local, piece, row_at, own_ref))
        sender.start(place.always, push(3, local, piece, twin_at, own_ref))
    yield
    for step in range(1, place.outer + 1):
        if step < place.outer:
            for piece in range(pieces):
                for there, block, onward, target, kind in place.along(step):
                    arrive(there, block, piece)
                    sender.start(there & onward, push(kind, block, piece, target))
                    sender.start(there, push(2, block, piece, row_at))
                    sender.start(there, push(3, block, piece, twin_at))
        for piece in range(pieces):
            for there, block, *_ in place.along(step - 1)[: 1 if step == 1 else 2]:
                arrive(there, block + place.row_step, piece)
                sender.start(there, push(3, block + place.row_step, piece, twin_at))
        yield
    for step in range(place.outer):
        for piece in range(pieces):
            for there, block, *_ in place.along(step)[: 1 if step == 0 else 2]:
                arrive(there, block + place.twin_step, piece)
                arrive(there, block + place.twin_step + place.row_step, piece)
    keep.wait()
    yield


def add_into(target, first, *others):
    rows = target.shape[0]
    chunk = 32

    def body(index, _):
        at = pl.ds(pl.multiple_of(index * chunk, chunk), chunk)
        total = first[at, :].astype(jnp.float32)
        for other in others:
            total = total + other[at, :].astype(jnp.float32)
        target[at, :] = total.astype(target.dtype)
        return 0

    lax.fori_loop(0, rows // chunk, body, 0)


def reduce_steps(place, part_ref, out_ref, scratch, sender):
    (own_buf, twin_buf, row_buf, up_buf, down_buf, load_sem, twin_send, twin_recv, row_send, row_recv,
     line_send, line_recv, out_buf, out_sem) = scratch
    outer, local, level = place.outer, place.local, place.level
    inner = lax.rem(local, INNER)
    row_bit, core = inner // 2, lax.rem(inner, 2)
    twin_at, row_at = {"expert": place.me + place.twin_step}, {"expert": place.me + place.row_step}
    order = []
    low, high = 0, outer - 1
    while low <= high:
        order.append(high)
        if low != high:
            order.append(low)
        low, high = low + 1, high - 1

    def slot(level_at, bit):
        return level_at * 2 + bit

    def block(level_at, bit, core_at):
        return level_at * INNER + bit * 2 + core_at

    other_bit, other_core = 1 - row_bit, 1 - core
    loads, twins, rows = {}, {}, {}
    for at in order:
        for kind, bit in ((0, other_bit), (1, row_bit)):
            where = slot(at, bit)
            copy = remote(part_ref.at[block(at, bit, other_core)], twin_buf.at[where], twin_send.at[where],
                          twin_recv.at[where], twin_at)
            sender.start(place.always, copy)
            load = pltpu.make_async_copy(part_ref.at[block(at, bit, core)], own_buf.at[where], load_sem.at[where])
            load.start()
            loads[at, kind] = load
            twins[at, kind] = pltpu.make_async_remote_copy(
                src_ref=part_ref.at[block(at, bit, other_core)], dst_ref=twin_buf.at[where],
                send_sem=twin_send.at[where], recv_sem=twin_recv.at[where], device_id=twin_at, device_id_type=MESH)
    yield
    for at in order:
        for kind, bit in ((0, other_bit), (1, row_bit)):
            where = slot(at, bit)
            loads[at, kind].wait()
            twins[at, kind].wait_recv()
            add_into(own_buf.at[where], own_buf.at[where], twin_buf.at[where])
            if kind == 0:
                copy = remote(own_buf.at[where], row_buf.at[at], row_send.at[at], row_recv.at[at], row_at)
                sender.start(place.always, copy)
                rows[at] = copy
        yield
    for at in order:
        mine = own_buf.at[slot(at, row_bit)]
        rows[at].wait_recv()

        @pl.when(level == at)
        def _():
            add_into(mine, mine, row_buf.at[at])

        up = remote(mine, up_buf.at[at], line_send.at[0, at], line_recv.at[0, at], {"expert": place.me + INNER})
        down = remote(mine, down_buf.at[at], line_send.at[1, at], line_recv.at[1, at], {"expert": place.me - INNER})
        for there, first, copy, buf in ((level < at, level == 0, up, up_buf), (level > at, level == outer - 1, down, down_buf)):
            @pl.when(there & first)
            def _():
                add_into(mine, mine, row_buf.at[at])

            @pl.when(there & ~first)
            def _():
                copy.wait_recv()
                add_into(mine, mine, row_buf.at[at], buf.at[at])

            sender.start(there, copy)
        yield
    for at in order:
        @pl.when(level == at)
        def _():
            mine = own_buf.at[slot(at, row_bit)]
            up = remote(mine, up_buf.at[at], line_send.at[0, at], line_recv.at[0, at], {"expert": place.me + INNER})
            down = remote(mine, down_buf.at[at], line_send.at[1, at], line_recv.at[1, at], {"expert": place.me - INNER})
            if at > 0:
                up.wait_recv()
            if at < outer - 1:
                down.wait_recv()
            if 0 < at < outer - 1:
                add_into(out_buf, mine, up_buf.at[at], down_buf.at[at])
            else:
                add_into(out_buf, mine, up_buf.at[at] if at else down_buf.at[at])
    done = pltpu.make_async_copy(out_buf, out_ref, out_sem)
    done.start()
    done.wait()
    yield


def reduce_scratch(group, rows, columns):
    outer = group // INNER
    bf = jnp.bfloat16
    return [
        pltpu.VMEM((2 * outer, rows, columns), bf),
        pltpu.VMEM((2 * outer, rows, columns), bf),
        pltpu.VMEM((outer, rows, columns), bf),
        pltpu.VMEM((outer, rows, columns), bf),
        pltpu.VMEM((outer, rows, columns), bf),
        pltpu.SemaphoreType.DMA((2 * outer,)),
        pltpu.SemaphoreType.DMA((2 * outer,)),
        pltpu.SemaphoreType.DMA((2 * outer,)),
        pltpu.SemaphoreType.DMA((outer,)),
        pltpu.SemaphoreType.DMA((outer,)),
        pltpu.SemaphoreType.DMA((2, outer)),
        pltpu.SemaphoreType.DMA((2, outer)),
        pltpu.VMEM((rows, columns), jnp.float32),
        pltpu.SemaphoreType.DMA(()),
    ]


class HeadRows:
    def __init__(self, started, received):
        self.started, self.received = started, received

    def wait(self):
        for there, local, copy, keep in self.started:
            @pl.when(there)
            def _():
                copy.wait_send()

            @pl.when(local)
            def _():
                keep.wait()
        for there, copy in self.received:
            @pl.when(there)
            def _():
                copy.wait_recv()


def head_rows(place, plane, shards, own_ref, out_ref, copy_sem, send_sem, recv_sem):
    count = own_ref.shape[0]
    number = place.shard * plane + place.me
    sequences = plane // place.group
    mine = place.shard * sequences + place.me // place.group
    started, received = [], []
    for index in range(count):
        target = place.local * count + index
        peer = {"shard": target // plane, "expert": lax.rem(target, plane)}
        copy = remote(own_ref.at[index], out_ref.at[mine], send_sem.at[index], recv_sem.at[mine], peer)
        keep = pltpu.make_async_copy(own_ref.at[index], out_ref.at[mine], copy_sem)

        @pl.when(target != number)
        def _():
            copy.start()

        @pl.when(target == number)
        def _():
            keep.start()

        started.append((target != number, target == number, copy, keep))
    for shard in range(shards):
        for sequence in range(sequences):
            source = shard * plane + sequence * place.group + number // count
            slot = shard * sequences + sequence
            peer = {"shard": source // plane, "expert": lax.rem(source, plane)}
            copy = remote(own_ref.at[0], out_ref.at[slot], send_sem.at[0], recv_sem.at[slot], peer)
            received.append((source != number, copy))
    return HeadRows(started, received), []


def bundle_kernel(group, shards, kinds, *refs):
    count = len(kinds)
    ins, outs, rest = refs[:count], refs[count : 2 * count], refs[2 * count :]
    place = Place(group)
    plane = lax.axis_size("expert")
    peers = []
    if "gather" in kinds or "reduce" in kinds:
        peers += place.neighbours()
    members = [{"expert": place.base + lax.rem(place.local + step, group)} for step in range(1, group)]
    if "trade" in kinds:
        peers = [(place.always, member) for member in members]
    across = [{"shard": lax.rem(place.shard + step, shards)} for step in range(1, shards)]
    if "swap" in kinds or "share" in kinds:
        peers += [(place.always, peer) for peer in across]
    everyone = []
    if "owners" in kinds or "rows" in kinds:
        total = shards * plane
        number = place.shard * plane + place.me
        for step in range(1, total):
            target = lax.rem(number + step, total)
            everyone.append((target, {"shard": target // plane, "expert": lax.rem(target, plane)}))
        peers = [(place.always, peer) for _, peer in everyone]
    greet(peers)
    sender = Sender()
    runs, waits = [], []
    for kind, own, out in zip(kinds, ins, outs):
        if kind == "gather":
            copy_sem, send_sem, recv_sem, *rest = rest
            runs.append(gather_steps(place, own, out, copy_sem, send_sem, recv_sem, sender))
        elif kind == "reduce":
            scratch, rest = rest[:14], rest[14:]
            runs.append(reduce_steps(place, own, out, scratch, sender))
        else:
            copy_sem, send_sem, recv_sem, *rest = rest
            if kind == "swap":
                mine, source = place.shard, lambda target: own
                targets = [(lax.rem(place.shard + step, shards), peer) for step, peer in enumerate(across, 1)]
            elif kind == "share":
                mine, source = place.shard, lambda target: own.at[target]
                targets = [(lax.rem(place.shard + step, shards), peer) for step, peer in enumerate(across, 1)]
            elif kind == "trade":
                mine, source = place.local, lambda target: own.at[target]
                targets = [(lax.rem(place.local + step, group), peer) for step, peer in enumerate(members, 1)]
            elif kind == "owners":
                mine, source = place.shard * plane + place.me, lambda target: own.at[target]
                targets = everyone
            else:
                waits.append(head_rows(place, plane, shards, own, out, copy_sem, send_sem, recv_sem))
                continue
            keep = pltpu.make_async_copy(source(mine), out.at[mine], copy_sem)
            keep.start()
            total = len(targets) + 1
            copies = []
            for step, (target, peer) in enumerate(targets, 1):
                copy = remote(source(target), out.at[mine], send_sem.at[step], recv_sem.at[step], peer)
                copy.start()
                copies.append(copy)
            waits.append((keep, copies))
    while runs:
        runs = [run for run in runs if next(run, "end") != "end"]
    for keep, copies in waits:
        keep.wait()
        for copy in copies:
            copy.wait()
    sender.finish()


def bundle(number, group, shards, transfers, limit=48 * 2**20):
    kinds, arrays, shapes, scratch = [], [], [], []
    members = shards * lax.axis_size("expert")
    for kind, array in transfers:
        kinds.append(kind)
        sems = [pltpu.SemaphoreType.DMA(())]
        if kind == "gather":
            pieces = PIECES if array.shape[0] % (16 * PIECES) == 0 else 1
            array = array.reshape((pieces, array.shape[0] // pieces) + array.shape[1:])
            shape = (group,) + array.shape
            sems += [pltpu.SemaphoreType.DMA((4, group, pieces)), pltpu.SemaphoreType.DMA((group, pieces))]
        elif kind == "reduce":
            shape = array.shape[1:]
            sems = reduce_scratch(group, *shape)
        else:
            total = {"swap": shards, "share": shards, "trade": group, "owners": members}.get(kind)
            shape = ((total,) + array.shape) if kind == "swap" else array.shape
            if kind == "rows":
                total = max(array.shape[0], members // group)
                shape = (members // group,) + array.shape[1:]
            sems += [pltpu.SemaphoreType.DMA((total,)), pltpu.SemaphoreType.DMA((total,))]
        arrays.append(array)
        shapes.append(jax.ShapeDtypeStruct(shape, jnp.float32 if kind == "reduce" else array.dtype))
        scratch += sems
    outs = pl.pallas_call(
        functools.partial(bundle_kernel, group, shards, tuple(kinds)),
        out_shape=shapes,
        in_specs=[pl.BlockSpec(memory_space=pl.ANY)] * len(arrays),
        out_specs=[pl.BlockSpec(memory_space=pl.ANY)] * len(arrays),
        scratch_shapes=scratch,
        compiler_params=pltpu.CompilerParams(
            collective_id=number, has_side_effects=True, vmem_limit_bytes=limit
        ),
        name="bundle_" + "_".join(kinds[:2]),
    )(*arrays)
    done = []
    for (kind, array), out in zip(transfers, outs):
        if kind == "gather":
            out = out.reshape((group,) + array.shape)
        done.append(out)
    return done


def tie(value, *awaited):
    return lax.optimization_barrier((value,) + awaited)


def other_blocks(pieces):
    count = lax.axis_size("shard")
    me = lax.axis_index("shard")
    return [
        lax.dynamic_index_in_dim(pieces, (me + step) % count, 0, keepdims=False)
        for step in range(1, count)
    ]


def other_rows(pieces):
    gathered = lax.all_gather(jnp.stack(other_blocks(pieces)), "expert", axis=1, tiled=True)
    return [gathered[step] for step in range(gathered.shape[0])]


def split_matmul(values, own, others):
    count = len(others) + 1
    me = lax.axis_index("shard")
    parts = values.reshape(values.shape[0], count, -1)
    total = 0.0
    for step, block in enumerate([own] + others):
        part = lax.dynamic_index_in_dim(parts, (me + step) % count, 1, keepdims=False)
        total = total + matmul(part, block)
    return total


def split_matmul_nt(values, own, others):
    count = len(others) + 1
    me = lax.axis_index("shard")
    whole = jnp.zeros((values.shape[0], count, own.shape[0]), jnp.float32)
    for step, block in enumerate([own] + others):
        whole = lax.dynamic_update_index_in_dim(
            whole, matmul_nt(values, block), (me + step) % count, 1
        )
    return whole.reshape(values.shape[0], -1)


def padded_rows(block):
    return jnp.pad(block, ((0, -block.shape[0] % 16), (0, 0)))


def shard_ring(block):
    count = lax.axis_size("shard")
    me = lax.axis_index("shard")
    whole = jnp.zeros((count,) + block.shape, block.dtype)
    whole = lax.dynamic_update_index_in_dim(whole, block, me, 0)
    for step in range(1, count):
        moved = lax.ppermute(
            block, "shard", [(source, (source + step) % count) for source in range(count)]
        )
        whole = lax.dynamic_update_index_in_dim(whole, moved, (me - step) % count, 0)
    return whole


def shard_rows(block):
    whole = shard_ring(block)
    return whole.reshape((-1,) + block.shape[1:])


def shard_sum(values):
    count = lax.axis_size("shard")
    me = lax.axis_index("shard")
    blocks = values.reshape((count, -1) + values.shape[1:])
    total = lax.dynamic_index_in_dim(blocks, me, 0, keepdims=False)
    for step in range(1, count):
        outgoing = lax.dynamic_index_in_dim(blocks, (me + step) % count, 0, keepdims=False)
        moved = lax.ppermute(
            outgoing.astype(jnp.bfloat16),
            "shard",
            [(source, (source + step) % count) for source in range(count)],
        )
        total = total + moved.astype(jnp.float32)
    return total


def on_device(
    tokens,
    document_lengths,
    routes,
    first_gain,
    query_weight,
    latent_down,
    latent_gain,
    latent_up,
    output_weight,
    second_gain,
    router_weight,
    shared_gate,
    shared_up,
    shared_down,
    expert_gate,
    expert_up,
    expert_down,
    cotangent,
):
    local_rows, width = tokens.shape
    shards = lax.axis_size("shard")
    plane = lax.axis_size("expert")
    everyone = ("shard", "expert")
    all_devices = shards * plane
    shard_at = lax.axis_index("shard")
    plane_at = lax.axis_index("expert")
    groups = plane_groups(plane)
    head_at = plane_at % SEQ_DEVICES
    sequence_at = (shard_at * plane + plane_at) // SEQ_DEVICES
    capacity = local_rows * TOP * 4 // (3 * plane)
    head_dim = QK_NOPE + QK_ROPE
    scale = 1.0 / math.sqrt(head_dim)
    own_at = head_at * local_rows

    def own_rows(values):
        return lax.dynamic_slice_in_dim(values, own_at, local_rows, 0)

    piece_rows = output_weight.shape[0] // plane
    tokens_all, query_pieces, down_pieces, up_pieces, out_pieces = bundle(
        1,
        SEQ_DEVICES,
        shards,
        [
            ("gather", tokens),
            ("swap", lax.dynamic_slice_in_dim(query_weight, head_at * head_dim, head_dim, 1)),
            ("swap", latent_down.T),
            (
                "swap",
                lax.dynamic_slice_in_dim(
                    latent_up, head_at * (QK_NOPE + V_HEAD), QK_NOPE + V_HEAD, 1
                ),
            ),
            ("swap", lax.dynamic_slice_in_dim(output_weight, plane_at * piece_rows, piece_rows, 0)),
        ],
    )
    query_head = query_pieces.reshape(width, head_dim)
    full_down = down_pieces.transpose(0, 2, 1).reshape(width, KV_RANK + QK_ROPE)
    up_head = up_pieces.reshape(KV_RANK, QK_NOPE + V_HEAD)
    other_out = other_rows(out_pieces)
    cotangent_late = tie(cotangent, other_out[0])[0]
    all_grads = lax.all_gather(cotangent_late, "expert", axis=0, tiled=True)
    units = shared_down.shape[0] // plane
    gate_columns, up_columns = (
        jnp.concatenate(
            [
                lax.dynamic_slice_in_dim(
                    weight, index * shared_down.shape[0] + plane_at * units, units, 1
                )
                for index in range(shards)
            ],
            axis=1,
        )
        for weight in (shared_gate, shared_up)
    )
    down_units = lax.dynamic_slice_in_dim(shared_down, plane_at * units, units, 0)

    all_tokens = tokens_all.reshape(SEQ, width).astype(jnp.float32)
    normed_one = norm_scale(all_tokens, first_gain).astype(jnp.bfloat16)
    positions = jnp.arange(SEQ, dtype=jnp.int32)
    cosine_part, sine_part = rotary_tables(positions, QK_ROPE)
    sequence_count, entry_count = document_lengths.shape
    ends = jnp.cumsum(document_lengths, axis=1)
    picked = jnp.arange(sequence_count, dtype=jnp.int32)[:, None] == sequence_at
    row_ends = jnp.sum(jnp.where(picked, ends, 0), axis=0)
    documents = jnp.sum((positions[:, None] >= row_ends[None, :]).astype(jnp.int32), axis=1)
    real = (documents < entry_count - 1).astype(jnp.float32)
    allowed = (
        (documents[:, None] == documents[None, :])
        & (positions[None, :] <= positions[:, None])
        & (positions[None, :] > positions[:, None] - WINDOW)
    )
    query = matmul(normed_one, query_head)
    query_nope = query[:, :QK_NOPE].astype(jnp.bfloat16)
    query_rope = rotate(query[:, QK_NOPE:], cosine_part, sine_part).astype(jnp.bfloat16)
    compressed = matmul(normed_one, full_down)
    key_latent = norm_scale(compressed[:, :KV_RANK], latent_gain).astype(jnp.bfloat16)
    key_rope = rotate(compressed[:, KV_RANK:], cosine_part, sine_part).astype(jnp.bfloat16)
    keys_values = matmul(key_latent, up_head).astype(jnp.bfloat16)
    key_nope = keys_values[:, :QK_NOPE]
    value = keys_values[:, QK_NOPE:]

    def scores_of():
        raw = matmul_nt(query_nope, key_nope) + matmul_nt(query_rope, key_rope)
        return jnp.where(allowed, raw * scale, NEG)

    scores = scores_of()
    top_score = jnp.max(scores, axis=1, keepdims=True)
    expo = jnp.exp(scores - top_score)
    expo_total = jnp.sum(expo, axis=1, keepdims=True)
    log_total = top_score + jnp.log(expo_total)
    probs = expo / expo_total
    head_out = (matmul(probs.astype(jnp.bfloat16), value) * real[:, None]).astype(jnp.bfloat16)
    gate_single = shard_rows(expert_gate[0])
    head_out, gate_single = tie(head_out, gate_single)
    heads_out, query_rows = bundle(
        2,
        SEQ_DEVICES,
        shards,
        [
            ("trade", head_out.reshape(SEQ_DEVICES, local_rows, V_HEAD)),
            ("swap", lax.dynamic_slice_in_dim(query_weight, plane_at * piece_rows, piece_rows, 0)),
        ],
    )
    heads_out = heads_out.transpose(1, 0, 2).reshape(local_rows, HEADS * V_HEAD)

    hidden_rows = tokens.astype(jnp.float32)
    middle = hidden_rows + split_matmul(heads_out, output_weight, other_out)
    second_normed = norm_scale(middle, second_gain).astype(jnp.bfloat16)

    all_normed, all_routes, up_single, gate_shared, up_shared, down_shared = bundle(
        3,
        plane,
        shards,
        [
            ("gather", second_normed),
            ("gather", jnp.pad(routes.T, ((0, 2), (0, 0)))),
            ("swap", expert_up[0]),
            ("swap", gate_columns.T),
            ("swap", up_columns.T),
            ("swap", padded_rows(down_units)),
        ],
    )
    all_normed = all_normed.reshape(-1, width)
    all_routes = all_routes[:, :TOP].transpose(0, 2, 1).reshape(-1, TOP)
    up_single = up_single.reshape(width, -1)
    gate_shared = gate_shared.transpose(0, 2, 1).reshape(width, -1)
    up_shared = up_shared.transpose(0, 2, 1).reshape(width, -1)
    down_shared = down_shared[:, :units].reshape(-1, width)
    down_single = shard_rows(expert_down[0])
    other_query = other_rows(tie(query_rows, all_grads)[0])
    plane_rows = plane * local_rows
    logits = matmul(all_normed, router_weight)
    expert_ids = jnp.arange(plane, dtype=jnp.int32)
    choose = all_routes[:, :, None] == expert_ids[None, None, :]
    chosen = jnp.sum(jnp.where(choose, logits[:, None, :], 0.0), axis=2)
    chosen_top = jnp.max(chosen, axis=1, keepdims=True)
    chosen_exp = jnp.exp(chosen - chosen_top)
    gate_values = chosen_exp / jnp.sum(chosen_exp, axis=1, keepdims=True)
    here = all_routes == plane_at
    gate_here = jnp.sum(jnp.where(here, gate_values, 0.0), axis=1).reshape(plane, local_rows)
    marks = jnp.any(here, axis=1).reshape(plane, local_rows)
    ranks = jnp.cumsum(marks.astype(jnp.int32), axis=1) - 1
    picks = marks[:, None, :] & (
        ranks[:, None, :] == jnp.arange(capacity, dtype=jnp.int32)[None, :, None]
    )
    select = picks.astype(jnp.bfloat16)

    def to_slots(values):
        return (
            jnp.einsum(
                "bct,btd->bcd",
                select,
                values.reshape(plane, local_rows, width),
                preferred_element_type=jnp.float32,
            )
            .astype(jnp.bfloat16)
            .reshape(plane * capacity, width)
        )

    def to_tokens(values):
        return jnp.einsum(
            "bct,bcd->btd",
            select,
            values.reshape(plane, capacity, width),
            preferred_element_type=jnp.float32,
        ).reshape(plane_rows, width)

    slot_rows = to_slots(all_normed)
    slot_cotangent = to_slots(all_grads).astype(jnp.float32)
    slot_gate = jnp.sum(jnp.where(picks, gate_here[:, None, :], 0.0), axis=2).reshape(-1, 1)
    gate_pre = matmul(slot_rows, gate_single)
    up_pre = matmul(slot_rows, up_single)
    swished, slope = swish_parts(gate_pre)
    hidden = (swished * up_pre).astype(jnp.bfloat16)
    expert_out = matmul(hidden, down_single).astype(jnp.bfloat16).astype(jnp.float32)
    slot_gate_grad = jnp.sum(slot_cotangent * expert_out, axis=1).reshape(plane, capacity)
    slot_grad = (slot_gate * slot_cotangent).astype(jnp.bfloat16)
    hidden_grad = matmul_nt(slot_grad, down_single)
    gate_pre_grad = (hidden_grad * up_pre * slope).astype(jnp.bfloat16)
    up_pre_grad = (hidden_grad * swished).astype(jnp.bfloat16)
    row_back = (
        matmul_nt(gate_pre_grad, gate_single) + matmul_nt(up_pre_grad, up_single)
    ).astype(jnp.bfloat16)

    shared_pre = matmul(all_normed, gate_shared)
    shared_up_pre = matmul(all_normed, up_shared)
    shared_swished, shared_slope = swish_parts(shared_pre)
    shared_hidden = (shared_swished * shared_up_pre).astype(jnp.bfloat16)
    shared_hidden_grad = matmul_nt(all_grads, down_shared)
    shared_gate_back = (shared_hidden_grad * shared_up_pre * shared_slope).astype(jnp.bfloat16)
    shared_up_back = (shared_hidden_grad * shared_swished).astype(jnp.bfloat16)

    normed_part = (
        to_tokens(row_back)
        + matmul_nt(shared_gate_back, gate_shared)
        + matmul_nt(shared_up_back, up_shared)
    ).astype(jnp.bfloat16)
    token_gate_grad = jnp.sum(jnp.where(picks, slot_gate_grad[:, :, None], 0.0), axis=1)
    expert_down_term = matmul_tn(hidden, slot_grad)
    back, gate_dense, down_blocks = bundle(
        4,
        plane,
        shards,
        [
            ("reduce", normed_part.reshape(plane, local_rows, width)),
            (
                "trade",
                jnp.broadcast_to(
                    token_gate_grad.reshape(plane, 1, local_rows), (plane, 8, local_rows)
                ),
            ),
            ("share", expert_down_term.astype(jnp.bfloat16).reshape(shards, -1, width)),
        ],
    )
    gate_dense = gate_dense[:, 0].T

    def sum_shards(term, blocks):
        own = lax.dynamic_index_in_dim(
            term.reshape((shards, -1) + term.shape[1:]), shard_at, 0, keepdims=False
        )
        for step in range(1, shards):
            own = own + lax.dynamic_index_in_dim(
                blocks, (shard_at + step) % shards, 0, keepdims=False
            ).astype(jnp.float32)
        return own

    expert_down_grad = sum_shards(expert_down_term, down_blocks)[None]
    output_part = (
        to_tokens((slot_gate * expert_out).astype(jnp.bfloat16))
        + matmul(shared_hidden, down_shared)
    ).astype(jnp.bfloat16)
    output_part = tie(output_part, back)[0]
    output_sum = lax.psum_scatter(output_part, "expert", scatter_dimension=0, tiled=True)
    activations = (middle + output_sum.astype(jnp.float32)).astype(jnp.bfloat16)
    expert_gate_grad = shard_sum(matmul_tn(slot_rows, gate_pre_grad))[None]
    expert_up_grad = shard_sum(matmul_tn(slot_rows, up_pre_grad))[None]
    shared_down_grad = shard_sum(matmul_tn(shared_hidden, all_grads))
    shared_term = jnp.concatenate(
        [matmul_tn(all_normed, shared_gate_back), matmul_tn(all_normed, shared_up_back)], axis=1
    )

    def to_owners(term):
        moved = lax.all_to_all(
            term.astype(jnp.bfloat16).reshape(all_devices, -1, term.shape[1]),
            everyone,
            split_axis=0,
            concat_axis=0,
            tiled=True,
        )
        moved = moved.reshape(shards, plane, -1, term.shape[1]).astype(jnp.float32)
        return jnp.sum(moved, axis=0)

    def by_head(moved):
        heads = moved.reshape((plane // SEQ_DEVICES, HEADS) + moved.shape[1:]).sum(axis=0)
        return heads.transpose(1, 0, 2).reshape(moved.shape[1], -1)

    shared_moved = to_owners(shared_term).reshape(plane, -1, 2, shards, units)
    shared_moved = shared_moved.transpose(2, 1, 3, 0, 4)
    shared_moved = shared_moved.reshape(2, shared_moved.shape[1], -1)
    shared_gate_grad = shared_moved[0]
    shared_up_grad = shared_moved[1]

    grad_out = cotangent.astype(jnp.float32)
    own_start = plane_at * local_rows
    own_gates = lax.dynamic_slice_in_dim(gate_values, own_start, local_rows, 0)
    own_choose = routes[:, :, None] == expert_ids[None, None, :]
    gate_grad = jnp.sum(jnp.where(own_choose, gate_dense[:, None, :], 0.0), axis=2)
    chosen_grad = own_gates * (
        gate_grad - jnp.sum(own_gates * gate_grad, axis=1, keepdims=True)
    )
    logit_grad = jnp.sum(jnp.where(own_choose, chosen_grad[:, :, None], 0.0), axis=1)
    router_term = lax.dot_general(
        second_normed.astype(jnp.float32),
        logit_grad,
        (((0,), (0,)), ((), ())),
        precision=HIGH,
        preferred_element_type=jnp.float32,
    )
    normed_grad = back + lax.dot_general(
        logit_grad,
        router_weight.astype(jnp.float32),
        (((1,), (1,)), ((), ())),
        precision=HIGH,
        preferred_element_type=jnp.float32,
    )
    unused_two, second_back = jax.vjp(norm_scale, middle, second_gain)
    middle_norm_grad, second_term = second_back(normed_grad)
    middle_grad = grad_out + middle_norm_grad
    middle_low = middle_grad.astype(jnp.bfloat16)
    small_sums = lax.psum_scatter(
        jnp.concatenate([router_term, second_term[:, None]], axis=1),
        everyone,
        scatter_dimension=0,
        tiled=True,
    )
    router_weight_grad = small_sums[:, :plane]
    second_gain_grad = small_sums[:, plane]

    heads_grad = split_matmul_nt(middle_low, output_weight, other_out).astype(jnp.bfloat16)
    heads_grad = heads_grad.reshape(local_rows, HEADS, V_HEAD).transpose(1, 0, 2)
    (head_grad,) = bundle(5, SEQ_DEVICES, shards, [("trade", heads_grad)])
    head_grad = head_grad.reshape(SEQ, V_HEAD)
    all_middle = lax.all_gather(
        tie(middle_low, head_grad)[0], "expert", axis=0, tiled=True, axis_index_groups=groups
    )
    head_grad = (head_grad.astype(jnp.float32) * real[:, None]).astype(jnp.bfloat16)
    again = jnp.exp(scores_of() - log_total)
    prob_grad = matmul_nt(head_grad, value)
    raw_grad = (
        again * (prob_grad - jnp.sum(again * prob_grad, axis=1, keepdims=True)) * scale
    ).astype(jnp.bfloat16)
    value_grad = matmul_tn(again.astype(jnp.bfloat16), head_grad)
    key_nope_grad = matmul_tn(raw_grad, query_nope)
    key_rope_grad = matmul_tn(raw_grad, query_rope)
    query_grad = jnp.concatenate(
        [
            matmul(raw_grad, key_nope),
            unrotate(matmul(raw_grad, key_rope), cosine_part, sine_part),
        ],
        axis=1,
    ).astype(jnp.bfloat16)
    pair_grad = jnp.concatenate([key_nope_grad, value_grad], axis=1).astype(jnp.bfloat16)
    latent_up_term = matmul_tn(key_latent, pair_grad)
    key_grad_part = jnp.concatenate(
        [
            matmul_nt(pair_grad, up_head),
            key_rope_grad,
            jnp.zeros((SEQ, -(KV_RANK + QK_ROPE) % 128), jnp.float32),
        ],
        axis=1,
    ).astype(jnp.bfloat16)
    own_key_grad, own_query_grad = bundle(
        6,
        SEQ_DEVICES,
        shards,
        [
            ("reduce", key_grad_part.reshape(SEQ_DEVICES, local_rows, -1)),
            ("trade", query_grad.reshape(SEQ_DEVICES, local_rows, head_dim)),
        ],
    )
    own_key_grad = own_key_grad[:, : KV_RANK + QK_ROPE]
    own_query_grad = own_query_grad.transpose(1, 0, 2).reshape(local_rows, HEADS * head_dim)
    own_compressed = own_rows(compressed)
    unused_latent, latent_back = jax.vjp(norm_scale, own_compressed[:, :KV_RANK], latent_gain)
    latent_in_grad, latent_gain_term = latent_back(own_key_grad[:, :KV_RANK])
    rope_in_grad = unrotate(
        own_key_grad[:, KV_RANK:], own_rows(cosine_part), own_rows(sine_part)
    )
    compressed_grad = jnp.concatenate([latent_in_grad, rope_in_grad], axis=1).astype(jnp.bfloat16)
    down_columns = (KV_RANK + QK_ROPE) // SEQ_DEVICES
    def owner_blocks(term):
        return term.astype(jnp.bfloat16).reshape(all_devices, -1, term.shape[1])

    def owner_sum(moved):
        blocks = moved.reshape((shards, plane) + moved.shape[1:]).astype(jnp.float32)
        return by_head(jnp.sum(blocks, axis=0))

    query_term = matmul_tn(normed_one, query_grad)
    column_grad, query_moved, up_moved = bundle(
        7,
        SEQ_DEVICES,
        shards,
        [
            (
                "trade",
                compressed_grad.reshape(local_rows, SEQ_DEVICES, down_columns).transpose(1, 0, 2),
            ),
            ("owners", owner_blocks(query_term)),
            ("owners", owner_blocks(latent_up_term)),
        ],
    )
    column_grad = column_grad.reshape(SEQ, down_columns)
    query_weight_grad = owner_sum(query_moved)
    latent_up_grad = owner_sum(up_moved)
    normed_one_grad = split_matmul_nt(
        own_query_grad, query_weight, other_query
    ) + matmul_nt(compressed_grad, full_down)
    unused_one, first_back = jax.vjp(norm_scale, hidden_rows, first_gain)
    input_norm_grad, first_term = first_back(normed_one_grad)
    input_grad = middle_grad + input_norm_grad
    down_term = matmul_tn(normed_one, column_grad)
    out_term = matmul_tn(head_out, all_middle.reshape(SEQ, width)).astype(jnp.bfloat16)
    gain_terms = jnp.concatenate(
        [
            first_term.reshape(all_devices, -1),
            latent_gain_term.reshape(all_devices, -1),
        ],
        axis=1,
    )
    gain_columns = gain_terms.shape[1]
    gain_terms = jnp.broadcast_to(
        jnp.pad(gain_terms, ((0, 0), (0, -gain_columns % 128)))[:, None],
        (all_devices, 8, gain_columns + -gain_columns % 128),
    )
    down_moved, gain_moved, out_moved = bundle(
        8,
        SEQ_DEVICES,
        shards,
        [
            ("owners", owner_blocks(down_term)),
            ("owners", gain_terms),
            ("rows", out_term.reshape(-1, width // all_devices, width)),
        ],
    )
    latent_down_grad = owner_sum(down_moved)
    output_weight_grad = jnp.sum(out_moved.astype(jnp.float32), axis=0)
    gain_sums = jnp.sum(gain_moved[:, 0, :gain_columns], axis=0)
    first_gain_grad = gain_sums[: width // all_devices]
    latent_gain_grad = gain_sums[width // all_devices :]
    return (
        activations,
        input_grad,
        first_gain_grad,
        query_weight_grad,
        latent_down_grad,
        latent_gain_grad,
        latent_up_grad,
        output_weight_grad,
        second_gain_grad,
        router_weight_grad,
        shared_gate_grad,
        shared_up_grad,
        shared_down_grad,
        expert_gate_grad,
        expert_up_grad,
        expert_down_grad,
    )


def solution(mesh):
    return jax.shard_map(
        on_device,
        mesh=mesh,
        in_specs=(
            P(("shard", "expert"), None),
            P(),
            P(("shard", "expert"), None),
            P(),
            P("shard", None),
            P("shard", None),
            P(),
            P("shard", None),
            P("shard", None),
            P(),
            P(),
            P("shard", None),
            P("shard", None),
            P("shard", None),
            P("expert", "shard", None),
            P("expert", "shard", None),
            P("expert", "shard", None),
            P(("shard", "expert"), None),
        ),
        out_specs=(
            P(("shard", "expert"), None),
            P(("shard", "expert"), None),
            P(("shard", "expert")),
            P(("shard", "expert"), None),
            P(("shard", "expert"), None),
            P(("shard", "expert")),
            P(("shard", "expert"), None),
            P(("shard", "expert"), None),
            P(("shard", "expert")),
            P(("shard", "expert"), None),
            P(("shard", "expert"), None),
            P(("shard", "expert"), None),
            P(("shard", "expert"), None),
            P("expert", "shard", None),
            P("expert", "shard", None),
            P("expert", "shard", None),
        ),
        check_vma=False,
    )
```

```python
import functools
import math

import jax
import jax.numpy as jnp
from jax import lax
from jax.experimental import pallas as pl
from jax.experimental.pallas import tpu as pltpu
from jax.sharding import PartitionSpec as P

HEADS = 16
QK_NOPE = 128
QK_ROPE = 64
V_HEAD = 128
KV_RANK = 512
TOP = 6
SEQ = 2048
WINDOW = 1024
TOK_DEV = 128
STEP_SENDERS = 4
SEQ_DEVICES = SEQ // TOK_DEV


EPS = 1e-06
THETA = 10000.0
NEG = -1e30
HIGH = lax.Precision.HIGHEST


def matmul(left, right):
    return jnp.dot(left, right, preferred_element_type=jnp.float32)


def matmul_tn(left, right):
    return lax.dot_general(
        left, right, (((0,), (0,)), ((), ())), preferred_element_type=jnp.float32
    )


def matmul_nt(left, right):
    return lax.dot_general(
        left, right, (((1,), (1,)), ((), ())), preferred_element_type=jnp.float32
    )


def norm_scale(values, gain):
    return values * lax.rsqrt(jnp.mean(values * values, axis=-1, keepdims=True) + EPS) * gain


def rotary_tables(positions, width):
    half = width // 2
    freqs = THETA ** (-jnp.arange(half, dtype=jnp.float32) / half)
    angles = positions.astype(jnp.float32)[:, None] * freqs[None, :]
    return (jnp.cos(angles), jnp.sin(angles))


def rotate(values, cosine_part, sine_part):
    half = values.shape[-1] // 2
    first = values[..., :half]
    second = values[..., half:]
    return jnp.concatenate(
        [first * cosine_part - second * sine_part, second * cosine_part + first * sine_part],
        axis=-1,
    )


def unrotate(values, cosine_part, sine_part):
    half = values.shape[-1] // 2
    first = values[..., :half]
    second = values[..., half:]
    return jnp.concatenate(
        [first * cosine_part + second * sine_part, second * cosine_part - first * sine_part],
        axis=-1,
    )


def swish_parts(values):
    sigmoid_part = jax.nn.sigmoid(values)
    return (values * sigmoid_part, sigmoid_part * (1.0 + values * (1.0 - sigmoid_part)))


def plane_groups(plane):
    members = SEQ_DEVICES
    if plane == members:
        return None
    return [list(range(low, low + members)) for low in range(0, plane, members)]


MESH = pl.DeviceIdType.MESH
INNER = 4
PIECES = 2


class Sender:
    def __init__(self):
        self.started = []

    def start(self, there, copy):
        @pl.when(there)
        def _():
            copy.start()

        self.started.append((there, copy))

    def finish(self):
        for there, copy in self.started:
            @pl.when(there)
            def _():
                copy.wait_send()


def remote(source, target, send_sem, recv_sem, place):
    return pltpu.make_async_remote_copy(
        src_ref=source,
        dst_ref=target,
        send_sem=send_sem,
        recv_sem=recv_sem,
        device_id=place,
        device_id_type=MESH,
    )


class Place:
    def __init__(self, group):
        self.me = lax.axis_index("expert")
        self.shard = lax.axis_index("shard")
        self.group = group
        self.outer = group // INNER
        self.local = lax.rem(self.me, group)
        self.base = self.me - self.local
        self.level = self.local // INNER
        inner = lax.rem(self.local, INNER)
        self.row_step = 2 - 4 * (inner // 2)
        self.twin_step = 1 - 2 * lax.rem(inner, 2)
        self.always = self.me >= 0
        self.upper = self.level < self.outer - 1
        self.lower = self.level > 0

    def neighbours(self):
        return [
            (self.upper, {"expert": self.me + INNER}),
            (self.lower, {"expert": self.me - INNER}),
            (self.always, {"expert": self.me + self.row_step}),
            (self.always, {"expert": self.me + self.twin_step}),
        ]

    def along(self, step):
        below = (self.level >= step, self.local - step * INNER, self.upper, self.me + INNER, 0)
        above = (self.level + step < self.outer, self.local + step * INNER, self.lower, self.me - INNER, 1)
        return (below, above)


def greet(peers):
    barrier = pltpu.get_barrier_semaphore()
    for there, peer in peers:
        @pl.when(there)
        def _():
            pl.semaphore_signal(barrier, inc=1, device_id=peer, device_id_type=MESH)
    pl.semaphore_wait(barrier, sum(there.astype(jnp.int32) for there, _ in peers))


def gather_steps(place, own_ref, out_ref, copy_sem, send_sem, recv_sem, sender):
    local = place.local
    row, twin = local + place.row_step, local + place.twin_step

    def push(kind, block, piece, target, source=None):
        spot = out_ref.at[block, piece]
        return remote(
            spot if source is None else source.at[piece],
            spot,
            send_sem.at[kind, block, piece],
            recv_sem.at[block, piece],
            {"expert": target},
        )

    def arrive(there, block, piece):
        @pl.when(there)
        def _():
            push(0, block, piece, place.me).wait_recv()

    pieces = own_ref.shape[0]
    row_at, twin_at = place.me + place.row_step, place.me + place.twin_step
    keep = pltpu.make_async_copy(own_ref, out_ref.at[local], copy_sem)
    keep.start()
    for piece in range(pieces):
        sender.start(place.upper, push(0, local, piece, place.me + INNER, own_ref))
        sender.start(place.lower, push(1, local, piece, place.me - INNER, own_ref))
        sender.start(place.always, push(2, local, piece, row_at, own_ref))
        sender.start(place.always, push(3, local, piece, twin_at, own_ref))
    yield
    for step in range(1, place.outer + 1):
        if step < place.outer:
            for piece in range(pieces):
                for there, block, onward, target, kind in place.along(step):
                    arrive(there, block, piece)
                    sender.start(there & onward, push(kind, block, piece, target))
                    sender.start(there, push(2, block, piece, row_at))
                    sender.start(there, push(3, block, piece, twin_at))
        for piece in range(pieces):
            for there, block, *_ in place.along(step - 1)[: 1 if step == 1 else 2]:
                arrive(there, block + place.row_step, piece)
                sender.start(there, push(3, block + place.row_step, piece, twin_at))
        yield
    for step in range(place.outer):
        for piece in range(pieces):
            for there, block, *_ in place.along(step)[: 1 if step == 0 else 2]:
                arrive(there, block + place.twin_step, piece)
                arrive(there, block + place.twin_step + place.row_step, piece)
    keep.wait()
    yield


def add_into(target, first, *others):
    rows = target.shape[0]
    chunk = 32

    def body(index, _):
        at = pl.ds(pl.multiple_of(index * chunk, chunk), chunk)
        total = first[at, :].astype(jnp.float32)
        for other in others:
            total = total + other[at, :].astype(jnp.float32)
        target[at, :] = total.astype(target.dtype)
        return 0

    lax.fori_loop(0, rows // chunk, body, 0)


def reduce_steps(place, part_ref, out_ref, scratch, sender):
    (own_buf, twin_buf, row_buf, line_buf, load_sem, twin_send, twin_recv, row_send, row_recv, line_send, line_recv,
     out_buf, out_sem) = scratch
    outer, local, level = place.outer, place.local, place.level
    pieces = part_ref.shape[1]
    inner = lax.rem(local, INNER)
    row_bit, core = inner // 2, lax.rem(inner, 2)
    twin_at, row_at = {"expert": place.me + place.twin_step}, {"expert": place.me + place.row_step}
    order = []
    low, high = 0, outer - 1
    while low <= high:
        order += [high] if low == high else [high, low]
        low, high = low + 1, high - 1
    units = [(at, piece) for at in order for piece in range(pieces)]
    bits = (1 - row_bit, row_bit)

    def loading(at, piece, bit):
        where = at * 2 + bit
        return pltpu.make_async_copy(
            part_ref.at[at * INNER + bit * 2 + core, piece], own_buf.at[where, piece], load_sem.at[where, piece]
        )

    def to_twin(at, piece, bit):
        where = at * 2 + bit
        return remote(
            part_ref.at[at * INNER + bit * 2 + 1 - core, piece],
            twin_buf.at[where, piece],
            twin_send.at[where, piece],
            twin_recv.at[where, piece],
            twin_at,
        )

    def to_row(at, piece):
        return remote(
            own_buf.at[at * 2 + bits[0], piece], row_buf.at[at, piece], row_send.at[at, piece], row_recv.at[at, piece], row_at
        )

    def mine(at, piece):
        return own_buf.at[at * 2 + row_bit, piece]

    def to_line(side, at, piece):
        return remote(
            mine(at, piece),
            line_buf.at[side, at, piece],
            line_send.at[side, at, piece],
            line_recv.at[side, at, piece],
            {"expert": place.me + (INNER if side == 0 else -INNER)},
        )

    for at, piece in units:
        for bit in bits:
            sender.start(place.always, to_twin(at, piece, bit))
            loading(at, piece, bit).start()
    yield
    for at, piece in units:
        for bit in bits:
            where = at * 2 + bit
            loading(at, piece, bit).wait()
            to_twin(at, piece, bit).wait_recv()
            add_into(own_buf.at[where, piece], own_buf.at[where, piece], twin_buf.at[where, piece])
            if bit is bits[0]:
                sender.start(place.always, to_row(at, piece))
    yield
    for at, piece in units:
        to_row(at, piece).wait_recv()
        spot, row = mine(at, piece), row_buf.at[at, piece]
        for side, there, first in ((0, level < at, level == 0), (1, level > at, level == outer - 1)):
            line = to_line(side, at, piece)

            @pl.when(there & first)
            def _():
                add_into(spot, spot, row)

            @pl.when(there & ~first)
            def _():
                line.wait_recv()
                add_into(spot, spot, row, line_buf.at[side, at, piece])

            sender.start(there, line)
    yield
    for at, piece in units:
        @pl.when(level == at)
        def _():
            parts = [mine(at, piece), row_buf.at[at, piece]]
            for side, there in ((0, at > 0), (1, at < outer - 1)):
                if there:
                    to_line(side, at, piece).wait_recv()
                    parts.append(line_buf.at[side, at, piece])
            add_into(out_buf.at[piece], *parts)
    done = pltpu.make_async_copy(out_buf, out_ref, out_sem)
    done.start()
    done.wait()
    yield


def reduce_scratch(group, pieces, rows, columns):
    outer = group // INNER
    bf = jnp.bfloat16
    pair, single, line = (2 * outer, pieces), (outer, pieces), (2, outer, pieces)
    block = (rows, columns)
    return [
        pltpu.VMEM(pair + block, bf),
        pltpu.VMEM(pair + block, bf),
        pltpu.VMEM(single + block, bf),
        pltpu.VMEM(line + block, bf),
        pltpu.SemaphoreType.DMA(pair),
        pltpu.SemaphoreType.DMA(pair),
        pltpu.SemaphoreType.DMA(pair),
        pltpu.SemaphoreType.DMA(single),
        pltpu.SemaphoreType.DMA(single),
        pltpu.SemaphoreType.DMA(line),
        pltpu.SemaphoreType.DMA(line),
        pltpu.VMEM((pieces,) + block, jnp.float32),
        pltpu.SemaphoreType.DMA(()),
    ]


class HeadRows:
    def __init__(self, started, received):
        self.started, self.received = started, received

    def wait(self):
        for there, local, copy, keep in self.started:
            @pl.when(there)
            def _():
                copy.wait_send()

            @pl.when(local)
            def _():
                keep.wait()
        for there, copy in self.received:
            @pl.when(there)
            def _():
                copy.wait_recv()


def head_rows(place, plane, shards, own_ref, out_ref, copy_sem, send_sem, recv_sem):
    count = own_ref.shape[0]
    number = place.shard * plane + place.me
    sequences = plane // place.group
    mine = place.shard * sequences + place.me // place.group
    started, received = [], []
    for index in range(count):
        target = place.local * count + index
        peer = {"shard": target // plane, "expert": lax.rem(target, plane)}
        copy = remote(own_ref.at[index], out_ref.at[mine], send_sem.at[index], recv_sem.at[mine], peer)
        keep = pltpu.make_async_copy(own_ref.at[index], out_ref.at[mine], copy_sem)

        @pl.when(target != number)
        def _():
            copy.start()

        @pl.when(target == number)
        def _():
            keep.start()

        started.append((target != number, target == number, copy, keep))
    for shard in range(shards):
        for sequence in range(sequences):
            source = shard * plane + sequence * place.group + number // count
            slot = shard * sequences + sequence
            peer = {"shard": source // plane, "expert": lax.rem(source, plane)}
            copy = remote(own_ref.at[0], out_ref.at[slot], send_sem.at[0], recv_sem.at[slot], peer)
            received.append((source != number, copy))
    return HeadRows(started, received), []


def bundle_kernel(group, shards, kinds, *refs):
    count = len(kinds)
    ins, outs, rest = refs[:count], refs[count : 2 * count], refs[2 * count :]
    place = Place(group)
    plane = lax.axis_size("expert")
    peers = []
    if "gather" in kinds or "reduce" in kinds:
        peers += place.neighbours()
    members = [{"expert": place.base + lax.rem(place.local + step, group)} for step in range(1, group)]
    if "trade" in kinds:
        peers = [(place.always, member) for member in members]
    across = [{"shard": lax.rem(place.shard + step, shards)} for step in range(1, shards)]
    if "swap" in kinds or "share" in kinds:
        peers += [(place.always, peer) for peer in across]
    everyone = []
    if "owners" in kinds or "rows" in kinds:
        total = shards * plane
        number = place.shard * plane + place.me
        for step in range(1, total):
            target = lax.rem(number + step, total)
            everyone.append((target, {"shard": target // plane, "expert": lax.rem(target, plane)}))
        peers = [(place.always, peer) for _, peer in everyone]
    greet(peers)
    sender = Sender()
    runs, waits = [], []
    for kind, own, out in zip(kinds, ins, outs):
        if kind == "gather":
            copy_sem, send_sem, recv_sem, *rest = rest
            runs.append(gather_steps(place, own, out, copy_sem, send_sem, recv_sem, sender))
        elif kind == "reduce":
            scratch, rest = rest[:13], rest[13:]
            runs.append(reduce_steps(place, own, out, scratch, sender))
        else:
            copy_sem, send_sem, recv_sem, *rest = rest
            if kind == "swap":
                mine, source = place.shard, lambda target: own
                targets = [(lax.rem(place.shard + step, shards), peer) for step, peer in enumerate(across, 1)]
            elif kind == "share":
                mine, source = place.shard, lambda target: own.at[target]
                targets = [(lax.rem(place.shard + step, shards), peer) for step, peer in enumerate(across, 1)]
            elif kind == "trade":
                mine, source = place.local, lambda target: own.at[target]
                targets = [(lax.rem(place.local + step, group), peer) for step, peer in enumerate(members, 1)]
            elif kind == "owners":
                mine, source = place.shard * plane + place.me, lambda target: own.at[target]
                targets = everyone
            else:
                waits.append(head_rows(place, plane, shards, own, out, copy_sem, send_sem, recv_sem))
                continue
            keep = pltpu.make_async_copy(source(mine), out.at[mine], copy_sem)
            keep.start()
            total = len(targets) + 1
            copies = []
            for step, (target, peer) in enumerate(targets, 1):
                copy = remote(source(target), out.at[mine], send_sem.at[step], recv_sem.at[step], peer)
                copy.start()
                copies.append(copy)
            waits.append((keep, copies))
    while runs:
        runs = [run for run in runs if next(run, "end") != "end"]
    for keep, copies in waits:
        keep.wait()
        for copy in copies:
            copy.wait()
    sender.finish()


def bundle(number, group, shards, transfers, limit=48 * 2**20):
    kinds, arrays, shapes, scratch = [], [], [], []
    members = shards * lax.axis_size("expert")
    for kind, array in transfers:
        kinds.append(kind)
        sems = [pltpu.SemaphoreType.DMA(())]
        if kind == "gather":
            pieces = PIECES if array.shape[0] % (16 * PIECES) == 0 else 1
            array = array.reshape((pieces, array.shape[0] // pieces) + array.shape[1:])
            shape = (group,) + array.shape
            sems += [pltpu.SemaphoreType.DMA((4, group, pieces)), pltpu.SemaphoreType.DMA((group, pieces))]
        elif kind == "reduce":
            pieces = 2 * PIECES
            array = array.reshape(group, pieces, array.shape[1] // pieces, array.shape[2])
            shape = array.shape[1:]
            sems = reduce_scratch(group, *shape)
        else:
            total = {"swap": shards, "share": shards, "trade": group, "owners": members}.get(kind)
            shape = ((total,) + array.shape) if kind == "swap" else array.shape
            if kind == "rows":
                total = max(array.shape[0], members // group)
                shape = (members // group,) + array.shape[1:]
            sems += [pltpu.SemaphoreType.DMA((total,)), pltpu.SemaphoreType.DMA((total,))]
        arrays.append(array)
        shapes.append(jax.ShapeDtypeStruct(shape, jnp.float32 if kind == "reduce" else array.dtype))
        scratch += sems
    outs = pl.pallas_call(
        functools.partial(bundle_kernel, group, shards, tuple(kinds)),
        out_shape=shapes,
        in_specs=[pl.BlockSpec(memory_space=pl.ANY)] * len(arrays),
        out_specs=[pl.BlockSpec(memory_space=pl.ANY)] * len(arrays),
        scratch_shapes=scratch,
        compiler_params=pltpu.CompilerParams(
            collective_id=number, has_side_effects=True, vmem_limit_bytes=limit
        ),
        name="bundle_" + "_".join(kinds[:2]),
    )(*arrays)
    done = []
    for (kind, array), out in zip(transfers, outs):
        if kind == "gather":
            out = out.reshape((group,) + array.shape)
        if kind == "reduce":
            out = out.reshape(array.shape[1:])
        done.append(out)
    return done


def pieces_of(size, most):
    return [(at, min(most, size - at)) for at in range(0, size, most)]


def expert_kernel(
    pick_ref, place_ref, gate_ref, rows_in, grads_in, gate_w, up_w, down_w, shared_gate_w, shared_up_w, shared_down_w,
    back_ref, out_ref, rows_ref, grad_ref, hidden_ref, gate_back_ref, up_back_ref, score_ref,
    shared_hidden_ref, shared_gate_back_ref, shared_up_back_ref, slot_cotangent,
):
    width = rows_in.shape[1]
    hidden_width = gate_w.shape[1]
    low = jnp.bfloat16
    gate = gate_ref[...]
    pick = pick_ref[0]

    def pick_step(index, _):
        at = pl.ds(pl.multiple_of(index * 512, 512), 512)
        rows_ref[:, at] = matmul(pick, rows_in[:, at]).astype(low)
        picked = matmul(pick, grads_in[:, at])
        slot_cotangent[:, at] = picked.astype(low)
        grad_ref[:, at] = (gate * picked).astype(low)
        return 0

    lax.fori_loop(0, width // 512, pick_step, 0)
    shared_pre = matmul(rows_in[...], shared_gate_w[...])
    shared_up = matmul(rows_in[...], shared_up_w[...])
    swished, slope = swish_parts(shared_pre)
    shared_hidden_ref[...] = (swished * shared_up).astype(low)
    shared_grad = matmul_nt(grads_in[...], shared_down_w[...])
    shared_gate_back_ref[...] = (shared_grad * shared_up * slope).astype(low)
    shared_up_back_ref[...] = (shared_grad * swished).astype(low)
    for at, size in pieces_of(hidden_width, 512):
        columns = slice(at, at + size)
        gate_pre = matmul(rows_ref[...], gate_w[:, columns])
        up_pre = matmul(rows_ref[...], up_w[:, columns])
        swished, slope = swish_parts(gate_pre)
        hidden_ref[:, columns] = (swished * up_pre).astype(low)
        hidden_grad = matmul_nt(grad_ref[...], down_w[columns, :])
        gate_back_ref[:, columns] = (hidden_grad * up_pre * slope).astype(low)
        up_back_ref[:, columns] = (hidden_grad * swished).astype(low)
    place = place_ref[0]

    def out_step(index, score):
        at = pl.ds(pl.multiple_of(index * 512, 512), 512)
        expert_out = matmul(hidden_ref[...], down_w[:, at]).astype(low).astype(jnp.float32)
        score = score + jnp.sum(expert_out * slot_cotangent[:, at].astype(jnp.float32), axis=1, keepdims=True)
        out = matmul(place, (gate * expert_out).astype(low)) + matmul(shared_hidden_ref[...], shared_down_w[:, at])
        out_ref[:, at] = out.astype(low)
        row_back = matmul_nt(gate_back_ref[...], gate_w[at, :]) + matmul_nt(up_back_ref[...], up_w[at, :])
        back = (
            matmul(place, row_back.astype(low))
            + matmul_nt(shared_gate_back_ref[...], shared_gate_w[at, :])
            + matmul_nt(shared_up_back_ref[...], shared_up_w[at, :])
        )
        back_ref[:, at] = back.astype(low)
        return score

    score = lax.fori_loop(0, width // 512, out_step, jnp.zeros((pick.shape[0], 1), jnp.float32))
    score_ref[...] = jnp.broadcast_to(score, score_ref.shape)


def expert_pass(pick, place, slot_gate, rows, grads, gate_w, up_w, down_w, shared_gate_w, shared_up_w, shared_down_w):
    steps, slots, tokens = pick.shape
    width, hidden_width = gate_w.shape
    shared_width = shared_gate_w.shape[1]
    low = jnp.bfloat16
    whole = lambda shape: pl.BlockSpec(shape, lambda i: (0, 0), pipeline_mode=pl.Buffered(1))
    by_step = lambda r, c: pl.BlockSpec((r, c), lambda i: (i, 0))
    total = steps * slots
    out_shape = [
        jax.ShapeDtypeStruct((steps * tokens, width), low),
        jax.ShapeDtypeStruct((steps * tokens, width), low),
        jax.ShapeDtypeStruct((total, width), low),
        jax.ShapeDtypeStruct((total, width), low),
        jax.ShapeDtypeStruct((total, hidden_width), low),
        jax.ShapeDtypeStruct((total, hidden_width), low),
        jax.ShapeDtypeStruct((total, hidden_width), low),
        jax.ShapeDtypeStruct((total, 128), jnp.float32),
        jax.ShapeDtypeStruct((steps * tokens, shared_width), low),
        jax.ShapeDtypeStruct((steps * tokens, shared_width), low),
        jax.ShapeDtypeStruct((steps * tokens, shared_width), low),
    ]
    return pl.pallas_call(
        expert_kernel,
        grid=(steps,),
        out_shape=out_shape,
        in_specs=[
            pl.BlockSpec((1, slots, tokens), lambda i: (i, 0, 0)),
            pl.BlockSpec((1, tokens, slots), lambda i: (i, 0, 0)),
            by_step(slots, 1),
            by_step(tokens, width),
            by_step(tokens, width),
            whole(gate_w.shape), whole(up_w.shape), whole(down_w.shape),
            whole(shared_gate_w.shape), whole(shared_up_w.shape), whole(shared_down_w.shape),
        ],
        out_specs=[
            by_step(tokens, width), by_step(tokens, width), by_step(slots, width), by_step(slots, width),
            by_step(slots, hidden_width), by_step(slots, hidden_width), by_step(slots, hidden_width), by_step(slots, 128),
            by_step(tokens, shared_width), by_step(tokens, shared_width), by_step(tokens, shared_width),
        ],
        scratch_shapes=[pltpu.VMEM((slots, width), low)],
        compiler_params=pltpu.CompilerParams(vmem_limit_bytes=60 * 2**20, dimension_semantics=("arbitrary",)),
        name="experts",
    )(pick, place, slot_gate, rows, grads, gate_w, up_w, down_w, shared_gate_w, shared_up_w, shared_down_w)


QUERIES = 256
KEYS = WINDOW + QUERIES


def score_block(step, scale, query, keys, query_docs, key_docs):
    raw = matmul_nt(query, keys) * scale
    row = lax.broadcasted_iota(jnp.int32, raw.shape, 0) + WINDOW
    column = lax.broadcasted_iota(jnp.int32, raw.shape, 1)
    allowed = (query_docs == key_docs) & (column <= row) & (column > row - WINDOW)
    return jnp.where(allowed, raw, NEG)


def attend_kernel(scale, last, query_ref, key_ref, value_ref, docs_ref, row_docs_ref, out_ref, total_ref):
    step = pl.program_id(0)
    at = pl.ds(pl.multiple_of(step * QUERIES, QUERIES), KEYS)
    scores = score_block(step, scale, query_ref[...], key_ref[at, :], docs_ref[...], row_docs_ref[:, at])
    top = jnp.max(scores, axis=1, keepdims=True)
    expo = jnp.exp(scores - top)
    total = jnp.sum(expo, axis=1, keepdims=True)
    probs = (expo / total).astype(jnp.bfloat16)
    real = jnp.where(docs_ref[...] < last, 1.0, 0.0)
    out_ref[...] = (matmul(probs, value_ref[at, :]) * real).astype(jnp.bfloat16)
    total_ref[...] = jnp.broadcast_to(top + jnp.log(total), total_ref.shape)


def attend_back_kernel(
    scale, last, query_ref, key_ref, value_ref, docs_ref, row_docs_ref, total_ref, grad_ref,
    query_grad_ref, key_grad_ref, value_grad_ref, key_sum, value_sum,
):
    step = pl.program_id(0)

    @pl.when(step == 0)
    def _():
        key_sum[...] = jnp.zeros_like(key_sum)
        value_sum[...] = jnp.zeros_like(value_sum)

    at = pl.ds(pl.multiple_of(step * QUERIES, QUERIES), KEYS)
    query, keys, grad = query_ref[...], key_ref[at, :], grad_ref[...]
    grad = jnp.where(docs_ref[...] < last, grad, jnp.zeros((), grad.dtype))
    scores = score_block(step, scale, query, keys, docs_ref[...], row_docs_ref[:, at])
    probs = jnp.exp(scores - total_ref[:, :1])
    prob_grad = matmul_nt(grad, value_ref[at, :])
    inner = jnp.sum(probs * prob_grad, axis=1, keepdims=True)
    raw_grad = (probs * (prob_grad - inner) * scale).astype(jnp.bfloat16)
    query_grad_ref[...] = matmul(raw_grad, keys)
    key_sum[at, :] += matmul_tn(raw_grad, query)
    value_sum[at, :] += matmul_tn(probs.astype(jnp.bfloat16), grad)

    @pl.when(step == pl.num_programs(0) - 1)
    def _():
        key_grad_ref[...] = key_sum[WINDOW:, :]
        value_grad_ref[...] = value_sum[WINDOW:, :]


def attend(scale, last, query, keys, value, docs, row_docs):
    rows, head_dim = query.shape
    whole = lambda a: pl.BlockSpec(a.shape, lambda i: (0, 0))
    by_step = lambda c: pl.BlockSpec((QUERIES, c), lambda i: (i, 0))
    return pl.pallas_call(
        functools.partial(attend_kernel, scale, last),
        grid=(rows // QUERIES,),
        out_shape=[jax.ShapeDtypeStruct((rows, V_HEAD), jnp.bfloat16), jax.ShapeDtypeStruct((rows, 128), jnp.float32)],
        in_specs=[by_step(head_dim), whole(keys), whole(value), by_step(1), whole(row_docs)],
        out_specs=[by_step(V_HEAD), by_step(128)],
        compiler_params=pltpu.CompilerParams(vmem_limit_bytes=48 * 2**20, dimension_semantics=("arbitrary",)),
        name="attend",
    )(query, keys, value, docs, row_docs)


def attend_back(scale, last, query, keys, value, docs, row_docs, totals, grad):
    rows, head_dim = query.shape
    whole = lambda a: pl.BlockSpec(a.shape, lambda i: (0, 0))
    by_step = lambda c: pl.BlockSpec((QUERIES, c), lambda i: (i, 0))
    full = lambda c: pl.BlockSpec((rows, c), lambda i: (0, 0))
    return pl.pallas_call(
        functools.partial(attend_back_kernel, scale, last),
        grid=(rows // QUERIES,),
        out_shape=[
            jax.ShapeDtypeStruct((rows, head_dim), jnp.float32),
            jax.ShapeDtypeStruct((rows, head_dim), jnp.float32),
            jax.ShapeDtypeStruct((rows, V_HEAD), jnp.float32),
        ],
        in_specs=[by_step(head_dim), whole(keys), whole(value), by_step(1), whole(row_docs), by_step(128), by_step(V_HEAD)],
        out_specs=[by_step(head_dim), full(head_dim), full(V_HEAD)],
        scratch_shapes=[pltpu.VMEM(keys.shape, jnp.float32), pltpu.VMEM(value.shape, jnp.float32)],
        compiler_params=pltpu.CompilerParams(vmem_limit_bytes=48 * 2**20, dimension_semantics=("arbitrary",)),
        name="attend_back",
    )(query, keys, value, docs, row_docs, totals, grad)


def front_kernel(tokens_ref, first_gain_ref, packed_ref, up_ref, latent_gain_ref, turn_ref, sway_ref,
                 normed_ref, query_ref, key_ref, value_ref, latent_ref, compressed_ref):
    low = jnp.bfloat16
    values = tokens_ref[...].astype(jnp.float32)
    r = lax.rsqrt(jnp.mean(values * values, axis=1, keepdims=True) + EPS)
    normed = (values * r * first_gain_ref[...]).astype(low)
    normed_ref[...] = normed
    rest = QK_NOPE + 4 * QK_ROPE
    first = matmul(normed, packed_ref[:, :rest])
    latent = matmul(normed, packed_ref[:, rest:])
    query_ref[:, :QK_NOPE] = first[:, :QK_NOPE].astype(low)
    plain = first[:, QK_NOPE : QK_NOPE + 2 * QK_ROPE]
    turned = (plain * turn_ref[...] + first[:, QK_NOPE + 2 * QK_ROPE :] * sway_ref[...]).astype(low)
    query_ref[:, QK_NOPE:] = turned[:, :QK_ROPE]
    compressed_ref[...] = latent
    r = lax.rsqrt(jnp.mean(latent * latent, axis=1, keepdims=True) + EPS)
    key_latent = (latent * r * latent_gain_ref[...]).astype(low)
    latent_ref[...] = key_latent
    both = matmul(key_latent, up_ref[...]).astype(low)
    key_ref[:, :QK_NOPE] = both[:, :QK_NOPE]
    key_ref[:, QK_NOPE:] = turned[:, QK_ROPE:]
    value_ref[...] = both[:, QK_NOPE:]


def front(tokens, first_gain, packed, up_head, latent_gain, turn, sway):
    rows, width = tokens.shape
    step = 256
    low = jnp.bfloat16
    whole = lambda a: pl.BlockSpec(a.shape, lambda i: (0, 0))
    by_step = lambda c: pl.BlockSpec((step, c), lambda i: (i, 0))
    head_dim = QK_NOPE + QK_ROPE
    return pl.pallas_call(
        front_kernel,
        grid=(rows // step,),
        out_shape=[
            jax.ShapeDtypeStruct((rows, width), low),
            jax.ShapeDtypeStruct((rows, head_dim), low),
            jax.ShapeDtypeStruct((rows, head_dim), low),
            jax.ShapeDtypeStruct((rows, V_HEAD), low),
            jax.ShapeDtypeStruct((rows, KV_RANK), low),
            jax.ShapeDtypeStruct((rows, KV_RANK), jnp.float32),
        ],
        in_specs=[by_step(width), whole(first_gain), whole(packed), whole(up_head), whole(latent_gain),
                  by_step(2 * QK_ROPE), by_step(2 * QK_ROPE)],
        out_specs=[by_step(width), by_step(head_dim), by_step(head_dim), by_step(V_HEAD), by_step(KV_RANK), by_step(KV_RANK)],
        compiler_params=pltpu.CompilerParams(vmem_limit_bytes=48 * 2**20, dimension_semantics=("arbitrary",)),
        name="front",
    )(tokens, first_gain, packed, up_head, latent_gain, turn, sway)


def tie(value, *awaited):
    return lax.optimization_barrier((value,) + awaited)


def other_blocks(pieces):
    count = lax.axis_size("shard")
    me = lax.axis_index("shard")
    return [
        lax.dynamic_index_in_dim(pieces, (me + step) % count, 0, keepdims=False)
        for step in range(1, count)
    ]


def other_rows(pieces):
    gathered = lax.all_gather(jnp.stack(other_blocks(pieces)), "expert", axis=1, tiled=True)
    return [gathered[step] for step in range(gathered.shape[0])]


def split_matmul(values, own, others):
    count = len(others) + 1
    me = lax.axis_index("shard")
    parts = values.reshape(values.shape[0], count, -1)
    total = 0.0
    for step, block in enumerate([own] + others):
        part = lax.dynamic_index_in_dim(parts, (me + step) % count, 1, keepdims=False)
        total = total + matmul(part, block)
    return total


def split_matmul_nt(values, own, others):
    count = len(others) + 1
    me = lax.axis_index("shard")
    whole = jnp.zeros((values.shape[0], count, own.shape[0]), jnp.float32)
    for step, block in enumerate([own] + others):
        whole = lax.dynamic_update_index_in_dim(
            whole, matmul_nt(values, block), (me + step) % count, 1
        )
    return whole.reshape(values.shape[0], -1)


def padded_rows(block):
    return jnp.pad(block, ((0, -block.shape[0] % 16), (0, 0)))


def shard_ring(block):
    count = lax.axis_size("shard")
    me = lax.axis_index("shard")
    whole = jnp.zeros((count,) + block.shape, block.dtype)
    whole = lax.dynamic_update_index_in_dim(whole, block, me, 0)
    for step in range(1, count):
        moved = lax.ppermute(
            block, "shard", [(source, (source + step) % count) for source in range(count)]
        )
        whole = lax.dynamic_update_index_in_dim(whole, moved, (me - step) % count, 0)
    return whole


def shard_rows(block):
    whole = shard_ring(block)
    return whole.reshape((-1,) + block.shape[1:])


def shard_sum(values):
    count = lax.axis_size("shard")
    me = lax.axis_index("shard")
    blocks = values.reshape((count, -1) + values.shape[1:])
    total = lax.dynamic_index_in_dim(blocks, me, 0, keepdims=False)
    for step in range(1, count):
        outgoing = lax.dynamic_index_in_dim(blocks, (me + step) % count, 0, keepdims=False)
        moved = lax.ppermute(
            outgoing.astype(jnp.bfloat16),
            "shard",
            [(source, (source + step) % count) for source in range(count)],
        )
        total = total + moved.astype(jnp.float32)
    return total


def on_device(
    tokens,
    document_lengths,
    routes,
    first_gain,
    query_weight,
    latent_down,
    latent_gain,
    latent_up,
    output_weight,
    second_gain,
    router_weight,
    shared_gate,
    shared_up,
    shared_down,
    expert_gate,
    expert_up,
    expert_down,
    cotangent,
):
    local_rows, width = tokens.shape
    shards = lax.axis_size("shard")
    plane = lax.axis_size("expert")
    everyone = ("shard", "expert")
    all_devices = shards * plane
    shard_at = lax.axis_index("shard")
    plane_at = lax.axis_index("expert")
    groups = plane_groups(plane)
    head_at = plane_at % SEQ_DEVICES
    sequence_at = (shard_at * plane + plane_at) // SEQ_DEVICES
    capacity = local_rows * TOP * 4 // (3 * plane)
    head_dim = QK_NOPE + QK_ROPE
    scale = 1.0 / math.sqrt(head_dim)
    own_at = head_at * local_rows

    def own_rows(values):
        return lax.dynamic_slice_in_dim(values, own_at, local_rows, 0)

    piece_rows = output_weight.shape[0] // plane
    half = QK_ROPE // 2
    query_columns = lax.dynamic_slice_in_dim(query_weight, head_at * head_dim, head_dim, 1)
    query_turn, key_turn = query_columns[:, QK_NOPE:], latent_down[:, KV_RANK:]
    packed_half = jnp.concatenate(
        [
            query_columns,
            key_turn,
            query_turn[:, half:],
            query_turn[:, :half],
            key_turn[:, half:],
            key_turn[:, :half],
            latent_down[:, :KV_RANK],
        ],
        axis=1,
    )
    tokens_all, packed, up_pieces, out_pieces = bundle(
        1,
        SEQ_DEVICES,
        shards,
        [
            ("gather", tokens),
            ("swap", packed_half),
            (
                "swap",
                lax.dynamic_slice_in_dim(
                    latent_up, head_at * (QK_NOPE + V_HEAD), QK_NOPE + V_HEAD, 1
                ),
            ),
            ("swap", lax.dynamic_slice_in_dim(output_weight, plane_at * piece_rows, piece_rows, 0)),
        ],
    )
    packed = packed.reshape(width, -1)
    up_head = up_pieces.reshape(KV_RANK, QK_NOPE + V_HEAD)
    other_out = other_rows(out_pieces)
    cotangent_late = tie(cotangent, other_out[0])[0]
    all_grads = lax.all_gather(cotangent_late, "expert", axis=0, tiled=True)
    units = shared_down.shape[0] // plane
    gate_columns, up_columns = (
        jnp.concatenate(
            [
                lax.dynamic_slice_in_dim(
                    weight, index * shared_down.shape[0] + plane_at * units, units, 1
                )
                for index in range(shards)
            ],
            axis=1,
        )
        for weight in (shared_gate, shared_up)
    )
    down_units = lax.dynamic_slice_in_dim(shared_down, plane_at * units, units, 0)

    positions = jnp.arange(SEQ, dtype=jnp.int32)
    cosine_part, sine_part = rotary_tables(positions, QK_ROPE)
    sequence_count, entry_count = document_lengths.shape
    ends = jnp.cumsum(document_lengths, axis=1)
    picked = jnp.arange(sequence_count, dtype=jnp.int32)[:, None] == sequence_at
    row_ends = jnp.sum(jnp.where(picked, ends, 0), axis=0)
    documents = jnp.sum((positions[:, None] >= row_ends[None, :]).astype(jnp.int32), axis=1)
    turn = jnp.tile(jnp.concatenate([cosine_part, cosine_part], axis=1), (1, 2))
    sway = jnp.tile(jnp.concatenate([-sine_part, sine_part], axis=1), (1, 2))
    normed_one, query, keys, value, key_latent, compressed = front(
        tokens_all.reshape(SEQ, width), first_gain[None], packed, up_head, latent_gain[None], turn, sway
    )
    ahead = ((WINDOW, 0), (0, 0))
    keys, value = jnp.pad(keys, ahead), jnp.pad(value, ahead)
    docs = documents[:, None]
    row_docs = jnp.pad(docs, ahead, constant_values=-1).T
    head_out, log_total = attend(scale, entry_count - 1, query, keys, value, docs, row_docs)
    gate_single = shard_rows(expert_gate[0])
    head_out, gate_single = tie(head_out, gate_single)
    heads_out, query_rows = bundle(
        2,
        SEQ_DEVICES,
        shards,
        [
            ("trade", head_out.reshape(SEQ_DEVICES, local_rows, V_HEAD)),
            ("swap", lax.dynamic_slice_in_dim(query_weight, plane_at * piece_rows, piece_rows, 0)),
        ],
    )
    heads_out = heads_out.transpose(1, 0, 2).reshape(local_rows, HEADS * V_HEAD)

    hidden_rows = tokens.astype(jnp.float32)
    middle = hidden_rows + split_matmul(heads_out, output_weight, other_out)
    second_normed = norm_scale(middle, second_gain).astype(jnp.bfloat16)

    all_normed, all_routes, up_single, gate_shared, up_shared, down_shared = bundle(
        3,
        plane,
        shards,
        [
            ("gather", second_normed),
            ("gather", jnp.pad(routes.T, ((0, 2), (0, 0)))),
            ("swap", expert_up[0]),
            ("swap", gate_columns.T),
            ("swap", up_columns.T),
            ("swap", padded_rows(down_units)),
        ],
    )
    all_normed = all_normed.reshape(-1, width)
    all_routes = all_routes[:, :TOP].transpose(0, 2, 1).reshape(-1, TOP)
    up_single = up_single.reshape(width, -1)
    gate_shared = gate_shared.transpose(0, 2, 1).reshape(width, -1)
    up_shared = up_shared.transpose(0, 2, 1).reshape(width, -1)
    down_shared = down_shared[:, :units].reshape(-1, width)
    down_single = shard_rows(expert_down[0])
    other_query = other_rows(tie(query_rows, all_grads)[0])
    plane_rows = plane * local_rows
    logits = matmul(all_normed, router_weight)
    expert_ids = jnp.arange(plane, dtype=jnp.int32)
    choose = all_routes[:, :, None] == expert_ids[None, None, :]
    chosen = jnp.sum(jnp.where(choose, logits[:, None, :], 0.0), axis=2)
    chosen_top = jnp.max(chosen, axis=1, keepdims=True)
    chosen_exp = jnp.exp(chosen - chosen_top)
    gate_values = chosen_exp / jnp.sum(chosen_exp, axis=1, keepdims=True)
    here = all_routes == plane_at
    gate_here = jnp.sum(jnp.where(here, gate_values, 0.0), axis=1).reshape(plane, local_rows)
    marks = jnp.any(here, axis=1).reshape(plane, local_rows)
    ranks = jnp.cumsum(marks.astype(jnp.int32), axis=1) - 1
    picks = marks[:, None, :] & (
        ranks[:, None, :] == jnp.arange(capacity, dtype=jnp.int32)[None, :, None]
    )
    senders = STEP_SENDERS
    steps = plane // senders
    pick = jnp.einsum(
        "sbct,bd->sbcdt",
        picks.reshape(steps, senders, capacity, local_rows).astype(jnp.bfloat16),
        jnp.eye(senders, dtype=jnp.bfloat16),
    ).reshape(steps, senders * capacity, senders * local_rows)
    slot_gate = jnp.sum(jnp.where(picks, gate_here[:, None, :], 0.0), axis=2).reshape(-1, 1)
    lanes = ((0, 0), (0, -(shards * units) % 128))
    (
        normed_part,
        output_part,
        slot_rows,
        slot_grad,
        hidden,
        gate_pre_grad,
        up_pre_grad,
        slot_gate_grad,
        shared_hidden,
        shared_gate_back,
        shared_up_back,
    ) = expert_pass(
        pick,
        pick.transpose(0, 2, 1),
        slot_gate,
        all_normed,
        all_grads,
        gate_single,
        up_single,
        down_single,
        jnp.pad(gate_shared, lanes),
        jnp.pad(up_shared, lanes),
        jnp.pad(down_shared, lanes[::-1]),
    )
    slot_gate_grad = slot_gate_grad[:, 0].reshape(plane, capacity)
    shared_hidden = shared_hidden[:, : shards * units]
    shared_gate_back = shared_gate_back[:, : shards * units]
    shared_up_back = shared_up_back[:, : shards * units]
    token_gate_grad = jnp.sum(jnp.where(picks, slot_gate_grad[:, :, None], 0.0), axis=1)
    expert_down_term = matmul_tn(hidden, slot_grad)
    back, gate_dense, down_blocks = bundle(
        4,
        plane,
        shards,
        [
            ("reduce", normed_part.reshape(plane, local_rows, width)),
            (
                "trade",
                jnp.broadcast_to(
                    token_gate_grad.reshape(plane, 1, local_rows), (plane, 8, local_rows)
                ),
            ),
            ("share", expert_down_term.astype(jnp.bfloat16).reshape(shards, -1, width)),
        ],
    )
    gate_dense = gate_dense[:, 0].T

    def sum_shards(term, blocks):
        own = lax.dynamic_index_in_dim(
            term.reshape((shards, -1) + term.shape[1:]), shard_at, 0, keepdims=False
        )
        for step in range(1, shards):
            own = own + lax.dynamic_index_in_dim(
                blocks, (shard_at + step) % shards, 0, keepdims=False
            ).astype(jnp.float32)
        return own

    expert_down_grad = sum_shards(expert_down_term, down_blocks)[None]
    output_part = tie(output_part, back)[0]
    output_sum = lax.psum_scatter(output_part, "expert", scatter_dimension=0, tiled=True)
    activations = (middle + output_sum.astype(jnp.float32)).astype(jnp.bfloat16)
    expert_gate_grad = shard_sum(matmul_tn(slot_rows, gate_pre_grad))[None]
    expert_up_grad = shard_sum(matmul_tn(slot_rows, up_pre_grad))[None]
    shared_down_grad = shard_sum(matmul_tn(shared_hidden, all_grads))
    shared_term = jnp.concatenate(
        [matmul_tn(all_normed, shared_gate_back), matmul_tn(all_normed, shared_up_back)], axis=1
    )

    def to_owners(term):
        moved = lax.all_to_all(
            term.astype(jnp.bfloat16).reshape(all_devices, -1, term.shape[1]),
            everyone,
            split_axis=0,
            concat_axis=0,
            tiled=True,
        )
        moved = moved.reshape(shards, plane, -1, term.shape[1]).astype(jnp.float32)
        return jnp.sum(moved, axis=0)

    def by_head(moved):
        heads = moved.reshape((plane // SEQ_DEVICES, HEADS) + moved.shape[1:]).sum(axis=0)
        return heads.transpose(1, 0, 2).reshape(moved.shape[1], -1)

    shared_moved = to_owners(shared_term).reshape(plane, -1, 2, shards, units)
    shared_moved = shared_moved.transpose(2, 1, 3, 0, 4)
    shared_moved = shared_moved.reshape(2, shared_moved.shape[1], -1)
    shared_gate_grad = shared_moved[0]
    shared_up_grad = shared_moved[1]

    grad_out = cotangent.astype(jnp.float32)
    own_start = plane_at * local_rows
    own_gates = lax.dynamic_slice_in_dim(gate_values, own_start, local_rows, 0)
    own_choose = routes[:, :, None] == expert_ids[None, None, :]
    gate_grad = jnp.sum(jnp.where(own_choose, gate_dense[:, None, :], 0.0), axis=2)
    chosen_grad = own_gates * (
        gate_grad - jnp.sum(own_gates * gate_grad, axis=1, keepdims=True)
    )
    logit_grad = jnp.sum(jnp.where(own_choose, chosen_grad[:, :, None], 0.0), axis=1)
    router_term = lax.dot_general(
        second_normed.astype(jnp.float32),
        logit_grad,
        (((0,), (0,)), ((), ())),
        precision=HIGH,
        preferred_element_type=jnp.float32,
    )
    normed_grad = back + lax.dot_general(
        logit_grad,
        router_weight.astype(jnp.float32),
        (((1,), (1,)), ((), ())),
        precision=HIGH,
        preferred_element_type=jnp.float32,
    )
    unused_two, second_back = jax.vjp(norm_scale, middle, second_gain)
    middle_norm_grad, second_term = second_back(normed_grad)
    middle_grad = grad_out + middle_norm_grad
    middle_low = middle_grad.astype(jnp.bfloat16)
    heads_grad = split_matmul_nt(middle_low, output_weight, other_out).astype(jnp.bfloat16)
    heads_grad = heads_grad.reshape(local_rows, HEADS, V_HEAD).transpose(1, 0, 2)
    (head_grad,) = bundle(5, SEQ_DEVICES, shards, [("trade", heads_grad)])
    head_grad = head_grad.reshape(SEQ, V_HEAD)
    all_middle = lax.all_gather(
        tie(middle_low, head_grad)[0], "expert", axis=0, tiled=True, axis_index_groups=groups
    )
    query_raw, keys_grad, value_grad = attend_back(
        scale, entry_count - 1, query, keys, value, docs, row_docs, log_total, head_grad
    )
    query_grad = jnp.concatenate(
        [query_raw[:, :QK_NOPE], unrotate(query_raw[:, QK_NOPE:], cosine_part, sine_part)],
        axis=1,
    ).astype(jnp.bfloat16)
    key_nope_grad, key_rope_grad = keys_grad[:, :QK_NOPE], keys_grad[:, QK_NOPE:]
    pair_grad = jnp.concatenate([key_nope_grad, value_grad], axis=1).astype(jnp.bfloat16)
    latent_up_term = matmul_tn(key_latent, pair_grad)
    key_grad_part = jnp.concatenate(
        [
            matmul_nt(pair_grad, up_head),
            key_rope_grad,
            jnp.zeros((SEQ, -(KV_RANK + QK_ROPE) % 128), jnp.float32),
        ],
        axis=1,
    ).astype(jnp.bfloat16)
    query_term = matmul_tn(normed_one, query_grad)
    query_moved, up_moved = (
        lax.all_to_all(
            term.astype(jnp.bfloat16).reshape(all_devices, -1, term.shape[1]),
            everyone,
            split_axis=0,
            concat_axis=0,
            tiled=True,
        )
        for term in (query_term, latent_up_term)
    )
    own_key_grad, own_query_grad = bundle(
        6,
        SEQ_DEVICES,
        shards,
        [
            ("reduce", key_grad_part.reshape(SEQ_DEVICES, local_rows, -1)),
            ("trade", query_grad.reshape(SEQ_DEVICES, local_rows, head_dim)),
        ],
    )
    own_key_grad = own_key_grad[:, : KV_RANK + QK_ROPE]
    own_query_grad = own_query_grad.transpose(1, 0, 2).reshape(local_rows, HEADS * head_dim)
    own_compressed = own_rows(compressed)
    unused_latent, latent_back = jax.vjp(norm_scale, own_compressed, latent_gain)
    latent_in_grad, latent_gain_term = latent_back(own_key_grad[:, :KV_RANK])
    rope_in_grad = unrotate(
        own_key_grad[:, KV_RANK:], own_rows(cosine_part), own_rows(sine_part)
    )
    compressed_grad = jnp.concatenate([latent_in_grad, rope_in_grad], axis=1).astype(jnp.bfloat16)
    down_columns = (KV_RANK + QK_ROPE) // SEQ_DEVICES
    def owner_blocks(term):
        return term.astype(jnp.bfloat16).reshape(all_devices, -1, term.shape[1])

    def owner_sum(moved):
        blocks = moved.reshape((shards, plane) + moved.shape[1:]).astype(jnp.float32)
        return by_head(jnp.sum(blocks, axis=0))

    column_grad = lax.all_to_all(
        compressed_grad.reshape(local_rows, SEQ_DEVICES, down_columns).transpose(1, 0, 2),
        "expert",
        split_axis=0,
        concat_axis=0,
        tiled=True,
        axis_index_groups=groups,
    )
    column_grad = column_grad.reshape(SEQ, down_columns)
    query_weight_grad = owner_sum(query_moved)
    latent_up_grad = owner_sum(up_moved)
    packed_rope = packed[:, head_dim : head_dim + QK_ROPE]
    packed_latent = packed[:, QK_NOPE + 4 * QK_ROPE :]
    normed_one_grad = (
        split_matmul_nt(own_query_grad, query_weight, other_query)
        + matmul_nt(compressed_grad[:, :KV_RANK], packed_latent)
        + matmul_nt(compressed_grad[:, KV_RANK:], packed_rope)
    )
    unused_one, first_back = jax.vjp(norm_scale, hidden_rows, first_gain)
    input_norm_grad, first_term = first_back(normed_one_grad)
    input_grad = middle_grad + input_norm_grad
    down_term = matmul_tn(normed_one, column_grad)
    out_term = matmul_tn(head_out, all_middle.reshape(SEQ, width)).astype(jnp.bfloat16)
    small_terms = jnp.concatenate(
        [
            router_term.reshape(all_devices, -1),
            second_term.reshape(all_devices, -1),
            first_term.reshape(all_devices, -1),
            latent_gain_term.reshape(all_devices, -1),
        ],
        axis=1,
    )
    small_count = small_terms.shape[1]
    small_terms = jnp.pad(small_terms, ((0, 0), (0, -small_count % 1024)))
    small_terms = small_terms.reshape(all_devices, -1, 128)
    down_moved, gain_moved, out_moved = bundle(
        8,
        SEQ_DEVICES,
        shards,
        [
            ("owners", owner_blocks(down_term)),
            ("owners", small_terms),
            ("rows", out_term.reshape(-1, width // all_devices, width)),
        ],
    )
    latent_down_grad = owner_sum(down_moved)
    output_weight_grad = jnp.sum(out_moved.astype(jnp.float32), axis=0)
    small_sums = jnp.sum(gain_moved, axis=0).reshape(-1)[:small_count]
    own_width = width // all_devices
    at_second = own_width * plane
    router_weight_grad = small_sums[:at_second].reshape(own_width, plane)
    second_gain_grad = small_sums[at_second : at_second + own_width]
    first_gain_grad = small_sums[at_second + own_width : at_second + 2 * own_width]
    latent_gain_grad = small_sums[at_second + 2 * own_width :]
    return (
        activations,
        input_grad,
        first_gain_grad,
        query_weight_grad,
        latent_down_grad,
        latent_gain_grad,
        latent_up_grad,
        output_weight_grad,
        second_gain_grad,
        router_weight_grad,
        shared_gate_grad,
        shared_up_grad,
        shared_down_grad,
        expert_gate_grad,
        expert_up_grad,
        expert_down_grad,
    )


def solution(mesh):
    return jax.shard_map(
        on_device,
        mesh=mesh,
        in_specs=(
            P(("shard", "expert"), None),
            P(),
            P(("shard", "expert"), None),
            P(),
            P("shard", None),
            P("shard", None),
            P(),
            P("shard", None),
            P("shard", None),
            P(),
            P(),
            P("shard", None),
            P("shard", None),
            P("shard", None),
            P("expert", "shard", None),
            P("expert", "shard", None),
            P("expert", "shard", None),
            P(("shard", "expert"), None),
        ),
        out_specs=(
            P(("shard", "expert"), None),
            P(("shard", "expert"), None),
            P(("shard", "expert")),
            P(("shard", "expert"), None),
            P(("shard", "expert"), None),
            P(("shard", "expert")),
            P(("shard", "expert"), None),
            P(("shard", "expert"), None),
            P(("shard", "expert")),
            P(("shard", "expert"), None),
            P(("shard", "expert"), None),
            P(("shard", "expert"), None),
            P(("shard", "expert"), None),
            P("expert", "shard", None),
            P("expert", "shard", None),
            P("expert", "shard", None),
        ),
        check_vma=False,
    )
```

```python
import functools
import math

import jax
import jax.numpy as jnp
from jax import lax
from jax.experimental import pallas as pl
from jax.experimental.pallas import tpu as pltpu
from jax.sharding import PartitionSpec as P

HEADS = 16
QK_NOPE = 128
QK_ROPE = 64
V_HEAD = 128
KV_RANK = 512
TOP = 6
SEQ = 2048
WINDOW = 1024
TOK_DEV = 128
STEP_SENDERS = 4
SEQ_DEVICES = SEQ // TOK_DEV


EPS = 1e-06
THETA = 10000.0
NEG = -1e30
HIGH = lax.Precision.HIGHEST


def matmul(left, right):
    return jnp.dot(left, right, preferred_element_type=jnp.float32)


def matmul_tn(left, right):
    return lax.dot_general(
        left, right, (((0,), (0,)), ((), ())), preferred_element_type=jnp.float32
    )


def matmul_nt(left, right):
    return lax.dot_general(
        left, right, (((1,), (1,)), ((), ())), preferred_element_type=jnp.float32
    )


def norm_scale(values, gain):
    return values * lax.rsqrt(jnp.mean(values * values, axis=-1, keepdims=True) + EPS) * gain


def rotary_tables(positions, width):
    half = width // 2
    freqs = THETA ** (-jnp.arange(half, dtype=jnp.float32) / half)
    angles = positions.astype(jnp.float32)[:, None] * freqs[None, :]
    return (jnp.cos(angles), jnp.sin(angles))


def rotate(values, cosine_part, sine_part):
    half = values.shape[-1] // 2
    first = values[..., :half]
    second = values[..., half:]
    return jnp.concatenate(
        [first * cosine_part - second * sine_part, second * cosine_part + first * sine_part],
        axis=-1,
    )


def unrotate(values, cosine_part, sine_part):
    half = values.shape[-1] // 2
    first = values[..., :half]
    second = values[..., half:]
    return jnp.concatenate(
        [first * cosine_part + second * sine_part, second * cosine_part - first * sine_part],
        axis=-1,
    )


def swish_parts(values):
    sigmoid_part = jax.nn.sigmoid(values)
    return (values * sigmoid_part, sigmoid_part * (1.0 + values * (1.0 - sigmoid_part)))


def plane_groups(plane):
    members = SEQ_DEVICES
    if plane == members:
        return None
    return [list(range(low, low + members)) for low in range(0, plane, members)]


MESH = pl.DeviceIdType.MESH
INNER = 4
PIECES = 2


class Sender:
    def __init__(self):
        self.started = []

    def start(self, there, copy):
        @pl.when(there)
        def _():
            copy.start()

        self.started.append((there, copy))

    def finish(self):
        for there, copy in self.started:
            @pl.when(there)
            def _():
                copy.wait_send()


def remote(source, target, send_sem, recv_sem, place):
    return pltpu.make_async_remote_copy(
        src_ref=source,
        dst_ref=target,
        send_sem=send_sem,
        recv_sem=recv_sem,
        device_id=place,
        device_id_type=MESH,
    )


class Place:
    def __init__(self, group):
        self.me = lax.axis_index("expert")
        self.shard = lax.axis_index("shard")
        self.group = group
        self.outer = group // INNER
        self.local = lax.rem(self.me, group)
        self.base = self.me - self.local
        self.level = self.local // INNER
        inner = lax.rem(self.local, INNER)
        self.row_step = 2 - 4 * (inner // 2)
        self.twin_step = 1 - 2 * lax.rem(inner, 2)
        self.always = self.me >= 0
        self.upper = self.level < self.outer - 1
        self.lower = self.level > 0

    def neighbours(self):
        return [
            (self.upper, {"expert": self.me + INNER}),
            (self.lower, {"expert": self.me - INNER}),
            (self.always, {"expert": self.me + self.row_step}),
            (self.always, {"expert": self.me + self.twin_step}),
        ]

    def along(self, step):
        below = (self.level >= step, self.local - step * INNER, self.upper, self.me + INNER, 0)
        above = (self.level + step < self.outer, self.local + step * INNER, self.lower, self.me - INNER, 1)
        return (below, above)


def greet(peers):
    barrier = pltpu.get_barrier_semaphore()
    for there, peer in peers:
        @pl.when(there)
        def _():
            pl.semaphore_signal(barrier, inc=1, device_id=peer, device_id_type=MESH)
    pl.semaphore_wait(barrier, sum(there.astype(jnp.int32) for there, _ in peers))


def gather_steps(place, own_ref, out_ref, copy_sem, send_sem, recv_sem, sender):
    local = place.local
    row, twin = local + place.row_step, local + place.twin_step

    def push(kind, block, piece, target, source=None):
        spot = out_ref.at[block, piece]
        return remote(
            spot if source is None else source.at[piece],
            spot,
            send_sem.at[kind, block, piece],
            recv_sem.at[block, piece],
            {"expert": target},
        )

    def arrive(there, block, piece):
        @pl.when(there)
        def _():
            push(0, block, piece, place.me).wait_recv()

    pieces = out_ref.shape[1]
    if own_ref is None:
        own_ref = out_ref.at[local]
    else:
        keep = pltpu.make_async_copy(own_ref, out_ref.at[local], copy_sem)
        keep.start()
    row_at, twin_at = place.me + place.row_step, place.me + place.twin_step
    for piece in range(pieces):
        sender.start(place.upper, push(0, local, piece, place.me + INNER, own_ref))
        sender.start(place.lower, push(1, local, piece, place.me - INNER, own_ref))
        sender.start(place.always, push(2, local, piece, row_at, own_ref))
        sender.start(place.always, push(3, local, piece, twin_at, own_ref))
    yield
    for step in range(1, place.outer + 1):
        if step < place.outer:
            for piece in range(pieces):
                for there, block, onward, target, kind in place.along(step):
                    arrive(there, block, piece)
                    sender.start(there & onward, push(kind, block, piece, target))
                    sender.start(there, push(2, block, piece, row_at))
                    sender.start(there, push(3, block, piece, twin_at))
        for piece in range(pieces):
            for there, block, *_ in place.along(step - 1)[: 1 if step == 1 else 2]:
                arrive(there, block + place.row_step, piece)
                sender.start(there, push(3, block + place.row_step, piece, twin_at))
        yield
    for step in range(place.outer):
        for piece in range(pieces):
            for there, block, *_ in place.along(step)[: 1 if step == 0 else 2]:
                arrive(there, block + place.twin_step, piece)
                arrive(there, block + place.twin_step + place.row_step, piece)
    if copy_sem is not None:
        keep.wait()
    yield


def add_into(target, first, *others):
    rows = target.shape[0]
    chunk = 32

    def body(index, _):
        at = pl.ds(pl.multiple_of(index * chunk, chunk), chunk)
        total = first[at, :].astype(jnp.float32)
        for other in others:
            total = total + other[at, :].astype(jnp.float32)
        target[at, :] = total.astype(target.dtype)
        return 0

    lax.fori_loop(0, rows // chunk, body, 0)


def reduce_steps(place, part_ref, out_ref, scratch, sender):
    (own_buf, twin_buf, row_buf, line_buf, load_sem, twin_send, twin_recv, row_send, row_recv, line_send, line_recv,
     out_buf, out_sem) = scratch
    outer, local, level = place.outer, place.local, place.level
    pieces = part_ref.shape[1]
    inner = lax.rem(local, INNER)
    row_bit, core = inner // 2, lax.rem(inner, 2)
    twin_at, row_at = {"expert": place.me + place.twin_step}, {"expert": place.me + place.row_step}
    order = []
    low, high = 0, outer - 1
    while low <= high:
        order += [high] if low == high else [high, low]
        low, high = low + 1, high - 1
    units = [(at, piece) for at in order for piece in range(pieces)]
    bits = (1 - row_bit, row_bit)

    def loading(at, piece, bit):
        where = at * 2 + bit
        return pltpu.make_async_copy(
            part_ref.at[at * INNER + bit * 2 + core, piece], own_buf.at[where, piece], load_sem.at[where, piece]
        )

    def to_twin(at, piece, bit):
        where = at * 2 + bit
        return remote(
            part_ref.at[at * INNER + bit * 2 + 1 - core, piece],
            twin_buf.at[where, piece],
            twin_send.at[where, piece],
            twin_recv.at[where, piece],
            twin_at,
        )

    def to_row(at, piece):
        return remote(
            own_buf.at[at * 2 + bits[0], piece], row_buf.at[at, piece], row_send.at[at, piece], row_recv.at[at, piece], row_at
        )

    def mine(at, piece):
        return own_buf.at[at * 2 + row_bit, piece]

    def to_line(side, at, piece):
        return remote(
            mine(at, piece),
            line_buf.at[side, at, piece],
            line_send.at[side, at, piece],
            line_recv.at[side, at, piece],
            {"expert": place.me + (INNER if side == 0 else -INNER)},
        )

    for at, piece in units:
        for bit in bits:
            sender.start(place.always, to_twin(at, piece, bit))
            loading(at, piece, bit).start()
    yield
    for at, piece in units:
        for bit in bits:
            where = at * 2 + bit
            loading(at, piece, bit).wait()
            to_twin(at, piece, bit).wait_recv()
            add_into(own_buf.at[where, piece], own_buf.at[where, piece], twin_buf.at[where, piece])
            if bit is bits[0]:
                sender.start(place.always, to_row(at, piece))
    yield
    for at, piece in units:
        to_row(at, piece).wait_recv()
        spot, row = mine(at, piece), row_buf.at[at, piece]
        for side, there, first in ((0, level < at, level == 0), (1, level > at, level == outer - 1)):
            line = to_line(side, at, piece)

            @pl.when(there & first)
            def _():
                add_into(spot, spot, row)

            @pl.when(there & ~first)
            def _():
                line.wait_recv()
                add_into(spot, spot, row, line_buf.at[side, at, piece])

            sender.start(there, line)
    yield
    for at, piece in units:
        @pl.when(level == at)
        def _():
            parts = [mine(at, piece), row_buf.at[at, piece]]
            for side, there in ((0, at > 0), (1, at < outer - 1)):
                if there:
                    to_line(side, at, piece).wait_recv()
                    parts.append(line_buf.at[side, at, piece])
            add_into(out_buf.at[piece], *parts)
    done = pltpu.make_async_copy(out_buf, out_ref, out_sem)
    done.start()
    done.wait()
    yield


def reduce_scratch(group, pieces, rows, columns):
    outer = group // INNER
    bf = jnp.bfloat16
    pair, single, line = (2 * outer, pieces), (outer, pieces), (2, outer, pieces)
    block = (rows, columns)
    return [
        pltpu.VMEM(pair + block, bf),
        pltpu.VMEM(pair + block, bf),
        pltpu.VMEM(single + block, bf),
        pltpu.VMEM(line + block, bf),
        pltpu.SemaphoreType.DMA(pair),
        pltpu.SemaphoreType.DMA(pair),
        pltpu.SemaphoreType.DMA(pair),
        pltpu.SemaphoreType.DMA(single),
        pltpu.SemaphoreType.DMA(single),
        pltpu.SemaphoreType.DMA(line),
        pltpu.SemaphoreType.DMA(line),
        pltpu.VMEM((pieces,) + block, jnp.float32),
        pltpu.SemaphoreType.DMA(()),
    ]


class HeadRows:
    def __init__(self, started, received):
        self.started, self.received = started, received

    def wait(self):
        for there, local, copy, keep in self.started:
            @pl.when(there)
            def _():
                copy.wait_send()

            @pl.when(local)
            def _():
                keep.wait()
        for there, copy in self.received:
            @pl.when(there)
            def _():
                copy.wait_recv()


def head_rows(place, plane, shards, own_ref, out_ref, copy_sem, send_sem, recv_sem):
    count = own_ref.shape[0]
    number = place.shard * plane + place.me
    sequences = plane // place.group
    mine = place.shard * sequences + place.me // place.group
    started, received = [], []
    for index in range(count):
        target = place.local * count + index
        peer = {"shard": target // plane, "expert": lax.rem(target, plane)}
        copy = remote(own_ref.at[index], out_ref.at[mine], send_sem.at[index], recv_sem.at[mine], peer)
        keep = pltpu.make_async_copy(own_ref.at[index], out_ref.at[mine], copy_sem)

        @pl.when(target != number)
        def _():
            copy.start()

        @pl.when(target == number)
        def _():
            keep.start()

        started.append((target != number, target == number, copy, keep))
    for shard in range(shards):
        for sequence in range(sequences):
            source = shard * plane + sequence * place.group + number // count
            slot = shard * sequences + sequence
            peer = {"shard": source // plane, "expert": lax.rem(source, plane)}
            copy = remote(own_ref.at[0], out_ref.at[slot], send_sem.at[0], recv_sem.at[slot], peer)
            received.append((source != number, copy))
    return HeadRows(started, received), []


def bundle_kernel(group, shards, kinds, *refs):
    count = len(kinds)
    ins, outs, rest = refs[:count], refs[count : 2 * count], refs[2 * count :]
    place = Place(group)
    plane = lax.axis_size("expert")
    peers = []
    if "gather" in kinds or "reduce" in kinds:
        peers += place.neighbours()
    members = [{"expert": place.base + lax.rem(place.local + step, group)} for step in range(1, group)]
    if "trade" in kinds:
        peers = [(place.always, member) for member in members]
    across = [{"shard": lax.rem(place.shard + step, shards)} for step in range(1, shards)]
    if "swap" in kinds or "share" in kinds:
        peers += [(place.always, peer) for peer in across]
    everyone = []
    if "owners" in kinds or "rows" in kinds:
        total = shards * plane
        number = place.shard * plane + place.me
        for step in range(1, total):
            target = lax.rem(number + step, total)
            everyone.append((target, {"shard": target // plane, "expert": lax.rem(target, plane)}))
        peers = [(place.always, peer) for _, peer in everyone]
    greet(peers)
    sender = Sender()
    runs, waits = [], []
    for kind, own, out in zip(kinds, ins, outs):
        if kind == "gather":
            copy_sem, send_sem, recv_sem, *rest = rest
            runs.append(gather_steps(place, own, out, copy_sem, send_sem, recv_sem, sender))
        elif kind == "reduce":
            scratch, rest = rest[:13], rest[13:]
            runs.append(reduce_steps(place, own, out, scratch, sender))
        else:
            copy_sem, send_sem, recv_sem, *rest = rest
            if kind == "swap":
                mine, source = place.shard, lambda target: own
                targets = [(lax.rem(place.shard + step, shards), peer) for step, peer in enumerate(across, 1)]
            elif kind == "share":
                mine, source = place.shard, lambda target: own.at[target]
                targets = [(lax.rem(place.shard + step, shards), peer) for step, peer in enumerate(across, 1)]
            elif kind == "trade":
                mine, source = place.local, lambda target: own.at[target]
                targets = [(lax.rem(place.local + step, group), peer) for step, peer in enumerate(members, 1)]
            elif kind == "owners":
                mine, source = place.shard * plane + place.me, lambda target: own.at[target]
                targets = everyone
            else:
                waits.append(head_rows(place, plane, shards, own, out, copy_sem, send_sem, recv_sem))
                continue
            keep = pltpu.make_async_copy(source(mine), out.at[mine], copy_sem)
            keep.start()
            total = len(targets) + 1
            copies = []
            for step, (target, peer) in enumerate(targets, 1):
                copy = remote(source(target), out.at[mine], send_sem.at[step], recv_sem.at[step], peer)
                copy.start()
                copies.append(copy)
            waits.append((keep, copies))
    while runs:
        runs = [run for run in runs if next(run, "end") != "end"]
    for keep, copies in waits:
        keep.wait()
        for copy in copies:
            copy.wait()
    sender.finish()


def bundle(number, group, shards, transfers, limit=48 * 2**20):
    kinds, arrays, shapes, scratch = [], [], [], []
    members = shards * lax.axis_size("expert")
    for kind, array in transfers:
        kinds.append(kind)
        sems = [pltpu.SemaphoreType.DMA(())]
        if kind == "gather":
            pieces = PIECES if array.shape[0] % (16 * PIECES) == 0 else 1
            array = array.reshape((pieces, array.shape[0] // pieces) + array.shape[1:])
            shape = (group,) + array.shape
            sems += [pltpu.SemaphoreType.DMA((4, group, pieces)), pltpu.SemaphoreType.DMA((group, pieces))]
        elif kind == "reduce":
            pieces = 2 * PIECES
            array = array.reshape(group, pieces, array.shape[1] // pieces, array.shape[2])
            shape = array.shape[1:]
            sems = reduce_scratch(group, *shape)
        else:
            total = {"swap": shards, "share": shards, "trade": group, "owners": members}.get(kind)
            shape = ((total,) + array.shape) if kind == "swap" else array.shape
            if kind == "rows":
                total = max(array.shape[0], members // group)
                shape = (members // group,) + array.shape[1:]
            sems += [pltpu.SemaphoreType.DMA((total,)), pltpu.SemaphoreType.DMA((total,))]
        arrays.append(array)
        shapes.append(jax.ShapeDtypeStruct(shape, jnp.float32 if kind == "reduce" else array.dtype))
        scratch += sems
    outs = pl.pallas_call(
        functools.partial(bundle_kernel, group, shards, tuple(kinds)),
        out_shape=shapes,
        in_specs=[pl.BlockSpec(memory_space=pl.ANY)] * len(arrays),
        out_specs=[pl.BlockSpec(memory_space=pl.ANY)] * len(arrays),
        scratch_shapes=scratch,
        compiler_params=pltpu.CompilerParams(
            collective_id=number, has_side_effects=True, vmem_limit_bytes=limit
        ),
        name="bundle_" + "_".join(kinds[:2]),
    )(*arrays)
    done = []
    for (kind, array), out in zip(transfers, outs):
        if kind == "gather":
            out = out.reshape((group,) + array.shape)
        if kind == "reduce":
            out = out.reshape(array.shape[1:])
        done.append(out)
    return done


def pieces_of(size, most):
    return [(at, min(most, size - at)) for at in range(0, size, most)]


def expert_kernel(
    me_ref, routes_ref, router_ref, rows_in, grads_in, gate_w, up_w, down_w, shared_gate_w, shared_up_w, shared_down_w,
    back_ref, out_ref, rows_ref, grad_ref, hidden_ref, gate_back_ref, up_back_ref, score_ref,
    shared_hidden_ref, shared_gate_back_ref, shared_up_back_ref, slot_cotangent, pick_buf, gate_buf,
):
    width = rows_in.shape[1]
    hidden_width = gate_w.shape[1]
    shards, own_width, _ = shared_gate_w.shape
    senders, _, rows = routes_ref.shape
    capacity = pick_buf.shape[0] // senders
    experts = router_ref.shape[0]
    low = jnp.bfloat16
    me = me_ref[0, 0]

    @pl.when(pl.program_id(0) == 0)
    def _():
        pick_buf[...] = jnp.zeros_like(pick_buf)

    logits = matmul_nt(router_ref[...], rows_in[...])
    names = lax.broadcasted_iota(jnp.int32, (experts, rows), 0)
    earlier = lax.broadcasted_iota(jnp.int32, (rows, rows), 0) <= lax.broadcasted_iota(jnp.int32, (rows, rows), 1)
    earlier = jnp.where(earlier, 1.0, 0.0).astype(low)
    slot_names = lax.broadcasted_iota(jnp.int32, (capacity, rows), 0).astype(jnp.float32)
    picks = []
    for sender in range(senders):
        routed = routes_ref[sender]
        chosen = jnp.zeros((experts, rows), jnp.float32)
        for choice in range(TOP):
            chosen = chosen + jnp.where(routed[choice : choice + 1] == names, 1.0, 0.0)
        logit = jnp.where(chosen > 0.0, logits[:, sender * rows : (sender + 1) * rows], NEG)
        expo = jnp.exp(logit - jnp.max(logit, axis=0, keepdims=True)) * chosen
        dense = expo / jnp.sum(expo, axis=0, keepdims=True)
        gate_row = jnp.sum(jnp.where(names == me, dense, 0.0), axis=0, keepdims=True)
        mark = jnp.sum(jnp.where(routed == me, 1.0, 0.0), axis=0, keepdims=True)
        rank = matmul(jnp.broadcast_to(mark, (8, rows)).astype(low), earlier)[:1] - 1.0
        pick = jnp.where((slot_names == rank) & (mark > 0.0), 1.0, 0.0)
        picks.append(pick)
        at = slice(sender * capacity, (sender + 1) * capacity)
        pick_buf[at, sender * rows : (sender + 1) * rows] = pick.astype(low)
        gate_buf[at, :] = jnp.sum(pick * gate_row, axis=1, keepdims=True)
    gate = gate_buf[...]

    def pick_step(index, _):
        at = pl.ds(pl.multiple_of(index * 512, 512), 512)
        rows_ref[:, at] = matmul(pick_buf[...], rows_in[:, at]).astype(low)
        picked = matmul(pick_buf[...], grads_in[:, at])
        slot_cotangent[:, at] = picked.astype(low)
        grad_ref[:, at] = (gate * picked).astype(low)
        return 0

    lax.fori_loop(0, width // 512, pick_step, 0)
    shared_pre, shared_up = 0.0, 0.0
    for shard in range(shards):
        part = rows_in[:, shard * own_width : (shard + 1) * own_width]
        shared_pre = shared_pre + matmul(part, shared_gate_w[shard])
        shared_up = shared_up + matmul(part, shared_up_w[shard])
    swished, slope = swish_parts(shared_pre)
    shared_hidden_ref[...] = (swished * shared_up).astype(low)
    shared_grad = matmul_nt(grads_in[...], shared_down_w[...])
    shared_gate_back_ref[...] = (shared_grad * shared_up * slope).astype(low)
    shared_up_back_ref[...] = (shared_grad * swished).astype(low)
    for at, size in pieces_of(hidden_width, 512):
        columns = slice(at, at + size)
        gate_pre = matmul(rows_ref[...], gate_w[:, columns])
        up_pre = matmul(rows_ref[...], up_w[:, columns])
        swished, slope = swish_parts(gate_pre)
        hidden_ref[:, columns] = (swished * up_pre).astype(low)
        hidden_grad = matmul_nt(grad_ref[...], down_w[columns, :])
        gate_back_ref[:, columns] = (hidden_grad * up_pre * slope).astype(low)
        up_back_ref[:, columns] = (hidden_grad * swished).astype(low)

    def out_step(index, score):
        at = pl.ds(pl.multiple_of(index * 512, 512), 512)
        shard = index * 512 // own_width
        within = pl.ds(pl.multiple_of(index * 512 - shard * own_width, 512), 512)
        expert_out = matmul(hidden_ref[...], down_w[:, at]).astype(low).astype(jnp.float32)
        score = score + jnp.sum(expert_out * slot_cotangent[:, at].astype(jnp.float32), axis=1, keepdims=True)
        out = matmul_tn(pick_buf[...], (gate * expert_out).astype(low))
        out_ref[:, at] = (out + matmul(shared_hidden_ref[...], shared_down_w[:, at])).astype(low)
        row_back = matmul_nt(gate_back_ref[...], gate_w[at, :]) + matmul_nt(up_back_ref[...], up_w[at, :])
        back = (
            matmul_tn(pick_buf[...], row_back.astype(low))
            + matmul_nt(shared_gate_back_ref[...], shared_gate_w[shard, within, :])
            + matmul_nt(shared_up_back_ref[...], shared_up_w[shard, within, :])
        )
        back_ref[:, at] = back.astype(low)
        return score

    score = lax.fori_loop(0, width // 512, out_step, jnp.zeros((gate.shape[0], 1), jnp.float32))
    for sender in range(senders):
        own = score[sender * capacity : (sender + 1) * capacity]
        total = jnp.sum(picks[sender] * own, axis=0, keepdims=True)
        score_ref[sender] = jnp.broadcast_to(total, score_ref.shape[1:])


def expert_pass(me, routes, router, rows, grads, gate_w, up_w, down_w, shared_gate_w, shared_up_w, shared_down_w, capacity):
    plane, _, local = routes.shape
    senders = STEP_SENDERS
    tokens, slots = senders * local, senders * capacity
    steps = plane // senders
    width, hidden_width = gate_w.shape
    units = shared_gate_w.shape[2]
    low = jnp.bfloat16

    def whole(array):
        return pl.BlockSpec(array.shape, lambda i: (0,) * array.ndim, pipeline_mode=pl.Buffered(1))

    def by_step(r, c):
        return pl.BlockSpec((r, c), lambda i: (i, 0))

    total = steps * slots
    shape = jax.ShapeDtypeStruct
    route_block = pl.BlockSpec((senders, 8, local), lambda i: (i, 0, 0))
    return pl.pallas_call(
        expert_kernel,
        grid=(steps,),
        out_shape=[
            shape((steps * tokens, width), low),
            shape((steps * tokens, width), low),
            shape((total, width), low),
            shape((total, width), low),
            shape((total, hidden_width), low),
            shape((total, hidden_width), low),
            shape((total, hidden_width), low),
            shape((plane, 8, local), jnp.float32),
            shape((steps * tokens, units), low),
            shape((steps * tokens, units), low),
            shape((steps * tokens, units), low),
        ],
        in_specs=[
            pl.BlockSpec(memory_space=pltpu.SMEM),
            route_block,
            whole(router),
            by_step(tokens, width),
            by_step(tokens, width),
            whole(gate_w),
            whole(up_w),
            whole(down_w),
            whole(shared_gate_w),
            whole(shared_up_w),
            whole(shared_down_w),
        ],
        out_specs=[
            by_step(tokens, width),
            by_step(tokens, width),
            by_step(slots, width),
            by_step(slots, width),
            by_step(slots, hidden_width),
            by_step(slots, hidden_width),
            by_step(slots, hidden_width),
            route_block,
            by_step(tokens, units),
            by_step(tokens, units),
            by_step(tokens, units),
        ],
        scratch_shapes=[
            pltpu.VMEM((slots, width), low),
            pltpu.VMEM((slots, tokens), low),
            pltpu.VMEM((slots, 1), jnp.float32),
        ],
        compiler_params=pltpu.CompilerParams(
            vmem_limit_bytes=60 * 2**20, dimension_semantics=("arbitrary",)
        ),
        name="experts",
    )(me, routes, router, rows, grads, gate_w, up_w, down_w, shared_gate_w, shared_up_w, shared_down_w)


QUERIES = 256
KEYS = WINDOW + QUERIES


def score_block(scale, query, keys, query_docs, key_docs):
    raw = matmul_nt(query, keys) * scale
    row = lax.broadcasted_iota(jnp.int32, raw.shape, 0) + WINDOW
    column = lax.broadcasted_iota(jnp.int32, raw.shape, 1)
    allowed = (query_docs == key_docs) & (column <= row) & (column > row - WINDOW)
    return jnp.where(allowed, raw, NEG)


def attend_back_kernel(
    scale, last, query_ref, key_ref, value_ref, docs_ref, row_docs_ref, total_ref, grad_ref,
    query_grad_ref, key_grad_ref, value_grad_ref, key_sum, value_sum,
):
    step = pl.program_id(0)

    @pl.when(step == 0)
    def _():
        key_sum[...] = jnp.zeros_like(key_sum)
        value_sum[...] = jnp.zeros_like(value_sum)

    at = pl.ds(pl.multiple_of(step * QUERIES, QUERIES), KEYS)
    query, keys, grad = query_ref[...], key_ref[at, :], grad_ref[...]
    grad = jnp.where(docs_ref[...] < last, grad, jnp.zeros((), grad.dtype))
    scores = score_block(scale, query, keys, docs_ref[...], row_docs_ref[:, at])
    probs = jnp.exp(scores - total_ref[:, :1])
    prob_grad = matmul_nt(grad, value_ref[at, :])
    inner = jnp.sum(probs * prob_grad, axis=1, keepdims=True)
    raw_grad = (probs * (prob_grad - inner) * scale).astype(jnp.bfloat16)
    query_grad_ref[...] = matmul(raw_grad, keys)
    key_sum[at, :] += matmul_tn(raw_grad, query)
    value_sum[at, :] += matmul_tn(probs.astype(jnp.bfloat16), grad)

    @pl.when(step == pl.num_programs(0) - 1)
    def _():
        key_grad_ref[...] = key_sum[WINDOW:, :]
        value_grad_ref[...] = value_sum[WINDOW:, :]


def attend_back(scale, last, query, keys, value, docs, row_docs, totals, grad):
    rows, head_dim = query.shape
    whole = lambda a: pl.BlockSpec(a.shape, lambda i: (0, 0))
    by_step = lambda c: pl.BlockSpec((QUERIES, c), lambda i: (i, 0))
    full = lambda c: pl.BlockSpec((rows, c), lambda i: (0, 0))
    return pl.pallas_call(
        functools.partial(attend_back_kernel, scale, last),
        grid=(rows // QUERIES,),
        out_shape=[
            jax.ShapeDtypeStruct((rows, head_dim), jnp.float32),
            jax.ShapeDtypeStruct((rows, head_dim), jnp.float32),
            jax.ShapeDtypeStruct((rows, V_HEAD), jnp.float32),
        ],
        in_specs=[by_step(head_dim), whole(keys), whole(value), by_step(1), whole(row_docs), by_step(128), by_step(V_HEAD)],
        out_specs=[by_step(head_dim), full(head_dim), full(V_HEAD)],
        scratch_shapes=[pltpu.VMEM(keys.shape, jnp.float32), pltpu.VMEM(value.shape, jnp.float32)],
        compiler_params=pltpu.CompilerParams(vmem_limit_bytes=48 * 2**20, dimension_semantics=("arbitrary",)),
        name="attend_back",
    )(query, keys, value, docs, row_docs, totals, grad)


class Swaps:
    def __init__(self, place, shards, sender):
        self.place, self.shards, self.sender = place, shards, sender

    def start(self, source, target, send_sem, recv_sem, keep=None):
        place, shards = self.place, self.shards
        arrivals = []
        for step in range(1, shards):
            other = lax.rem(place.shard + step, shards)
            self.sender.start(
                place.always,
                remote(source, target(place.shard), send_sem.at[step], recv_sem.at[place.shard], {"shard": other}),
            )
            arrivals.append(
                remote(source, target(other), send_sem.at[step], recv_sem.at[other], {"shard": other})
            )
        if keep is not None:
            copy = pltpu.make_async_copy(source, target(place.shard), keep)
            copy.start()

        def wait():
            for arrival in arrivals:
                arrival.wait_recv()
            if keep is not None:
                copy.wait()

        return wait


def drain(run):
    for _ in run:
        pass


def forward_kernel(shards, plane, scale, last, *refs):
    (tokens, cotangent, query_cols, down_half, up_half, out_half, query_half, gate_half, wide_half, narrow_half,
     shared_gate, shared_up, shared_down, routes, first_gain, latent_gain, second_gain, turn, sway, docs, row_docs,
     all_normed, all_grads, all_routes, full_down, full_out, full_query, full_gate, full_up, full_narrow,
     full_shared_gate, full_shared_up, full_shared_down, normed_one,
     query, keys, value, key_latent, compressed, head_out, log_total, middle,
     token_buf, normed_buf, query_buf, up_buf, down_buf, out_buf, heads_buf, second_buf,
     swap_send, swap_recv, keep_sem, gather_send, gather_recv, gather_keep, piece_send, piece_recv,
     trade_send, trade_recv, load_sem) = refs
    low = jnp.bfloat16
    group = SEQ_DEVICES
    place, wide = Place(group), Place(plane)
    width = tokens.shape[-1]
    rows = docs.shape[0] // group
    sender = Sender()
    members = [lax.rem(place.local + step, group) for step in range(1, group)]
    peers = [(place.always, {"expert": place.base + member}) for member in members]
    if plane != group:
        peers += [
            (wide.upper & ~place.upper, {"expert": place.me + INNER}),
            (wide.lower & ~place.lower, {"expert": place.me - INNER}),
        ]
    others = [lax.rem(place.shard + step, shards) for step in range(1, shards)]
    peers += [(place.always, {"shard": other}) for other in others]
    greet(peers)

    swaps = Swaps(place, shards, sender)
    numbers = iter(range(16))

    def swap(source, target, keep=False):
        at = next(numbers)
        return swaps.start(
            source, target, swap_send.at[at], swap_recv.at[at], keep_sem.at[at] if keep else None
        )

    at_piece = lambda ref: ref.at[wide.me]
    got_query = swap(query_cols, lambda shard: query_buf.at[shard], True)
    got_down = swap(at_piece(down_half), lambda shard: full_down.at[shard, wide.me])
    got_up = swap(up_half, lambda shard: up_buf.at[shard], True)
    token_run = gather_steps(
        place, tokens, token_buf, gather_keep.at[0], gather_send.at[0], gather_recv.at[0], sender
    )
    next(token_run)
    got_out = swap(at_piece(out_half), lambda shard: full_out.at[shard, wide.me])
    got_wq = swap(at_piece(query_half), lambda shard: full_query.at[shard, wide.me])
    owns = [
        pltpu.make_async_copy(half, full.at[place.shard], load_sem.at[index])
        for index, (half, full) in enumerate(((down_half, full_down), (out_half, full_out), (query_half, full_query)))
    ]
    for own in owns:
        own.start()

    def piece_gathers(kind, full):
        return [
            gather_steps(
                wide, None, full.at[other], None, piece_send.at[kind, step], piece_recv.at[kind, step], sender
            )
            for step, other in enumerate(others)
        ]

    next(token_run)
    got_down()
    down_runs = piece_gathers(0, full_down)
    for run in down_runs:
        next(run)
    next(token_run)
    for run in down_runs:
        next(run)
    got_query()
    got_up()
    waits = [
        swap(gate_half, lambda shard: full_gate.at[shard], True),
        swap(wide_half, lambda shard: full_up.at[shard], True),
    ]
    drain(token_run)
    got_out()
    got_wq()
    waits += [
        swap(shared_gate, lambda shard: full_shared_gate.at[shard], True),
        swap(shared_up, lambda shard: full_shared_up.at[shard], True),
        swap(shared_down, lambda shard: full_shared_down.at[shard], True),
        swap(narrow_half, lambda shard: full_narrow.at[shard], True),
    ]
    for run in down_runs:
        drain(run)
    for own in owns:
        own.wait()
    route_run = gather_steps(
        wide, routes, all_routes, gather_keep.at[1], gather_send.at[1], gather_recv.at[1], sender
    )
    next(route_run)
    out_runs = piece_gathers(1, full_out)
    for run in out_runs:
        next(run)
    load_down = pltpu.make_async_copy(full_down, down_buf, load_sem.at[0])
    load_down.start()
    load_down.wait()

    keys[:WINDOW, :] = jnp.zeros((WINDOW, keys.shape[1]), low)
    value[:WINDOW, :] = jnp.zeros((WINDOW, value.shape[1]), low)
    tile = 2 * rows
    own_width = width // shards

    def whole_dot(at, weight_of):
        total = 0.0
        for shard in range(shards):
            total = total + matmul(normed_buf[at, shard * own_width : (shard + 1) * own_width], weight_of(shard))
        return total

    def front_tile(index, _):
        at = pl.ds(pl.multiple_of(index * tile, tile), tile)
        values = token_buf[pl.ds(index * 2, 2)].reshape(tile, width).astype(jnp.float32)
        root = lax.rsqrt(jnp.mean(values * values, axis=1, keepdims=True) + EPS)
        normed_buf[at, :] = (values * root * first_gain[...]).astype(low)
        first = whole_dot(at, lambda shard: query_buf[shard])
        latent = whole_dot(at, lambda shard: down_buf[shard].reshape(own_width, -1))
        turn_at, sway_at = turn[at, :], sway[at, :]
        end = QK_NOPE + QK_ROPE
        query[at, :QK_NOPE] = first[:, :QK_NOPE].astype(low)
        query[at, QK_NOPE:] = (first[:, QK_NOPE:end] * turn_at + first[:, end:] * sway_at).astype(low)
        end = KV_RANK + QK_ROPE
        key_rope = (latent[:, KV_RANK:end] * turn_at + latent[:, end:] * sway_at).astype(low)
        latent = latent[:, :KV_RANK]
        compressed[at, :] = latent
        root = lax.rsqrt(jnp.mean(latent * latent, axis=1, keepdims=True) + EPS)
        normed_latent = (latent * root * latent_gain[...]).astype(low)
        key_latent[at, :] = normed_latent
        up_rows = KV_RANK // shards
        both = 0.0
        for shard in range(shards):
            both = both + matmul(normed_latent[:, shard * up_rows : (shard + 1) * up_rows], up_buf[shard])
        both = both.astype(low)
        later = pl.ds(pl.multiple_of(index * tile + WINDOW, tile), tile)
        keys[later, :QK_NOPE] = both[:, :QK_NOPE]
        keys[later, QK_NOPE:] = key_rope
        value[later, :] = both[:, QK_NOPE:]
        return 0

    tiles = group // 2
    for part in range(2):
        lax.fori_loop(part * tiles // 2, (part + 1) * tiles // 2, front_tile, 0)
        for run in out_runs + [route_run]:
            next(run, None)
    save = pltpu.make_async_copy(normed_buf, normed_one, load_sem.at[1])
    save.start()
    for run in out_runs + [route_run]:
        next(run, None)

    def attend_tile(index, _):
        at = pl.ds(pl.multiple_of(index * QUERIES, QUERIES), QUERIES)
        window = pl.ds(pl.multiple_of(index * QUERIES, QUERIES), KEYS)
        scores = score_block(scale, query[at, :], keys[window, :], docs[at, :], row_docs[:, window])
        top = jnp.max(scores, axis=1, keepdims=True)
        expo = jnp.exp(scores - top)
        total = jnp.sum(expo, axis=1, keepdims=True)
        probs = (expo / total).astype(low)
        real = jnp.where(docs[at, :] < last, 1.0, 0.0)
        head_out[at, :] = (matmul(probs, value[window, :]) * real).astype(low)
        log_total[at, :] = jnp.broadcast_to(top + jnp.log(total), (QUERIES, log_total.shape[1]))
        return 0

    blocks = docs.shape[0] // QUERIES
    lax.fori_loop(0, blocks // 2, attend_tile, 0)
    for run in out_runs + [route_run]:
        drain(run)
    load_out = pltpu.make_async_copy(full_out, out_buf, load_sem.at[0])
    load_out.start()
    lax.fori_loop(blocks // 2, blocks, attend_tile, 0)

    def head_at(member):
        return head_out.at[pl.ds(pl.multiple_of(member * rows, rows), rows), :]

    def lands(head):
        return heads_buf.at[:, pl.ds(pl.multiple_of(head * V_HEAD, V_HEAD), V_HEAD)]

    keep = pltpu.make_async_copy(head_at(place.local), lands(place.local), load_sem.at[2])
    keep.start()
    for step, member in enumerate(members):
        sender.start(
            place.always,
            remote(
                head_at(member), lands(place.local), trade_send.at[step], trade_recv.at[place.local],
                {"expert": place.base + member},
            ),
        )
    for step, member in enumerate(members):
        remote(
            head_at(member), lands(member), trade_send.at[step], trade_recv.at[member], {"expert": place.base + member}
        ).wait_recv()
    keep.wait()
    load_out.wait()

    for at, size in pieces_of(width, 512):
        columns = slice(at, at + size)
        total = token_buf[place.local].reshape(rows, width)[:, columns].astype(jnp.float32)
        for shard in range(shards):
            weight = out_buf[shard, :, :, :, columns].reshape(own_width, size)
            total = total + matmul(heads_buf[:, shard * own_width : (shard + 1) * own_width], weight)
        middle[:, columns] = total
    values = middle[...]
    root = lax.rsqrt(jnp.mean(values * values, axis=1, keepdims=True) + EPS)
    second_buf[...] = (values * root * second_gain[...]).astype(low).reshape(second_buf.shape)

    normed_run = gather_steps(
        wide, second_buf, all_normed, gather_keep.at[2], gather_send.at[2], gather_recv.at[2], sender
    )
    grad_run = gather_steps(
        wide, cotangent, all_grads, gather_keep.at[3], gather_send.at[3], gather_recv.at[3], sender
    )
    wq_runs = piece_gathers(2, full_query)
    runs = [normed_run, grad_run] + wq_runs
    while runs:
        runs = [run for run in runs if next(run, "end") != "end"]
    save.wait()
    for wait in waits:
        wait()
    sender.finish()


def forward_pass(scale, last, tokens, cotangent, blocks, routes, gains, tables):
    shards, plane = lax.axis_size("shard"), lax.axis_size("expert")
    local, width = tokens.shape
    low, shape = jnp.bfloat16, jax.ShapeDtypeStruct
    pieces = (PIECES, local // PIECES, width)
    any_space, vmem = pl.BlockSpec(memory_space=pl.ANY), pl.BlockSpec(memory_space=pltpu.VMEM)
    head_dim = QK_NOPE + QK_ROPE
    query_cols, down_half, up_half, out_half, query_half = blocks[:5]
    out_shape = [
        shape((plane,) + pieces, low),
        shape((plane,) + pieces, low),
        shape((plane, 1) + routes.shape, jnp.int32),
    ]
    out_shape += [shape((shards,) + block.shape, low) for block in (down_half, out_half, query_half) + blocks[5:]]
    out_shape += [
        shape((SEQ, width), low),
        shape((SEQ, head_dim), low),
        shape((SEQ + WINDOW, head_dim), low),
        shape((SEQ + WINDOW, V_HEAD), low),
        shape((SEQ, KV_RANK), low),
        shape((SEQ, KV_RANK), jnp.float32),
        shape((SEQ, V_HEAD), low),
        shape((SEQ, 128), jnp.float32),
        shape((local, width), jnp.float32),
    ]
    hbm_out = 13
    own_width = width // shards
    dma = pltpu.SemaphoreType.DMA
    return pl.pallas_call(
        functools.partial(forward_kernel, shards, plane, scale, last),
        out_shape=out_shape,
        in_specs=[any_space] * (3 + len(blocks)) + [vmem] * (len(gains) + len(tables)),
        out_specs=[any_space] * hbm_out + [vmem] * (len(out_shape) - hbm_out),
        scratch_shapes=[
            pltpu.VMEM((SEQ_DEVICES,) + pieces, low),
            pltpu.VMEM((SEQ, width), low),
            pltpu.VMEM((shards,) + query_cols.shape, low),
            pltpu.VMEM((shards,) + up_half.shape, low),
            pltpu.VMEM((shards,) + down_half.shape, low),
            pltpu.VMEM((shards,) + out_half.shape, low),
            pltpu.VMEM((local, HEADS * V_HEAD), low),
            pltpu.VMEM(pieces, low),
            dma((12, shards)),
            dma((12, shards)),
            dma((12,)),
            dma((4, 4, plane, PIECES)),
            dma((4, plane, PIECES)),
            dma((4,)),
            dma((3, shards, 4, plane, 1)),
            dma((3, shards, plane, 1)),
            dma((SEQ_DEVICES,)),
            dma((SEQ_DEVICES,)),
            dma((4,)),
        ],
        compiler_params=pltpu.CompilerParams(
            collective_id=1, has_side_effects=True, vmem_limit_bytes=60 * 2**20
        ),
        name="forward",
    )(tokens.reshape(pieces), cotangent.reshape(pieces), *blocks, routes[None], *gains, *tables)


def tie(value, *awaited):
    return lax.optimization_barrier((value,) + awaited)


def shard_ring(block):
    count = lax.axis_size("shard")
    me = lax.axis_index("shard")
    whole = jnp.zeros((count,) + block.shape, block.dtype)
    whole = lax.dynamic_update_index_in_dim(whole, block, me, 0)
    for step in range(1, count):
        moved = lax.ppermute(
            block, "shard", [(source, (source + step) % count) for source in range(count)]
        )
        whole = lax.dynamic_update_index_in_dim(whole, moved, (me - step) % count, 0)
    return whole


def shard_rows(block):
    whole = shard_ring(block)
    return whole.reshape((-1,) + block.shape[1:])


def shard_sum(values):
    count = lax.axis_size("shard")
    me = lax.axis_index("shard")
    blocks = values.reshape((count, -1) + values.shape[1:])
    total = lax.dynamic_index_in_dim(blocks, me, 0, keepdims=False)
    for step in range(1, count):
        outgoing = lax.dynamic_index_in_dim(blocks, (me + step) % count, 0, keepdims=False)
        moved = lax.ppermute(
            outgoing.astype(jnp.bfloat16),
            "shard",
            [(source, (source + step) % count) for source in range(count)],
        )
        total = total + moved.astype(jnp.float32)
    return total


def on_device(
    tokens,
    document_lengths,
    routes,
    first_gain,
    query_weight,
    latent_down,
    latent_gain,
    latent_up,
    output_weight,
    second_gain,
    router_weight,
    shared_gate,
    shared_up,
    shared_down,
    expert_gate,
    expert_up,
    expert_down,
    cotangent,
):
    local_rows, width = tokens.shape
    shards = lax.axis_size("shard")
    plane = lax.axis_size("expert")
    everyone = ("shard", "expert")
    all_devices = shards * plane
    shard_at = lax.axis_index("shard")
    plane_at = lax.axis_index("expert")
    groups = plane_groups(plane)
    head_at = plane_at % SEQ_DEVICES
    sequence_at = (shard_at * plane + plane_at) // SEQ_DEVICES
    capacity = local_rows * TOP * 4 // (3 * plane)
    head_dim = QK_NOPE + QK_ROPE
    scale = 1.0 / math.sqrt(head_dim)
    own_at = head_at * local_rows

    def own_rows(values):
        return lax.dynamic_slice_in_dim(values, own_at, local_rows, 0)

    piece_rows = output_weight.shape[0] // plane
    half = QK_ROPE // 2
    query_columns = lax.dynamic_slice_in_dim(query_weight, head_at * head_dim, head_dim, 1)
    query_turn, key_turn = query_columns[:, QK_NOPE:], latent_down[:, KV_RANK:]
    query_cols = jnp.concatenate(
        [query_columns, query_turn[:, half:], query_turn[:, :half]], axis=1
    )
    down_half = jnp.concatenate(
        [latent_down, key_turn[:, half:], key_turn[:, :half]], axis=1
    )
    units = shared_down.shape[0] // plane
    unit_pad = -units % 16
    padded_units = units + unit_pad
    gate_columns, up_columns = (
        jnp.concatenate(
            [
                jnp.pad(
                    lax.dynamic_slice_in_dim(
                        weight, index * shared_down.shape[0] + plane_at * units, units, 1
                    ),
                    ((0, 0), (0, unit_pad)),
                )
                for index in range(shards)
            ],
            axis=1,
        )
        for weight in (shared_gate, shared_up)
    )
    down_units = lax.dynamic_slice_in_dim(shared_down, plane_at * units, units, 0)
    down_units = jnp.pad(down_units, ((0, unit_pad), (0, 0)))

    def plane_pieces(weight):
        return weight.reshape(plane, 1, -1, weight.shape[1])

    positions = jnp.arange(SEQ, dtype=jnp.int32)
    cosine_part, sine_part = rotary_tables(positions, QK_ROPE)
    sequence_count, entry_count = document_lengths.shape
    ends = jnp.cumsum(document_lengths, axis=1)
    picked = jnp.arange(sequence_count, dtype=jnp.int32)[:, None] == sequence_at
    row_ends = jnp.sum(jnp.where(picked, ends, 0), axis=0)
    documents = jnp.sum((positions[:, None] >= row_ends[None, :]).astype(jnp.int32), axis=1)
    turn = jnp.concatenate([cosine_part, cosine_part], axis=1)
    sway = jnp.concatenate([-sine_part, sine_part], axis=1)
    docs = documents[:, None]
    row_docs = jnp.pad(docs, ((WINDOW, 0), (0, 0)), constant_values=-1).T
    route_rows = jnp.pad(routes.T, ((0, 8 - TOP), (0, 0)), constant_values=-1)
    (
        all_normed,
        all_grads,
        all_routes,
        full_down,
        full_out,
        full_query,
        gate_single,
        up_single,
        down_single,
        gate_shared,
        up_shared,
        down_shared,
        normed_one,
        query,
        keys,
        value,
        key_latent,
        compressed,
        head_out,
        log_total,
        middle,
    ) = forward_pass(
        scale,
        entry_count - 1,
        tokens,
        cotangent,
        (
            query_cols,
            plane_pieces(down_half),
            lax.dynamic_slice_in_dim(
                latent_up, head_at * (QK_NOPE + V_HEAD), QK_NOPE + V_HEAD, 1
            ),
            plane_pieces(output_weight),
            plane_pieces(query_weight),
            expert_gate[0],
            expert_up[0],
            expert_down[0],
            gate_columns,
            up_columns,
            down_units,
        ),
        route_rows,
        (first_gain[None], latent_gain[None], second_gain[None]),
        (turn, sway, docs, row_docs),
    )
    all_normed = all_normed.reshape(-1, width)
    all_grads = all_grads.reshape(-1, width)
    full_out = full_out.reshape(-1, width)
    full_query = full_query.reshape(width, -1)
    full_down = full_down.reshape(width, -1)
    hidden_rows = tokens.astype(jnp.float32)
    second_normed = norm_scale(middle, second_gain).astype(jnp.bfloat16)
    expert_ids = jnp.arange(plane, dtype=jnp.int32)
    (
        normed_part,
        output_part,
        slot_rows,
        slot_grad,
        hidden,
        gate_pre_grad,
        up_pre_grad,
        token_scores,
        shared_hidden,
        shared_gate_back,
        shared_up_back,
    ) = expert_pass(
        plane_at.astype(jnp.int32).reshape(1, 1),
        all_routes[:, 0],
        router_weight.T,
        all_normed,
        all_grads,
        gate_single.reshape(width, -1),
        up_single.reshape(width, -1),
        down_single.reshape(-1, width),
        gate_shared,
        up_shared,
        down_shared.reshape(-1, width),
        capacity,
    )
    plane_rows = plane * local_rows
    expert_down_term = matmul_tn(hidden, slot_grad)
    back, gate_dense, down_blocks = bundle(
        4,
        plane,
        shards,
        [
            ("reduce", normed_part.reshape(plane, local_rows, width)),
            ("trade", token_scores),
            ("share", expert_down_term.astype(jnp.bfloat16).reshape(shards, -1, width)),
        ],
    )
    gate_dense = gate_dense[:, 0].T

    def sum_shards(term, blocks):
        own = lax.dynamic_index_in_dim(
            term.reshape((shards, -1) + term.shape[1:]), shard_at, 0, keepdims=False
        )
        for step in range(1, shards):
            own = own + lax.dynamic_index_in_dim(
                blocks, (shard_at + step) % shards, 0, keepdims=False
            ).astype(jnp.float32)
        return own

    expert_down_grad = sum_shards(expert_down_term, down_blocks)[None]
    output_part = tie(output_part, back)[0]
    output_sum = lax.psum_scatter(output_part, "expert", scatter_dimension=0, tiled=True)
    activations = (middle + output_sum.astype(jnp.float32)).astype(jnp.bfloat16)
    expert_gate_grad = shard_sum(matmul_tn(slot_rows, gate_pre_grad))[None]
    expert_up_grad = shard_sum(matmul_tn(slot_rows, up_pre_grad))[None]
    shared_down_term = matmul_tn(shared_hidden, all_grads).reshape(shards, padded_units, width)
    shared_down_grad = shard_sum(shared_down_term[:, :units].reshape(-1, width))
    shared_term = jnp.concatenate(
        [matmul_tn(all_normed, shared_gate_back), matmul_tn(all_normed, shared_up_back)], axis=1
    )

    def to_owners(term):
        moved = lax.all_to_all(
            term.astype(jnp.bfloat16).reshape(all_devices, -1, term.shape[1]),
            everyone,
            split_axis=0,
            concat_axis=0,
            tiled=True,
        )
        moved = moved.reshape(shards, plane, -1, term.shape[1]).astype(jnp.float32)
        return jnp.sum(moved, axis=0)

    def by_head(moved):
        heads = moved.reshape((plane // SEQ_DEVICES, HEADS) + moved.shape[1:]).sum(axis=0)
        return heads.transpose(1, 0, 2).reshape(moved.shape[1], -1)

    shared_moved = to_owners(shared_term).reshape(plane, -1, 2, shards, padded_units)[..., :units]
    shared_moved = shared_moved.transpose(2, 1, 3, 0, 4)
    shared_moved = shared_moved.reshape(2, shared_moved.shape[1], -1)
    shared_gate_grad = shared_moved[0]
    shared_up_grad = shared_moved[1]

    grad_out = cotangent.astype(jnp.float32)
    own_choose = routes[:, :, None] == expert_ids[None, None, :]
    own_logits = matmul(second_normed, router_weight)
    chosen = jnp.sum(jnp.where(own_choose, own_logits[:, None, :], 0.0), axis=2)
    chosen_exp = jnp.exp(chosen - jnp.max(chosen, axis=1, keepdims=True))
    own_gates = chosen_exp / jnp.sum(chosen_exp, axis=1, keepdims=True)
    gate_grad = jnp.sum(jnp.where(own_choose, gate_dense[:, None, :], 0.0), axis=2)
    chosen_grad = own_gates * (
        gate_grad - jnp.sum(own_gates * gate_grad, axis=1, keepdims=True)
    )
    logit_grad = jnp.sum(jnp.where(own_choose, chosen_grad[:, :, None], 0.0), axis=1)
    router_term = lax.dot_general(
        second_normed.astype(jnp.float32),
        logit_grad,
        (((0,), (0,)), ((), ())),
        precision=HIGH,
        preferred_element_type=jnp.float32,
    )
    normed_grad = back + lax.dot_general(
        logit_grad,
        router_weight.astype(jnp.float32),
        (((1,), (1,)), ((), ())),
        precision=HIGH,
        preferred_element_type=jnp.float32,
    )
    unused_two, second_back = jax.vjp(norm_scale, middle, second_gain)
    middle_norm_grad, second_term = second_back(normed_grad)
    middle_grad = grad_out + middle_norm_grad
    middle_low = middle_grad.astype(jnp.bfloat16)
    heads_grad = matmul_nt(middle_low, full_out).astype(jnp.bfloat16)
    heads_grad = heads_grad.reshape(local_rows, HEADS, V_HEAD).transpose(1, 0, 2)
    (head_grad,) = bundle(5, SEQ_DEVICES, shards, [("trade", heads_grad)])
    head_grad = head_grad.reshape(SEQ, V_HEAD)
    all_middle = lax.all_gather(
        tie(middle_low, head_grad)[0], "expert", axis=0, tiled=True, axis_index_groups=groups
    )
    query_raw, keys_grad, value_grad = attend_back(
        scale, entry_count - 1, query, keys, value, docs, row_docs, log_total, head_grad
    )
    query_grad = jnp.concatenate(
        [query_raw[:, :QK_NOPE], unrotate(query_raw[:, QK_NOPE:], cosine_part, sine_part)],
        axis=1,
    ).astype(jnp.bfloat16)
    key_nope_grad, key_rope_grad = keys_grad[:, :QK_NOPE], keys_grad[:, QK_NOPE:]
    pair_grad = jnp.concatenate([key_nope_grad, value_grad], axis=1).astype(jnp.bfloat16)
    latent_up_term = matmul_tn(key_latent, pair_grad)
    up_half = lax.dynamic_slice_in_dim(
        latent_up, head_at * (QK_NOPE + V_HEAD), QK_NOPE + V_HEAD, 1
    )
    up_head = shard_rows(up_half)
    key_grad_part = jnp.concatenate(
        [
            matmul_nt(pair_grad, up_head),
            key_rope_grad,
            jnp.zeros((SEQ, -(KV_RANK + QK_ROPE) % 128), jnp.float32),
        ],
        axis=1,
    ).astype(jnp.bfloat16)
    query_term = matmul_tn(normed_one, query_grad)
    query_moved, up_moved = (
        lax.all_to_all(
            term.astype(jnp.bfloat16).reshape(all_devices, -1, term.shape[1]),
            everyone,
            split_axis=0,
            concat_axis=0,
            tiled=True,
        )
        for term in (query_term, latent_up_term)
    )
    own_key_grad, own_query_grad = bundle(
        6,
        SEQ_DEVICES,
        shards,
        [
            ("reduce", key_grad_part.reshape(SEQ_DEVICES, local_rows, -1)),
            ("trade", query_grad.reshape(SEQ_DEVICES, local_rows, head_dim)),
        ],
    )
    own_key_grad = own_key_grad[:, : KV_RANK + QK_ROPE]
    own_query_grad = own_query_grad.transpose(1, 0, 2).reshape(local_rows, HEADS * head_dim)
    own_compressed = own_rows(compressed)
    unused_latent, latent_back = jax.vjp(norm_scale, own_compressed, latent_gain)
    latent_in_grad, latent_gain_term = latent_back(own_key_grad[:, :KV_RANK])
    rope_in_grad = unrotate(
        own_key_grad[:, KV_RANK:], own_rows(cosine_part), own_rows(sine_part)
    )
    compressed_grad = jnp.concatenate([latent_in_grad, rope_in_grad], axis=1).astype(jnp.bfloat16)
    down_columns = (KV_RANK + QK_ROPE) // SEQ_DEVICES
    def owner_blocks(term):
        return term.astype(jnp.bfloat16).reshape(all_devices, -1, term.shape[1])

    def owner_sum(moved):
        blocks = moved.reshape((shards, plane) + moved.shape[1:]).astype(jnp.float32)
        return by_head(jnp.sum(blocks, axis=0))

    column_grad = lax.all_to_all(
        compressed_grad.reshape(local_rows, SEQ_DEVICES, down_columns).transpose(1, 0, 2),
        "expert",
        split_axis=0,
        concat_axis=0,
        tiled=True,
        axis_index_groups=groups,
    )
    column_grad = column_grad.reshape(SEQ, down_columns)
    query_weight_grad = owner_sum(query_moved)
    latent_up_grad = owner_sum(up_moved)
    normed_one_grad = matmul_nt(own_query_grad, full_query) + matmul_nt(
        compressed_grad, full_down[:, : KV_RANK + QK_ROPE]
    )
    unused_one, first_back = jax.vjp(norm_scale, hidden_rows, first_gain)
    input_norm_grad, first_term = first_back(normed_one_grad)
    input_grad = middle_grad + input_norm_grad
    down_term = matmul_tn(normed_one, column_grad)
    out_term = matmul_tn(head_out, all_middle.reshape(SEQ, width)).astype(jnp.bfloat16)
    small_terms = jnp.concatenate(
        [
            router_term.reshape(all_devices, -1),
            second_term.reshape(all_devices, -1),
            first_term.reshape(all_devices, -1),
            latent_gain_term.reshape(all_devices, -1),
        ],
        axis=1,
    )
    small_count = small_terms.shape[1]
    small_terms = jnp.pad(small_terms, ((0, 0), (0, -small_count % 1024)))
    small_terms = small_terms.reshape(all_devices, -1, 128)
    down_moved, gain_moved, out_moved = bundle(
        8,
        SEQ_DEVICES,
        shards,
        [
            ("owners", owner_blocks(down_term)),
            ("owners", small_terms),
            ("rows", out_term.reshape(-1, width // all_devices, width)),
        ],
    )
    latent_down_grad = owner_sum(down_moved)
    output_weight_grad = jnp.sum(out_moved.astype(jnp.float32), axis=0)
    small_sums = jnp.sum(gain_moved, axis=0).reshape(-1)[:small_count]
    own_width = width // all_devices
    at_second = own_width * plane
    router_weight_grad = small_sums[:at_second].reshape(own_width, plane)
    second_gain_grad = small_sums[at_second : at_second + own_width]
    first_gain_grad = small_sums[at_second + own_width : at_second + 2 * own_width]
    latent_gain_grad = small_sums[at_second + 2 * own_width :]
    return (
        activations,
        input_grad,
        first_gain_grad,
        query_weight_grad,
        latent_down_grad,
        latent_gain_grad,
        latent_up_grad,
        output_weight_grad,
        second_gain_grad,
        router_weight_grad,
        shared_gate_grad,
        shared_up_grad,
        shared_down_grad,
        expert_gate_grad,
        expert_up_grad,
        expert_down_grad,
    )


def solution(mesh):
    return jax.shard_map(
        on_device,
        mesh=mesh,
        in_specs=(
            P(("shard", "expert"), None),
            P(),
            P(("shard", "expert"), None),
            P(),
            P("shard", None),
            P("shard", None),
            P(),
            P("shard", None),
            P("shard", None),
            P(),
            P(),
            P("shard", None),
            P("shard", None),
            P("shard", None),
            P("expert", "shard", None),
            P("expert", "shard", None),
            P("expert", "shard", None),
            P(("shard", "expert"), None),
        ),
        out_specs=(
            P(("shard", "expert"), None),
            P(("shard", "expert"), None),
            P(("shard", "expert")),
            P(("shard", "expert"), None),
            P(("shard", "expert"), None),
            P(("shard", "expert")),
            P(("shard", "expert"), None),
            P(("shard", "expert"), None),
            P(("shard", "expert")),
            P(("shard", "expert"), None),
            P(("shard", "expert"), None),
            P(("shard", "expert"), None),
            P(("shard", "expert"), None),
            P("expert", "shard", None),
            P("expert", "shard", None),
            P("expert", "shard", None),
        ),
        check_vma=False,
    )
```

```python
import functools
import math

import jax
import jax.numpy as jnp
from jax import lax
from jax.experimental import pallas as pl
from jax.experimental.pallas import tpu as pltpu
from jax.sharding import PartitionSpec as P

HEADS = 16
QK_NOPE = 128
QK_ROPE = 64
V_HEAD = 128
KV_RANK = 512
TOP = 6
SEQ = 2048
WINDOW = 1024
TOK_DEV = 128
STEP_SENDERS = 4
SEQ_DEVICES = SEQ // TOK_DEV


EPS = 1e-06
THETA = 10000.0
NEG = -1e30
HIGH = lax.Precision.HIGHEST


def matmul(left, right):
    return jnp.dot(left, right, preferred_element_type=jnp.float32)


def matmul_tn(left, right):
    return lax.dot_general(
        left, right, (((0,), (0,)), ((), ())), preferred_element_type=jnp.float32
    )


def matmul_nt(left, right):
    return lax.dot_general(
        left, right, (((1,), (1,)), ((), ())), preferred_element_type=jnp.float32
    )


def norm_scale(values, gain):
    return values * lax.rsqrt(jnp.mean(values * values, axis=-1, keepdims=True) + EPS) * gain


def rotary_tables(positions, width):
    half = width // 2
    freqs = THETA ** (-jnp.arange(half, dtype=jnp.float32) / half)
    angles = positions.astype(jnp.float32)[:, None] * freqs[None, :]
    return (jnp.cos(angles), jnp.sin(angles))


def rotate(values, cosine_part, sine_part):
    half = values.shape[-1] // 2
    first = values[..., :half]
    second = values[..., half:]
    return jnp.concatenate(
        [first * cosine_part - second * sine_part, second * cosine_part + first * sine_part],
        axis=-1,
    )


def unrotate(values, cosine_part, sine_part):
    half = values.shape[-1] // 2
    first = values[..., :half]
    second = values[..., half:]
    return jnp.concatenate(
        [first * cosine_part + second * sine_part, second * cosine_part - first * sine_part],
        axis=-1,
    )


def swish_parts(values):
    sigmoid_part = jax.nn.sigmoid(values)
    return (values * sigmoid_part, sigmoid_part * (1.0 + values * (1.0 - sigmoid_part)))


MESH = pl.DeviceIdType.MESH
INNER = 4
PIECES = 2


class Sender:
    def __init__(self):
        self.started = []

    def start(self, there, copy):
        @pl.when(there)
        def _():
            copy.start()

        self.started.append((there, copy))

    def finish(self):
        for there, copy in self.started:
            @pl.when(there)
            def _():
                copy.wait_send()


def remote(source, target, send_sem, recv_sem, place):
    return pltpu.make_async_remote_copy(
        src_ref=source,
        dst_ref=target,
        send_sem=send_sem,
        recv_sem=recv_sem,
        device_id=place,
        device_id_type=MESH,
    )


class Place:
    def __init__(self, group):
        self.me = lax.axis_index("expert")
        self.shard = lax.axis_index("shard")
        self.group = group
        self.outer = group // INNER
        self.local = lax.rem(self.me, group)
        self.base = self.me - self.local
        self.level = self.local // INNER
        inner = lax.rem(self.local, INNER)
        self.row_step = 2 - 4 * (inner // 2)
        self.twin_step = 1 - 2 * lax.rem(inner, 2)
        self.always = self.me >= 0
        self.upper = self.level < self.outer - 1
        self.lower = self.level > 0

    def neighbours(self):
        return [
            (self.upper, {"expert": self.me + INNER}),
            (self.lower, {"expert": self.me - INNER}),
            (self.always, {"expert": self.me + self.row_step}),
            (self.always, {"expert": self.me + self.twin_step}),
        ]

    def along(self, step):
        below = (self.level >= step, self.local - step * INNER, self.upper, self.me + INNER, 0)
        above = (self.level + step < self.outer, self.local + step * INNER, self.lower, self.me - INNER, 1)
        return (below, above)


def greet(peers):
    barrier = pltpu.get_barrier_semaphore()
    for there, peer in peers:
        @pl.when(there)
        def _():
            pl.semaphore_signal(barrier, inc=1, device_id=peer, device_id_type=MESH)
    pl.semaphore_wait(barrier, sum(there.astype(jnp.int32) for there, _ in peers))


def gather_steps(place, own_ref, out_ref, copy_sem, send_sem, recv_sem, sender):
    local = place.local
    row, twin = local + place.row_step, local + place.twin_step

    def push(kind, block, piece, target, source=None):
        spot = out_ref.at[block, piece]
        return remote(
            spot if source is None else source.at[piece],
            spot,
            send_sem.at[kind, block, piece],
            recv_sem.at[block, piece],
            {"expert": target},
        )

    def arrive(there, block, piece):
        @pl.when(there)
        def _():
            push(0, block, piece, place.me).wait_recv()

    pieces = out_ref.shape[1]
    if own_ref is None:
        own_ref = out_ref.at[local]
    else:
        keep = pltpu.make_async_copy(own_ref, out_ref.at[local], copy_sem)
        keep.start()
    row_at, twin_at = place.me + place.row_step, place.me + place.twin_step
    for piece in range(pieces):
        sender.start(place.upper, push(0, local, piece, place.me + INNER, own_ref))
        sender.start(place.lower, push(1, local, piece, place.me - INNER, own_ref))
        sender.start(place.always, push(2, local, piece, row_at, own_ref))
        sender.start(place.always, push(3, local, piece, twin_at, own_ref))
    yield
    for step in range(1, place.outer + 1):
        if step < place.outer:
            for piece in range(pieces):
                for there, block, onward, target, kind in place.along(step):
                    arrive(there, block, piece)
                    sender.start(there & onward, push(kind, block, piece, target))
                    sender.start(there, push(2, block, piece, row_at))
                    sender.start(there, push(3, block, piece, twin_at))
        for piece in range(pieces):
            for there, block, *_ in place.along(step - 1)[: 1 if step == 1 else 2]:
                arrive(there, block + place.row_step, piece)
                sender.start(there, push(3, block + place.row_step, piece, twin_at))
        yield
    for step in range(place.outer):
        for piece in range(pieces):
            for there, block, *_ in place.along(step)[: 1 if step == 0 else 2]:
                arrive(there, block + place.twin_step, piece)
                arrive(there, block + place.twin_step + place.row_step, piece)
    if copy_sem is not None:
        keep.wait()
    yield


def add_into(target, first, *others):
    rows = target.shape[0]
    chunk = 32

    def body(index, _):
        at = pl.ds(pl.multiple_of(index * chunk, chunk), chunk)
        total = first[at, :].astype(jnp.float32)
        for other in others:
            total = total + other[at, :].astype(jnp.float32)
        target[at, :] = total.astype(target.dtype)
        return 0

    lax.fori_loop(0, rows // chunk, body, 0)


def reduce_steps(place, part_ref, out_ref, scratch, sender):
    (own_buf, twin_buf, row_buf, line_buf, load_sem, twin_send, twin_recv, row_send, row_recv, line_send, line_recv,
     out_buf, out_sem) = scratch
    outer, local, level = place.outer, place.local, place.level
    pieces = part_ref.shape[1]
    inner = lax.rem(local, INNER)
    row_bit, core = inner // 2, lax.rem(inner, 2)
    twin_at, row_at = {"expert": place.me + place.twin_step}, {"expert": place.me + place.row_step}
    order = []
    low, high = 0, outer - 1
    while low <= high:
        order += [high] if low == high else [high, low]
        low, high = low + 1, high - 1
    units = [(at, piece) for at in order for piece in range(pieces)]
    bits = (1 - row_bit, row_bit)

    def loading(at, piece, bit):
        where = at * 2 + bit
        return pltpu.make_async_copy(
            part_ref.at[at * INNER + bit * 2 + core, piece], own_buf.at[where, piece], load_sem.at[where, piece]
        )

    def to_twin(at, piece, bit):
        where = at * 2 + bit
        return remote(
            part_ref.at[at * INNER + bit * 2 + 1 - core, piece],
            twin_buf.at[where, piece],
            twin_send.at[where, piece],
            twin_recv.at[where, piece],
            twin_at,
        )

    def to_row(at, piece):
        return remote(
            own_buf.at[at * 2 + bits[0], piece], row_buf.at[at, piece], row_send.at[at, piece], row_recv.at[at, piece], row_at
        )

    def mine(at, piece):
        return own_buf.at[at * 2 + row_bit, piece]

    def to_line(side, at, piece):
        return remote(
            mine(at, piece),
            line_buf.at[side, at, piece],
            line_send.at[side, at, piece],
            line_recv.at[side, at, piece],
            {"expert": place.me + (INNER if side == 0 else -INNER)},
        )

    for at, piece in units:
        for bit in bits:
            sender.start(place.always, to_twin(at, piece, bit))
            loading(at, piece, bit).start()
    yield
    for at, piece in units:
        for bit in bits:
            where = at * 2 + bit
            loading(at, piece, bit).wait()
            to_twin(at, piece, bit).wait_recv()
            add_into(own_buf.at[where, piece], own_buf.at[where, piece], twin_buf.at[where, piece])
            if bit is bits[0]:
                sender.start(place.always, to_row(at, piece))
    yield
    for at, piece in units:
        to_row(at, piece).wait_recv()
        spot, row = mine(at, piece), row_buf.at[at, piece]
        for side, there, first in ((0, level < at, level == 0), (1, level > at, level == outer - 1)):
            line = to_line(side, at, piece)

            @pl.when(there & first)
            def _():
                add_into(spot, spot, row)

            @pl.when(there & ~first)
            def _():
                line.wait_recv()
                add_into(spot, spot, row, line_buf.at[side, at, piece])

            sender.start(there, line)
    yield
    for at, piece in units:
        @pl.when(level == at)
        def _():
            parts = [mine(at, piece), row_buf.at[at, piece]]
            for side, there in ((0, at > 0), (1, at < outer - 1)):
                if there:
                    to_line(side, at, piece).wait_recv()
                    parts.append(line_buf.at[side, at, piece])
            add_into(out_buf.at[piece], *parts)
    done = pltpu.make_async_copy(out_buf, out_ref, out_sem)
    done.start()
    done.wait()
    yield


def reduce_scratch(group, pieces, rows, columns):
    outer = group // INNER
    bf = jnp.bfloat16
    pair, single, line = (2 * outer, pieces), (outer, pieces), (2, outer, pieces)
    block = (rows, columns)
    return [
        pltpu.VMEM(pair + block, bf),
        pltpu.VMEM(pair + block, bf),
        pltpu.VMEM(single + block, bf),
        pltpu.VMEM(line + block, bf),
        pltpu.SemaphoreType.DMA(pair),
        pltpu.SemaphoreType.DMA(pair),
        pltpu.SemaphoreType.DMA(pair),
        pltpu.SemaphoreType.DMA(single),
        pltpu.SemaphoreType.DMA(single),
        pltpu.SemaphoreType.DMA(line),
        pltpu.SemaphoreType.DMA(line),
        pltpu.VMEM((pieces,) + block, jnp.float32),
        pltpu.SemaphoreType.DMA(()),
    ]


class HeadRows:
    def __init__(self, started, received):
        self.started, self.received = started, received

    def wait(self):
        for there, local, copy, keep in self.started:
            @pl.when(there)
            def _():
                copy.wait_send()

            @pl.when(local)
            def _():
                keep.wait()
        for there, copy in self.received:
            @pl.when(there)
            def _():
                copy.wait_recv()


def head_rows(place, plane, shards, own_ref, out_ref, copy_sem, send_sem, recv_sem):
    count = own_ref.shape[0]
    number = place.shard * plane + place.me
    sequences = plane // place.group
    mine = place.shard * sequences + place.me // place.group
    started, received = [], []
    for index in range(count):
        target = place.local * count + index
        peer = {"shard": target // plane, "expert": lax.rem(target, plane)}
        copy = remote(own_ref.at[index], out_ref.at[mine], send_sem.at[index], recv_sem.at[mine], peer)
        keep = pltpu.make_async_copy(own_ref.at[index], out_ref.at[mine], copy_sem)

        @pl.when(target != number)
        def _():
            copy.start()

        @pl.when(target == number)
        def _():
            keep.start()

        started.append((target != number, target == number, copy, keep))
    for shard in range(shards):
        for sequence in range(sequences):
            source = shard * plane + sequence * place.group + number // count
            slot = shard * sequences + sequence
            peer = {"shard": source // plane, "expert": lax.rem(source, plane)}
            copy = remote(own_ref.at[0], out_ref.at[slot], send_sem.at[0], recv_sem.at[slot], peer)
            received.append((source != number, copy))
    return HeadRows(started, received), []


def bundle_kernel(group, shards, kinds, *refs):
    count = len(kinds)
    ins, outs, rest = refs[:count], refs[count : 2 * count], refs[2 * count :]
    place = Place(group)
    plane = lax.axis_size("expert")
    peers = []
    if "gather" in kinds or "reduce" in kinds:
        peers += place.neighbours()
    members = [{"expert": place.base + lax.rem(place.local + step, group)} for step in range(1, group)]
    if "trade" in kinds:
        peers = [(place.always, member) for member in members]
    across = [{"shard": lax.rem(place.shard + step, shards)} for step in range(1, shards)]
    if "swap" in kinds or "share" in kinds:
        peers += [(place.always, peer) for peer in across]
    everyone = []
    if "owners" in kinds or "rows" in kinds:
        total = shards * plane
        number = place.shard * plane + place.me
        for step in range(1, total):
            target = lax.rem(number + step, total)
            everyone.append((target, {"shard": target // plane, "expert": lax.rem(target, plane)}))
        peers = [(place.always, peer) for _, peer in everyone]
    greet(peers)
    sender = Sender()
    runs, waits = [], []
    for kind, own, out in zip(kinds, ins, outs):
        if kind == "gather":
            copy_sem, send_sem, recv_sem, *rest = rest
            runs.append(gather_steps(place, own, out, copy_sem, send_sem, recv_sem, sender))
        elif kind == "reduce":
            scratch, rest = rest[:13], rest[13:]
            runs.append(reduce_steps(place, own, out, scratch, sender))
        else:
            copy_sem, send_sem, recv_sem, *rest = rest
            if kind == "swap":
                mine, source = place.shard, lambda target: own
                targets = [(lax.rem(place.shard + step, shards), peer) for step, peer in enumerate(across, 1)]
            elif kind == "share":
                mine, source = place.shard, lambda target: own.at[target]
                targets = [(lax.rem(place.shard + step, shards), peer) for step, peer in enumerate(across, 1)]
            elif kind == "trade":
                mine, source = place.local, lambda target: own.at[target]
                targets = [(lax.rem(place.local + step, group), peer) for step, peer in enumerate(members, 1)]
            elif kind == "owners":
                mine, source = place.shard * plane + place.me, lambda target: own.at[target]
                targets = everyone
            else:
                waits.append(head_rows(place, plane, shards, own, out, copy_sem, send_sem, recv_sem))
                continue
            keep = None
            if kind != "share":
                keep = pltpu.make_async_copy(source(mine), out.at[mine], copy_sem)
                keep.start()
            total = len(targets) + 1
            copies = []
            for step, (target, peer) in enumerate(targets, 1):
                copy = remote(source(target), out.at[mine], send_sem.at[step], recv_sem.at[step], peer)
                copy.start()
                copies.append(copy)
            waits.append((keep, copies))
    while runs:
        runs = [run for run in runs if next(run, "end") != "end"]
    for keep, copies in waits:
        if keep is not None:
            keep.wait()
        for copy in copies:
            copy.wait()
    sender.finish()


def bundle(number, group, shards, transfers, limit=48 * 2**20):
    kinds, arrays, shapes, scratch = [], [], [], []
    members = shards * lax.axis_size("expert")
    for kind, array in transfers:
        kinds.append(kind)
        sems = [pltpu.SemaphoreType.DMA(())]
        if kind == "gather":
            pieces = PIECES if array.shape[0] % (16 * PIECES) == 0 else 1
            array = array.reshape((pieces, array.shape[0] // pieces) + array.shape[1:])
            shape = (group,) + array.shape
            sems += [pltpu.SemaphoreType.DMA((4, group, pieces)), pltpu.SemaphoreType.DMA((group, pieces))]
        elif kind == "reduce":
            pieces = 2 * PIECES
            array = array.reshape(group, pieces, array.shape[1] // pieces, array.shape[2])
            shape = array.shape[1:]
            sems = reduce_scratch(group, *shape)
        else:
            total = {"swap": shards, "share": shards, "trade": group, "owners": members}.get(kind)
            shape = ((total,) + array.shape) if kind == "swap" else array.shape
            if kind == "rows":
                total = max(array.shape[0], members // group)
                shape = (members // group,) + array.shape[1:]
            sems += [pltpu.SemaphoreType.DMA((total,)), pltpu.SemaphoreType.DMA((total,))]
        arrays.append(array)
        shapes.append(jax.ShapeDtypeStruct(shape, jnp.float32 if kind == "reduce" else array.dtype))
        scratch += sems
    outs = pl.pallas_call(
        functools.partial(bundle_kernel, group, shards, tuple(kinds)),
        out_shape=shapes,
        in_specs=[pl.BlockSpec(memory_space=pl.ANY)] * len(arrays),
        out_specs=[pl.BlockSpec(memory_space=pl.ANY)] * len(arrays),
        scratch_shapes=scratch,
        compiler_params=pltpu.CompilerParams(
            collective_id=number, has_side_effects=True, vmem_limit_bytes=limit
        ),
        name="bundle_" + "_".join(kinds[:2]),
    )(*arrays)
    done = []
    for (kind, array), out in zip(transfers, outs):
        if kind == "gather":
            out = out.reshape((group,) + array.shape)
        if kind == "reduce":
            out = out.reshape(array.shape[1:])
        done.append(out)
    return done


def pieces_of(size, most):
    return [(at, min(most, size - at)) for at in range(0, size, most)]


def expert_kernel(
    me_ref, routes_ref, router_ref, rows_in, grads_in, *rest
):
    weights, rest = rest[:12], rest[12:]
    (back_ref, out_ref, rows_ref, grad_ref, hidden_ref, gate_back_ref, up_back_ref, score_ref,
     shared_hidden_ref, shared_gate_back_ref, shared_up_back_ref, slot_cotangent, pick_buf, gate_buf,
     gate_w, up_w, down_w, shared_gate_w, shared_up_w, shared_down_w, weight_sem) = rest
    targets = (shared_gate_w, shared_up_w, shared_down_w, gate_w, up_w, down_w)
    shard_at = me_ref[0, 1]
    loads = []
    for index, target in enumerate(targets):
        own, got = weights[2 * index], weights[2 * index + 1]
        count = got.shape[0]
        for step in range(count):
            at = lax.rem(shard_at + step, count)
            block = own.shape[0]
            spot = target.at[at] if len(target.shape) == 3 else target.at[pl.ds(pl.multiple_of(at * block, 16), block), :]
            source = own if step == 0 else got.at[at]
            loads.append(pltpu.make_async_copy(source, spot, weight_sem.at[index, step]))

    def when_first(action):
        @pl.when(pl.program_id(0) == 0)
        def _():
            action()

    def start_loads():
        for load in loads:
            load.start()

    def wait_loads():
        for load in loads:
            load.wait()

    when_first(start_loads)
    width = rows_in.shape[1]
    hidden_width = gate_w.shape[1]
    shards, own_width, _ = shared_gate_w.shape
    senders, _, rows = routes_ref.shape
    capacity = pick_buf.shape[0] // senders
    experts = router_ref.shape[0]
    low = jnp.bfloat16
    me = me_ref[0, 0]

    @pl.when(pl.program_id(0) == 0)
    def _():
        pick_buf[...] = jnp.zeros_like(pick_buf)

    logits = matmul_nt(router_ref[...], rows_in[...])
    names = lax.broadcasted_iota(jnp.int32, (experts, rows), 0)
    earlier = lax.broadcasted_iota(jnp.int32, (rows, rows), 0) <= lax.broadcasted_iota(jnp.int32, (rows, rows), 1)
    earlier = jnp.where(earlier, 1.0, 0.0).astype(low)
    slot_names = lax.broadcasted_iota(jnp.int32, (capacity, rows), 0).astype(jnp.float32)
    picks = []
    for sender in range(senders):
        routed = routes_ref[sender]
        chosen = jnp.zeros((experts, rows), jnp.float32)
        for choice in range(TOP):
            chosen = chosen + jnp.where(routed[choice : choice + 1] == names, 1.0, 0.0)
        logit = jnp.where(chosen > 0.0, logits[:, sender * rows : (sender + 1) * rows], NEG)
        expo = jnp.exp(logit - jnp.max(logit, axis=0, keepdims=True)) * chosen
        dense = expo / jnp.sum(expo, axis=0, keepdims=True)
        gate_row = jnp.sum(jnp.where(names == me, dense, 0.0), axis=0, keepdims=True)
        mark = jnp.sum(jnp.where(routed == me, 1.0, 0.0), axis=0, keepdims=True)
        rank = matmul(jnp.broadcast_to(mark, (8, rows)).astype(low), earlier)[:1] - 1.0
        pick = jnp.where((slot_names == rank) & (mark > 0.0), 1.0, 0.0)
        picks.append(pick)
        at = slice(sender * capacity, (sender + 1) * capacity)
        pick_buf[at, sender * rows : (sender + 1) * rows] = pick.astype(low)
        gate_buf[at, :] = jnp.sum(pick * gate_row, axis=1, keepdims=True)
    gate = gate_buf[...]

    def pick_step(index, _):
        at = pl.ds(pl.multiple_of(index * 512, 512), 512)
        rows_ref[:, at] = matmul(pick_buf[...], rows_in[:, at]).astype(low)
        picked = matmul(pick_buf[...], grads_in[:, at])
        slot_cotangent[:, at] = picked.astype(low)
        grad_ref[:, at] = (gate * picked).astype(low)
        return 0

    lax.fori_loop(0, width // 512, pick_step, 0)
    when_first(wait_loads)
    shared_pre, shared_up = 0.0, 0.0
    for shard in range(shards):
        part = rows_in[:, shard * own_width : (shard + 1) * own_width]
        shared_pre = shared_pre + matmul(part, shared_gate_w[shard])
        shared_up = shared_up + matmul(part, shared_up_w[shard])
    swished, slope = swish_parts(shared_pre)
    shared_hidden_ref[...] = (swished * shared_up).astype(low)
    shared_grad = matmul_nt(grads_in[...], shared_down_w[...])
    shared_gate_back_ref[...] = (shared_grad * shared_up * slope).astype(low)
    shared_up_back_ref[...] = (shared_grad * swished).astype(low)
    for at, size in pieces_of(hidden_width, 512):
        columns = slice(at, at + size)
        gate_pre = matmul(rows_ref[...], gate_w[:, columns])
        up_pre = matmul(rows_ref[...], up_w[:, columns])
        swished, slope = swish_parts(gate_pre)
        hidden_ref[:, columns] = (swished * up_pre).astype(low)
        hidden_grad = matmul_nt(grad_ref[...], down_w[columns, :])
        gate_back_ref[:, columns] = (hidden_grad * up_pre * slope).astype(low)
        up_back_ref[:, columns] = (hidden_grad * swished).astype(low)

    def out_step(index, score):
        at = pl.ds(pl.multiple_of(index * 512, 512), 512)
        shard = index * 512 // own_width
        within = pl.ds(pl.multiple_of(index * 512 - shard * own_width, 512), 512)
        expert_out = matmul(hidden_ref[...], down_w[:, at]).astype(low).astype(jnp.float32)
        score = score + jnp.sum(expert_out * slot_cotangent[:, at].astype(jnp.float32), axis=1, keepdims=True)
        out = matmul_tn(pick_buf[...], (gate * expert_out).astype(low))
        out_ref[:, at] = (out + matmul(shared_hidden_ref[...], shared_down_w[:, at])).astype(low)
        row_back = matmul_nt(gate_back_ref[...], gate_w[at, :]) + matmul_nt(up_back_ref[...], up_w[at, :])
        back = (
            matmul_tn(pick_buf[...], row_back.astype(low))
            + matmul_nt(shared_gate_back_ref[...], shared_gate_w[shard, within, :])
            + matmul_nt(shared_up_back_ref[...], shared_up_w[shard, within, :])
        )
        back_ref[:, at] = back.astype(low)
        return score

    score = lax.fori_loop(0, width // 512, out_step, jnp.zeros((gate.shape[0], 1), jnp.float32))
    for sender in range(senders):
        own = score[sender * capacity : (sender + 1) * capacity]
        total = jnp.sum(picks[sender] * own, axis=0, keepdims=True)
        score_ref[sender] = jnp.broadcast_to(total, score_ref.shape[1:])


def expert_pass(me, routes, router, rows, grads, weights, capacity):
    plane, _, local = routes.shape
    senders = STEP_SENDERS
    tokens, slots = senders * local, senders * capacity
    steps = plane // senders
    shards = weights[1].shape[0]
    width, hidden_width = rows.shape[1], weights[6].shape[1]
    units = weights[0].shape[1]
    low = jnp.bfloat16

    def whole(array):
        return pl.BlockSpec(array.shape, lambda i: (0,) * array.ndim, pipeline_mode=pl.Buffered(1))

    def by_step(r, c):
        return pl.BlockSpec((r, c), lambda i: (i, 0))

    total = steps * slots
    shape = jax.ShapeDtypeStruct
    route_block = pl.BlockSpec((senders, 8, local), lambda i: (i, 0, 0))
    return pl.pallas_call(
        expert_kernel,
        grid=(steps,),
        out_shape=[
            shape((steps * tokens, width), low),
            shape((steps * tokens, width), low),
            shape((total, width), low),
            shape((total, width), low),
            shape((total, hidden_width), low),
            shape((total, hidden_width), low),
            shape((total, hidden_width), low),
            shape((plane, 8, local), jnp.float32),
            shape((steps * tokens, units), low),
            shape((steps * tokens, units), low),
            shape((steps * tokens, units), low),
        ],
        in_specs=[
            pl.BlockSpec(memory_space=pltpu.SMEM),
            route_block,
            whole(router),
            by_step(tokens, width),
            by_step(tokens, width),
        ]
        + [pl.BlockSpec(memory_space=pl.ANY)] * len(weights),
        out_specs=[
            by_step(tokens, width),
            by_step(tokens, width),
            by_step(slots, width),
            by_step(slots, width),
            by_step(slots, hidden_width),
            by_step(slots, hidden_width),
            by_step(slots, hidden_width),
            route_block,
            by_step(tokens, units),
            by_step(tokens, units),
            by_step(tokens, units),
        ],
        scratch_shapes=[
            pltpu.VMEM((slots, width), low),
            pltpu.VMEM((slots, tokens), low),
            pltpu.VMEM((slots, 1), jnp.float32),
            pltpu.VMEM((width, hidden_width), low),
            pltpu.VMEM((width, hidden_width), low),
            pltpu.VMEM((hidden_width, width), low),
            pltpu.VMEM((shards, width // shards, units), low),
            pltpu.VMEM((shards, width // shards, units), low),
            pltpu.VMEM((units, width), low),
            pltpu.SemaphoreType.DMA((6, shards)),
        ],
        compiler_params=pltpu.CompilerParams(
            vmem_limit_bytes=60 * 2**20, dimension_semantics=("arbitrary",)
        ),
        name="experts",
    )(me, routes, router, rows, grads, *weights)


QUERIES = 256
KEYS = WINDOW + QUERIES


def score_block(scale, query, keys, query_docs, key_docs):
    raw = matmul_nt(query, keys) * scale
    row = lax.broadcasted_iota(jnp.int32, raw.shape, 0) + WINDOW
    column = lax.broadcasted_iota(jnp.int32, raw.shape, 1)
    allowed = (query_docs == key_docs) & (column <= row) & (column > row - WINDOW)
    return jnp.where(allowed, raw, NEG)


class Swaps:
    def __init__(self, place, shards, sender):
        self.place, self.shards, self.sender = place, shards, sender

    def start(self, source, target, send_sem, recv_sem, keep=None):
        place, shards = self.place, self.shards
        arrivals = []
        for step in range(1, shards):
            other = lax.rem(place.shard + step, shards)
            self.sender.start(
                place.always,
                remote(source, target(place.shard), send_sem.at[step], recv_sem.at[place.shard], {"shard": other}),
            )
            arrivals.append(
                remote(source, target(other), send_sem.at[step], recv_sem.at[other], {"shard": other})
            )
        if keep is not None:
            copy = pltpu.make_async_copy(source, target(place.shard), keep)
            copy.start()

        def wait():
            for arrival in arrivals:
                arrival.wait_recv()
            if keep is not None:
                copy.wait()

        return wait


def whole_weight(place, others, own_ref, full_ref, buf, sem):
    copies = [pltpu.make_async_copy(own_ref, buf.at[place.shard], sem.at[0])]
    for step, other in enumerate(others, 1):
        copies.append(pltpu.make_async_copy(full_ref.at[other], buf.at[other], sem.at[step]))
    for copy in copies:
        copy.start()
    return copies


def drain(run):
    for _ in run:
        pass


def forward_kernel(shards, plane, scale, last, *refs):
    (tokens, cotangent, query_cols, down_half, up_half, out_half, query_half, gate_half, wide_half, narrow_half,
     shared_gate, shared_up, shared_down, routes, first_gain, latent_gain, second_gain, turn, sway, docs, row_docs,
     all_normed, all_grads, all_routes, full_down, full_out, full_query, full_gate, full_up, full_narrow,
     full_shared_gate, full_shared_up, full_shared_down, normed_one,
     query, keys, value, key_latent, compressed, head_out, log_total, middle, up_buf,
     token_buf, normed_buf, query_buf, down_buf, out_buf, heads_buf, second_buf,
     swap_send, swap_recv, keep_sem, gather_send, gather_recv, gather_keep, piece_send, piece_recv,
     trade_send, trade_recv, load_sem, whole_sem) = refs
    low = jnp.bfloat16
    group = SEQ_DEVICES
    place, wide = Place(group), Place(plane)
    width = tokens.shape[-1]
    rows = docs.shape[0] // group
    sender = Sender()
    members = [lax.rem(place.local + step, group) for step in range(1, group)]
    peers = [(place.always, {"expert": place.base + member}) for member in members]
    if plane != group:
        peers += [
            (wide.upper & ~place.upper, {"expert": place.me + INNER}),
            (wide.lower & ~place.lower, {"expert": place.me - INNER}),
        ]
    others = [lax.rem(place.shard + step, shards) for step in range(1, shards)]
    peers += [(place.always, {"shard": other}) for other in others]
    greet(peers)

    swaps = Swaps(place, shards, sender)
    numbers = iter(range(16))

    def swap(source, target, keep=False):
        at = next(numbers)
        return swaps.start(
            source, target, swap_send.at[at], swap_recv.at[at], keep_sem.at[at] if keep else None
        )

    at_piece = lambda ref: ref.at[wide.me]
    got_query = swap(query_cols, lambda shard: query_buf.at[shard], True)
    got_down = swap(at_piece(down_half), lambda shard: full_down.at[shard, wide.me])
    got_up = swap(up_half, lambda shard: up_buf.at[shard], True)
    token_run = gather_steps(
        place, tokens, token_buf, gather_keep.at[0], gather_send.at[0], gather_recv.at[0], sender
    )
    next(token_run)
    got_out = swap(at_piece(out_half), lambda shard: full_out.at[shard, wide.me])
    got_wq = swap(at_piece(query_half), lambda shard: full_query.at[shard, wide.me])
    def piece_gathers(kind, full):
        return [
            gather_steps(
                wide, None, full.at[other], None, piece_send.at[kind, step], piece_recv.at[kind, step], sender
            )
            for step, other in enumerate(others)
        ]

    next(token_run)
    got_down()
    down_runs = piece_gathers(0, full_down)
    for run in down_runs:
        next(run)
    next(token_run)
    for run in down_runs:
        next(run)
    got_query()
    got_up()
    waits = [
        swap(gate_half, lambda shard: full_gate.at[shard]),
        swap(wide_half, lambda shard: full_up.at[shard]),
    ]
    drain(token_run)
    got_out()
    got_wq()
    waits += [
        swap(shared_gate, lambda shard: full_shared_gate.at[shard]),
        swap(shared_up, lambda shard: full_shared_up.at[shard]),
        swap(shared_down, lambda shard: full_shared_down.at[shard]),
        swap(narrow_half, lambda shard: full_narrow.at[shard]),
    ]
    for run in down_runs:
        drain(run)
    route_run = gather_steps(
        wide, routes, all_routes, gather_keep.at[1], gather_send.at[1], gather_recv.at[1], sender
    )
    next(route_run)
    out_runs = piece_gathers(1, full_out)
    for run in out_runs:
        next(run)
    for copy in whole_weight(place, others, down_half, full_down, down_buf, whole_sem.at[0]):
        copy.wait()

    keys[:WINDOW, :] = jnp.zeros((WINDOW, keys.shape[1]), low)
    value[:WINDOW, :] = jnp.zeros((WINDOW, value.shape[1]), low)
    tile = 2 * rows
    own_width = width // shards

    def whole_dot(at, weight_of):
        total = 0.0
        for shard in range(shards):
            total = total + matmul(normed_buf[at, shard * own_width : (shard + 1) * own_width], weight_of(shard))
        return total

    def front_tile(index, _):
        at = pl.ds(pl.multiple_of(index * tile, tile), tile)
        values = token_buf[pl.ds(index * 2, 2)].reshape(tile, width).astype(jnp.float32)
        root = lax.rsqrt(jnp.mean(values * values, axis=1, keepdims=True) + EPS)
        normed_buf[at, :] = (values * root * first_gain[...]).astype(low)
        first = whole_dot(at, lambda shard: query_buf[shard])
        latent = whole_dot(at, lambda shard: down_buf[shard].reshape(own_width, -1))
        turn_at, sway_at = turn[at, :QK_ROPE], sway[at, :QK_ROPE]
        end = QK_NOPE + QK_ROPE
        query[at, :QK_NOPE] = first[:, :QK_NOPE].astype(low)
        query[at, QK_NOPE:end] = (first[:, QK_NOPE:end] * turn_at + first[:, end:] * sway_at).astype(low)
        query[at, end:] = jnp.zeros((tile, QK_ROPE), low)
        end = KV_RANK + QK_ROPE
        key_rope = (latent[:, KV_RANK:end] * turn_at + latent[:, end:] * sway_at).astype(low)
        latent = latent[:, :KV_RANK]
        compressed[at, :] = latent
        root = lax.rsqrt(jnp.mean(latent * latent, axis=1, keepdims=True) + EPS)
        normed_latent = (latent * root * latent_gain[...]).astype(low)
        key_latent[at, :] = normed_latent
        up_rows = KV_RANK // shards
        both = 0.0
        for shard in range(shards):
            both = both + matmul(normed_latent[:, shard * up_rows : (shard + 1) * up_rows], up_buf[shard])
        both = both.astype(low)
        later = pl.ds(pl.multiple_of(index * tile + WINDOW, tile), tile)
        keys[later, :QK_NOPE] = both[:, :QK_NOPE]
        keys[later, QK_NOPE : QK_NOPE + QK_ROPE] = key_rope
        keys[later, QK_NOPE + QK_ROPE :] = key_rope
        value[later, :] = both[:, QK_NOPE:]
        return 0

    tiles = group // 2
    grad_run = gather_steps(
        wide, cotangent, all_grads, gather_keep.at[3], gather_send.at[3], gather_recv.at[3], sender
    )
    for part in range(2):
        lax.fori_loop(part * tiles // 2, (part + 1) * tiles // 2, front_tile, 0)
        for run in out_runs + [route_run]:
            next(run, None)
    next(grad_run)
    save = pltpu.make_async_copy(normed_buf, normed_one, load_sem.at[1])
    save.start()
    for run in out_runs + [route_run]:
        next(run, None)

    def attend_tile(index, _):
        at = pl.ds(pl.multiple_of(index * QUERIES, QUERIES), QUERIES)
        window = pl.ds(pl.multiple_of(index * QUERIES, QUERIES), KEYS)
        scores = score_block(scale, query[at, :], keys[window, :], docs[at, :], row_docs[:, window])
        top = jnp.max(scores, axis=1, keepdims=True)
        expo = jnp.exp(scores - top)
        total = jnp.sum(expo, axis=1, keepdims=True)
        probs = (expo / total).astype(low)
        real = jnp.where(docs[at, :] < last, 1.0, 0.0)
        head_out[at, :] = (matmul(probs, value[window, :]) * real).astype(low)
        log_total[at, :] = jnp.broadcast_to(top + jnp.log(total), (QUERIES, log_total.shape[1]))
        return 0

    blocks = docs.shape[0] // QUERIES
    lax.fori_loop(0, blocks // 2, attend_tile, 0)
    for run in out_runs + [route_run]:
        drain(run)
    load_out = whole_weight(place, others, out_half, full_out, out_buf, whole_sem.at[1])
    next(grad_run)
    lax.fori_loop(blocks // 2, blocks, attend_tile, 0)

    def head_at(member):
        return head_out.at[pl.ds(pl.multiple_of(member * rows, rows), rows), :]

    def lands(head):
        return heads_buf.at[:, pl.ds(pl.multiple_of(head * V_HEAD, V_HEAD), V_HEAD)]

    keep = pltpu.make_async_copy(head_at(place.local), lands(place.local), load_sem.at[2])
    keep.start()
    for step, member in enumerate(members):
        sender.start(
            place.always,
            remote(
                head_at(member), lands(place.local), trade_send.at[step], trade_recv.at[place.local],
                {"expert": place.base + member},
            ),
        )
    for step, member in enumerate(members):
        remote(
            head_at(member), lands(member), trade_send.at[step], trade_recv.at[member], {"expert": place.base + member}
        ).wait_recv()
    keep.wait()
    for copy in load_out:
        copy.wait()

    for at, size in pieces_of(width, 512):
        columns = slice(at, at + size)
        total = token_buf[place.local].reshape(rows, width)[:, columns].astype(jnp.float32)
        for shard in range(shards):
            weight = out_buf[shard, :, :, :, columns].reshape(own_width, size)
            total = total + matmul(heads_buf[:, shard * own_width : (shard + 1) * own_width], weight)
        middle[:, columns] = total
    values = middle[...]
    root = lax.rsqrt(jnp.mean(values * values, axis=1, keepdims=True) + EPS)
    second_buf[...] = (values * root * second_gain[...]).astype(low).reshape(second_buf.shape)

    normed_run = gather_steps(
        wide, second_buf, all_normed, gather_keep.at[2], gather_send.at[2], gather_recv.at[2], sender
    )
    wq_runs = piece_gathers(2, full_query)
    runs = [normed_run, grad_run] + wq_runs
    while runs:
        runs = [run for run in runs if next(run, "end") != "end"]
    save.wait()
    for wait in waits:
        wait()
    sender.finish()


def forward_pass(scale, last, tokens, cotangent, blocks, routes, gains, tables):
    shards, plane = lax.axis_size("shard"), lax.axis_size("expert")
    local, width = tokens.shape
    low, shape = jnp.bfloat16, jax.ShapeDtypeStruct
    pieces = (PIECES, local // PIECES, width)
    any_space, vmem = pl.BlockSpec(memory_space=pl.ANY), pl.BlockSpec(memory_space=pltpu.VMEM)
    head_dim = QK_NOPE + QK_ROPE
    query_cols, down_half, up_half, out_half, query_half = blocks[:5]
    out_shape = [
        shape((plane,) + pieces, low),
        shape((plane,) + pieces, low),
        shape((plane, 1) + routes.shape, jnp.int32),
    ]
    out_shape += [shape((shards,) + block.shape, low) for block in (down_half, out_half, query_half) + blocks[5:]]
    out_shape += [
        shape((SEQ, width), low),
        shape((SEQ, head_dim + QK_ROPE), low),
        shape((SEQ + WINDOW, head_dim + QK_ROPE), low),
        shape((SEQ + WINDOW, V_HEAD), low),
        shape((SEQ, KV_RANK), low),
        shape((SEQ, KV_RANK), jnp.float32),
        shape((SEQ, V_HEAD), low),
        shape((SEQ, 128), jnp.float32),
        shape((local, width), jnp.float32),
        shape((shards,) + up_half.shape, low),
    ]
    hbm_out = 13
    dma = pltpu.SemaphoreType.DMA
    return pl.pallas_call(
        functools.partial(forward_kernel, shards, plane, scale, last),
        out_shape=out_shape,
        in_specs=[any_space] * (3 + len(blocks)) + [vmem] * (len(gains) + len(tables)),
        out_specs=[any_space] * hbm_out + [vmem] * (len(out_shape) - hbm_out),
        scratch_shapes=[
            pltpu.VMEM((SEQ_DEVICES,) + pieces, low),
            pltpu.VMEM((SEQ, width), low),
            pltpu.VMEM((shards,) + query_cols.shape, low),
            pltpu.VMEM((shards,) + down_half.shape, low),
            pltpu.VMEM((shards,) + out_half.shape, low),
            pltpu.VMEM((local, HEADS * V_HEAD), low),
            pltpu.VMEM(pieces, low),
            dma((12, shards)),
            dma((12, shards)),
            dma((12,)),
            dma((4, 4, plane, PIECES)),
            dma((4, plane, PIECES)),
            dma((4,)),
            dma((3, shards, 4, plane, 1)),
            dma((3, shards, plane, 1)),
            dma((SEQ_DEVICES,)),
            dma((SEQ_DEVICES,)),
            dma((4,)),
            dma((2, shards)),
        ],
        compiler_params=pltpu.CompilerParams(
            collective_id=1, has_side_effects=True, vmem_limit_bytes=60 * 2**20
        ),
        name="forward",
    )(tokens.reshape(pieces), cotangent.reshape(pieces), *blocks, routes[None], *gains, *tables)


class Everyone:
    def __init__(self, place, plane, shards, source, got, send_sem, recv_sem, keep_sem):
        self.total = shards * plane
        self.plane = plane
        self.number = place.shard * plane + place.me
        self.source, self.got = source, got
        self.send_sem, self.recv_sem = send_sem, recv_sem
        self.keep = pltpu.make_async_copy(source(self.number), got.at[self.number], keep_sem)

    def copy(self, step, arriving):
        other = lax.rem(self.number + step, self.total)
        spot = other if arriving else self.number
        return remote(
            self.source(other),
            self.got.at[spot],
            self.send_sem.at[step],
            self.recv_sem.at[spot],
            {"shard": other // self.plane, "expert": lax.rem(other, self.plane)},
        )

    def start(self):
        self.keep.start()

        def body(step, _):
            self.copy(step, False).start()
            return 0

        lax.fori_loop(1, self.total, body, 0)

    def wait(self):
        self.keep.wait()

        def body(step, _):
            self.copy(step, True).wait_recv()
            return 0

        lax.fori_loop(1, self.total, body, 0)

    def finish(self):
        def body(step, _):
            self.copy(step, False).wait_send()
            return 0

        lax.fori_loop(1, self.total, body, 0)


def greet_everyone(place, plane, shards):
    barrier = pltpu.get_barrier_semaphore()
    total = shards * plane
    number = place.shard * plane + place.me

    def body(step, _):
        other = lax.rem(number + step, total)
        pl.semaphore_signal(
            barrier,
            inc=1,
            device_id={"shard": other // plane, "expert": lax.rem(other, plane)},
            device_id_type=MESH,
        )
        return 0

    lax.fori_loop(1, total, body, 0)
    pl.semaphore_wait(barrier, total - 1)


def norm_back(values, gain, grad):
    root = lax.rsqrt(jnp.mean(values * values, axis=1, keepdims=True) + EPS)
    weighted = grad * gain
    inner = jnp.mean(weighted * values, axis=1, keepdims=True)
    scaled = values * root
    return root * (weighted - scaled * (root * inner)), jnp.sum(grad * scaled, axis=0, keepdims=True)


def two_parts(values):
    high = values.astype(jnp.bfloat16)
    return high, (values - high.astype(jnp.float32)).astype(jnp.bfloat16)


def swapped_halves(pair):
    return pltpu.roll(pair, QK_ROPE // 2, 1)


def backward_kernel(shards, plane, scale, last, *refs):
    (back, scores, routes, middle, cotangent, tokens, first_gain, second_gain, latent_gain, router,
     query, keys, value, docs, row_docs, log_total, turn, sway, key_latent, up_head, head_out,
     compressed, full_out, full_query, full_down, normed_one, out_half, query_half, down_half, gate_send, up_send, narrow_send, shared_term,
     input_grad, query_out, up_out, down_out, out_out, small_out,
     gate_got, up_got, narrow_got, shared_got, mid_all,
     stream_buf, wq_buf, wd_buf, own_columns, own_compressed, heads_sum, mid_buf, low_buf, heads_buf, grad_buf, key_sum, value_sum,
     part_buf, trade_buf, trade_got, pair_buf, query_term, query_got, up_term, up_got_buf, own_query, low_grad, low_all,
     down_rows, down_got, out_rows, out_got, small_buf, small_got, key_got, *sems) = refs
    (load_sem, whole_sem, stream_sem, swap_send, swap_recv, trade_send, trade_recv, gather_send, gather_recv, gather_keep,
     all_send, all_recv, all_keep, rows_send, rows_recv, rows_keep, *reduce_scratch_refs) = sems
    low = jnp.bfloat16
    group = SEQ_DEVICES
    place = Place(group)
    local, width = middle.shape
    total = shards * plane
    sender = Sender()
    greet_everyone(place, plane, shards)
    members = [lax.rem(place.local + step, group) for step in range(1, group)]
    others = [lax.rem(place.shard + step, shards) for step in range(1, shards)]

    shares = []
    for number, (source, got) in enumerate(((gate_send, gate_got), (up_send, up_got), (narrow_send, narrow_got))):
        for step, other in enumerate(others, 1):
            sender.start(
                place.always,
                remote(source.at[other], got.at[place.shard], swap_send.at[number, step],
                       swap_recv.at[number, place.shard], {"shard": other}),
            )
            shares.append(
                remote(source.at[other], got.at[other], swap_send.at[number, step], swap_recv.at[number, other],
                       {"shard": other})
            )
    numbers = iter(range(16))

    def load(source, target):
        copy = pltpu.make_async_copy(source, target, load_sem.at[next(numbers)])
        copy.start()
        return copy

    own_lanes = pl.ds(pl.multiple_of(place.local * 128, 128), 128)
    got_wd = whole_weight(place, others, down_half, full_down, wd_buf, whole_sem)
    got_columns = load(normed_one.at[:, :, :, own_lanes], own_columns)
    tile = stream_buf.shape[-1]
    tiles = [slice(at, at + tile) for at in range(0, width, tile)]

    def streamed(buf, count, sources):
        def copies(index):
            half = index % 2
            return [
                (there, pltpu.make_async_copy(source, target, stream_sem.at[half, number]))
                for there, source, target, number in sources(index, buf.at[half])
            ]

        def start(index):
            for there, copy in copies(index):
                @pl.when(there)
                def _():
                    copy.start()

        start(0)
        for index in range(count):
            if index + 1 < count:
                start(index + 1)
            for there, copy in copies(index):
                @pl.when(there)
                def _():
                    copy.wait()
            yield index, buf.at[index % 2]

    own_at = pl.ds(pl.multiple_of(place.local * local, local), local)
    per_shard = group // shards

    def columns_of(array):
        def sources(index, target):
            return [
                (place.always, array.at[pl.ds(shard * per_shard, per_shard), :, :, tiles[index]], target.at[shard], shard)
                for shard in range(shards)
            ]

        return sources

    def out_columns(index, target):
        found = []
        for shard in range(shards):
            mine = place.shard == shard
            found.append((mine, out_half.at[:, :, :, tiles[index]], target.at[shard], shard))
            found.append((~mine, full_out.at[shard, :, :, :, tiles[index]], target.at[shard], shard))
        return found

    row_tile = wq_buf.shape[1]
    own_rows = width // shards

    def query_rows(index, target):
        shard = index * row_tile // own_rows
        rows = slice(index * row_tile - shard * own_rows, (index + 1) * row_tile - shard * own_rows)
        mine = place.shard == shard
        return [(mine, query_half.at[rows], target, 0), (~mine, full_query.at[shard, rows], target, 0)]

    got_compressed = load(compressed.at[own_at, :], own_compressed)

    def everyone(index, source, got):
        return Everyone(place, plane, shards, source, got, all_send.at[index], all_recv.at[index], all_keep.at[index])

    experts = router.shape[0]
    values = middle[...]
    root = lax.rsqrt(jnp.mean(values * values, axis=1, keepdims=True) + EPS)
    second_normed = (values * root * second_gain[...]).astype(low)
    logits = matmul_nt(router[...], second_normed)
    names = lax.broadcasted_iota(jnp.int32, (experts, local), 0)
    chosen = jnp.zeros((experts, local), jnp.float32)
    for choice in range(TOP):
        chosen = chosen + jnp.where(routes[choice : choice + 1, :] == names, 1.0, 0.0)
    logits = jnp.where(chosen > 0.0, logits, NEG)
    gates = jnp.exp(logits - jnp.max(logits, axis=0, keepdims=True)) * chosen
    gates = gates / jnp.sum(gates, axis=0, keepdims=True)
    gate_grad = jnp.concatenate([scores[index, :1, :] for index in range(experts)], axis=0)
    logit_grad = gates * (gate_grad - jnp.sum(gates * gate_grad, axis=0, keepdims=True))
    high, rest = two_parts(logit_grad)
    router_term = matmul(high, second_normed) + matmul(rest, second_normed)
    grad = back[...] + matmul_tn(high, router[...]) + matmul_tn(rest, router[...])
    row_grad, second_term = norm_back(values, second_gain[...], grad)
    mid_buf[...] = cotangent[...].astype(jnp.float32) + row_grad
    low_buf[...] = mid_buf[...].astype(low).reshape(low_buf.shape)

    for index, piece in streamed(stream_buf, len(tiles), out_columns):
        part = matmul_nt(low_buf[:, :, tiles[index]].reshape(local, tile), piece[...].reshape(-1, tile))
        heads_sum[...] = part if index == 0 else heads_sum[...] + part
    heads_buf[...] = heads_sum[...].astype(low)

    def lands(member):
        return heads_buf.at[:, pl.ds(pl.multiple_of(member * V_HEAD, V_HEAD), V_HEAD)]

    def head_trade(step, member, source):
        spot = pl.ds(pl.multiple_of(source * local, local), local)
        return remote(lands(member), grad_buf.at[spot, :], trade_send.at[0, step], trade_recv.at[0, source],
                      {"expert": place.base + member})

    keep_head = pltpu.make_async_copy(lands(place.local), grad_buf.at[own_at, :], load_sem.at[next(numbers)])
    keep_head.start()
    for step, member in enumerate(members):
        sender.start(place.always, head_trade(step, member, place.local))
    mid_run = gather_steps(place, low_buf, mid_all, gather_keep.at[0], gather_send.at[0], gather_recv.at[0], sender)
    for step, member in enumerate(members):
        head_trade(step, member, member).wait_recv()
    keep_head.wait()
    next(mid_run)
    shared_trade = everyone(0, lambda target: shared_term.at[target], shared_got)
    shared_trade.start()

    key_sum[...] = jnp.zeros_like(key_sum)
    value_sum[...] = jnp.zeros_like(value_sum)

    def attend_tile(index, _):
        at = pl.ds(pl.multiple_of(index * QUERIES, QUERIES), QUERIES)
        window = pl.ds(pl.multiple_of(index * QUERIES, QUERIES), KEYS)
        tile, key_tile = query[at, :], keys[window, :]
        head_grad = jnp.where(docs[at, :] < last, grad_buf[at, :], jnp.zeros((), low))
        scores_at = score_block(scale, tile, key_tile, docs[at, :], row_docs[:, window])
        probs = jnp.exp(scores_at - log_total[at, :1])
        prob_grad = matmul_nt(head_grad, value[window, :])
        inner = jnp.sum(probs * prob_grad, axis=1, keepdims=True)
        raw_grad = (probs * (prob_grad - inner) * scale).astype(low)
        grads = matmul(raw_grad, key_tile)
        trade_buf[at, :QK_NOPE] = grads[:, :QK_NOPE].astype(low)
        pair = grads[:, QK_NOPE:]
        trade_buf[at, QK_NOPE:] = (pair * turn[at, :] - swapped_halves(pair) * sway[at, :]).astype(low)
        key_sum[window, :] += matmul_tn(raw_grad, tile)
        value_sum[window, :] += matmul_tn(probs.astype(low), head_grad)
        return 0

    blocks = docs.shape[0] // QUERIES
    for index in range(blocks // 2):
        attend_tile(jnp.int32(index), 0)
    next(mid_run)
    for index in range(blocks // 2, blocks):
        attend_tile(jnp.int32(index), 0)
    next(mid_run)

    lane = lax.broadcasted_iota(jnp.int32, (QUERIES, 2 * QK_ROPE), 1)

    def key_tile(index, _):
        at = pl.ds(pl.multiple_of(index * QUERIES, QUERIES), QUERIES)
        later = pl.ds(pl.multiple_of(index * QUERIES + WINDOW, QUERIES), QUERIES)
        key_rope = pltpu.roll(key_sum[later, QK_NOPE:], QK_ROPE, 1).astype(low)
        trade_buf[at, QK_NOPE:] = jnp.where(lane < QK_ROPE, trade_buf[at, QK_NOPE:], key_rope)
        pair_buf[at, :QK_NOPE] = key_sum[later, :QK_NOPE].astype(low)
        pair_buf[at, QK_NOPE:] = value_sum[later, :].astype(low)
        part = matmul_nt(pair_buf[at, :], up_head[...]).astype(low)
        per = QUERIES // local
        part_buf[pl.ds(index * per, per)] = part.reshape((per,) + part_buf.shape[1:])
        return 0

    for index in range(blocks):
        key_tile(jnp.int32(index), 0)

    def token_trade(step, member, source):
        spot = pl.ds(pl.multiple_of(member * local, local), local)
        return remote(trade_buf.at[spot, :], trade_got.at[source], trade_send.at[1, step], trade_recv.at[1, source],
                      {"expert": place.base + member})

    reduce_run = reduce_steps(place, part_buf, key_got, reduce_scratch_refs, sender)
    next(reduce_run)
    keep_token = pltpu.make_async_copy(trade_buf.at[own_at, :], trade_got.at[place.local], load_sem.at[next(numbers)])
    keep_token.start()
    for step, member in enumerate(members):
        sender.start(place.always, token_trade(step, member, place.local))

    for index, piece in streamed(stream_buf, len(tiles), columns_of(normed_one)):
        term = matmul_tn(trade_buf[...], piece[...].reshape(SEQ, tile))
        per = tile // query_term.shape[1]
        query_term[index * per : (index + 1) * per] = term.T.astype(low).reshape((per,) + query_term.shape[1:])
    up_term[...] = matmul_tn(key_latent[...], pair_buf[...]).astype(low).reshape(up_term.shape)
    next(reduce_run)
    query_trade = everyone(1, lambda target: query_term.at[target], query_got)
    query_trade.start()
    up_trade = everyone(2, lambda target: up_term.at[target], up_got_buf)
    up_trade.start()
    next(reduce_run)
    drain(reduce_run)
    for step, member in enumerate(members):
        token_trade(step, member, member).wait_recv()
    keep_token.wait()

    got_compressed.wait()
    head_dim = QK_NOPE + QK_ROPE
    rope = jnp.zeros((local, 2 * QK_ROPE), jnp.float32)
    for head in range(group):
        own_query[:, head * head_dim : (head + 1) * head_dim] = trade_got[head, :, :head_dim]
        rope = rope + trade_got[head, :, QK_NOPE:].astype(jnp.float32)
    lane = lax.broadcasted_iota(jnp.int32, rope.shape, 1)
    rope = jnp.where(lane < QK_ROPE, pltpu.roll(rope, QK_ROPE, 1), rope)
    rope = rope * turn[own_at, :] - swapped_halves(rope) * sway[own_at, :]
    latent_grad, latent_term = norm_back(own_compressed[...], latent_gain[...], key_got[...].reshape(local, KV_RANK))
    low_grad[0, 0, :, :KV_RANK] = latent_grad.astype(low)
    low_grad[0, 0, :, KV_RANK:] = jnp.where(lane < QK_ROPE, rope, 0.0).astype(low)
    low_run = gather_steps(place, low_grad.at[0], low_all, gather_keep.at[1], gather_send.at[1], gather_recv.at[1], sender)
    next(low_run)
    for copy in got_wd:
        copy.wait()
    for index, piece in streamed(wq_buf, width // row_tile, query_rows):
        rows = slice(index * row_tile, (index + 1) * row_tile)
        shard = index * row_tile // own_rows
        within = slice(rows.start - shard * own_rows, rows.stop - shard * own_rows)
        term = matmul_nt(own_query[...], piece[...])
        input_grad[:, rows] = term + matmul_nt(low_grad[0, 0], wd_buf[shard, within, :])
    next(low_run)
    row_grad, first_term = norm_back(tokens[...].astype(jnp.float32), first_gain[...], input_grad[...])
    input_grad[...] = mid_buf[...] + row_grad
    next(low_run)
    drain(mid_run)
    per_lane = width // 128
    for block in range(per_lane):
        columns = slice(block * 128, (block + 1) * 128)
        small_buf[block, :experts, :] = router_term[:, columns]
        small_buf[block, experts : experts + 1, :] = second_term[:, columns]
        small_buf[block, experts + 1 : experts + 2, :] = first_term[:, columns]
        at = block // (per_lane * 128 // KV_RANK) * 128
        small_buf[block, experts + 2 : experts + 3, :] = latent_term[:, at : at + 128]
        small_buf[block, experts + 3 :, :] = jnp.zeros((small_buf.shape[1] - experts - 3, 128), jnp.float32)
    small_trade = everyone(3, lambda target: small_buf.at[target // (total // per_lane)], small_got)
    small_trade.start()
    drain(low_run)
    got_columns.wait()
    down = matmul_tn(own_columns[...].reshape(SEQ, -1), low_all[...].reshape(SEQ, -1))
    down_rows[...] = down.astype(low).reshape(down_rows.shape)
    down_trade = head_rows(place, plane, shards, down_rows, down_got, rows_keep.at[0], rows_send.at[0], rows_recv.at[0])[0]
    for index, piece in streamed(stream_buf, len(tiles), columns_of(mid_all)):
        term = matmul_tn(head_out[...], piece[...].reshape(SEQ, tile)).astype(low)
        out_rows[:, :, tiles[index]] = term.reshape(out_rows.shape[:2] + (tile,))
    out_trade = head_rows(place, plane, shards, out_rows, out_got, rows_keep.at[1], rows_send.at[1], rows_recv.at[1])[0]

    sequences = total // group
    query_trade.wait()
    up_trade.wait()
    for head in range(group):
        query_sum, up_sum = 0.0, 0.0
        for sequence in range(sequences):
            query_sum = query_sum + query_got[sequence * group + head].astype(jnp.float32)
            up_sum = up_sum + up_got_buf[sequence * group + head].astype(jnp.float32)
        query_out[:, head * head_dim : (head + 1) * head_dim] = query_sum[:, :head_dim]
        both = QK_NOPE + V_HEAD
        up_out[:, head * both : (head + 1) * both] = up_sum
    small_trade.wait()
    small_out[...] = small_got[0]

    def small_sum(source, _):
        small_out[...] += small_got[source]
        return 0

    lax.fori_loop(1, total, small_sum, 0)
    down_trade.wait()
    out_trade.wait()
    down_sum, out_sum = 0.0, 0.0
    for sequence in range(sequences):
        down_sum = down_sum + down_got[sequence].astype(jnp.float32)
        out_sum = out_sum + out_got[sequence].astype(jnp.float32)
    down_out[...] = down_sum[:, : down_out.shape[1]]
    out_out[...] = out_sum
    shared_trade.wait()
    for share in shares:
        share.wait_recv()
    for trade in (shared_trade, query_trade, up_trade, small_trade):
        trade.finish()
    sender.finish()


def backward_pass(scale, last, small, tables, saved, weights, sends):
    shards, plane = lax.axis_size("shard"), lax.axis_size("expert")
    total = shards * plane
    low, shape = jnp.bfloat16, jax.ShapeDtypeStruct
    local, width = small[3].shape
    head_dim = QK_NOPE + QK_ROPE
    vmem, any_space = pl.BlockSpec(memory_space=pltpu.VMEM), pl.BlockSpec(memory_space=pl.ANY)
    inputs = list(small) + list(tables) + list(saved)
    hbm = list(weights) + list(sends)
    gate_send, up_send, narrow_send, shared_term = sends
    experts = small[9].shape[0]
    small_rows = experts + 3 + -(experts + 3) % 8
    own_width = width // total
    out_shape = [
        shape((local, width), jnp.float32),
        shape((own_width, HEADS * head_dim), jnp.float32),
        shape((KV_RANK // total, HEADS * (QK_NOPE + V_HEAD)), jnp.float32),
        shape((own_width, KV_RANK + QK_ROPE), jnp.float32),
        shape((own_width, width), jnp.float32),
        shape((small_rows, 128), jnp.float32),
        shape(gate_send.shape, low),
        shape(up_send.shape, low),
        shape(narrow_send.shape, low),
        shape(shared_term.shape, low),
        shape((SEQ_DEVICES, PIECES, local // PIECES, width), low),
    ]
    hbm_out = 5
    dma, scratch = pltpu.SemaphoreType.DMA, pltpu.VMEM
    pieces = (PIECES, local // PIECES)
    down_width = weights[3].shape[2]
    row_count = 128 // own_width
    sequences = total // SEQ_DEVICES
    wide_head = 2 * QK_NOPE
    return pl.pallas_call(
        functools.partial(backward_kernel, shards, plane, scale, last),
        out_shape=out_shape,
        in_specs=[vmem] * len(inputs) + [any_space] * len(hbm),
        out_specs=[vmem] * (len(out_shape) - hbm_out) + [any_space] * hbm_out,
        scratch_shapes=[
            scratch((2, shards, SEQ_DEVICES // shards) + pieces + (512,), low),
            scratch((2, 256, HEADS * head_dim), low),
            scratch((shards, width // shards, down_width), low),
            scratch((SEQ_DEVICES,) + pieces + (128,), low),
            scratch((local, KV_RANK), jnp.float32),
            scratch((local, width), jnp.float32),
            scratch((local, width), jnp.float32),
            scratch(pieces + (width,), low),
            scratch((local, width), low),
            scratch((SEQ, V_HEAD), low),
            scratch((SEQ + WINDOW, wide_head), jnp.float32),
            scratch((SEQ + WINDOW, V_HEAD), jnp.float32),
            scratch((SEQ_DEVICES,) + pieces + (KV_RANK,), low),
            scratch((SEQ, wide_head), low),
            scratch((SEQ_DEVICES, local, wide_head), low),
            scratch((SEQ, wide_head), low),
            scratch((total, own_width, wide_head), low),
            scratch((total, own_width, wide_head), low),
            scratch((total, KV_RANK // total, wide_head), low),
            scratch((total, KV_RANK // total, wide_head), low),
            scratch((local, HEADS * head_dim), low),
            scratch((1, 1, local, down_width), low),
            scratch((SEQ_DEVICES, 1, local, down_width), low),
            scratch((row_count, own_width, down_width), low),
            scratch((sequences, own_width, down_width), low),
            scratch((row_count, own_width, width), low),
            scratch((sequences, own_width, width), low),
            scratch((width // 128, small_rows, 128), jnp.float32),
            scratch((total, small_rows, 128), jnp.float32),
            scratch(pieces + (KV_RANK,), jnp.float32),
            dma((8,)),
            dma((shards,)),
            dma((2, shards)),
            dma((3, shards)),
            dma((3, shards)),
            dma((2, SEQ_DEVICES)),
            dma((2, SEQ_DEVICES)),
            dma((2, 4, SEQ_DEVICES, PIECES)),
            dma((2, SEQ_DEVICES, PIECES)),
            dma((2,)),
            dma((4, total)),
            dma((4, total)),
            dma((4,)),
            dma((2, max(row_count, sequences))),
            dma((2, max(row_count, sequences))),
            dma((2,)),
        ]
        + reduce_scratch(SEQ_DEVICES, PIECES, local // PIECES, KV_RANK),
        compiler_params=pltpu.CompilerParams(
            collective_id=3, has_side_effects=True, vmem_limit_bytes=62 * 2**20
        ),
        name="backward",
    )(*inputs, *hbm)


def on_device(
    tokens,
    document_lengths,
    routes,
    first_gain,
    query_weight,
    latent_down,
    latent_gain,
    latent_up,
    output_weight,
    second_gain,
    router_weight,
    shared_gate,
    shared_up,
    shared_down,
    expert_gate,
    expert_up,
    expert_down,
    cotangent,
):
    local_rows, width = tokens.shape
    shards = lax.axis_size("shard")
    plane = lax.axis_size("expert")
    everyone = ("shard", "expert")
    all_devices = shards * plane
    shard_at = lax.axis_index("shard")
    plane_at = lax.axis_index("expert")
    head_at = plane_at % SEQ_DEVICES
    sequence_at = (shard_at * plane + plane_at) // SEQ_DEVICES
    capacity = local_rows * TOP * 4 // (3 * plane)
    head_dim = QK_NOPE + QK_ROPE
    scale = 1.0 / math.sqrt(head_dim)
    own_at = head_at * local_rows

    def own_rows(values):
        return lax.dynamic_slice_in_dim(values, own_at, local_rows, 0)

    piece_rows = output_weight.shape[0] // plane
    half = QK_ROPE // 2
    query_columns = lax.dynamic_slice_in_dim(query_weight, head_at * head_dim, head_dim, 1)
    query_turn, key_turn = query_columns[:, QK_NOPE:], latent_down[:, KV_RANK:]
    query_cols = jnp.concatenate(
        [query_columns, query_turn[:, half:], query_turn[:, :half]], axis=1
    )
    down_half = jnp.concatenate(
        [latent_down, key_turn[:, half:], key_turn[:, :half]], axis=1
    )
    units = shared_down.shape[0] // plane
    unit_pad = -units % 16
    padded_units = units + unit_pad
    gate_columns, up_columns = (
        jnp.concatenate(
            [
                jnp.pad(
                    lax.dynamic_slice_in_dim(
                        weight, index * shared_down.shape[0] + plane_at * units, units, 1
                    ),
                    ((0, 0), (0, unit_pad)),
                )
                for index in range(shards)
            ],
            axis=1,
        )
        for weight in (shared_gate, shared_up)
    )
    down_units = lax.dynamic_slice_in_dim(shared_down, plane_at * units, units, 0)
    down_units = jnp.pad(down_units, ((0, unit_pad), (0, 0)))

    def plane_pieces(weight):
        return weight.reshape(plane, 1, -1, weight.shape[1])

    positions = jnp.arange(SEQ, dtype=jnp.int32)
    cosine_part, sine_part = rotary_tables(positions, QK_ROPE)
    sequence_count, entry_count = document_lengths.shape
    ends = jnp.cumsum(document_lengths, axis=1)
    picked = jnp.arange(sequence_count, dtype=jnp.int32)[:, None] == sequence_at
    row_ends = jnp.sum(jnp.where(picked, ends, 0), axis=0)
    documents = jnp.sum((positions[:, None] >= row_ends[None, :]).astype(jnp.int32), axis=1)
    turn = jnp.tile(cosine_part, (1, 4))
    sway = jnp.tile(jnp.concatenate([-sine_part, sine_part], axis=1), (1, 2))
    docs = documents[:, None]
    row_docs = jnp.pad(docs, ((WINDOW, 0), (0, 0)), constant_values=-1).T
    route_rows = jnp.pad(routes.T, ((0, 8 - TOP), (0, 0)), constant_values=-1)
    (
        all_normed,
        all_grads,
        all_routes,
        full_down,
        full_out,
        full_query,
        gate_single,
        up_single,
        down_single,
        gate_shared,
        up_shared,
        down_shared,
        normed_one,
        query,
        keys,
        value,
        key_latent,
        compressed,
        head_out,
        log_total,
        middle,
        up_head,
    ) = forward_pass(
        scale,
        entry_count - 1,
        tokens,
        cotangent,
        (
            query_cols,
            plane_pieces(down_half),
            lax.dynamic_slice_in_dim(
                latent_up, head_at * (QK_NOPE + V_HEAD), QK_NOPE + V_HEAD, 1
            ),
            plane_pieces(output_weight),
            plane_pieces(query_weight),
            expert_gate[0],
            expert_up[0],
            expert_down[0],
            gate_columns,
            up_columns,
            down_units,
        ),
        route_rows,
        (first_gain[None], latent_gain[None], second_gain[None]),
        (turn, sway, docs, row_docs),
    )
    all_normed = all_normed.reshape(-1, width)
    all_grads = all_grads.reshape(-1, width)
    blocked = (SEQ_DEVICES, PIECES, local_rows // PIECES, width)
    shard_blocked = (shards, SEQ_DEVICES // shards) + blocked[1:]
    (
        normed_part,
        output_part,
        slot_rows,
        slot_grad,
        hidden,
        gate_pre_grad,
        up_pre_grad,
        token_scores,
        shared_hidden,
        shared_gate_back,
        shared_up_back,
    ) = expert_pass(
        jnp.stack([plane_at, shard_at]).astype(jnp.int32)[None],
        all_routes[:, 0],
        router_weight.T,
        all_normed,
        all_grads,
        (
            gate_columns,
            gate_shared,
            up_columns,
            up_shared,
            down_units,
            down_shared,
            expert_gate[0],
            gate_single,
            expert_up[0],
            up_single,
            expert_down[0],
            down_single,
        ),
        capacity,
    )
    expert_down_term = matmul_tn(hidden, slot_grad)
    transfers = [
        ("reduce", normed_part.reshape(plane, local_rows, width)),
        ("trade", token_scores),
        ("share", expert_down_term.astype(jnp.bfloat16).reshape(shards, -1, width)),
    ]
    output_transfer = ("reduce", output_part.reshape(plane, local_rows, width))
    if plane == SEQ_DEVICES:
        back, scores, down_blocks, output_sum = bundle(
            2, plane, shards, transfers + [output_transfer], 56 * 2**20
        )
    else:
        back, scores, down_blocks = bundle(2, plane, shards, transfers, 56 * 2**20)
        (output_sum,) = bundle(4, plane, shards, [output_transfer], 56 * 2**20)
    activations = (middle + output_sum).astype(jnp.bfloat16)

    def sum_shards(term, blocks):
        own = lax.dynamic_index_in_dim(
            term.reshape((shards, -1) + term.shape[1:]), shard_at, 0, keepdims=False
        )
        for step in range(1, shards):
            own = own + lax.dynamic_index_in_dim(
                blocks, (shard_at + step) % shards, 0, keepdims=False
            ).astype(jnp.float32)
        return own

    expert_down_grad = sum_shards(expert_down_term, down_blocks)[None]
    gate_term = matmul_tn(slot_rows, gate_pre_grad)
    up_term = matmul_tn(slot_rows, up_pre_grad)
    shared_down_term = matmul_tn(shared_hidden, all_grads)
    shared_term = jnp.concatenate(
        [matmul_tn(all_normed, shared_gate_back), matmul_tn(all_normed, shared_up_back)], axis=1
    ).astype(jnp.bfloat16)

    def for_shards(term):
        return term.astype(jnp.bfloat16).reshape((shards, -1) + term.shape[1:])

    (
        input_grad,
        query_weight_grad,
        latent_up_grad,
        latent_down_grad,
        output_weight_grad,
        small_sums,
        gate_blocks,
        up_blocks,
        shared_blocks,
        shared_moved,
        _,
    ) = backward_pass(
        scale,
        entry_count - 1,
        (
            back,
            scores,
            route_rows,
            middle,
            cotangent,
            tokens,
            first_gain[None],
            second_gain[None],
            latent_gain[None],
            router_weight.T,
        ),
        (query, keys, value, docs, row_docs, log_total, turn, sway),
        (key_latent, up_head.reshape(KV_RANK, -1), head_out),
        (
            compressed,
            full_out.reshape(shard_blocked),
            full_query.reshape((shards,) + query_weight.shape),
            full_down.reshape((shards,) + down_half.shape),
            normed_one.reshape(blocked),
            output_weight.reshape(shard_blocked[1:]),
            query_weight,
            down_half,
        ),
        (
            for_shards(gate_term),
            for_shards(up_term),
            for_shards(shared_down_term),
            shared_term.reshape(all_devices, -1, shared_term.shape[1]),
        ),
    )
    expert_gate_grad = sum_shards(gate_term, gate_blocks)[None]
    expert_up_grad = sum_shards(up_term, up_blocks)[None]
    shared_down_grad = sum_shards(shared_down_term, shared_blocks)[:units]
    shared_moved = shared_moved.astype(jnp.float32).reshape(shards, plane, -1, 2, shards, padded_units)
    shared_moved = jnp.sum(shared_moved, axis=0)[..., :units].transpose(2, 1, 3, 0, 4)
    shared_moved = shared_moved.reshape(2, shared_moved.shape[1], -1)
    shared_gate_grad = shared_moved[0]
    shared_up_grad = shared_moved[1]
    own_width = width // all_devices
    number = shard_at * plane + plane_at
    own_small = lax.dynamic_slice_in_dim(small_sums, number * own_width % 128, own_width, 1)
    router_weight_grad = own_small[:plane].T
    second_gain_grad = own_small[plane]
    first_gain_grad = own_small[plane + 1]
    latent_width = KV_RANK // all_devices
    latent_gain_grad = lax.dynamic_slice_in_dim(
        small_sums[plane + 2], number * latent_width % 128, latent_width, 0
    )
    return (
        activations,
        input_grad,
        first_gain_grad,
        query_weight_grad,
        latent_down_grad,
        latent_gain_grad,
        latent_up_grad,
        output_weight_grad,
        second_gain_grad,
        router_weight_grad,
        shared_gate_grad,
        shared_up_grad,
        shared_down_grad,
        expert_gate_grad,
        expert_up_grad,
        expert_down_grad,
    )


def solution(mesh):
    return jax.shard_map(
        on_device,
        mesh=mesh,
        in_specs=(
            P(("shard", "expert"), None),
            P(),
            P(("shard", "expert"), None),
            P(),
            P("shard", None),
            P("shard", None),
            P(),
            P("shard", None),
            P("shard", None),
            P(),
            P(),
            P("shard", None),
            P("shard", None),
            P("shard", None),
            P("expert", "shard", None),
            P("expert", "shard", None),
            P("expert", "shard", None),
            P(("shard", "expert"), None),
        ),
        out_specs=(
            P(("shard", "expert"), None),
            P(("shard", "expert"), None),
            P(("shard", "expert")),
            P(("shard", "expert"), None),
            P(("shard", "expert"), None),
            P(("shard", "expert")),
            P(("shard", "expert"), None),
            P(("shard", "expert"), None),
            P(("shard", "expert")),
            P(("shard", "expert"), None),
            P(("shard", "expert"), None),
            P(("shard", "expert"), None),
            P(("shard", "expert"), None),
            P("expert", "shard", None),
            P("expert", "shard", None),
            P("expert", "shard", None),
        ),
        check_vma=False,
    )
```

```python
import functools
import math

import jax
import jax.numpy as jnp
from jax import lax
from jax.experimental import pallas as pl
from jax.experimental.pallas import tpu as pltpu
from jax.sharding import PartitionSpec as P

HEADS = 16
QK_NOPE = 128
QK_ROPE = 64
V_HEAD = 128
KV_RANK = 512
TOP = 6
SEQ = 2048
WINDOW = 1024
TOK_DEV = 128
STEP_SENDERS = 4
SEQ_DEVICES = SEQ // TOK_DEV


EPS = 1e-06
THETA = 10000.0
NEG = -1e30
HIGH = lax.Precision.HIGHEST


def matmul(left, right):
    return jnp.dot(left, right, preferred_element_type=jnp.float32)


def matmul_tn(left, right):
    return lax.dot_general(
        left, right, (((0,), (0,)), ((), ())), preferred_element_type=jnp.float32
    )


def matmul_nt(left, right):
    return lax.dot_general(
        left, right, (((1,), (1,)), ((), ())), preferred_element_type=jnp.float32
    )


def norm_scale(values, gain):
    return values * lax.rsqrt(jnp.mean(values * values, axis=-1, keepdims=True) + EPS) * gain


def rotary_tables(positions, width):
    half = width // 2
    freqs = THETA ** (-jnp.arange(half, dtype=jnp.float32) / half)
    angles = positions.astype(jnp.float32)[:, None] * freqs[None, :]
    return (jnp.cos(angles), jnp.sin(angles))


def rotate(values, cosine_part, sine_part):
    half = values.shape[-1] // 2
    first = values[..., :half]
    second = values[..., half:]
    return jnp.concatenate(
        [first * cosine_part - second * sine_part, second * cosine_part + first * sine_part],
        axis=-1,
    )


def unrotate(values, cosine_part, sine_part):
    half = values.shape[-1] // 2
    first = values[..., :half]
    second = values[..., half:]
    return jnp.concatenate(
        [first * cosine_part + second * sine_part, second * cosine_part - first * sine_part],
        axis=-1,
    )


def swish_parts(values):
    sigmoid_part = jax.nn.sigmoid(values)
    return (values * sigmoid_part, sigmoid_part * (1.0 + values * (1.0 - sigmoid_part)))


MESH = pl.DeviceIdType.MESH
INNER = 4
PIECES = 2


class Sender:
    def __init__(self):
        self.started = []

    def start(self, there, copy):
        @pl.when(there)
        def _():
            copy.start()

        self.started.append((there, copy))

    def finish(self):
        for there, copy in self.started:
            @pl.when(there)
            def _():
                copy.wait_send()


def remote(source, target, send_sem, recv_sem, place):
    return pltpu.make_async_remote_copy(
        src_ref=source,
        dst_ref=target,
        send_sem=send_sem,
        recv_sem=recv_sem,
        device_id=place,
        device_id_type=MESH,
    )


class Place:
    def __init__(self, group):
        self.me = lax.axis_index("expert")
        self.shard = lax.axis_index("shard")
        self.group = group
        self.outer = group // INNER
        self.local = lax.rem(self.me, group)
        self.base = self.me - self.local
        self.level = self.local // INNER
        inner = lax.rem(self.local, INNER)
        self.row_step = 2 - 4 * (inner // 2)
        self.twin_step = 1 - 2 * lax.rem(inner, 2)
        self.always = self.me >= 0
        self.upper = self.level < self.outer - 1
        self.lower = self.level > 0

    def neighbours(self):
        return [
            (self.upper, {"expert": self.me + INNER}),
            (self.lower, {"expert": self.me - INNER}),
            (self.always, {"expert": self.me + self.row_step}),
            (self.always, {"expert": self.me + self.twin_step}),
        ]

    def along(self, step):
        below = (self.level >= step, self.local - step * INNER, self.upper, self.me + INNER, 0)
        above = (self.level + step < self.outer, self.local + step * INNER, self.lower, self.me - INNER, 1)
        return (below, above)


def greet(peers):
    barrier = pltpu.get_barrier_semaphore()
    for there, peer in peers:
        @pl.when(there)
        def _():
            pl.semaphore_signal(barrier, inc=1, device_id=peer, device_id_type=MESH)
    pl.semaphore_wait(barrier, sum(there.astype(jnp.int32) for there, _ in peers))


def gather_steps(place, own_ref, out_ref, copy_sem, send_sem, recv_sem, sender):
    local = place.local
    row, twin = local + place.row_step, local + place.twin_step

    def push(kind, block, piece, target, source=None):
        spot = out_ref.at[block, piece]
        return remote(
            spot if source is None else source.at[piece],
            spot,
            send_sem.at[kind, block, piece],
            recv_sem.at[block, piece],
            {"expert": target},
        )

    def arrive(there, block, piece):
        @pl.when(there)
        def _():
            push(0, block, piece, place.me).wait_recv()

    pieces = out_ref.shape[1]
    if own_ref is None:
        own_ref = out_ref.at[local]
    else:
        keep = pltpu.make_async_copy(own_ref, out_ref.at[local], copy_sem)
        keep.start()
    row_at, twin_at = place.me + place.row_step, place.me + place.twin_step
    for piece in range(pieces):
        sender.start(place.upper, push(0, local, piece, place.me + INNER, own_ref))
        sender.start(place.lower, push(1, local, piece, place.me - INNER, own_ref))
        sender.start(place.always, push(2, local, piece, row_at, own_ref))
        sender.start(place.always, push(3, local, piece, twin_at, own_ref))
    yield
    for step in range(1, place.outer + 1):
        if step < place.outer:
            for piece in range(pieces):
                for there, block, onward, target, kind in place.along(step):
                    arrive(there, block, piece)
                    sender.start(there & onward, push(kind, block, piece, target))
                    sender.start(there, push(2, block, piece, row_at))
                    sender.start(there, push(3, block, piece, twin_at))
        for piece in range(pieces):
            for there, block, *_ in place.along(step - 1)[: 1 if step == 1 else 2]:
                arrive(there, block + place.row_step, piece)
                sender.start(there, push(3, block + place.row_step, piece, twin_at))
        yield
    for step in range(place.outer):
        for piece in range(pieces):
            for there, block, *_ in place.along(step)[: 1 if step == 0 else 2]:
                arrive(there, block + place.twin_step, piece)
                arrive(there, block + place.twin_step + place.row_step, piece)
    if copy_sem is not None:
        keep.wait()
    yield


def add_into(target, first, *others):
    rows = target.shape[0]
    chunk = 32

    def body(index, _):
        at = pl.ds(pl.multiple_of(index * chunk, chunk), chunk)
        total = first[at, :].astype(jnp.float32)
        for other in others:
            total = total + other[at, :].astype(jnp.float32)
        target[at, :] = total.astype(target.dtype)
        return 0

    lax.fori_loop(0, rows // chunk, body, 0)


def reduce_steps(place, part_ref, out_ref, scratch, sender, fine=False):
    (own_buf, twin_buf, row_buf, line_buf, load_sem, twin_send, twin_recv, row_send, row_recv, line_send, line_recv,
     out_buf, out_sem) = scratch
    outer, local, level = place.outer, place.local, place.level
    pieces = part_ref.shape[1]
    inner = lax.rem(local, INNER)
    row_bit, core = inner // 2, lax.rem(inner, 2)
    twin_at, row_at = {"expert": place.me + place.twin_step}, {"expert": place.me + place.row_step}
    order = []
    low, high = 0, outer - 1
    while low <= high:
        order += [high] if low == high else [high, low]
        low, high = low + 1, high - 1
    units = [(at, piece) for at in order for piece in range(pieces)]
    bits = (1 - row_bit, row_bit)

    def loading(at, piece, bit):
        where = at * 2 + bit
        return pltpu.make_async_copy(
            part_ref.at[at * INNER + bit * 2 + core, piece], own_buf.at[where, piece], load_sem.at[where, piece]
        )

    def to_twin(at, piece, bit):
        where = at * 2 + bit
        return remote(
            part_ref.at[at * INNER + bit * 2 + 1 - core, piece],
            twin_buf.at[where, piece],
            twin_send.at[where, piece],
            twin_recv.at[where, piece],
            twin_at,
        )

    def to_row(at, piece):
        return remote(
            own_buf.at[at * 2 + bits[0], piece], row_buf.at[at, piece], row_send.at[at, piece], row_recv.at[at, piece], row_at
        )

    def mine(at, piece):
        return own_buf.at[at * 2 + row_bit, piece]

    def to_line(side, at, piece):
        return remote(
            mine(at, piece),
            line_buf.at[side, at, piece],
            line_send.at[side, at, piece],
            line_recv.at[side, at, piece],
            {"expert": place.me + (INNER if side == 0 else -INNER)},
        )

    for at, piece in units:
        for bit in bits:
            sender.start(place.always, to_twin(at, piece, bit))
            loading(at, piece, bit).start()
    yield
    for at, piece in units:
        for bit in bits:
            where = at * 2 + bit
            loading(at, piece, bit).wait()
            to_twin(at, piece, bit).wait_recv()
            add_into(own_buf.at[where, piece], own_buf.at[where, piece], twin_buf.at[where, piece])
            if bit is bits[0]:
                sender.start(place.always, to_row(at, piece))
        if fine:
            yield
    if not fine:
        yield
    for at, piece in units:
        to_row(at, piece).wait_recv()
        spot, row = mine(at, piece), row_buf.at[at, piece]
        for side, there, first in ((0, level < at, level == 0), (1, level > at, level == outer - 1)):
            line = to_line(side, at, piece)

            @pl.when(there & first)
            def _():
                add_into(spot, spot, row)

            @pl.when(there & ~first)
            def _():
                line.wait_recv()
                add_into(spot, spot, row, line_buf.at[side, at, piece])

            sender.start(there, line)
        if fine:
            yield
    if not fine:
        yield
    for at, piece in units:
        @pl.when(level == at)
        def _():
            parts = [mine(at, piece), row_buf.at[at, piece]]
            for side, there in ((0, at > 0), (1, at < outer - 1)):
                if there:
                    to_line(side, at, piece).wait_recv()
                    parts.append(line_buf.at[side, at, piece])
            add_into(out_buf.at[piece], *parts)
    done = pltpu.make_async_copy(out_buf, out_ref, out_sem)
    done.start()
    done.wait()
    yield


def reduce_scratch(group, pieces, rows, columns):
    outer = group // INNER
    bf = jnp.bfloat16
    pair, single, line = (2 * outer, pieces), (outer, pieces), (2, outer, pieces)
    block = (rows, columns)
    return [
        pltpu.VMEM(pair + block, bf),
        pltpu.VMEM(pair + block, bf),
        pltpu.VMEM(single + block, bf),
        pltpu.VMEM(line + block, bf),
        pltpu.SemaphoreType.DMA(pair),
        pltpu.SemaphoreType.DMA(pair),
        pltpu.SemaphoreType.DMA(pair),
        pltpu.SemaphoreType.DMA(single),
        pltpu.SemaphoreType.DMA(single),
        pltpu.SemaphoreType.DMA(line),
        pltpu.SemaphoreType.DMA(line),
        pltpu.VMEM((pieces,) + block, jnp.float32),
        pltpu.SemaphoreType.DMA(()),
    ]


class HeadRows:
    def __init__(self, started, received):
        self.started, self.received = started, received

    def wait(self):
        for there, local, copy, keep in self.started:
            @pl.when(there)
            def _():
                copy.wait_send()

            @pl.when(local)
            def _():
                keep.wait()
        for there, copy in self.received:
            @pl.when(there)
            def _():
                copy.wait_recv()


def head_rows(place, plane, shards, own_ref, out_ref, copy_sem, send_sem, recv_sem):
    count = own_ref.shape[0]
    number = place.shard * plane + place.me
    sequences = plane // place.group
    mine = place.shard * sequences + place.me // place.group
    started, received = [], []
    for index in range(count):
        target = place.local * count + index
        peer = {"shard": target // plane, "expert": lax.rem(target, plane)}
        copy = remote(own_ref.at[index], out_ref.at[mine], send_sem.at[index], recv_sem.at[mine], peer)
        keep = pltpu.make_async_copy(own_ref.at[index], out_ref.at[mine], copy_sem)

        @pl.when(target != number)
        def _():
            copy.start()

        @pl.when(target == number)
        def _():
            keep.start()

        started.append((target != number, target == number, copy, keep))
    for shard in range(shards):
        for sequence in range(sequences):
            source = shard * plane + sequence * place.group + number // count
            slot = shard * sequences + sequence
            peer = {"shard": source // plane, "expert": lax.rem(source, plane)}
            copy = remote(own_ref.at[0], out_ref.at[slot], send_sem.at[0], recv_sem.at[slot], peer)
            received.append((source != number, copy))
    return HeadRows(started, received), []


def bundle_kernel(group, shards, kinds, *refs):
    count = len(kinds)
    ins, outs, rest = refs[:count], refs[count : 2 * count], refs[2 * count :]
    place = Place(group)
    plane = lax.axis_size("expert")
    peers = []
    if "gather" in kinds or "reduce" in kinds:
        peers += place.neighbours()
    members = [{"expert": place.base + lax.rem(place.local + step, group)} for step in range(1, group)]
    if "trade" in kinds:
        peers = [(place.always, member) for member in members]
    across = [{"shard": lax.rem(place.shard + step, shards)} for step in range(1, shards)]
    if "swap" in kinds or "share" in kinds:
        peers += [(place.always, peer) for peer in across]
    everyone = []
    if "owners" in kinds or "rows" in kinds:
        total = shards * plane
        number = place.shard * plane + place.me
        for step in range(1, total):
            target = lax.rem(number + step, total)
            everyone.append((target, {"shard": target // plane, "expert": lax.rem(target, plane)}))
        peers = [(place.always, peer) for _, peer in everyone]
    greet(peers)
    sender = Sender()
    runs, waits = [], []
    for kind, own, out in zip(kinds, ins, outs):
        if kind == "gather":
            copy_sem, send_sem, recv_sem, *rest = rest
            runs.append(gather_steps(place, own, out, copy_sem, send_sem, recv_sem, sender))
        elif kind == "reduce":
            scratch, rest = rest[:13], rest[13:]
            runs.append(reduce_steps(place, own, out, scratch, sender))
        else:
            copy_sem, send_sem, recv_sem, *rest = rest
            if kind == "swap":
                mine, source = place.shard, lambda target: own
                targets = [(lax.rem(place.shard + step, shards), peer) for step, peer in enumerate(across, 1)]
            elif kind == "share":
                mine, source = place.shard, lambda target: own.at[target]
                targets = [(lax.rem(place.shard + step, shards), peer) for step, peer in enumerate(across, 1)]
            elif kind == "trade":
                mine, source = place.local, lambda target: own.at[target]
                targets = [(lax.rem(place.local + step, group), peer) for step, peer in enumerate(members, 1)]
            elif kind == "owners":
                mine, source = place.shard * plane + place.me, lambda target: own.at[target]
                targets = everyone
            else:
                waits.append(head_rows(place, plane, shards, own, out, copy_sem, send_sem, recv_sem))
                continue
            keep = None
            if kind != "share":
                keep = pltpu.make_async_copy(source(mine), out.at[mine], copy_sem)
                keep.start()
            total = len(targets) + 1
            copies = []
            for step, (target, peer) in enumerate(targets, 1):
                copy = remote(source(target), out.at[mine], send_sem.at[step], recv_sem.at[step], peer)
                copy.start()
                copies.append(copy)
            waits.append((keep, copies))
    while runs:
        runs = [run for run in runs if next(run, "end") != "end"]
    for keep, copies in waits:
        if keep is not None:
            keep.wait()
        for copy in copies:
            copy.wait()
    sender.finish()


def bundle(number, group, shards, transfers, limit=48 * 2**20):
    kinds, arrays, shapes, scratch = [], [], [], []
    members = shards * lax.axis_size("expert")
    for kind, array in transfers:
        kinds.append(kind)
        sems = [pltpu.SemaphoreType.DMA(())]
        if kind == "gather":
            pieces = PIECES if array.shape[0] % (16 * PIECES) == 0 else 1
            array = array.reshape((pieces, array.shape[0] // pieces) + array.shape[1:])
            shape = (group,) + array.shape
            sems += [pltpu.SemaphoreType.DMA((4, group, pieces)), pltpu.SemaphoreType.DMA((group, pieces))]
        elif kind == "reduce":
            pieces = 2 * PIECES
            array = array.reshape(group, pieces, array.shape[1] // pieces, array.shape[2])
            shape = array.shape[1:]
            sems = reduce_scratch(group, *shape)
        else:
            total = {"swap": shards, "share": shards, "trade": group, "owners": members}.get(kind)
            shape = ((total,) + array.shape) if kind == "swap" else array.shape
            if kind == "rows":
                total = max(array.shape[0], members // group)
                shape = (members // group,) + array.shape[1:]
            sems += [pltpu.SemaphoreType.DMA((total,)), pltpu.SemaphoreType.DMA((total,))]
        arrays.append(array)
        shapes.append(jax.ShapeDtypeStruct(shape, jnp.float32 if kind == "reduce" else array.dtype))
        scratch += sems
    outs = pl.pallas_call(
        functools.partial(bundle_kernel, group, shards, tuple(kinds)),
        out_shape=shapes,
        in_specs=[pl.BlockSpec(memory_space=pl.ANY)] * len(arrays),
        out_specs=[pl.BlockSpec(memory_space=pl.ANY)] * len(arrays),
        scratch_shapes=scratch,
        compiler_params=pltpu.CompilerParams(
            collective_id=number, has_side_effects=True, vmem_limit_bytes=limit
        ),
        name="bundle_" + "_".join(kinds[:2]),
    )(*arrays)
    done = []
    for (kind, array), out in zip(transfers, outs):
        if kind == "gather":
            out = out.reshape((group,) + array.shape)
        if kind == "reduce":
            out = out.reshape(array.shape[1:])
        done.append(out)
    return done


def pieces_of(size, most):
    return [(at, min(most, size - at)) for at in range(0, size, most)]


def expert_kernel(
    me_ref, routes_ref, router_ref, rows_in, grads_in, *rest
):
    weights, rest = rest[:12], rest[12:]
    (back_ref, out_ref, rows_ref, grad_ref, hidden_ref, gate_back_ref, up_back_ref, score_ref,
     shared_hidden_ref, shared_gate_back_ref, shared_up_back_ref, slot_cotangent, pick_buf, gate_buf,
     gate_w, up_w, down_w, shared_gate_w, shared_up_w, shared_down_w, weight_sem) = rest
    targets = (shared_gate_w, shared_up_w, shared_down_w, gate_w, up_w, down_w)
    shard_at = me_ref[0, 1]
    loads = []
    for index, target in enumerate(targets):
        own, got = weights[2 * index], weights[2 * index + 1]
        count = got.shape[0]
        for step in range(count):
            at = lax.rem(shard_at + step, count)
            block = own.shape[0]
            spot = target.at[at] if len(target.shape) == 3 else target.at[pl.ds(pl.multiple_of(at * block, 16), block), :]
            source = own if step == 0 else got.at[at]
            loads.append(pltpu.make_async_copy(source, spot, weight_sem.at[index, step]))

    def when_first(action):
        @pl.when(pl.program_id(0) == 0)
        def _():
            action()

    def start_loads():
        for load in loads:
            load.start()

    def wait_loads():
        for load in loads:
            load.wait()

    when_first(start_loads)
    width = rows_in.shape[1]
    hidden_width = gate_w.shape[1]
    shards, own_width, _ = shared_gate_w.shape
    senders, _, rows = routes_ref.shape
    capacity = pick_buf.shape[0] // senders
    experts = router_ref.shape[0]
    low = jnp.bfloat16
    me = me_ref[0, 0]

    @pl.when(pl.program_id(0) == 0)
    def _():
        pick_buf[...] = jnp.zeros_like(pick_buf)

    logits = matmul_nt(router_ref[...], rows_in[...])
    names = lax.broadcasted_iota(jnp.int32, (experts, rows), 0)
    earlier = lax.broadcasted_iota(jnp.int32, (rows, rows), 0) <= lax.broadcasted_iota(jnp.int32, (rows, rows), 1)
    earlier = jnp.where(earlier, 1.0, 0.0).astype(low)
    slot_names = lax.broadcasted_iota(jnp.int32, (capacity, rows), 0).astype(jnp.float32)
    picks = []
    for sender in range(senders):
        routed = routes_ref[sender]
        chosen = jnp.zeros((experts, rows), jnp.float32)
        for choice in range(TOP):
            chosen = chosen + jnp.where(routed[choice : choice + 1] == names, 1.0, 0.0)
        logit = jnp.where(chosen > 0.0, logits[:, sender * rows : (sender + 1) * rows], NEG)
        expo = jnp.exp(logit - jnp.max(logit, axis=0, keepdims=True)) * chosen
        dense = expo / jnp.sum(expo, axis=0, keepdims=True)
        gate_row = jnp.sum(jnp.where(names == me, dense, 0.0), axis=0, keepdims=True)
        mark = jnp.sum(jnp.where(routed == me, 1.0, 0.0), axis=0, keepdims=True)
        rank = matmul(jnp.broadcast_to(mark, (8, rows)).astype(low), earlier)[:1] - 1.0
        pick = jnp.where((slot_names == rank) & (mark > 0.0), 1.0, 0.0)
        picks.append(pick)
        at = slice(sender * capacity, (sender + 1) * capacity)
        pick_buf[at, sender * rows : (sender + 1) * rows] = pick.astype(low)
        gate_buf[at, :] = jnp.sum(pick * gate_row, axis=1, keepdims=True)
    gate = gate_buf[...]

    def pick_step(index, _):
        at = pl.ds(pl.multiple_of(index * 512, 512), 512)
        rows_ref[:, at] = matmul(pick_buf[...], rows_in[:, at]).astype(low)
        picked = matmul(pick_buf[...], grads_in[:, at])
        slot_cotangent[:, at] = picked.astype(low)
        grad_ref[:, at] = (gate * picked).astype(low)
        return 0

    lax.fori_loop(0, width // 512, pick_step, 0)
    when_first(wait_loads)
    shared_pre, shared_up = 0.0, 0.0
    for shard in range(shards):
        part = rows_in[:, shard * own_width : (shard + 1) * own_width]
        shared_pre = shared_pre + matmul(part, shared_gate_w[shard])
        shared_up = shared_up + matmul(part, shared_up_w[shard])
    swished, slope = swish_parts(shared_pre)
    shared_hidden_ref[...] = (swished * shared_up).astype(low)
    shared_grad = matmul_nt(grads_in[...], shared_down_w[...])
    shared_gate_back_ref[...] = (shared_grad * shared_up * slope).astype(low)
    shared_up_back_ref[...] = (shared_grad * swished).astype(low)
    for at, size in pieces_of(hidden_width, 512):
        columns = slice(at, at + size)
        gate_pre = matmul(rows_ref[...], gate_w[:, columns])
        up_pre = matmul(rows_ref[...], up_w[:, columns])
        swished, slope = swish_parts(gate_pre)
        hidden_ref[:, columns] = (swished * up_pre).astype(low)
        hidden_grad = matmul_nt(grad_ref[...], down_w[columns, :])
        gate_back_ref[:, columns] = (hidden_grad * up_pre * slope).astype(low)
        up_back_ref[:, columns] = (hidden_grad * swished).astype(low)

    def out_step(index, score):
        at = pl.ds(pl.multiple_of(index * 512, 512), 512)
        shard = index * 512 // own_width
        within = pl.ds(pl.multiple_of(index * 512 - shard * own_width, 512), 512)
        expert_out = matmul(hidden_ref[...], down_w[:, at]).astype(low).astype(jnp.float32)
        score = score + jnp.sum(expert_out * slot_cotangent[:, at].astype(jnp.float32), axis=1, keepdims=True)
        out = matmul_tn(pick_buf[...], (gate * expert_out).astype(low))
        out_ref[:, at] = (out + matmul(shared_hidden_ref[...], shared_down_w[:, at])).astype(low)
        row_back = matmul_nt(gate_back_ref[...], gate_w[at, :]) + matmul_nt(up_back_ref[...], up_w[at, :])
        back = (
            matmul_tn(pick_buf[...], row_back.astype(low))
            + matmul_nt(shared_gate_back_ref[...], shared_gate_w[shard, within, :])
            + matmul_nt(shared_up_back_ref[...], shared_up_w[shard, within, :])
        )
        back_ref[:, at] = back.astype(low)
        return score

    score = lax.fori_loop(0, width // 512, out_step, jnp.zeros((gate.shape[0], 1), jnp.float32))
    for sender in range(senders):
        own = score[sender * capacity : (sender + 1) * capacity]
        total = jnp.sum(picks[sender] * own, axis=0, keepdims=True)
        score_ref[sender] = jnp.broadcast_to(total, score_ref.shape[1:])


def expert_pass(me, routes, router, rows, grads, weights, capacity):
    plane, _, local = routes.shape
    senders = STEP_SENDERS
    tokens, slots = senders * local, senders * capacity
    steps = plane // senders
    shards = weights[1].shape[0]
    width, hidden_width = rows.shape[1], weights[6].shape[1]
    units = weights[0].shape[1]
    low = jnp.bfloat16

    def whole(array):
        return pl.BlockSpec(array.shape, lambda i: (0,) * array.ndim, pipeline_mode=pl.Buffered(1))

    def by_step(r, c):
        return pl.BlockSpec((r, c), lambda i: (i, 0))

    total = steps * slots
    shape = jax.ShapeDtypeStruct
    route_block = pl.BlockSpec((senders, 8, local), lambda i: (i, 0, 0))
    return pl.pallas_call(
        expert_kernel,
        grid=(steps,),
        out_shape=[
            shape((steps * tokens, width), low),
            shape((steps * tokens, width), low),
            shape((total, width), low),
            shape((total, width), low),
            shape((total, hidden_width), low),
            shape((total, hidden_width), low),
            shape((total, hidden_width), low),
            shape((plane, 8, local), jnp.float32),
            shape((steps * tokens, units), low),
            shape((steps * tokens, units), low),
            shape((steps * tokens, units), low),
        ],
        in_specs=[
            pl.BlockSpec(memory_space=pltpu.SMEM),
            route_block,
            whole(router),
            by_step(tokens, width),
            by_step(tokens, width),
        ]
        + [pl.BlockSpec(memory_space=pl.ANY)] * len(weights),
        out_specs=[
            by_step(tokens, width),
            by_step(tokens, width),
            by_step(slots, width),
            by_step(slots, width),
            by_step(slots, hidden_width),
            by_step(slots, hidden_width),
            by_step(slots, hidden_width),
            route_block,
            by_step(tokens, units),
            by_step(tokens, units),
            by_step(tokens, units),
        ],
        scratch_shapes=[
            pltpu.VMEM((slots, width), low),
            pltpu.VMEM((slots, tokens), low),
            pltpu.VMEM((slots, 1), jnp.float32),
            pltpu.VMEM((width, hidden_width), low),
            pltpu.VMEM((width, hidden_width), low),
            pltpu.VMEM((hidden_width, width), low),
            pltpu.VMEM((shards, width // shards, units), low),
            pltpu.VMEM((shards, width // shards, units), low),
            pltpu.VMEM((units, width), low),
            pltpu.SemaphoreType.DMA((6, shards)),
        ],
        compiler_params=pltpu.CompilerParams(
            vmem_limit_bytes=60 * 2**20, dimension_semantics=("arbitrary",)
        ),
        name="experts",
    )(me, routes, router, rows, grads, *weights)


QUERIES = 256
KEYS = WINDOW + QUERIES


def score_block(scale, query, keys, query_docs, key_docs):
    raw = matmul_nt(query, keys) * scale
    row = lax.broadcasted_iota(jnp.int32, raw.shape, 0) + WINDOW
    column = lax.broadcasted_iota(jnp.int32, raw.shape, 1)
    allowed = (query_docs == key_docs) & (column <= row) & (column > row - WINDOW)
    return jnp.where(allowed, raw, NEG)


class Swaps:
    def __init__(self, place, shards, sender):
        self.place, self.shards, self.sender = place, shards, sender

    def start(self, source, target, send_sem, recv_sem, keep=None):
        place, shards = self.place, self.shards
        arrivals = []
        for step in range(1, shards):
            other = lax.rem(place.shard + step, shards)
            self.sender.start(
                place.always,
                remote(source, target(place.shard), send_sem.at[step], recv_sem.at[place.shard], {"shard": other}),
            )
            arrivals.append(
                remote(source, target(other), send_sem.at[step], recv_sem.at[other], {"shard": other})
            )
        if keep is not None:
            copy = pltpu.make_async_copy(source, target(place.shard), keep)
            copy.start()

        def wait():
            for arrival in arrivals:
                arrival.wait_recv()
            if keep is not None:
                copy.wait()

        return wait


def whole_weight(place, others, own_ref, full_ref, buf, sem):
    copies = [pltpu.make_async_copy(own_ref, buf.at[place.shard], sem.at[0])]
    for step, other in enumerate(others, 1):
        copies.append(pltpu.make_async_copy(full_ref.at[other], buf.at[other], sem.at[step]))
    for copy in copies:
        copy.start()
    return copies


def drain(run):
    for _ in run:
        pass


def forward_kernel(shards, plane, scale, last, *refs):
    (tokens, cotangent, query_cols, down_half, up_half, out_half, query_half, gate_half, wide_half, narrow_half,
     shared_gate, shared_up, shared_down, routes, first_gain, latent_gain, second_gain, turn, sway, docs, row_docs,
     all_normed, all_grads, all_routes, full_down, full_out, full_query, full_gate, full_up, full_narrow,
     full_shared_gate, full_shared_up, full_shared_down, normed_one,
     query, keys, value, key_latent, compressed, head_out, log_total, middle, up_buf,
     token_buf, normed_buf, query_buf, down_buf, out_buf, heads_buf, second_buf,
     swap_send, swap_recv, keep_sem, gather_send, gather_recv, gather_keep, piece_send, piece_recv,
     trade_send, trade_recv, load_sem, whole_sem) = refs
    low = jnp.bfloat16
    group = SEQ_DEVICES
    place, wide = Place(group), Place(plane)
    width = tokens.shape[-1]
    rows = docs.shape[0] // group
    sender = Sender()
    members = [lax.rem(place.local + step, group) for step in range(1, group)]
    peers = [(place.always, {"expert": place.base + member}) for member in members]
    if plane != group:
        peers += [
            (wide.upper & ~place.upper, {"expert": place.me + INNER}),
            (wide.lower & ~place.lower, {"expert": place.me - INNER}),
        ]
    others = [lax.rem(place.shard + step, shards) for step in range(1, shards)]
    peers += [(place.always, {"shard": other}) for other in others]
    greet(peers)

    swaps = Swaps(place, shards, sender)
    numbers = iter(range(16))

    def swap(source, target, keep=False):
        at = next(numbers)
        return swaps.start(
            source, target, swap_send.at[at], swap_recv.at[at], keep_sem.at[at] if keep else None
        )

    at_piece = lambda ref: ref.at[wide.me]
    got_query = swap(query_cols, lambda shard: query_buf.at[shard], True)
    got_down = swap(at_piece(down_half), lambda shard: full_down.at[shard, wide.me])
    got_up = swap(up_half, lambda shard: up_buf.at[shard], True)
    token_run = gather_steps(
        place, tokens, token_buf, gather_keep.at[0], gather_send.at[0], gather_recv.at[0], sender
    )
    next(token_run)
    got_out = swap(at_piece(out_half), lambda shard: full_out.at[shard, wide.me])
    got_wq = swap(at_piece(query_half), lambda shard: full_query.at[shard, wide.me])
    def piece_gathers(kind, full):
        return [
            gather_steps(
                wide, None, full.at[other], None, piece_send.at[kind, step], piece_recv.at[kind, step], sender
            )
            for step, other in enumerate(others)
        ]

    next(token_run)
    got_down()
    down_runs = piece_gathers(0, full_down)
    for run in down_runs:
        next(run)
    next(token_run)
    for run in down_runs:
        next(run)
    got_query()
    got_up()
    waits = [
        swap(gate_half, lambda shard: full_gate.at[shard]),
        swap(wide_half, lambda shard: full_up.at[shard]),
    ]
    drain(token_run)
    got_out()
    got_wq()
    waits += [
        swap(shared_gate, lambda shard: full_shared_gate.at[shard]),
        swap(shared_up, lambda shard: full_shared_up.at[shard]),
        swap(shared_down, lambda shard: full_shared_down.at[shard]),
        swap(narrow_half, lambda shard: full_narrow.at[shard]),
    ]
    for run in down_runs:
        drain(run)
    route_run = gather_steps(
        wide, routes, all_routes, gather_keep.at[1], gather_send.at[1], gather_recv.at[1], sender
    )
    next(route_run)
    out_runs = piece_gathers(1, full_out)
    for run in out_runs:
        next(run)
    for copy in whole_weight(place, others, down_half, full_down, down_buf, whole_sem.at[0]):
        copy.wait()

    keys[:WINDOW, :] = jnp.zeros((WINDOW, keys.shape[1]), low)
    value[:WINDOW, :] = jnp.zeros((WINDOW, value.shape[1]), low)
    tile = 2 * rows
    own_width = width // shards

    def whole_dot(at, weight_of):
        total = 0.0
        for shard in range(shards):
            total = total + matmul(normed_buf[at, shard * own_width : (shard + 1) * own_width], weight_of(shard))
        return total

    def front_tile(index, _):
        at = pl.ds(pl.multiple_of(index * tile, tile), tile)
        values = token_buf[pl.ds(index * 2, 2)].reshape(tile, width).astype(jnp.float32)
        root = lax.rsqrt(jnp.mean(values * values, axis=1, keepdims=True) + EPS)
        normed_buf[at, :] = (values * root * first_gain[...]).astype(low)
        first = whole_dot(at, lambda shard: query_buf[shard])
        latent = whole_dot(at, lambda shard: down_buf[shard].reshape(own_width, -1))
        turn_at, sway_at = turn[at, :QK_ROPE], sway[at, :QK_ROPE]
        end = QK_NOPE + QK_ROPE
        query[at, :QK_NOPE] = first[:, :QK_NOPE].astype(low)
        query[at, QK_NOPE:end] = (first[:, QK_NOPE:end] * turn_at + first[:, end:] * sway_at).astype(low)
        query[at, end:] = jnp.zeros((tile, QK_ROPE), low)
        end = KV_RANK + QK_ROPE
        key_rope = (latent[:, KV_RANK:end] * turn_at + latent[:, end:] * sway_at).astype(low)
        latent = latent[:, :KV_RANK]
        compressed[at, :] = latent
        root = lax.rsqrt(jnp.mean(latent * latent, axis=1, keepdims=True) + EPS)
        normed_latent = (latent * root * latent_gain[...]).astype(low)
        key_latent[at, :] = normed_latent
        up_rows = KV_RANK // shards
        both = 0.0
        for shard in range(shards):
            both = both + matmul(normed_latent[:, shard * up_rows : (shard + 1) * up_rows], up_buf[shard])
        both = both.astype(low)
        later = pl.ds(pl.multiple_of(index * tile + WINDOW, tile), tile)
        keys[later, :QK_NOPE] = both[:, :QK_NOPE]
        keys[later, QK_NOPE : QK_NOPE + QK_ROPE] = key_rope
        keys[later, QK_NOPE + QK_ROPE :] = key_rope
        value[later, :] = both[:, QK_NOPE:]
        return 0

    tiles = group // 2
    grad_run = gather_steps(
        wide, cotangent, all_grads, gather_keep.at[3], gather_send.at[3], gather_recv.at[3], sender
    )
    for part in range(2):
        lax.fori_loop(part * tiles // 2, (part + 1) * tiles // 2, front_tile, 0)
        for run in out_runs + [route_run]:
            next(run, None)
    next(grad_run)
    save = pltpu.make_async_copy(normed_buf, normed_one, load_sem.at[1])
    save.start()
    for run in out_runs + [route_run]:
        next(run, None)

    def attend_tile(index, _):
        at = pl.ds(pl.multiple_of(index * QUERIES, QUERIES), QUERIES)
        window = pl.ds(pl.multiple_of(index * QUERIES, QUERIES), KEYS)
        scores = score_block(scale, query[at, :], keys[window, :], docs[at, :], row_docs[:, window])
        top = jnp.max(scores, axis=1, keepdims=True)
        expo = jnp.exp(scores - top)
        total = jnp.sum(expo, axis=1, keepdims=True)
        probs = (expo / total).astype(low)
        real = jnp.where(docs[at, :] < last, 1.0, 0.0)
        head_out[at, :] = (matmul(probs, value[window, :]) * real).astype(low)
        log_total[at, :] = jnp.broadcast_to(top + jnp.log(total), (QUERIES, log_total.shape[1]))
        return 0

    blocks = docs.shape[0] // QUERIES
    lax.fori_loop(0, blocks // 2, attend_tile, 0)
    for run in out_runs + [route_run]:
        drain(run)
    load_out = whole_weight(place, others, out_half, full_out, out_buf, whole_sem.at[1])
    next(grad_run)
    lax.fori_loop(blocks // 2, blocks, attend_tile, 0)

    def head_at(member):
        return head_out.at[pl.ds(pl.multiple_of(member * rows, rows), rows), :]

    def lands(head):
        return heads_buf.at[:, pl.ds(pl.multiple_of(head * V_HEAD, V_HEAD), V_HEAD)]

    keep = pltpu.make_async_copy(head_at(place.local), lands(place.local), load_sem.at[2])
    keep.start()
    for step, member in enumerate(members):
        sender.start(
            place.always,
            remote(
                head_at(member), lands(place.local), trade_send.at[step], trade_recv.at[place.local],
                {"expert": place.base + member},
            ),
        )
    for step, member in enumerate(members):
        remote(
            head_at(member), lands(member), trade_send.at[step], trade_recv.at[member], {"expert": place.base + member}
        ).wait_recv()
    keep.wait()
    for copy in load_out:
        copy.wait()

    for at, size in pieces_of(width, 512):
        columns = slice(at, at + size)
        total = token_buf[place.local].reshape(rows, width)[:, columns].astype(jnp.float32)
        for shard in range(shards):
            weight = out_buf[shard, :, :, :, columns].reshape(own_width, size)
            total = total + matmul(heads_buf[:, shard * own_width : (shard + 1) * own_width], weight)
        middle[:, columns] = total
    values = middle[...]
    root = lax.rsqrt(jnp.mean(values * values, axis=1, keepdims=True) + EPS)
    second_buf[...] = (values * root * second_gain[...]).astype(low).reshape(second_buf.shape)

    normed_run = gather_steps(
        wide, second_buf, all_normed, gather_keep.at[2], gather_send.at[2], gather_recv.at[2], sender
    )
    wq_runs = piece_gathers(2, full_query)
    runs = [normed_run, grad_run] + wq_runs
    while runs:
        runs = [run for run in runs if next(run, "end") != "end"]
    save.wait()
    for wait in waits:
        wait()
    sender.finish()


def forward_pass(scale, last, tokens, cotangent, blocks, routes, gains, tables):
    shards, plane = lax.axis_size("shard"), lax.axis_size("expert")
    local, width = tokens.shape
    low, shape = jnp.bfloat16, jax.ShapeDtypeStruct
    pieces = (PIECES, local // PIECES, width)
    any_space, vmem = pl.BlockSpec(memory_space=pl.ANY), pl.BlockSpec(memory_space=pltpu.VMEM)
    head_dim = QK_NOPE + QK_ROPE
    query_cols, down_half, up_half, out_half, query_half = blocks[:5]
    out_shape = [
        shape((plane,) + pieces, low),
        shape((plane,) + pieces, low),
        shape((plane, 1) + routes.shape, jnp.int32),
    ]
    out_shape += [shape((shards,) + block.shape, low) for block in (down_half, out_half, query_half) + blocks[5:]]
    out_shape += [
        shape((SEQ, width), low),
        shape((SEQ, head_dim + QK_ROPE), low),
        shape((SEQ + WINDOW, head_dim + QK_ROPE), low),
        shape((SEQ + WINDOW, V_HEAD), low),
        shape((SEQ, KV_RANK), low),
        shape((SEQ, KV_RANK), jnp.float32),
        shape((SEQ, V_HEAD), low),
        shape((SEQ, 128), jnp.float32),
        shape((local, width), jnp.float32),
        shape((shards,) + up_half.shape, low),
    ]
    hbm_out = 13
    dma = pltpu.SemaphoreType.DMA
    return pl.pallas_call(
        functools.partial(forward_kernel, shards, plane, scale, last),
        out_shape=out_shape,
        in_specs=[any_space] * (3 + len(blocks)) + [vmem] * (len(gains) + len(tables)),
        out_specs=[any_space] * hbm_out + [vmem] * (len(out_shape) - hbm_out),
        scratch_shapes=[
            pltpu.VMEM((SEQ_DEVICES,) + pieces, low),
            pltpu.VMEM((SEQ, width), low),
            pltpu.VMEM((shards,) + query_cols.shape, low),
            pltpu.VMEM((shards,) + down_half.shape, low),
            pltpu.VMEM((shards,) + out_half.shape, low),
            pltpu.VMEM((local, HEADS * V_HEAD), low),
            pltpu.VMEM(pieces, low),
            dma((12, shards)),
            dma((12, shards)),
            dma((12,)),
            dma((4, 4, plane, PIECES)),
            dma((4, plane, PIECES)),
            dma((4,)),
            dma((3, shards, 4, plane, 1)),
            dma((3, shards, plane, 1)),
            dma((SEQ_DEVICES,)),
            dma((SEQ_DEVICES,)),
            dma((4,)),
            dma((2, shards)),
        ],
        compiler_params=pltpu.CompilerParams(
            collective_id=1, has_side_effects=True, vmem_limit_bytes=60 * 2**20
        ),
        name="forward",
    )(tokens.reshape(pieces), cotangent.reshape(pieces), *blocks, routes[None], *gains, *tables)


def sums_kernel(shards, plane, *refs):
    (normed_part, output_part, token_scores, slot_rows, slot_grad, hidden, gate_back, up_back, all_normed, all_grads,
     shared_hidden, shared_gate_back, shared_up_back,
     back, output_sum, scores, down_got, down_own, gate_own, up_own, gate_send, up_send, narrow_own, narrow_send,
     shared_term,
     down_send, pair_buf, stream_buf, wide_buf, own_stage, send_stage, down_stage,
     load_sem, stream_sem, stage_sem, score_send, score_recv, swap_send, swap_recv, *reduces) = refs
    low = jnp.bfloat16
    place = Place(plane)
    sender = Sender()
    members = [lax.rem(place.me + step, plane) for step in range(1, plane)]
    others = [lax.rem(place.shard + step, shards) for step in range(1, shards)]
    greet([(place.always, {"expert": member}) for member in members] + [(place.always, {"shard": other}) for other in others])
    count = 13
    back_run = reduce_steps(place, normed_part, back, reduces[:count], sender, True)
    output_run = iter(())
    if len(reduces) > count:
        output_run = reduce_steps(place, output_part, output_sum, reduces[count:], sender, True)
    next(back_run)
    keep = pltpu.make_async_copy(token_scores.at[place.me], scores.at[place.me], load_sem.at[0])
    keep.start()

    def score_trade(step, member, source):
        return remote(token_scores.at[member], scores.at[source], score_send.at[step], score_recv.at[source],
                      {"expert": member})

    for step, member in enumerate(members):
        sender.start(place.always, score_trade(step, member, place.me))
    load_hidden = pltpu.make_async_copy(hidden, pair_buf.at[0], load_sem.at[1])
    load_hidden.start()
    load_up = pltpu.make_async_copy(up_back, pair_buf.at[1], load_sem.at[2])
    load_up.start()
    width = slot_rows.shape[1]
    tile = stream_buf.shape[-1]
    tiles = [slice(at, at + tile) for at in range(0, width, tile)]
    hidden_width = hidden.shape[1]
    own_hidden, own_width = hidden_width // shards, width // shards

    def streamed(source, buf, sem):
        copies = [
            pltpu.make_async_copy(source.at[:, columns], buf.at[index % 2], sem.at[index % 2])
            for index, columns in enumerate(tiles)
        ]
        copies[0].start()
        for index, copy in enumerate(copies):
            if index + 1 < len(copies):
                copies[index + 1].start()
            copy.wait()
            yield index, buf.at[index % 2]

    def down_chunks():
        load_hidden.wait()
        before = None
        for index, piece in streamed(slot_grad, stream_buf, stream_sem.at[0]):
            term = matmul_tn(pair_buf[0], piece[...])
            if before is not None:
                before.wait()
            for shard in range(shards):
                part = term[shard * own_hidden : (shard + 1) * own_hidden]

                @pl.when(place.shard == shard)
                def _():
                    down_stage[...] = part

                @pl.when(place.shard != shard)
                def _():
                    down_send[shard, :, tiles[index]] = part.astype(low)

            before = pltpu.make_async_copy(down_stage, down_own.at[:, tiles[index]], stage_sem.at[0])
            before.start()
            yield
        before.wait()
        for step, other in enumerate(others, 1):
            sender.start(
                place.always,
                remote(down_send.at[other], down_got.at[place.shard], swap_send.at[step], swap_recv.at[place.shard],
                       {"shard": other}),
            )

    def gate_chunks():
        load_gate = pltpu.make_async_copy(gate_back, pair_buf.at[0], load_sem.at[1])
        load_gate.start()
        load_gate.wait()
        load_up.wait()
        before = []
        for index, piece in streamed(slot_rows, stream_buf, stream_sem.at[0]):
            shard = index * tile // own_width
            within = pl.ds(index * tile - shard * own_width, tile)
            mine = place.shard == shard
            after = []
            for matrix, (own, send) in enumerate(((gate_own, gate_send), (up_own, up_send))):
                term = matmul_tn(piece[...], pair_buf[matrix])
                for there, copy in before[2 * matrix : 2 * matrix + 2]:
                    @pl.when(there)
                    def _():
                        copy.wait()

                to_own = pltpu.make_async_copy(own_stage.at[matrix], own.at[within], stage_sem.at[1 + matrix])
                to_send = pltpu.make_async_copy(send_stage.at[matrix], send.at[shard, within], stage_sem.at[3 + matrix])

                @pl.when(mine)
                def _():
                    own_stage[matrix] = term
                    to_own.start()

                @pl.when(~mine)
                def _():
                    send_stage[matrix] = term.astype(low)
                    to_send.start()

                after += [(mine, to_own), (~mine, to_send)]
                yield
            before = after
        for there, copy in before:
            @pl.when(there)
            def _():
                copy.wait()

    def shared_chunks():
        units = shared_hidden.shape[1]
        per = tile // shared_term.shape[1]
        for index, piece in streamed(all_normed, wide_buf, stream_sem.at[1]):
            both = [matmul_tn(piece[...], grads[...]).astype(low) for grads in (shared_gate_back, shared_up_back)]
            spot = slice(index * per, (index + 1) * per)
            shape = (per, shared_term.shape[1], units)
            shared_term[spot, :, :units] = both[0].reshape(shape)
            shared_term[spot, :, units:] = both[1].reshape(shape)
            yield
        own_units = units // shards
        for index, piece in streamed(all_grads, wide_buf, stream_sem.at[1]):
            term = matmul_tn(shared_hidden[...], piece[...])
            for shard in range(shards):
                part = term[shard * own_units : (shard + 1) * own_units]
                narrow_send[shard, :, tiles[index]] = part.astype(low)

                @pl.when(place.shard == shard)
                def _():
                    narrow_own[:, tiles[index]] = part

            yield

    def chunks():
        yield from down_chunks()
        yield from gate_chunks()
        yield from shared_chunks()

    work = chunks()
    units = plane // INNER * normed_part.shape[1]
    next(work)
    for _ in range(units):
        next(back_run)
    next(output_run, None)
    for index in range(8):
        next(work)
    for index in range(units):
        next(work, None)
        next(back_run)
    for index in range(units):
        next(work, None)
        next(output_run, None)
    drain(back_run)
    drain(work)
    drain(output_run)
    for step, member in enumerate(members):
        score_trade(step, member, member).wait_recv()
    keep.wait()
    for step, other in enumerate(others, 1):
        remote(down_send.at[other], down_got.at[other], swap_send.at[step], swap_recv.at[other], {"shard": other}).wait_recv()
    sender.finish()


def sums_pass(normed_part, output_part, token_scores, expert_terms, plane_terms, shared_terms):
    shards, plane = lax.axis_size("shard"), lax.axis_size("expert")
    low, shape = jnp.bfloat16, jax.ShapeDtypeStruct
    slot_rows, slot_grad, hidden, gate_back, up_back = expert_terms
    local, width = normed_part.shape[1:]
    slots, hidden_width = hidden.shape
    units = shared_terms[0].shape[1]
    count = 2 * PIECES
    pieces = (plane, count, local // count, width)
    own_width, own_hidden = width // shards, hidden_width // shards
    any_space, vmem = pl.BlockSpec(memory_space=pl.ANY), pl.BlockSpec(memory_space=pltpu.VMEM)
    reduces = 2 if plane == SEQ_DEVICES else 1
    out_shape = [
        shape(pieces[1:], jnp.float32),
        shape(pieces[1:], jnp.float32),
        shape(token_scores.shape, jnp.float32),
        shape((shards, own_hidden, width), low),
        shape((own_hidden, width), jnp.float32),
        shape((own_width, hidden_width), jnp.float32),
        shape((own_width, hidden_width), jnp.float32),
        shape((shards, own_width, hidden_width), low),
        shape((shards, own_width, hidden_width), low),
        shape((units // shards, width), jnp.float32),
        shape((shards, units // shards, width), low),
        shape((shards * plane, width // (shards * plane), 2 * units), low),
    ]
    dma, scratch = pltpu.SemaphoreType.DMA, pltpu.VMEM
    tile = 256
    outs = pl.pallas_call(
        functools.partial(sums_kernel, shards, plane),
        out_shape=out_shape,
        in_specs=[any_space] * 10 + [vmem] * 3,
        out_specs=[any_space] * 9 + [vmem] * 3,
        scratch_shapes=[
            scratch((shards, own_hidden, width), low),
            scratch((2, slots, hidden_width), low),
            scratch((2, slots, tile), low),
            scratch((2, plane * local, tile), low),
            scratch((2, tile, hidden_width), jnp.float32),
            scratch((2, tile, hidden_width), low),
            scratch((own_hidden, tile), jnp.float32),
            dma((3,)),
            dma((2, 2)),
            dma((5,)),
            dma((plane,)),
            dma((plane,)),
            dma((shards,)),
            dma((shards,)),
        ]
        + reduces * reduce_scratch(plane, count, local // count, width),
        compiler_params=pltpu.CompilerParams(
            collective_id=2, has_side_effects=True, vmem_limit_bytes=63 * 2**20
        ),
        name="sums",
    )(
        normed_part.reshape(pieces),
        output_part.reshape(pieces),
        token_scores,
        *expert_terms,
        *plane_terms,
        *shared_terms,
    )
    output_sum = outs[1].reshape(local, width)
    if reduces == 1:
        (output_sum,) = bundle(4, plane, shards, [("reduce", output_part)], 56 * 2**20)
    return (outs[0].reshape(local, width), output_sum) + tuple(outs[2:])


class Everyone:
    def __init__(self, place, plane, shards, source, got, send_sem, recv_sem, keep_sem):
        self.total = shards * plane
        self.plane = plane
        self.number = place.shard * plane + place.me
        self.source, self.got = source, got
        self.send_sem, self.recv_sem = send_sem, recv_sem
        self.keep = pltpu.make_async_copy(source(self.number), got.at[self.number], keep_sem)

    def copy(self, step, arriving):
        other = lax.rem(self.number + step, self.total)
        spot = other if arriving else self.number
        return remote(
            self.source(other),
            self.got.at[spot],
            self.send_sem.at[step],
            self.recv_sem.at[spot],
            {"shard": other // self.plane, "expert": lax.rem(other, self.plane)},
        )

    def start(self):
        self.keep.start()

        def body(step, _):
            self.copy(step, False).start()
            return 0

        lax.fori_loop(1, self.total, body, 0)

    def wait(self):
        self.keep.wait()

        def body(step, _):
            self.copy(step, True).wait_recv()
            return 0

        lax.fori_loop(1, self.total, body, 0)

    def finish(self):
        def body(step, _):
            self.copy(step, False).wait_send()
            return 0

        lax.fori_loop(1, self.total, body, 0)


def greet_everyone(place, plane, shards):
    barrier = pltpu.get_barrier_semaphore()
    total = shards * plane
    number = place.shard * plane + place.me

    def body(step, _):
        other = lax.rem(number + step, total)
        pl.semaphore_signal(
            barrier,
            inc=1,
            device_id={"shard": other // plane, "expert": lax.rem(other, plane)},
            device_id_type=MESH,
        )
        return 0

    lax.fori_loop(1, total, body, 0)
    pl.semaphore_wait(barrier, total - 1)


def norm_back(values, gain, grad):
    root = lax.rsqrt(jnp.mean(values * values, axis=1, keepdims=True) + EPS)
    weighted = grad * gain
    inner = jnp.mean(weighted * values, axis=1, keepdims=True)
    scaled = values * root
    return root * (weighted - scaled * (root * inner)), jnp.sum(grad * scaled, axis=0, keepdims=True)


def two_parts(values):
    high = values.astype(jnp.bfloat16)
    return high, (values - high.astype(jnp.float32)).astype(jnp.bfloat16)


def swapped_halves(pair):
    return pltpu.roll(pair, QK_ROPE // 2, 1)


def backward_kernel(shards, plane, scale, last, *refs):
    (back, scores, routes, middle, cotangent, tokens, first_gain, second_gain, latent_gain, router,
     query, keys, value, docs, row_docs, log_total, turn, sway, key_latent, up_head, head_out,
     compressed, full_out, full_query, full_down, normed_one, out_half, query_half, down_half, gate_send, up_send, narrow_send, shared_term,
     input_grad, query_out, up_out, down_out, out_out, small_out,
     gate_got, up_got, narrow_got, shared_got, mid_all,
     stream_buf, wq_buf, wd_buf, own_columns, own_compressed, heads_sum, mid_buf, low_buf, heads_buf, grad_buf, key_sum, value_sum,
     part_buf, trade_buf, trade_got, pair_buf, query_term, query_got, up_term, up_got_buf, own_query, low_grad, low_all,
     down_rows, down_got, out_rows, out_got, small_buf, small_got, key_got, *sems) = refs
    (load_sem, whole_sem, stream_sem, swap_send, swap_recv, trade_send, trade_recv, gather_send, gather_recv, gather_keep,
     all_send, all_recv, all_keep, rows_send, rows_recv, rows_keep, *reduce_scratch_refs) = sems
    low = jnp.bfloat16
    group = SEQ_DEVICES
    place = Place(group)
    local, width = middle.shape
    total = shards * plane
    sender = Sender()
    greet_everyone(place, plane, shards)
    members = [lax.rem(place.local + step, group) for step in range(1, group)]
    others = [lax.rem(place.shard + step, shards) for step in range(1, shards)]

    shares = []
    for number, (source, got) in enumerate(((gate_send, gate_got), (up_send, up_got), (narrow_send, narrow_got))):
        for step, other in enumerate(others, 1):
            sender.start(
                place.always,
                remote(source.at[other], got.at[place.shard], swap_send.at[number, step],
                       swap_recv.at[number, place.shard], {"shard": other}),
            )
            shares.append(
                remote(source.at[other], got.at[other], swap_send.at[number, step], swap_recv.at[number, other],
                       {"shard": other})
            )
    numbers = iter(range(16))

    def load(source, target):
        copy = pltpu.make_async_copy(source, target, load_sem.at[next(numbers)])
        copy.start()
        return copy

    own_lanes = pl.ds(pl.multiple_of(place.local * 128, 128), 128)
    got_wd = whole_weight(place, others, down_half, full_down, wd_buf, whole_sem)
    got_columns = load(normed_one.at[:, :, :, own_lanes], own_columns)
    tile = stream_buf.shape[-1]
    tiles = [slice(at, at + tile) for at in range(0, width, tile)]

    def streamed(buf, count, sources):
        def copies(index):
            half = index % 2
            return [
                (there, pltpu.make_async_copy(source, target, stream_sem.at[half, number]))
                for there, source, target, number in sources(index, buf.at[half])
            ]

        def start(index):
            for there, copy in copies(index):
                @pl.when(there)
                def _():
                    copy.start()

        start(0)
        for index in range(count):
            if index + 1 < count:
                start(index + 1)
            for there, copy in copies(index):
                @pl.when(there)
                def _():
                    copy.wait()
            yield index, buf.at[index % 2]

    own_at = pl.ds(pl.multiple_of(place.local * local, local), local)
    per_shard = group // shards

    def columns_of(array):
        def sources(index, target):
            return [
                (place.always, array.at[pl.ds(shard * per_shard, per_shard), :, :, tiles[index]], target.at[shard], shard)
                for shard in range(shards)
            ]

        return sources

    def out_columns(index, target):
        found = []
        for shard in range(shards):
            mine = place.shard == shard
            found.append((mine, out_half.at[:, :, :, tiles[index]], target.at[shard], shard))
            found.append((~mine, full_out.at[shard, :, :, :, tiles[index]], target.at[shard], shard))
        return found

    row_tile = wq_buf.shape[1]
    own_rows = width // shards

    def query_rows(index, target):
        shard = index * row_tile // own_rows
        rows = slice(index * row_tile - shard * own_rows, (index + 1) * row_tile - shard * own_rows)
        mine = place.shard == shard
        return [(mine, query_half.at[rows], target, 0), (~mine, full_query.at[shard, rows], target, 0)]

    got_compressed = load(compressed.at[own_at, :], own_compressed)

    def everyone(index, source, got):
        return Everyone(place, plane, shards, source, got, all_send.at[index], all_recv.at[index], all_keep.at[index])

    experts = router.shape[0]
    values = middle[...]
    root = lax.rsqrt(jnp.mean(values * values, axis=1, keepdims=True) + EPS)
    second_normed = (values * root * second_gain[...]).astype(low)
    logits = matmul_nt(router[...], second_normed)
    names = lax.broadcasted_iota(jnp.int32, (experts, local), 0)
    chosen = jnp.zeros((experts, local), jnp.float32)
    for choice in range(TOP):
        chosen = chosen + jnp.where(routes[choice : choice + 1, :] == names, 1.0, 0.0)
    logits = jnp.where(chosen > 0.0, logits, NEG)
    gates = jnp.exp(logits - jnp.max(logits, axis=0, keepdims=True)) * chosen
    gates = gates / jnp.sum(gates, axis=0, keepdims=True)
    gate_grad = jnp.concatenate([scores[index, :1, :] for index in range(experts)], axis=0)
    logit_grad = gates * (gate_grad - jnp.sum(gates * gate_grad, axis=0, keepdims=True))
    high, rest = two_parts(logit_grad)
    router_term = matmul(high, second_normed) + matmul(rest, second_normed)
    grad = back[...] + matmul_tn(high, router[...]) + matmul_tn(rest, router[...])
    row_grad, second_term = norm_back(values, second_gain[...], grad)
    mid_buf[...] = cotangent[...].astype(jnp.float32) + row_grad
    low_buf[...] = mid_buf[...].astype(low).reshape(low_buf.shape)

    for index, piece in streamed(stream_buf, len(tiles), out_columns):
        part = matmul_nt(low_buf[:, :, tiles[index]].reshape(local, tile), piece[...].reshape(-1, tile))
        heads_sum[...] = part if index == 0 else heads_sum[...] + part
    heads_buf[...] = heads_sum[...].astype(low)

    def lands(member):
        return heads_buf.at[:, pl.ds(pl.multiple_of(member * V_HEAD, V_HEAD), V_HEAD)]

    def head_trade(step, member, source):
        spot = pl.ds(pl.multiple_of(source * local, local), local)
        return remote(lands(member), grad_buf.at[spot, :], trade_send.at[0, step], trade_recv.at[0, source],
                      {"expert": place.base + member})

    keep_head = pltpu.make_async_copy(lands(place.local), grad_buf.at[own_at, :], load_sem.at[next(numbers)])
    keep_head.start()
    for step, member in enumerate(members):
        sender.start(place.always, head_trade(step, member, place.local))
    mid_run = gather_steps(place, low_buf, mid_all, gather_keep.at[0], gather_send.at[0], gather_recv.at[0], sender)
    for step, member in enumerate(members):
        head_trade(step, member, member).wait_recv()
    keep_head.wait()
    next(mid_run)
    shared_trade = everyone(0, lambda target: shared_term.at[target], shared_got)
    shared_trade.start()

    key_sum[...] = jnp.zeros_like(key_sum)
    value_sum[...] = jnp.zeros_like(value_sum)

    def attend_tile(index, _):
        at = pl.ds(pl.multiple_of(index * QUERIES, QUERIES), QUERIES)
        window = pl.ds(pl.multiple_of(index * QUERIES, QUERIES), KEYS)
        tile, key_tile = query[at, :], keys[window, :]
        head_grad = jnp.where(docs[at, :] < last, grad_buf[at, :], jnp.zeros((), low))
        scores_at = score_block(scale, tile, key_tile, docs[at, :], row_docs[:, window])
        probs = jnp.exp(scores_at - log_total[at, :1])
        prob_grad = matmul_nt(head_grad, value[window, :])
        inner = jnp.sum(probs * prob_grad, axis=1, keepdims=True)
        raw_grad = (probs * (prob_grad - inner) * scale).astype(low)
        grads = matmul(raw_grad, key_tile)
        trade_buf[at, :QK_NOPE] = grads[:, :QK_NOPE].astype(low)
        pair = grads[:, QK_NOPE:]
        trade_buf[at, QK_NOPE:] = (pair * turn[at, :] - swapped_halves(pair) * sway[at, :]).astype(low)
        key_sum[window, :] += matmul_tn(raw_grad, tile)
        value_sum[window, :] += matmul_tn(probs.astype(low), head_grad)
        return 0

    blocks = docs.shape[0] // QUERIES
    for index in range(blocks // 2):
        attend_tile(jnp.int32(index), 0)
    next(mid_run)
    for index in range(blocks // 2, blocks):
        attend_tile(jnp.int32(index), 0)
    next(mid_run)

    lane = lax.broadcasted_iota(jnp.int32, (QUERIES, 2 * QK_ROPE), 1)

    def key_tile(index, _):
        at = pl.ds(pl.multiple_of(index * QUERIES, QUERIES), QUERIES)
        later = pl.ds(pl.multiple_of(index * QUERIES + WINDOW, QUERIES), QUERIES)
        key_rope = pltpu.roll(key_sum[later, QK_NOPE:], QK_ROPE, 1).astype(low)
        trade_buf[at, QK_NOPE:] = jnp.where(lane < QK_ROPE, trade_buf[at, QK_NOPE:], key_rope)
        pair_buf[at, :QK_NOPE] = key_sum[later, :QK_NOPE].astype(low)
        pair_buf[at, QK_NOPE:] = value_sum[later, :].astype(low)
        part = matmul_nt(pair_buf[at, :], up_head[...]).astype(low)
        per = QUERIES // local
        part_buf[pl.ds(index * per, per)] = part.reshape((per,) + part_buf.shape[1:])
        return 0

    for index in range(blocks):
        key_tile(jnp.int32(index), 0)

    def token_trade(step, member, source):
        spot = pl.ds(pl.multiple_of(member * local, local), local)
        return remote(trade_buf.at[spot, :], trade_got.at[source], trade_send.at[1, step], trade_recv.at[1, source],
                      {"expert": place.base + member})

    reduce_run = reduce_steps(place, part_buf, key_got, reduce_scratch_refs, sender)
    next(reduce_run)
    keep_token = pltpu.make_async_copy(trade_buf.at[own_at, :], trade_got.at[place.local], load_sem.at[next(numbers)])
    keep_token.start()
    for step, member in enumerate(members):
        sender.start(place.always, token_trade(step, member, place.local))

    for index, piece in streamed(stream_buf, len(tiles), columns_of(normed_one)):
        term = matmul_tn(trade_buf[...], piece[...].reshape(SEQ, tile))
        per = tile // query_term.shape[1]
        query_term[index * per : (index + 1) * per] = term.T.astype(low).reshape((per,) + query_term.shape[1:])
    up_term[...] = matmul_tn(key_latent[...], pair_buf[...]).astype(low).reshape(up_term.shape)
    next(reduce_run)
    query_trade = everyone(1, lambda target: query_term.at[target], query_got)
    query_trade.start()
    up_trade = everyone(2, lambda target: up_term.at[target], up_got_buf)
    up_trade.start()
    next(reduce_run)
    drain(reduce_run)
    for step, member in enumerate(members):
        token_trade(step, member, member).wait_recv()
    keep_token.wait()

    got_compressed.wait()
    head_dim = QK_NOPE + QK_ROPE
    rope = jnp.zeros((local, 2 * QK_ROPE), jnp.float32)
    for head in range(group):
        own_query[:, head * head_dim : (head + 1) * head_dim] = trade_got[head, :, :head_dim]
        rope = rope + trade_got[head, :, QK_NOPE:].astype(jnp.float32)
    lane = lax.broadcasted_iota(jnp.int32, rope.shape, 1)
    rope = jnp.where(lane < QK_ROPE, pltpu.roll(rope, QK_ROPE, 1), rope)
    rope = rope * turn[own_at, :] - swapped_halves(rope) * sway[own_at, :]
    latent_grad, latent_term = norm_back(own_compressed[...], latent_gain[...], key_got[...].reshape(local, KV_RANK))
    low_grad[0, 0, :, :KV_RANK] = latent_grad.astype(low)
    low_grad[0, 0, :, KV_RANK:] = jnp.where(lane < QK_ROPE, rope, 0.0).astype(low)
    low_run = gather_steps(place, low_grad.at[0], low_all, gather_keep.at[1], gather_send.at[1], gather_recv.at[1], sender)
    next(low_run)
    for copy in got_wd:
        copy.wait()
    for index, piece in streamed(wq_buf, width // row_tile, query_rows):
        rows = slice(index * row_tile, (index + 1) * row_tile)
        shard = index * row_tile // own_rows
        within = slice(rows.start - shard * own_rows, rows.stop - shard * own_rows)
        term = matmul_nt(own_query[...], piece[...])
        input_grad[:, rows] = term + matmul_nt(low_grad[0, 0], wd_buf[shard, within, :])
    next(low_run)
    row_grad, first_term = norm_back(tokens[...].astype(jnp.float32), first_gain[...], input_grad[...])
    input_grad[...] = mid_buf[...] + row_grad
    next(low_run)
    drain(mid_run)
    per_lane = width // 128
    for block in range(per_lane):
        columns = slice(block * 128, (block + 1) * 128)
        small_buf[block, :experts, :] = router_term[:, columns]
        small_buf[block, experts : experts + 1, :] = second_term[:, columns]
        small_buf[block, experts + 1 : experts + 2, :] = first_term[:, columns]
        at = block // (per_lane * 128 // KV_RANK) * 128
        small_buf[block, experts + 2 : experts + 3, :] = latent_term[:, at : at + 128]
        small_buf[block, experts + 3 :, :] = jnp.zeros((small_buf.shape[1] - experts - 3, 128), jnp.float32)
    small_trade = everyone(3, lambda target: small_buf.at[target // (total // per_lane)], small_got)
    small_trade.start()
    drain(low_run)
    got_columns.wait()
    down = matmul_tn(own_columns[...].reshape(SEQ, -1), low_all[...].reshape(SEQ, -1))
    down_rows[...] = down.astype(low).reshape(down_rows.shape)
    down_trade = head_rows(place, plane, shards, down_rows, down_got, rows_keep.at[0], rows_send.at[0], rows_recv.at[0])[0]
    for index, piece in streamed(stream_buf, len(tiles), columns_of(mid_all)):
        term = matmul_tn(head_out[...], piece[...].reshape(SEQ, tile)).astype(low)
        out_rows[:, :, tiles[index]] = term.reshape(out_rows.shape[:2] + (tile,))
    out_trade = head_rows(place, plane, shards, out_rows, out_got, rows_keep.at[1], rows_send.at[1], rows_recv.at[1])[0]

    sequences = total // group
    query_trade.wait()
    up_trade.wait()
    for head in range(group):
        query_sum, up_sum = 0.0, 0.0
        for sequence in range(sequences):
            query_sum = query_sum + query_got[sequence * group + head].astype(jnp.float32)
            up_sum = up_sum + up_got_buf[sequence * group + head].astype(jnp.float32)
        query_out[:, head * head_dim : (head + 1) * head_dim] = query_sum[:, :head_dim]
        both = QK_NOPE + V_HEAD
        up_out[:, head * both : (head + 1) * both] = up_sum
    small_trade.wait()
    small_out[...] = small_got[0]

    def small_sum(source, _):
        small_out[...] += small_got[source]
        return 0

    lax.fori_loop(1, total, small_sum, 0)
    down_trade.wait()
    out_trade.wait()
    down_sum, out_sum = 0.0, 0.0
    for sequence in range(sequences):
        down_sum = down_sum + down_got[sequence].astype(jnp.float32)
        out_sum = out_sum + out_got[sequence].astype(jnp.float32)
    down_out[...] = down_sum[:, : down_out.shape[1]]
    out_out[...] = out_sum
    shared_trade.wait()
    for share in shares:
        share.wait_recv()
    for trade in (shared_trade, query_trade, up_trade, small_trade):
        trade.finish()
    sender.finish()


def backward_pass(scale, last, small, tables, saved, weights, sends):
    shards, plane = lax.axis_size("shard"), lax.axis_size("expert")
    total = shards * plane
    low, shape = jnp.bfloat16, jax.ShapeDtypeStruct
    local, width = small[3].shape
    head_dim = QK_NOPE + QK_ROPE
    vmem, any_space = pl.BlockSpec(memory_space=pltpu.VMEM), pl.BlockSpec(memory_space=pl.ANY)
    inputs = list(small) + list(tables) + list(saved)
    hbm = list(weights) + list(sends)
    gate_send, up_send, narrow_send, shared_term = sends
    experts = small[9].shape[0]
    small_rows = experts + 3 + -(experts + 3) % 8
    own_width = width // total
    out_shape = [
        shape((local, width), jnp.float32),
        shape((own_width, HEADS * head_dim), jnp.float32),
        shape((KV_RANK // total, HEADS * (QK_NOPE + V_HEAD)), jnp.float32),
        shape((own_width, KV_RANK + QK_ROPE), jnp.float32),
        shape((own_width, width), jnp.float32),
        shape((small_rows, 128), jnp.float32),
        shape(gate_send.shape, low),
        shape(up_send.shape, low),
        shape(narrow_send.shape, low),
        shape(shared_term.shape, low),
        shape((SEQ_DEVICES, PIECES, local // PIECES, width), low),
    ]
    hbm_out = 5
    dma, scratch = pltpu.SemaphoreType.DMA, pltpu.VMEM
    pieces = (PIECES, local // PIECES)
    down_width = weights[3].shape[2]
    row_count = 128 // own_width
    sequences = total // SEQ_DEVICES
    wide_head = 2 * QK_NOPE
    return pl.pallas_call(
        functools.partial(backward_kernel, shards, plane, scale, last),
        out_shape=out_shape,
        in_specs=[vmem] * len(inputs) + [any_space] * len(hbm),
        out_specs=[vmem] * (len(out_shape) - hbm_out) + [any_space] * hbm_out,
        scratch_shapes=[
            scratch((2, shards, SEQ_DEVICES // shards) + pieces + (512,), low),
            scratch((2, 256, HEADS * head_dim), low),
            scratch((shards, width // shards, down_width), low),
            scratch((SEQ_DEVICES,) + pieces + (128,), low),
            scratch((local, KV_RANK), jnp.float32),
            scratch((local, width), jnp.float32),
            scratch((local, width), jnp.float32),
            scratch(pieces + (width,), low),
            scratch((local, width), low),
            scratch((SEQ, V_HEAD), low),
            scratch((SEQ + WINDOW, wide_head), jnp.float32),
            scratch((SEQ + WINDOW, V_HEAD), jnp.float32),
            scratch((SEQ_DEVICES,) + pieces + (KV_RANK,), low),
            scratch((SEQ, wide_head), low),
            scratch((SEQ_DEVICES, local, wide_head), low),
            scratch((SEQ, wide_head), low),
            scratch((total, own_width, wide_head), low),
            scratch((total, own_width, wide_head), low),
            scratch((total, KV_RANK // total, wide_head), low),
            scratch((total, KV_RANK // total, wide_head), low),
            scratch((local, HEADS * head_dim), low),
            scratch((1, 1, local, down_width), low),
            scratch((SEQ_DEVICES, 1, local, down_width), low),
            scratch((row_count, own_width, down_width), low),
            scratch((sequences, own_width, down_width), low),
            scratch((row_count, own_width, width), low),
            scratch((sequences, own_width, width), low),
            scratch((width // 128, small_rows, 128), jnp.float32),
            scratch((total, small_rows, 128), jnp.float32),
            scratch(pieces + (KV_RANK,), jnp.float32),
            dma((8,)),
            dma((shards,)),
            dma((2, shards)),
            dma((3, shards)),
            dma((3, shards)),
            dma((2, SEQ_DEVICES)),
            dma((2, SEQ_DEVICES)),
            dma((2, 4, SEQ_DEVICES, PIECES)),
            dma((2, SEQ_DEVICES, PIECES)),
            dma((2,)),
            dma((4, total)),
            dma((4, total)),
            dma((4,)),
            dma((2, max(row_count, sequences))),
            dma((2, max(row_count, sequences))),
            dma((2,)),
        ]
        + reduce_scratch(SEQ_DEVICES, PIECES, local // PIECES, KV_RANK),
        compiler_params=pltpu.CompilerParams(
            collective_id=3, has_side_effects=True, vmem_limit_bytes=62 * 2**20
        ),
        name="backward",
    )(*inputs, *hbm)


def on_device(
    tokens,
    document_lengths,
    routes,
    first_gain,
    query_weight,
    latent_down,
    latent_gain,
    latent_up,
    output_weight,
    second_gain,
    router_weight,
    shared_gate,
    shared_up,
    shared_down,
    expert_gate,
    expert_up,
    expert_down,
    cotangent,
):
    local_rows, width = tokens.shape
    shards = lax.axis_size("shard")
    plane = lax.axis_size("expert")
    everyone = ("shard", "expert")
    all_devices = shards * plane
    shard_at = lax.axis_index("shard")
    plane_at = lax.axis_index("expert")
    head_at = plane_at % SEQ_DEVICES
    sequence_at = (shard_at * plane + plane_at) // SEQ_DEVICES
    capacity = local_rows * TOP * 4 // (3 * plane)
    head_dim = QK_NOPE + QK_ROPE
    scale = 1.0 / math.sqrt(head_dim)
    own_at = head_at * local_rows

    def own_rows(values):
        return lax.dynamic_slice_in_dim(values, own_at, local_rows, 0)

    piece_rows = output_weight.shape[0] // plane
    half = QK_ROPE // 2
    query_columns = lax.dynamic_slice_in_dim(query_weight, head_at * head_dim, head_dim, 1)
    query_turn, key_turn = query_columns[:, QK_NOPE:], latent_down[:, KV_RANK:]
    query_cols = jnp.concatenate(
        [query_columns, query_turn[:, half:], query_turn[:, :half]], axis=1
    )
    down_half = jnp.concatenate(
        [latent_down, key_turn[:, half:], key_turn[:, :half]], axis=1
    )
    units = shared_down.shape[0] // plane
    unit_pad = -units % 16
    padded_units = units + unit_pad
    gate_columns, up_columns = (
        jnp.concatenate(
            [
                jnp.pad(
                    lax.dynamic_slice_in_dim(
                        weight, index * shared_down.shape[0] + plane_at * units, units, 1
                    ),
                    ((0, 0), (0, unit_pad)),
                )
                for index in range(shards)
            ],
            axis=1,
        )
        for weight in (shared_gate, shared_up)
    )
    down_units = lax.dynamic_slice_in_dim(shared_down, plane_at * units, units, 0)
    down_units = jnp.pad(down_units, ((0, unit_pad), (0, 0)))

    def plane_pieces(weight):
        return weight.reshape(plane, 1, -1, weight.shape[1])

    positions = jnp.arange(SEQ, dtype=jnp.int32)
    cosine_part, sine_part = rotary_tables(positions, QK_ROPE)
    sequence_count, entry_count = document_lengths.shape
    ends = jnp.cumsum(document_lengths, axis=1)
    picked = jnp.arange(sequence_count, dtype=jnp.int32)[:, None] == sequence_at
    row_ends = jnp.sum(jnp.where(picked, ends, 0), axis=0)
    documents = jnp.sum((positions[:, None] >= row_ends[None, :]).astype(jnp.int32), axis=1)
    turn = jnp.tile(cosine_part, (1, 4))
    sway = jnp.tile(jnp.concatenate([-sine_part, sine_part], axis=1), (1, 2))
    docs = documents[:, None]
    row_docs = jnp.pad(docs, ((WINDOW, 0), (0, 0)), constant_values=-1).T
    route_rows = jnp.pad(routes.T, ((0, 8 - TOP), (0, 0)), constant_values=-1)
    (
        all_normed,
        all_grads,
        all_routes,
        full_down,
        full_out,
        full_query,
        gate_single,
        up_single,
        down_single,
        gate_shared,
        up_shared,
        down_shared,
        normed_one,
        query,
        keys,
        value,
        key_latent,
        compressed,
        head_out,
        log_total,
        middle,
        up_head,
    ) = forward_pass(
        scale,
        entry_count - 1,
        tokens,
        cotangent,
        (
            query_cols,
            plane_pieces(down_half),
            lax.dynamic_slice_in_dim(
                latent_up, head_at * (QK_NOPE + V_HEAD), QK_NOPE + V_HEAD, 1
            ),
            plane_pieces(output_weight),
            plane_pieces(query_weight),
            expert_gate[0],
            expert_up[0],
            expert_down[0],
            gate_columns,
            up_columns,
            down_units,
        ),
        route_rows,
        (first_gain[None], latent_gain[None], second_gain[None]),
        (turn, sway, docs, row_docs),
    )
    all_normed = all_normed.reshape(-1, width)
    all_grads = all_grads.reshape(-1, width)
    blocked = (SEQ_DEVICES, PIECES, local_rows // PIECES, width)
    shard_blocked = (shards, SEQ_DEVICES // shards) + blocked[1:]
    (
        normed_part,
        output_part,
        slot_rows,
        slot_grad,
        hidden,
        gate_pre_grad,
        up_pre_grad,
        token_scores,
        shared_hidden,
        shared_gate_back,
        shared_up_back,
    ) = expert_pass(
        jnp.stack([plane_at, shard_at]).astype(jnp.int32)[None],
        all_routes[:, 0],
        router_weight.T,
        all_normed,
        all_grads,
        (
            gate_columns,
            gate_shared,
            up_columns,
            up_shared,
            down_units,
            down_shared,
            expert_gate[0],
            gate_single,
            expert_up[0],
            up_single,
            expert_down[0],
            down_single,
        ),
        capacity,
    )
    (
        back,
        output_sum,
        scores,
        down_blocks,
        down_own,
        gate_own,
        up_own,
        gate_send,
        up_send,
        shared_down_own,
        shared_down_send,
        shared_term,
    ) = sums_pass(
        normed_part.reshape(plane, local_rows, width),
        output_part.reshape(plane, local_rows, width),
        token_scores,
        (slot_rows, slot_grad, hidden, gate_pre_grad, up_pre_grad),
        (all_normed, all_grads),
        (shared_hidden, shared_gate_back, shared_up_back),
    )
    activations = (middle + output_sum).astype(jnp.bfloat16)

    def sum_shards(own, blocks):
        for step in range(1, shards):
            own = own + lax.dynamic_index_in_dim(
                blocks, (shard_at + step) % shards, 0, keepdims=False
            ).astype(jnp.float32)
        return own

    (
        input_grad,
        query_weight_grad,
        latent_up_grad,
        latent_down_grad,
        output_weight_grad,
        small_sums,
        gate_blocks,
        up_blocks,
        shared_blocks,
        shared_moved,
        _,
    ) = backward_pass(
        scale,
        entry_count - 1,
        (
            back,
            scores,
            route_rows,
            middle,
            cotangent,
            tokens,
            first_gain[None],
            second_gain[None],
            latent_gain[None],
            router_weight.T,
        ),
        (query, keys, value, docs, row_docs, log_total, turn, sway),
        (key_latent, up_head.reshape(KV_RANK, -1), head_out),
        (
            compressed,
            full_out.reshape(shard_blocked),
            full_query.reshape((shards,) + query_weight.shape),
            full_down.reshape((shards,) + down_half.shape),
            normed_one.reshape(blocked),
            output_weight.reshape(shard_blocked[1:]),
            query_weight,
            down_half,
        ),
        (gate_send, up_send, shared_down_send, shared_term),
    )
    expert_gate_grad = sum_shards(gate_own, gate_blocks)[None]
    expert_up_grad = sum_shards(up_own, up_blocks)[None]
    expert_down_grad = sum_shards(down_own, down_blocks)[None]
    shared_down_grad = sum_shards(shared_down_own, shared_blocks)[:units]
    shared_moved = shared_moved.astype(jnp.float32).reshape(shards, plane, -1, 2, shards, padded_units)
    shared_moved = jnp.sum(shared_moved, axis=0)[..., :units].transpose(2, 1, 3, 0, 4)
    shared_moved = shared_moved.reshape(2, shared_moved.shape[1], -1)
    shared_gate_grad = shared_moved[0]
    shared_up_grad = shared_moved[1]
    own_width = width // all_devices
    number = shard_at * plane + plane_at
    own_small = lax.dynamic_slice_in_dim(small_sums, number * own_width % 128, own_width, 1)
    router_weight_grad = own_small[:plane].T
    second_gain_grad = own_small[plane]
    first_gain_grad = own_small[plane + 1]
    latent_width = KV_RANK // all_devices
    latent_gain_grad = lax.dynamic_slice_in_dim(
        small_sums[plane + 2], number * latent_width % 128, latent_width, 0
    )
    return (
        activations,
        input_grad,
        first_gain_grad,
        query_weight_grad,
        latent_down_grad,
        latent_gain_grad,
        latent_up_grad,
        output_weight_grad,
        second_gain_grad,
        router_weight_grad,
        shared_gate_grad,
        shared_up_grad,
        shared_down_grad,
        expert_gate_grad,
        expert_up_grad,
        expert_down_grad,
    )


def solution(mesh):
    return jax.shard_map(
        on_device,
        mesh=mesh,
        in_specs=(
            P(("shard", "expert"), None),
            P(),
            P(("shard", "expert"), None),
            P(),
            P("shard", None),
            P("shard", None),
            P(),
            P("shard", None),
            P("shard", None),
            P(),
            P(),
            P("shard", None),
            P("shard", None),
            P("shard", None),
            P("expert", "shard", None),
            P("expert", "shard", None),
            P("expert", "shard", None),
            P(("shard", "expert"), None),
        ),
        out_specs=(
            P(("shard", "expert"), None),
            P(("shard", "expert"), None),
            P(("shard", "expert")),
            P(("shard", "expert"), None),
            P(("shard", "expert"), None),
            P(("shard", "expert")),
            P(("shard", "expert"), None),
            P(("shard", "expert"), None),
            P(("shard", "expert")),
            P(("shard", "expert"), None),
            P(("shard", "expert"), None),
            P(("shard", "expert"), None),
            P(("shard", "expert"), None),
            P("expert", "shard", None),
            P("expert", "shard", None),
            P("expert", "shard", None),
        ),
        check_vma=False,
    )
```

```python
import functools
import math

import jax
import jax.numpy as jnp
from jax import lax
from jax.experimental import pallas as pl
from jax.experimental.pallas import tpu as pltpu
from jax.sharding import PartitionSpec as P

HEADS = 16
QK_NOPE = 128
QK_ROPE = 64
V_HEAD = 128
KV_RANK = 512
TOP = 6
SEQ = 2048
WINDOW = 1024
TOK_DEV = 128
STEP_SENDERS = 4
SEQ_DEVICES = SEQ // TOK_DEV


EPS = 1e-06
THETA = 10000.0
NEG = -1e30
HIGH = lax.Precision.HIGHEST


def matmul(left, right):
    return jnp.dot(left, right, preferred_element_type=jnp.float32)


def matmul_tn(left, right):
    return lax.dot_general(
        left, right, (((0,), (0,)), ((), ())), preferred_element_type=jnp.float32
    )


def matmul_nt(left, right):
    return lax.dot_general(
        left, right, (((1,), (1,)), ((), ())), preferred_element_type=jnp.float32
    )


def norm_scale(values, gain):
    return values * lax.rsqrt(jnp.mean(values * values, axis=-1, keepdims=True) + EPS) * gain


def rotary_tables(positions, width):
    half = width // 2
    freqs = THETA ** (-jnp.arange(half, dtype=jnp.float32) / half)
    angles = positions.astype(jnp.float32)[:, None] * freqs[None, :]
    return (jnp.cos(angles), jnp.sin(angles))


def rotate(values, cosine_part, sine_part):
    half = values.shape[-1] // 2
    first = values[..., :half]
    second = values[..., half:]
    return jnp.concatenate(
        [first * cosine_part - second * sine_part, second * cosine_part + first * sine_part],
        axis=-1,
    )


def unrotate(values, cosine_part, sine_part):
    half = values.shape[-1] // 2
    first = values[..., :half]
    second = values[..., half:]
    return jnp.concatenate(
        [first * cosine_part + second * sine_part, second * cosine_part - first * sine_part],
        axis=-1,
    )


def swish_parts(values):
    sigmoid_part = jax.nn.sigmoid(values)
    return (values * sigmoid_part, sigmoid_part * (1.0 + values * (1.0 - sigmoid_part)))


MESH = pl.DeviceIdType.MESH
INNER = 4
PIECES = 2


class Sender:
    def __init__(self):
        self.started = []

    def start(self, there, copy):
        @pl.when(there)
        def _():
            copy.start()

        self.started.append((there, copy))

    def finish(self):
        for there, copy in self.started:
            @pl.when(there)
            def _():
                copy.wait_send()


def remote(source, target, send_sem, recv_sem, place):
    return pltpu.make_async_remote_copy(
        src_ref=source,
        dst_ref=target,
        send_sem=send_sem,
        recv_sem=recv_sem,
        device_id=place,
        device_id_type=MESH,
    )


class Place:
    def __init__(self, group):
        self.me = lax.axis_index("expert")
        self.shard = lax.axis_index("shard")
        self.group = group
        self.outer = group // INNER
        self.local = lax.rem(self.me, group)
        self.base = self.me - self.local
        self.level = self.local // INNER
        inner = lax.rem(self.local, INNER)
        self.row_step = 2 - 4 * (inner // 2)
        self.twin_step = 1 - 2 * lax.rem(inner, 2)
        self.always = self.me >= 0
        self.upper = self.level < self.outer - 1
        self.lower = self.level > 0

    def neighbours(self):
        return [
            (self.upper, {"expert": self.me + INNER}),
            (self.lower, {"expert": self.me - INNER}),
            (self.always, {"expert": self.me + self.row_step}),
            (self.always, {"expert": self.me + self.twin_step}),
        ]

    def along(self, step):
        below = (self.level >= step, self.local - step * INNER, self.upper, self.me + INNER, 0)
        above = (self.level + step < self.outer, self.local + step * INNER, self.lower, self.me - INNER, 1)
        return (below, above)


def greet(peers):
    barrier = pltpu.get_barrier_semaphore()
    for there, peer in peers:
        @pl.when(there)
        def _():
            pl.semaphore_signal(barrier, inc=1, device_id=peer, device_id_type=MESH)
    pl.semaphore_wait(barrier, sum(there.astype(jnp.int32) for there, _ in peers))


def gather_plan(place, own_ref, out_ref, copy_sem, send_sem, recv_sem):
    local = place.local
    pieces = out_ref.shape[1]
    row_at, twin_at = place.me + place.row_step, place.me + place.twin_step
    segments, sends = [[]], []

    def push(kind, block, piece, target, source=None):
        spot = out_ref.at[block, piece]
        return remote(
            spot if source is None else source.at[piece],
            spot,
            send_sem.at[kind, block, piece],
            recv_sem.at[block, piece],
            {"expert": target},
        )

    def start(there, copy):
        segments[-1].append((there, copy.start))
        sends.append((there, copy))

    def arrive(there, block, piece):
        segments[-1].append((there, push(0, block, piece, place.me).wait_recv))

    if own_ref is None:
        own_ref = out_ref.at[local]
    else:
        keep = pltpu.make_async_copy(own_ref, out_ref.at[local], copy_sem)
        segments[-1].append((place.always, keep.start))
    for piece in range(pieces):
        start(place.upper, push(0, local, piece, place.me + INNER, own_ref))
        start(place.lower, push(1, local, piece, place.me - INNER, own_ref))
        start(place.always, push(2, local, piece, row_at, own_ref))
        start(place.always, push(3, local, piece, twin_at, own_ref))
    for step in range(1, place.outer + 1):
        segments.append([])
        if step < place.outer:
            for piece in range(pieces):
                for there, block, onward, target, kind in place.along(step):
                    arrive(there, block, piece)
                    start(there & onward, push(kind, block, piece, target))
                    start(there, push(2, block, piece, row_at))
                    start(there, push(3, block, piece, twin_at))
        for piece in range(pieces):
            for there, block, *_ in place.along(step - 1)[: 1 if step == 1 else 2]:
                arrive(there, block + place.row_step, piece)
                start(there, push(3, block + place.row_step, piece, twin_at))
    segments.append([])
    for step in range(place.outer):
        for piece in range(pieces):
            for there, block, *_ in place.along(step)[: 1 if step == 0 else 2]:
                arrive(there, block + place.twin_step, piece)
                arrive(there, block + place.twin_step + place.row_step, piece)
    if copy_sem is not None:
        segments[-1].append((place.always, keep.wait))
    return segments, sends


def emit(actions):
    for there, action in actions:
        @pl.when(there)
        def _():
            action()


def gather_steps(place, own_ref, out_ref, copy_sem, send_sem, recv_sem, sender):
    segments, sends = gather_plan(place, own_ref, out_ref, copy_sem, send_sem, recv_sem)
    sender.started += sends
    for actions in segments:
        emit(actions)
        yield


def add_into(target, first, *others):
    rows = target.shape[0]
    chunk = 32

    def body(index, _):
        at = pl.ds(pl.multiple_of(index * chunk, chunk), chunk)
        total = first[at, :].astype(jnp.float32)
        for other in others:
            total = total + other[at, :].astype(jnp.float32)
        target[at, :] = total.astype(target.dtype)
        return 0

    lax.fori_loop(0, rows // chunk, body, 0)


def reduce_steps(place, part_ref, out_ref, scratch, sender, fine=False):
    (own_buf, twin_buf, row_buf, line_buf, load_sem, twin_send, twin_recv, row_send, row_recv, line_send, line_recv,
     out_buf, out_sem) = scratch
    outer, local, level = place.outer, place.local, place.level
    pieces = part_ref.shape[1]
    inner = lax.rem(local, INNER)
    row_bit, core = inner // 2, lax.rem(inner, 2)
    twin_at, row_at = {"expert": place.me + place.twin_step}, {"expert": place.me + place.row_step}
    order = []
    low, high = 0, outer - 1
    while low <= high:
        order += [high] if low == high else [high, low]
        low, high = low + 1, high - 1
    units = [(at, piece) for at in order for piece in range(pieces)]
    bits = (1 - row_bit, row_bit)

    def loading(at, piece, bit):
        where = at * 2 + bit
        return pltpu.make_async_copy(
            part_ref.at[at * INNER + bit * 2 + core, piece], own_buf.at[where, piece], load_sem.at[where, piece]
        )

    def to_twin(at, piece, bit):
        where = at * 2 + bit
        return remote(
            part_ref.at[at * INNER + bit * 2 + 1 - core, piece],
            twin_buf.at[where, piece],
            twin_send.at[where, piece],
            twin_recv.at[where, piece],
            twin_at,
        )

    def to_row(at, piece):
        return remote(
            own_buf.at[at * 2 + bits[0], piece], row_buf.at[at, piece], row_send.at[at, piece], row_recv.at[at, piece], row_at
        )

    def mine(at, piece):
        return own_buf.at[at * 2 + row_bit, piece]

    def to_line(side, at, piece):
        return remote(
            mine(at, piece),
            line_buf.at[side, at, piece],
            line_send.at[side, at, piece],
            line_recv.at[side, at, piece],
            {"expert": place.me + (INNER if side == 0 else -INNER)},
        )

    for at, piece in units:
        for bit in bits:
            sender.start(place.always, to_twin(at, piece, bit))
            loading(at, piece, bit).start()
    yield
    for at, piece in units:
        for bit in bits:
            where = at * 2 + bit
            loading(at, piece, bit).wait()
            to_twin(at, piece, bit).wait_recv()
            add_into(own_buf.at[where, piece], own_buf.at[where, piece], twin_buf.at[where, piece])
            if bit is bits[0]:
                sender.start(place.always, to_row(at, piece))
        if fine:
            yield
    if not fine:
        yield
    for at, piece in units:
        to_row(at, piece).wait_recv()
        spot, row = mine(at, piece), row_buf.at[at, piece]
        for side, there, first in ((0, level < at, level == 0), (1, level > at, level == outer - 1)):
            line = to_line(side, at, piece)

            @pl.when(there & first)
            def _():
                add_into(spot, spot, row)

            @pl.when(there & ~first)
            def _():
                line.wait_recv()
                add_into(spot, spot, row, line_buf.at[side, at, piece])

            sender.start(there, line)
        if fine:
            yield
    if not fine:
        yield
    for at, piece in units:
        @pl.when(level == at)
        def _():
            parts = [mine(at, piece), row_buf.at[at, piece]]
            for side, there in ((0, at > 0), (1, at < outer - 1)):
                if there:
                    to_line(side, at, piece).wait_recv()
                    parts.append(line_buf.at[side, at, piece])
            add_into(out_buf.at[piece], *parts)
    done = pltpu.make_async_copy(out_buf, out_ref, out_sem)
    done.start()
    done.wait()
    yield


def reduce_scratch(group, pieces, rows, columns):
    outer = group // INNER
    bf = jnp.bfloat16
    pair, single, line = (2 * outer, pieces), (outer, pieces), (2, outer, pieces)
    block = (rows, columns)
    return [
        pltpu.VMEM(pair + block, bf),
        pltpu.VMEM(pair + block, bf),
        pltpu.VMEM(single + block, bf),
        pltpu.VMEM(line + block, bf),
        pltpu.SemaphoreType.DMA(pair),
        pltpu.SemaphoreType.DMA(pair),
        pltpu.SemaphoreType.DMA(pair),
        pltpu.SemaphoreType.DMA(single),
        pltpu.SemaphoreType.DMA(single),
        pltpu.SemaphoreType.DMA(line),
        pltpu.SemaphoreType.DMA(line),
        pltpu.VMEM((pieces,) + block, jnp.float32),
        pltpu.SemaphoreType.DMA(()),
    ]


class HeadRows:
    def __init__(self, started, received):
        self.started, self.received = started, received

    def wait(self):
        for there, local, copy, keep in self.started:
            @pl.when(there)
            def _():
                copy.wait_send()

            @pl.when(local)
            def _():
                keep.wait()
        for there, copy in self.received:
            @pl.when(there)
            def _():
                copy.wait_recv()


def head_rows(place, plane, shards, own_ref, out_ref, copy_sem, send_sem, recv_sem):
    count = own_ref.shape[0]
    number = place.shard * plane + place.me
    sequences = plane // place.group
    mine = place.shard * sequences + place.me // place.group
    started, received = [], []
    for index in range(count):
        target = place.local * count + index
        peer = {"shard": target // plane, "expert": lax.rem(target, plane)}
        copy = remote(own_ref.at[index], out_ref.at[mine], send_sem.at[index], recv_sem.at[mine], peer)
        keep = pltpu.make_async_copy(own_ref.at[index], out_ref.at[mine], copy_sem)

        @pl.when(target != number)
        def _():
            copy.start()

        @pl.when(target == number)
        def _():
            keep.start()

        started.append((target != number, target == number, copy, keep))
    for shard in range(shards):
        for sequence in range(sequences):
            source = shard * plane + sequence * place.group + number // count
            slot = shard * sequences + sequence
            peer = {"shard": source // plane, "expert": lax.rem(source, plane)}
            copy = remote(own_ref.at[0], out_ref.at[slot], send_sem.at[0], recv_sem.at[slot], peer)
            received.append((source != number, copy))
    return HeadRows(started, received), []


def bundle_kernel(group, shards, kinds, *refs):
    count = len(kinds)
    ins, outs, rest = refs[:count], refs[count : 2 * count], refs[2 * count :]
    place = Place(group)
    plane = lax.axis_size("expert")
    peers = []
    if "gather" in kinds or "reduce" in kinds:
        peers += place.neighbours()
    members = [{"expert": place.base + lax.rem(place.local + step, group)} for step in range(1, group)]
    if "trade" in kinds:
        peers = [(place.always, member) for member in members]
    across = [{"shard": lax.rem(place.shard + step, shards)} for step in range(1, shards)]
    if "swap" in kinds or "share" in kinds:
        peers += [(place.always, peer) for peer in across]
    everyone = []
    if "owners" in kinds or "rows" in kinds:
        total = shards * plane
        number = place.shard * plane + place.me
        for step in range(1, total):
            target = lax.rem(number + step, total)
            everyone.append((target, {"shard": target // plane, "expert": lax.rem(target, plane)}))
        peers = [(place.always, peer) for _, peer in everyone]
    greet(peers)
    sender = Sender()
    runs, waits = [], []
    for kind, own, out in zip(kinds, ins, outs):
        if kind == "gather":
            copy_sem, send_sem, recv_sem, *rest = rest
            runs.append(gather_steps(place, own, out, copy_sem, send_sem, recv_sem, sender))
        elif kind == "reduce":
            scratch, rest = rest[:13], rest[13:]
            runs.append(reduce_steps(place, own, out, scratch, sender))
        else:
            copy_sem, send_sem, recv_sem, *rest = rest
            if kind == "swap":
                mine, source = place.shard, lambda target: own
                targets = [(lax.rem(place.shard + step, shards), peer) for step, peer in enumerate(across, 1)]
            elif kind == "share":
                mine, source = place.shard, lambda target: own.at[target]
                targets = [(lax.rem(place.shard + step, shards), peer) for step, peer in enumerate(across, 1)]
            elif kind == "trade":
                mine, source = place.local, lambda target: own.at[target]
                targets = [(lax.rem(place.local + step, group), peer) for step, peer in enumerate(members, 1)]
            elif kind == "owners":
                mine, source = place.shard * plane + place.me, lambda target: own.at[target]
                targets = everyone
            else:
                waits.append(head_rows(place, plane, shards, own, out, copy_sem, send_sem, recv_sem))
                continue
            keep = None
            if kind != "share":
                keep = pltpu.make_async_copy(source(mine), out.at[mine], copy_sem)
                keep.start()
            total = len(targets) + 1
            copies = []
            for step, (target, peer) in enumerate(targets, 1):
                copy = remote(source(target), out.at[mine], send_sem.at[step], recv_sem.at[step], peer)
                copy.start()
                copies.append(copy)
            waits.append((keep, copies))
    while runs:
        runs = [run for run in runs if next(run, "end") != "end"]
    for keep, copies in waits:
        if keep is not None:
            keep.wait()
        for copy in copies:
            copy.wait()
    sender.finish()


def bundle(number, group, shards, transfers, limit=48 * 2**20):
    kinds, arrays, shapes, scratch = [], [], [], []
    members = shards * lax.axis_size("expert")
    for kind, array in transfers:
        kinds.append(kind)
        sems = [pltpu.SemaphoreType.DMA(())]
        if kind == "gather":
            pieces = PIECES if array.shape[0] % (16 * PIECES) == 0 else 1
            array = array.reshape((pieces, array.shape[0] // pieces) + array.shape[1:])
            shape = (group,) + array.shape
            sems += [pltpu.SemaphoreType.DMA((4, group, pieces)), pltpu.SemaphoreType.DMA((group, pieces))]
        elif kind == "reduce":
            pieces = 2 * PIECES
            array = array.reshape(group, pieces, array.shape[1] // pieces, array.shape[2])
            shape = array.shape[1:]
            sems = reduce_scratch(group, *shape)
        else:
            total = {"swap": shards, "share": shards, "trade": group, "owners": members}.get(kind)
            shape = ((total,) + array.shape) if kind == "swap" else array.shape
            if kind == "rows":
                total = max(array.shape[0], members // group)
                shape = (members // group,) + array.shape[1:]
            sems += [pltpu.SemaphoreType.DMA((total,)), pltpu.SemaphoreType.DMA((total,))]
        arrays.append(array)
        shapes.append(jax.ShapeDtypeStruct(shape, jnp.float32 if kind == "reduce" else array.dtype))
        scratch += sems
    outs = pl.pallas_call(
        functools.partial(bundle_kernel, group, shards, tuple(kinds)),
        out_shape=shapes,
        in_specs=[pl.BlockSpec(memory_space=pl.ANY)] * len(arrays),
        out_specs=[pl.BlockSpec(memory_space=pl.ANY)] * len(arrays),
        scratch_shapes=scratch,
        compiler_params=pltpu.CompilerParams(
            collective_id=number, has_side_effects=True, vmem_limit_bytes=limit
        ),
        name="bundle_" + "_".join(kinds[:2]),
    )(*arrays)
    done = []
    for (kind, array), out in zip(transfers, outs):
        if kind == "gather":
            out = out.reshape((group,) + array.shape)
        if kind == "reduce":
            out = out.reshape(array.shape[1:])
        done.append(out)
    return done


def pieces_of(size, most):
    return [(at, min(most, size - at)) for at in range(0, size, most)]


def expert_kernel(shards, *refs):
    (routes_ref, router_ref, rows_in, grads_in, shared_gate_own, shared_gate_got, shared_up_own, shared_up_got,
     shared_down_own, shared_down_got, gate_own, gate_got, up_own, up_got, narrow_own, query_piece,
     rows_ref, grad_ref, back_ref, out_ref, score_ref, hidden_ref, gate_back_ref, up_back_ref, shared_hidden_ref,
     shared_gate_back_ref, shared_up_back_ref, narrow_got, full_query,
     cotangent, hidden, gate_part, up_part, pick_all, gate_all, shared_hidden, shared_gate_back, shared_up_back,
     gate_w, up_w, down_w, shared_gate_w, shared_up_w, shared_down_w,
     weight_sem, save_sem, swap_send, swap_recv, piece_keep, piece_send, piece_recv) = refs
    low = jnp.bfloat16
    turn, step = pl.program_id(0), pl.program_id(1)
    steps = pl.num_programs(1)
    width, hidden_width = gate_w.shape
    own_width = width // shards
    senders, _, rows = routes_ref.shape
    slots, tokens = pick_all.shape[1:]
    capacity = slots // senders
    experts = router_ref.shape[0]
    plane = full_query.shape[1]
    place = Place(plane)
    me = place.me
    sender = Sender()
    others = [lax.rem(place.shard + other, shards) for other in range(1, shards)]

    def at_step(number, turn_at=0):
        return pl.when((turn == turn_at) & (step == number))

    arrivals = []
    for number, other in enumerate(others, 1):
        push = remote(narrow_own, narrow_got.at[place.shard], swap_send.at[number], swap_recv.at[place.shard], {"shard": other})
        arrivals.append(remote(narrow_own, narrow_got.at[other], swap_send.at[number], swap_recv.at[other], {"shard": other}))
        sender.started.append((place.always, push))
    pushes = [copy for _, copy in sender.started]
    plans = [
        gather_plan(
            place, query_piece.at[other], full_query.at[other], piece_keep.at[number], piece_send.at[number],
            piece_recv.at[number],
        )
        for number, other in enumerate(others)
    ]
    segments = [sum(parts, []) for parts in zip(*[plan[0] for plan in plans])]
    for plan in plans:
        sender.started += plan[1]

    def loading(source, target, index, number):
        return pltpu.make_async_copy(source, target, weight_sem.at[index, number])

    def loads_of(index, own, got, target):
        copies = []
        for number in range(shards):
            at = lax.rem(place.shard + number, shards)
            block = own.shape[0]
            spot = target.at[at] if len(target.shape) == 3 else target.at[pl.ds(pl.multiple_of(at * block, 16), block), :]
            copies.append(loading(own if number == 0 else got.at[at], spot, index, number))
        return copies

    early = (
        loads_of(0, shared_gate_own, shared_gate_got, shared_gate_w)
        + loads_of(1, shared_up_own, shared_up_got, shared_up_w)
        + loads_of(2, shared_down_own, shared_down_got, shared_down_w)
        + loads_of(3, gate_own, gate_got, gate_w)
        + loads_of(4, up_own, up_got, up_w)
    )
    late = loads_of(5, narrow_own, narrow_got, down_w)

    @at_step(0)
    def _():
        greet(place.neighbours() + [(place.always, {"shard": other}) for other in others])
        for push in pushes:
            push.start()
        for load in early:
            load.start()
        emit(segments[0])

    for number in range(1, len(segments)):

        @at_step(number if number < 4 else min(number - 4, 2), number // 4 and 1)
        def _():
            emit(segments[number])

    at_slots = pl.ds(pl.multiple_of(step * slots, slots), slots)
    at_tokens = pl.ds(pl.multiple_of(step * tokens, tokens), tokens)

    @pl.when(turn == 0)
    def _():
        logits = matmul_nt(router_ref[...], rows_in[...])
        names = lax.broadcasted_iota(jnp.int32, (experts, rows), 0)
        earlier = lax.broadcasted_iota(jnp.int32, (rows, rows), 0) <= lax.broadcasted_iota(jnp.int32, (rows, rows), 1)
        earlier = jnp.where(earlier, 1.0, 0.0).astype(low)
        slot_names = lax.broadcasted_iota(jnp.int32, (capacity, rows), 0).astype(jnp.float32)
        pick_buf, gate_buf = pick_all.at[step], gate_all.at[at_slots, :]
        pick_buf[...] = jnp.zeros(pick_buf.shape, low)
        for number in range(senders):
            routed = routes_ref[number]
            chosen = jnp.zeros((experts, rows), jnp.float32)
            for choice in range(TOP):
                chosen = chosen + jnp.where(routed[choice : choice + 1] == names, 1.0, 0.0)
            logit = jnp.where(chosen > 0.0, logits[:, number * rows : (number + 1) * rows], NEG)
            expo = jnp.exp(logit - jnp.max(logit, axis=0, keepdims=True)) * chosen
            dense = expo / jnp.sum(expo, axis=0, keepdims=True)
            gate_row = jnp.sum(jnp.where(names == me, dense, 0.0), axis=0, keepdims=True)
            mark = jnp.sum(jnp.where(routed == me, 1.0, 0.0), axis=0, keepdims=True)
            rank = matmul(jnp.broadcast_to(mark, (8, rows)).astype(low), earlier)[:1] - 1.0
            pick = jnp.where((slot_names == rank) & (mark > 0.0), 1.0, 0.0)
            at = slice(number * capacity, (number + 1) * capacity)
            pick_buf[at, number * rows : (number + 1) * rows] = pick.astype(low)
            gate_buf[at, :] = jnp.sum(pick * gate_row, axis=1, keepdims=True)
        gate = gate_buf[...]

        def pick_step(index, _):
            at = pl.ds(pl.multiple_of(index * 512, 512), 512)
            rows_ref[:, at] = matmul(pick_buf[...], rows_in[:, at]).astype(low)
            picked = matmul(pick_buf[...], grads_in[:, at])
            cotangent[at_slots, at] = picked.astype(low)
            grad_ref[:, at] = (gate * picked).astype(low)
            return 0

        lax.fori_loop(0, width // 512, pick_step, 0)

        @pl.when(step == 0)
        def _():
            for load in early:
                load.wait()

        shared_pre, shared_up = 0.0, 0.0
        for shard in range(shards):
            part = rows_in[:, shard * own_width : (shard + 1) * own_width]
            shared_pre = shared_pre + matmul(part, shared_gate_w[shard])
            shared_up = shared_up + matmul(part, shared_up_w[shard])
        swished, slope = swish_parts(shared_pre)
        shared_hidden[at_tokens, :] = (swished * shared_up).astype(low)
        shared_grad = matmul_nt(grads_in[...], shared_down_w[...])
        shared_gate_back[at_tokens, :] = (shared_grad * shared_up * slope).astype(low)
        shared_up_back[at_tokens, :] = (shared_grad * swished).astype(low)
        for at, size in pieces_of(hidden_width, 512):
            columns = slice(at, at + size)
            gate_pre = matmul(rows_ref[...], gate_w[:, columns])
            up_pre = matmul(rows_ref[...], up_w[:, columns])
            swished, slope = swish_parts(gate_pre)
            hidden[at_slots, columns] = (swished * up_pre).astype(low)
            gate_part[at_slots, columns] = (up_pre * slope).astype(low)
            up_part[at_slots, columns] = swished.astype(low)

    @at_step(0, 1)
    def _():
        for arrival in arrivals:
            arrival.wait_recv()
        for load in late:
            load.start()
        for load in late:
            load.wait()

    @pl.when(turn == 1)
    def _():
        gate = gate_all[at_slots, :]
        pick = pick_all[step]
        slot_grad = (gate * cotangent[at_slots, :].astype(jnp.float32)).astype(low)
        for at, size in pieces_of(hidden_width, 512):
            columns = slice(at, at + size)
            hidden_grad = matmul_nt(slot_grad, down_w[columns, :])
            gate_part[at_slots, columns] = (hidden_grad * gate_part[at_slots, columns].astype(jnp.float32)).astype(low)
            up_part[at_slots, columns] = (hidden_grad * up_part[at_slots, columns].astype(jnp.float32)).astype(low)

        def out_step(index, score):
            at = pl.ds(pl.multiple_of(index * 512, 512), 512)
            shard = index * 512 // own_width
            within = pl.ds(pl.multiple_of(index * 512 - shard * own_width, 512), 512)
            expert_out = matmul(hidden[at_slots, :], down_w[:, at]).astype(low).astype(jnp.float32)
            score = score + jnp.sum(expert_out * cotangent[at_slots, at].astype(jnp.float32), axis=1, keepdims=True)
            out = matmul_tn(pick, (gate * expert_out).astype(low))
            out_ref[:, at] = (out + matmul(shared_hidden[at_tokens, :], shared_down_w[:, at])).astype(low)
            row_back = matmul_nt(gate_part[at_slots, :], gate_w[at, :]) + matmul_nt(up_part[at_slots, :], up_w[at, :])
            back = (
                matmul_tn(pick, row_back.astype(low))
                + matmul_nt(shared_gate_back[at_tokens, :], shared_gate_w[shard, within, :])
                + matmul_nt(shared_up_back[at_tokens, :], shared_up_w[shard, within, :])
            )
            back_ref[:, at] = back.astype(low)
            return score

        score = lax.fori_loop(0, width // 512, out_step, jnp.zeros((slots, 1), jnp.float32))
        for number in range(senders):
            at = slice(number * capacity, (number + 1) * capacity)
            own_pick = pick[at, number * rows : (number + 1) * rows].astype(jnp.float32)
            total = jnp.sum(own_pick * score[at], axis=0, keepdims=True)
            score_ref[number] = jnp.broadcast_to(total, score_ref.shape[1:])

    @pl.when((turn == 1) & (step == steps - 1))
    def _():
        saves = [
            pltpu.make_async_copy(source, target, save_sem.at[index])
            for index, (source, target) in enumerate(
                (
                    (hidden, hidden_ref),
                    (gate_part, gate_back_ref),
                    (up_part, up_back_ref),
                    (shared_hidden, shared_hidden_ref),
                    (shared_gate_back, shared_gate_back_ref),
                    (shared_up_back, shared_up_back_ref),
                )
            )
        ]
        for save in saves:
            save.start()
        for save in saves:
            save.wait()
        sender.finish()


def expert_pass(routes, router, rows, grads, weights, query_piece, capacity):
    plane, _, local = routes.shape
    senders = STEP_SENDERS
    tokens, slots = senders * local, senders * capacity
    steps = plane // senders
    shards = weights[1].shape[0]
    width, hidden_width = rows.shape[1], weights[6].shape[1]
    units = weights[0].shape[1]
    low = jnp.bfloat16
    total = steps * slots
    shape, scratch, dma = jax.ShapeDtypeStruct, pltpu.VMEM, pltpu.SemaphoreType.DMA
    any_space = pl.BlockSpec(memory_space=pl.ANY)

    def first(r, c):
        return pl.BlockSpec((r, c), lambda turn, i: (i + turn * (steps - 1 - i), 0))

    def second(r, c):
        return pl.BlockSpec((r, c), lambda turn, i: (i * turn, 0))

    return pl.pallas_call(
        functools.partial(expert_kernel, shards),
        grid=(2, steps),
        out_shape=[
            shape((total, width), low),
            shape((total, width), low),
            shape((steps * tokens, width), low),
            shape((steps * tokens, width), low),
            shape((plane, 8, local), jnp.float32),
            shape((total, hidden_width), low),
            shape((total, hidden_width), low),
            shape((total, hidden_width), low),
            shape((steps * tokens, units), low),
            shape((steps * tokens, units), low),
            shape((steps * tokens, units), low),
            shape((shards,) + weights[10].shape, low),
            shape((shards, plane) + query_piece.shape[1:], low),
        ],
        in_specs=[
            pl.BlockSpec((senders, 8, local), lambda turn, i: (i + turn * (steps - 1 - i), 0, 0)),
            pl.BlockSpec(router.shape, lambda turn, i: (0, 0), pipeline_mode=pl.Buffered(1)),
            first(tokens, width),
            first(tokens, width),
        ]
        + [any_space] * (len(weights) + 1),
        out_specs=[
            first(slots, width),
            first(slots, width),
            second(tokens, width),
            second(tokens, width),
            pl.BlockSpec((senders, 8, local), lambda turn, i: (i * turn, 0, 0)),
        ]
        + [any_space] * 8,
        scratch_shapes=[
            scratch((total, width), low),
            scratch((total, hidden_width), low),
            scratch((total, hidden_width), low),
            scratch((total, hidden_width), low),
            scratch((steps, slots, tokens), low),
            scratch((total, 1), jnp.float32),
            scratch((steps * tokens, units), low),
            scratch((steps * tokens, units), low),
            scratch((steps * tokens, units), low),
            scratch((width, hidden_width), low),
            scratch((width, hidden_width), low),
            scratch((hidden_width, width), low),
            scratch((shards, width // shards, units), low),
            scratch((shards, width // shards, units), low),
            scratch((units, width), low),
            dma((6, shards)),
            dma((6,)),
            dma((shards,)),
            dma((shards,)),
            dma((shards,)),
            dma((shards, 4, plane, 1)),
            dma((shards, plane, 1)),
        ],
        compiler_params=pltpu.CompilerParams(
            vmem_limit_bytes=63 * 2**20,
            dimension_semantics=("arbitrary", "arbitrary"),
            collective_id=5,
            has_side_effects=True,
        ),
        name="experts",
    )(routes, router, rows, grads, *weights, query_piece)


QUERIES = 256
KEYS = WINDOW + QUERIES


def score_block(scale, query, keys, query_docs, key_docs):
    raw = matmul_nt(query, keys) * scale
    row = lax.broadcasted_iota(jnp.int32, raw.shape, 0) + WINDOW
    column = lax.broadcasted_iota(jnp.int32, raw.shape, 1)
    allowed = (query_docs == key_docs) & (column <= row) & (column > row - WINDOW)
    return jnp.where(allowed, raw, NEG)


class Swaps:
    def __init__(self, place, shards, sender):
        self.place, self.shards, self.sender = place, shards, sender

    def start(self, source, target, send_sem, recv_sem, keep=None):
        place, shards = self.place, self.shards
        arrivals = []
        for step in range(1, shards):
            other = lax.rem(place.shard + step, shards)
            self.sender.start(
                place.always,
                remote(source, target(place.shard), send_sem.at[step], recv_sem.at[place.shard], {"shard": other}),
            )
            arrivals.append(
                remote(source, target(other), send_sem.at[step], recv_sem.at[other], {"shard": other})
            )
        if keep is not None:
            copy = pltpu.make_async_copy(source, target(place.shard), keep)
            copy.start()

        def wait():
            for arrival in arrivals:
                arrival.wait_recv()
            if keep is not None:
                copy.wait()

        return wait


def whole_weight(place, others, own_ref, full_ref, buf, sem):
    copies = [pltpu.make_async_copy(own_ref, buf.at[place.shard], sem.at[0])]
    for step, other in enumerate(others, 1):
        copies.append(pltpu.make_async_copy(full_ref.at[other], buf.at[other], sem.at[step]))
    for copy in copies:
        copy.start()
    return copies


def drain(run):
    for _ in run:
        pass


def forward_kernel(shards, plane, scale, last, *refs):
    (tokens, cotangent, query_cols, down_half, up_half, out_half, query_half, gate_half, wide_half,
     shared_gate, shared_up, shared_down, routes, first_gain, latent_gain, second_gain, turn, sway, docs, row_docs,
     all_normed, all_grads, all_routes, full_down, full_out, query_piece, full_gate, full_up,
     full_shared_gate, full_shared_up, full_shared_down, normed_one,
     query, keys, value, key_latent, compressed, head_out, log_total, middle, up_buf,
     token_buf, normed_buf, query_buf, down_buf, out_buf, heads_buf, second_buf,
     swap_send, swap_recv, keep_sem, gather_send, gather_recv, gather_keep, piece_send, piece_recv,
     trade_send, trade_recv, load_sem, whole_sem) = refs
    low = jnp.bfloat16
    group = SEQ_DEVICES
    place, wide = Place(group), Place(plane)
    width = tokens.shape[-1]
    rows = docs.shape[0] // group
    sender = Sender()
    members = [lax.rem(place.local + step, group) for step in range(1, group)]
    peers = [(place.always, {"expert": place.base + member}) for member in members]
    if plane != group:
        peers += [
            (wide.upper & ~place.upper, {"expert": place.me + INNER}),
            (wide.lower & ~place.lower, {"expert": place.me - INNER}),
        ]
    others = [lax.rem(place.shard + step, shards) for step in range(1, shards)]
    peers += [(place.always, {"shard": other}) for other in others]
    greet(peers)

    swaps = Swaps(place, shards, sender)
    numbers = iter(range(16))

    def swap(source, target, keep=False):
        at = next(numbers)
        return swaps.start(
            source, target, swap_send.at[at], swap_recv.at[at], keep_sem.at[at] if keep else None
        )

    at_piece = lambda ref: ref.at[wide.me]
    got_query = swap(query_cols, lambda shard: query_buf.at[shard], True)
    got_down = swap(at_piece(down_half), lambda shard: full_down.at[shard, wide.me])
    got_up = swap(up_half, lambda shard: up_buf.at[shard], True)
    token_run = gather_steps(
        place, tokens, token_buf, gather_keep.at[0], gather_send.at[0], gather_recv.at[0], sender
    )
    next(token_run)
    got_out = swap(at_piece(out_half), lambda shard: full_out.at[shard, wide.me])
    waits = [swap(at_piece(query_half), lambda shard: query_piece.at[shard])]
    def piece_gathers(kind, full):
        return [
            gather_steps(
                wide, None, full.at[other], None, piece_send.at[kind, step], piece_recv.at[kind, step], sender
            )
            for step, other in enumerate(others)
        ]

    next(token_run)
    got_down()
    down_runs = piece_gathers(0, full_down)
    for run in down_runs:
        next(run)
    next(token_run)
    for run in down_runs:
        next(run)
    got_query()
    got_up()
    waits += [
        swap(gate_half, lambda shard: full_gate.at[shard]),
        swap(wide_half, lambda shard: full_up.at[shard]),
    ]
    drain(token_run)
    got_out()
    waits += [
        swap(shared_gate, lambda shard: full_shared_gate.at[shard]),
        swap(shared_up, lambda shard: full_shared_up.at[shard]),
        swap(shared_down, lambda shard: full_shared_down.at[shard]),
    ]
    for run in down_runs:
        drain(run)
    route_run = gather_steps(
        wide, routes, all_routes, gather_keep.at[1], gather_send.at[1], gather_recv.at[1], sender
    )
    next(route_run)
    out_runs = piece_gathers(1, full_out)
    for run in out_runs:
        next(run)
    for copy in whole_weight(place, others, down_half, full_down, down_buf, whole_sem.at[0]):
        copy.wait()

    keys[:WINDOW, :] = jnp.zeros((WINDOW, keys.shape[1]), low)
    value[:WINDOW, :] = jnp.zeros((WINDOW, value.shape[1]), low)
    tile = 2 * rows
    own_width = width // shards

    def whole_dot(at, weight_of):
        total = 0.0
        for shard in range(shards):
            total = total + matmul(normed_buf[at, shard * own_width : (shard + 1) * own_width], weight_of(shard))
        return total

    def front_tile(index, _):
        at = pl.ds(pl.multiple_of(index * tile, tile), tile)
        values = token_buf[pl.ds(index * 2, 2)].reshape(tile, width).astype(jnp.float32)
        root = lax.rsqrt(jnp.mean(values * values, axis=1, keepdims=True) + EPS)
        normed_buf[at, :] = (values * root * first_gain[...]).astype(low)
        first = whole_dot(at, lambda shard: query_buf[shard])
        latent = whole_dot(at, lambda shard: down_buf[shard].reshape(own_width, -1))
        turn_at, sway_at = turn[at, :QK_ROPE], sway[at, :QK_ROPE]
        end = QK_NOPE + QK_ROPE
        query[at, :QK_NOPE] = first[:, :QK_NOPE].astype(low)
        query[at, QK_NOPE:end] = (first[:, QK_NOPE:end] * turn_at + first[:, end:] * sway_at).astype(low)
        query[at, end:] = jnp.zeros((tile, QK_ROPE), low)
        end = KV_RANK + QK_ROPE
        key_rope = (latent[:, KV_RANK:end] * turn_at + latent[:, end:] * sway_at).astype(low)
        latent = latent[:, :KV_RANK]
        compressed[at, :] = latent
        root = lax.rsqrt(jnp.mean(latent * latent, axis=1, keepdims=True) + EPS)
        normed_latent = (latent * root * latent_gain[...]).astype(low)
        key_latent[at, :] = normed_latent
        up_rows = KV_RANK // shards
        both = 0.0
        for shard in range(shards):
            both = both + matmul(normed_latent[:, shard * up_rows : (shard + 1) * up_rows], up_buf[shard])
        both = both.astype(low)
        later = pl.ds(pl.multiple_of(index * tile + WINDOW, tile), tile)
        keys[later, :QK_NOPE] = both[:, :QK_NOPE]
        keys[later, QK_NOPE : QK_NOPE + QK_ROPE] = key_rope
        keys[later, QK_NOPE + QK_ROPE :] = key_rope
        value[later, :] = both[:, QK_NOPE:]
        return 0

    tiles = group // 2
    grad_run = gather_steps(
        wide, cotangent, all_grads, gather_keep.at[3], gather_send.at[3], gather_recv.at[3], sender
    )
    for part in range(2):
        lax.fori_loop(part * tiles // 2, (part + 1) * tiles // 2, front_tile, 0)
        for run in out_runs + [route_run]:
            next(run, None)
    next(grad_run)
    save = pltpu.make_async_copy(normed_buf, normed_one, load_sem.at[1])
    save.start()
    for run in out_runs + [route_run]:
        next(run, None)

    def attend_tile(index, _):
        at = pl.ds(pl.multiple_of(index * QUERIES, QUERIES), QUERIES)
        window = pl.ds(pl.multiple_of(index * QUERIES, QUERIES), KEYS)
        scores = score_block(scale, query[at, :], keys[window, :], docs[at, :], row_docs[:, window])
        top = jnp.max(scores, axis=1, keepdims=True)
        expo = jnp.exp(scores - top)
        total = jnp.sum(expo, axis=1, keepdims=True)
        probs = (expo / total).astype(low)
        real = jnp.where(docs[at, :] < last, 1.0, 0.0)
        head_out[at, :] = (matmul(probs, value[window, :]) * real).astype(low)
        log_total[at, :] = jnp.broadcast_to(top + jnp.log(total), (QUERIES, log_total.shape[1]))
        return 0

    blocks = docs.shape[0] // QUERIES
    lax.fori_loop(0, blocks // 2, attend_tile, 0)
    for run in out_runs + [route_run]:
        drain(run)
    load_out = whole_weight(place, others, out_half, full_out, out_buf, whole_sem.at[1])
    next(grad_run)
    lax.fori_loop(blocks // 2, blocks, attend_tile, 0)

    def head_at(member):
        return head_out.at[pl.ds(pl.multiple_of(member * rows, rows), rows), :]

    def lands(head):
        return heads_buf.at[:, pl.ds(pl.multiple_of(head * V_HEAD, V_HEAD), V_HEAD)]

    keep = pltpu.make_async_copy(head_at(place.local), lands(place.local), load_sem.at[2])
    keep.start()
    for step, member in enumerate(members):
        sender.start(
            place.always,
            remote(
                head_at(member), lands(place.local), trade_send.at[step], trade_recv.at[place.local],
                {"expert": place.base + member},
            ),
        )
    for step, member in enumerate(members):
        remote(
            head_at(member), lands(member), trade_send.at[step], trade_recv.at[member], {"expert": place.base + member}
        ).wait_recv()
    keep.wait()
    for copy in load_out:
        copy.wait()

    for at, size in pieces_of(width, 512):
        columns = slice(at, at + size)
        total = token_buf[place.local].reshape(rows, width)[:, columns].astype(jnp.float32)
        for shard in range(shards):
            weight = out_buf[shard, :, :, :, columns].reshape(own_width, size)
            total = total + matmul(heads_buf[:, shard * own_width : (shard + 1) * own_width], weight)
        middle[:, columns] = total
    values = middle[...]
    root = lax.rsqrt(jnp.mean(values * values, axis=1, keepdims=True) + EPS)
    second_buf[...] = (values * root * second_gain[...]).astype(low).reshape(second_buf.shape)

    normed_run = gather_steps(
        wide, second_buf, all_normed, gather_keep.at[2], gather_send.at[2], gather_recv.at[2], sender
    )
    runs = [normed_run, grad_run]
    while runs:
        runs = [run for run in runs if next(run, "end") != "end"]
    save.wait()
    for wait in waits:
        wait()
    sender.finish()


def forward_pass(scale, last, tokens, cotangent, blocks, routes, gains, tables):
    shards, plane = lax.axis_size("shard"), lax.axis_size("expert")
    local, width = tokens.shape
    low, shape = jnp.bfloat16, jax.ShapeDtypeStruct
    pieces = (PIECES, local // PIECES, width)
    any_space, vmem = pl.BlockSpec(memory_space=pl.ANY), pl.BlockSpec(memory_space=pltpu.VMEM)
    head_dim = QK_NOPE + QK_ROPE
    query_cols, down_half, up_half, out_half, query_half = blocks[:5]
    out_shape = [
        shape((plane,) + pieces, low),
        shape((plane,) + pieces, low),
        shape((plane, 1) + routes.shape, jnp.int32),
    ]
    stacked = [down_half.shape, out_half.shape, query_half.shape[1:]] + [block.shape for block in blocks[5:]]
    out_shape += [shape((shards,) + block, low) for block in stacked]
    out_shape += [
        shape((SEQ, width), low),
        shape((SEQ, head_dim + QK_ROPE), low),
        shape((SEQ + WINDOW, head_dim + QK_ROPE), low),
        shape((SEQ + WINDOW, V_HEAD), low),
        shape((SEQ, KV_RANK), low),
        shape((SEQ, KV_RANK), jnp.float32),
        shape((SEQ, V_HEAD), low),
        shape((SEQ, 128), jnp.float32),
        shape((local, width), jnp.float32),
        shape((shards,) + up_half.shape, low),
    ]
    hbm_out = 12
    dma = pltpu.SemaphoreType.DMA
    return pl.pallas_call(
        functools.partial(forward_kernel, shards, plane, scale, last),
        out_shape=out_shape,
        in_specs=[any_space] * (3 + len(blocks)) + [vmem] * (len(gains) + len(tables)),
        out_specs=[any_space] * hbm_out + [vmem] * (len(out_shape) - hbm_out),
        scratch_shapes=[
            pltpu.VMEM((SEQ_DEVICES,) + pieces, low),
            pltpu.VMEM((SEQ, width), low),
            pltpu.VMEM((shards,) + query_cols.shape, low),
            pltpu.VMEM((shards,) + down_half.shape, low),
            pltpu.VMEM((shards,) + out_half.shape, low),
            pltpu.VMEM((local, HEADS * V_HEAD), low),
            pltpu.VMEM(pieces, low),
            dma((12, shards)),
            dma((12, shards)),
            dma((12,)),
            dma((4, 4, plane, PIECES)),
            dma((4, plane, PIECES)),
            dma((4,)),
            dma((3, shards, 4, plane, 1)),
            dma((3, shards, plane, 1)),
            dma((SEQ_DEVICES,)),
            dma((SEQ_DEVICES,)),
            dma((4,)),
            dma((2, shards)),
        ],
        compiler_params=pltpu.CompilerParams(
            collective_id=1, has_side_effects=True, vmem_limit_bytes=60 * 2**20
        ),
        name="forward",
    )(tokens.reshape(pieces), cotangent.reshape(pieces), *blocks, routes[None], *gains, *tables)


def sums_kernel(shards, plane, *refs):
    (normed_part, output_part, token_scores, slot_rows, slot_grad, hidden, gate_back, up_back, all_normed, all_grads,
     shared_hidden, shared_gate_back, shared_up_back,
     back, output_sum, scores, down_got, down_own, gate_own, up_own, gate_send, up_send, narrow_own, narrow_send,
     shared_term,
     down_send, pair_buf, stream_buf, wide_buf, own_stage, send_stage, down_stage,
     load_sem, stream_sem, stage_sem, score_send, score_recv, swap_send, swap_recv, *reduces) = refs
    low = jnp.bfloat16
    place = Place(plane)
    sender = Sender()
    members = [lax.rem(place.me + step, plane) for step in range(1, plane)]
    others = [lax.rem(place.shard + step, shards) for step in range(1, shards)]
    greet([(place.always, {"expert": member}) for member in members] + [(place.always, {"shard": other}) for other in others])
    count = 13
    back_run = reduce_steps(place, normed_part, back, reduces[:count], sender, True)
    output_run = iter(())
    if len(reduces) > count:
        output_run = reduce_steps(place, output_part, output_sum, reduces[count:], sender, True)
    next(back_run)
    keep = pltpu.make_async_copy(token_scores.at[place.me], scores.at[place.me], load_sem.at[0])
    keep.start()

    def score_trade(step, member, source):
        return remote(token_scores.at[member], scores.at[source], score_send.at[step], score_recv.at[source],
                      {"expert": member})

    for step, member in enumerate(members):
        sender.start(place.always, score_trade(step, member, place.me))
    load_hidden = pltpu.make_async_copy(hidden, pair_buf.at[0], load_sem.at[1])
    load_hidden.start()
    load_up = pltpu.make_async_copy(up_back, pair_buf.at[1], load_sem.at[2])
    load_up.start()
    width = slot_rows.shape[1]
    tile = stream_buf.shape[-1]
    tiles = [slice(at, at + tile) for at in range(0, width, tile)]
    hidden_width = hidden.shape[1]
    own_hidden, own_width = hidden_width // shards, width // shards

    def streamed(source, buf, sem):
        copies = [
            pltpu.make_async_copy(source.at[:, columns], buf.at[index % 2], sem.at[index % 2])
            for index, columns in enumerate(tiles)
        ]
        copies[0].start()
        for index, copy in enumerate(copies):
            if index + 1 < len(copies):
                copies[index + 1].start()
            copy.wait()
            yield index, buf.at[index % 2]

    def down_chunks():
        load_hidden.wait()
        before = None
        for index, piece in streamed(slot_grad, stream_buf, stream_sem.at[0]):
            term = matmul_tn(pair_buf[0], piece[...])
            if before is not None:
                before.wait()
            for shard in range(shards):
                part = term[shard * own_hidden : (shard + 1) * own_hidden]

                @pl.when(place.shard == shard)
                def _():
                    down_stage[...] = part

                @pl.when(place.shard != shard)
                def _():
                    down_send[shard, :, tiles[index]] = part.astype(low)

            before = pltpu.make_async_copy(down_stage, down_own.at[:, tiles[index]], stage_sem.at[0])
            before.start()
            yield
        before.wait()
        for step, other in enumerate(others, 1):
            sender.start(
                place.always,
                remote(down_send.at[other], down_got.at[place.shard], swap_send.at[step], swap_recv.at[place.shard],
                       {"shard": other}),
            )

    def gate_chunks():
        load_gate = pltpu.make_async_copy(gate_back, pair_buf.at[0], load_sem.at[1])
        load_gate.start()
        load_gate.wait()
        load_up.wait()
        before = []
        for index, piece in streamed(slot_rows, stream_buf, stream_sem.at[0]):
            shard = index * tile // own_width
            within = pl.ds(index * tile - shard * own_width, tile)
            mine = place.shard == shard
            after = []
            for matrix, (own, send) in enumerate(((gate_own, gate_send), (up_own, up_send))):
                term = matmul_tn(piece[...], pair_buf[matrix])
                for there, copy in before[2 * matrix : 2 * matrix + 2]:
                    @pl.when(there)
                    def _():
                        copy.wait()

                to_own = pltpu.make_async_copy(own_stage.at[matrix], own.at[within], stage_sem.at[1 + matrix])
                to_send = pltpu.make_async_copy(send_stage.at[matrix], send.at[shard, within], stage_sem.at[3 + matrix])

                @pl.when(mine)
                def _():
                    own_stage[matrix] = term
                    to_own.start()

                @pl.when(~mine)
                def _():
                    send_stage[matrix] = term.astype(low)
                    to_send.start()

                after += [(mine, to_own), (~mine, to_send)]
                yield
            before = after
        for there, copy in before:
            @pl.when(there)
            def _():
                copy.wait()

    def shared_chunks():
        units = shared_hidden.shape[1]
        per = tile // shared_term.shape[1]
        for index, piece in streamed(all_normed, wide_buf, stream_sem.at[1]):
            both = [matmul_tn(piece[...], grads[...]).astype(low) for grads in (shared_gate_back, shared_up_back)]
            spot = slice(index * per, (index + 1) * per)
            shape = (per, shared_term.shape[1], units)
            shared_term[spot, :, :units] = both[0].reshape(shape)
            shared_term[spot, :, units:] = both[1].reshape(shape)
            yield
        own_units = units // shards
        for index, piece in streamed(all_grads, wide_buf, stream_sem.at[1]):
            term = matmul_tn(shared_hidden[...], piece[...])
            for shard in range(shards):
                part = term[shard * own_units : (shard + 1) * own_units]
                narrow_send[shard, :, tiles[index]] = part.astype(low)

                @pl.when(place.shard == shard)
                def _():
                    narrow_own[:, tiles[index]] = part

            yield

    def chunks():
        yield from down_chunks()
        yield from gate_chunks()
        yield from shared_chunks()

    work = chunks()
    units = plane // INNER * normed_part.shape[1]
    next(work)
    for _ in range(units):
        next(back_run)
    next(output_run, None)
    for index in range(8):
        next(work)
    for index in range(units):
        next(work, None)
        next(back_run)
    for index in range(units):
        next(work, None)
        next(output_run, None)
    drain(back_run)
    drain(work)
    drain(output_run)
    for step, member in enumerate(members):
        score_trade(step, member, member).wait_recv()
    keep.wait()
    for step, other in enumerate(others, 1):
        remote(down_send.at[other], down_got.at[other], swap_send.at[step], swap_recv.at[other], {"shard": other}).wait_recv()
    sender.finish()


def sums_pass(normed_part, output_part, token_scores, expert_terms, plane_terms, shared_terms):
    shards, plane = lax.axis_size("shard"), lax.axis_size("expert")
    low, shape = jnp.bfloat16, jax.ShapeDtypeStruct
    slot_rows, slot_grad, hidden, gate_back, up_back = expert_terms
    local, width = normed_part.shape[1:]
    slots, hidden_width = hidden.shape
    units = shared_terms[0].shape[1]
    count = 2 * PIECES
    pieces = (plane, count, local // count, width)
    own_width, own_hidden = width // shards, hidden_width // shards
    any_space, vmem = pl.BlockSpec(memory_space=pl.ANY), pl.BlockSpec(memory_space=pltpu.VMEM)
    reduces = 2 if plane == SEQ_DEVICES else 1
    out_shape = [
        shape(pieces[1:], jnp.float32),
        shape(pieces[1:], jnp.float32),
        shape(token_scores.shape, jnp.float32),
        shape((shards, own_hidden, width), low),
        shape((own_hidden, width), jnp.float32),
        shape((own_width, hidden_width), jnp.float32),
        shape((own_width, hidden_width), jnp.float32),
        shape((shards, own_width, hidden_width), low),
        shape((shards, own_width, hidden_width), low),
        shape((units // shards, width), jnp.float32),
        shape((shards, units // shards, width), low),
        shape((shards * plane, width // (shards * plane), 2 * units), low),
    ]
    dma, scratch = pltpu.SemaphoreType.DMA, pltpu.VMEM
    tile = 256
    outs = pl.pallas_call(
        functools.partial(sums_kernel, shards, plane),
        out_shape=out_shape,
        in_specs=[any_space] * 10 + [vmem] * 3,
        out_specs=[any_space] * 9 + [vmem] * 3,
        scratch_shapes=[
            scratch((shards, own_hidden, width), low),
            scratch((2, slots, hidden_width), low),
            scratch((2, slots, tile), low),
            scratch((2, plane * local, tile), low),
            scratch((2, tile, hidden_width), jnp.float32),
            scratch((2, tile, hidden_width), low),
            scratch((own_hidden, tile), jnp.float32),
            dma((3,)),
            dma((2, 2)),
            dma((5,)),
            dma((plane,)),
            dma((plane,)),
            dma((shards,)),
            dma((shards,)),
        ]
        + reduces * reduce_scratch(plane, count, local // count, width),
        compiler_params=pltpu.CompilerParams(
            collective_id=2, has_side_effects=True, vmem_limit_bytes=63 * 2**20
        ),
        name="sums",
    )(
        normed_part.reshape(pieces),
        output_part.reshape(pieces),
        token_scores,
        *expert_terms,
        *plane_terms,
        *shared_terms,
    )
    output_sum = outs[1].reshape(local, width)
    if reduces == 1:
        (output_sum,) = bundle(4, plane, shards, [("reduce", output_part)], 56 * 2**20)
    return (outs[0].reshape(local, width), output_sum) + tuple(outs[2:])


class Everyone:
    def __init__(self, place, plane, shards, source, got, send_sem, recv_sem, keep_sem):
        self.total = shards * plane
        self.plane = plane
        self.number = place.shard * plane + place.me
        self.source, self.got = source, got
        self.send_sem, self.recv_sem = send_sem, recv_sem
        self.keep = pltpu.make_async_copy(source(self.number), got.at[self.number], keep_sem)

    def copy(self, step, arriving):
        other = lax.rem(self.number + step, self.total)
        spot = other if arriving else self.number
        return remote(
            self.source(other),
            self.got.at[spot],
            self.send_sem.at[step],
            self.recv_sem.at[spot],
            {"shard": other // self.plane, "expert": lax.rem(other, self.plane)},
        )

    def start(self):
        self.keep.start()

        def body(step, _):
            self.copy(step, False).start()
            return 0

        lax.fori_loop(1, self.total, body, 0)

    def wait(self):
        self.keep.wait()

        def body(step, _):
            self.copy(step, True).wait_recv()
            return 0

        lax.fori_loop(1, self.total, body, 0)

    def finish(self):
        def body(step, _):
            self.copy(step, False).wait_send()
            return 0

        lax.fori_loop(1, self.total, body, 0)


def greet_everyone(place, plane, shards):
    barrier = pltpu.get_barrier_semaphore()
    total = shards * plane
    number = place.shard * plane + place.me

    def body(step, _):
        other = lax.rem(number + step, total)
        pl.semaphore_signal(
            barrier,
            inc=1,
            device_id={"shard": other // plane, "expert": lax.rem(other, plane)},
            device_id_type=MESH,
        )
        return 0

    lax.fori_loop(1, total, body, 0)
    pl.semaphore_wait(barrier, total - 1)


def norm_back(values, gain, grad):
    root = lax.rsqrt(jnp.mean(values * values, axis=1, keepdims=True) + EPS)
    weighted = grad * gain
    inner = jnp.mean(weighted * values, axis=1, keepdims=True)
    scaled = values * root
    return root * (weighted - scaled * (root * inner)), jnp.sum(grad * scaled, axis=0, keepdims=True)


def two_parts(values):
    high = values.astype(jnp.bfloat16)
    return high, (values - high.astype(jnp.float32)).astype(jnp.bfloat16)


def swapped_halves(pair):
    return pltpu.roll(pair, QK_ROPE // 2, 1)


def backward_kernel(shards, plane, scale, last, *refs):
    (back, scores, routes, middle, cotangent, tokens, first_gain, second_gain, latent_gain, router,
     query, keys, value, docs, row_docs, log_total, turn, sway, key_latent, up_head, head_out,
     compressed, full_out, full_query, full_down, normed_one, out_half, query_half, down_half, gate_send, up_send, narrow_send, shared_term,
     input_grad, query_out, up_out, down_out, out_out, small_out,
     gate_got, up_got, narrow_got, shared_got, mid_all,
     stream_buf, wq_buf, wd_buf, own_columns, own_compressed, heads_sum, mid_buf, low_buf, heads_buf, grad_buf, key_sum, value_sum,
     part_buf, trade_buf, trade_got, pair_buf, query_term, query_got, up_term, up_got_buf, own_query, low_grad, low_all,
     down_rows, down_got, out_rows, out_got, small_buf, small_got, key_got, *sems) = refs
    (load_sem, whole_sem, stream_sem, swap_send, swap_recv, trade_send, trade_recv, gather_send, gather_recv, gather_keep,
     all_send, all_recv, all_keep, rows_send, rows_recv, rows_keep, *reduce_scratch_refs) = sems
    low = jnp.bfloat16
    group = SEQ_DEVICES
    place = Place(group)
    local, width = middle.shape
    total = shards * plane
    sender = Sender()
    greet_everyone(place, plane, shards)
    members = [lax.rem(place.local + step, group) for step in range(1, group)]
    others = [lax.rem(place.shard + step, shards) for step in range(1, shards)]

    shares = []
    for number, (source, got) in enumerate(((gate_send, gate_got), (up_send, up_got), (narrow_send, narrow_got))):
        for step, other in enumerate(others, 1):
            sender.start(
                place.always,
                remote(source.at[other], got.at[place.shard], swap_send.at[number, step],
                       swap_recv.at[number, place.shard], {"shard": other}),
            )
            shares.append(
                remote(source.at[other], got.at[other], swap_send.at[number, step], swap_recv.at[number, other],
                       {"shard": other})
            )
    numbers = iter(range(16))

    def load(source, target):
        copy = pltpu.make_async_copy(source, target, load_sem.at[next(numbers)])
        copy.start()
        return copy

    own_lanes = pl.ds(pl.multiple_of(place.local * 128, 128), 128)
    got_wd = whole_weight(place, others, down_half, full_down, wd_buf, whole_sem)
    got_columns = load(normed_one.at[:, :, :, own_lanes], own_columns)
    tile = stream_buf.shape[-1]
    tiles = [slice(at, at + tile) for at in range(0, width, tile)]

    def streamed(buf, count, sources):
        def copies(index):
            half = index % 2
            return [
                (there, pltpu.make_async_copy(source, target, stream_sem.at[half, number]))
                for there, source, target, number in sources(index, buf.at[half])
            ]

        def start(index):
            for there, copy in copies(index):
                @pl.when(there)
                def _():
                    copy.start()

        start(0)
        for index in range(count):
            if index + 1 < count:
                start(index + 1)
            for there, copy in copies(index):
                @pl.when(there)
                def _():
                    copy.wait()
            yield index, buf.at[index % 2]

    own_at = pl.ds(pl.multiple_of(place.local * local, local), local)
    per_shard = group // shards

    def columns_of(array):
        def sources(index, target):
            return [
                (place.always, array.at[pl.ds(shard * per_shard, per_shard), :, :, tiles[index]], target.at[shard], shard)
                for shard in range(shards)
            ]

        return sources

    def out_columns(index, target):
        found = []
        for shard in range(shards):
            mine = place.shard == shard
            found.append((mine, out_half.at[:, :, :, tiles[index]], target.at[shard], shard))
            found.append((~mine, full_out.at[shard, :, :, :, tiles[index]], target.at[shard], shard))
        return found

    row_tile = wq_buf.shape[1]
    own_rows = width // shards

    def query_rows(index, target):
        shard = index * row_tile // own_rows
        rows = slice(index * row_tile - shard * own_rows, (index + 1) * row_tile - shard * own_rows)
        mine = place.shard == shard
        return [(mine, query_half.at[rows], target, 0), (~mine, full_query.at[shard, rows], target, 0)]

    got_compressed = load(compressed.at[own_at, :], own_compressed)

    def everyone(index, source, got):
        return Everyone(place, plane, shards, source, got, all_send.at[index], all_recv.at[index], all_keep.at[index])

    experts = router.shape[0]
    values = middle[...]
    root = lax.rsqrt(jnp.mean(values * values, axis=1, keepdims=True) + EPS)
    second_normed = (values * root * second_gain[...]).astype(low)
    logits = matmul_nt(router[...], second_normed)
    names = lax.broadcasted_iota(jnp.int32, (experts, local), 0)
    chosen = jnp.zeros((experts, local), jnp.float32)
    for choice in range(TOP):
        chosen = chosen + jnp.where(routes[choice : choice + 1, :] == names, 1.0, 0.0)
    logits = jnp.where(chosen > 0.0, logits, NEG)
    gates = jnp.exp(logits - jnp.max(logits, axis=0, keepdims=True)) * chosen
    gates = gates / jnp.sum(gates, axis=0, keepdims=True)
    gate_grad = jnp.concatenate([scores[index, :1, :] for index in range(experts)], axis=0)
    logit_grad = gates * (gate_grad - jnp.sum(gates * gate_grad, axis=0, keepdims=True))
    high, rest = two_parts(logit_grad)
    router_term = matmul(high, second_normed) + matmul(rest, second_normed)
    grad = back[...] + matmul_tn(high, router[...]) + matmul_tn(rest, router[...])
    row_grad, second_term = norm_back(values, second_gain[...], grad)
    mid_buf[...] = cotangent[...].astype(jnp.float32) + row_grad
    low_buf[...] = mid_buf[...].astype(low).reshape(low_buf.shape)

    for index, piece in streamed(stream_buf, len(tiles), out_columns):
        part = matmul_nt(low_buf[:, :, tiles[index]].reshape(local, tile), piece[...].reshape(-1, tile))
        heads_sum[...] = part if index == 0 else heads_sum[...] + part
    heads_buf[...] = heads_sum[...].astype(low)

    def lands(member):
        return heads_buf.at[:, pl.ds(pl.multiple_of(member * V_HEAD, V_HEAD), V_HEAD)]

    def head_trade(step, member, source):
        spot = pl.ds(pl.multiple_of(source * local, local), local)
        return remote(lands(member), grad_buf.at[spot, :], trade_send.at[0, step], trade_recv.at[0, source],
                      {"expert": place.base + member})

    keep_head = pltpu.make_async_copy(lands(place.local), grad_buf.at[own_at, :], load_sem.at[next(numbers)])
    keep_head.start()
    for step, member in enumerate(members):
        sender.start(place.always, head_trade(step, member, place.local))
    mid_run = gather_steps(place, low_buf, mid_all, gather_keep.at[0], gather_send.at[0], gather_recv.at[0], sender)
    for step, member in enumerate(members):
        head_trade(step, member, member).wait_recv()
    keep_head.wait()
    next(mid_run)
    shared_trade = everyone(0, lambda target: shared_term.at[target], shared_got)
    shared_trade.start()

    key_sum[...] = jnp.zeros_like(key_sum)
    value_sum[...] = jnp.zeros_like(value_sum)

    def attend_tile(index, _):
        at = pl.ds(pl.multiple_of(index * QUERIES, QUERIES), QUERIES)
        window = pl.ds(pl.multiple_of(index * QUERIES, QUERIES), KEYS)
        tile, key_tile = query[at, :], keys[window, :]
        head_grad = jnp.where(docs[at, :] < last, grad_buf[at, :], jnp.zeros((), low))
        scores_at = score_block(scale, tile, key_tile, docs[at, :], row_docs[:, window])
        probs = jnp.exp(scores_at - log_total[at, :1])
        prob_grad = matmul_nt(head_grad, value[window, :])
        inner = jnp.sum(probs * prob_grad, axis=1, keepdims=True)
        raw_grad = (probs * (prob_grad - inner) * scale).astype(low)
        grads = matmul(raw_grad, key_tile)
        trade_buf[at, :QK_NOPE] = grads[:, :QK_NOPE].astype(low)
        pair = grads[:, QK_NOPE:]
        trade_buf[at, QK_NOPE:] = (pair * turn[at, :] - swapped_halves(pair) * sway[at, :]).astype(low)
        key_sum[window, :] += matmul_tn(raw_grad, tile)
        value_sum[window, :] += matmul_tn(probs.astype(low), head_grad)
        return 0

    blocks = docs.shape[0] // QUERIES
    for index in range(blocks // 2):
        attend_tile(jnp.int32(index), 0)
    next(mid_run)
    for index in range(blocks // 2, blocks):
        attend_tile(jnp.int32(index), 0)
    next(mid_run)

    lane = lax.broadcasted_iota(jnp.int32, (QUERIES, 2 * QK_ROPE), 1)

    def key_tile(index, _):
        at = pl.ds(pl.multiple_of(index * QUERIES, QUERIES), QUERIES)
        later = pl.ds(pl.multiple_of(index * QUERIES + WINDOW, QUERIES), QUERIES)
        key_rope = pltpu.roll(key_sum[later, QK_NOPE:], QK_ROPE, 1).astype(low)
        trade_buf[at, QK_NOPE:] = jnp.where(lane < QK_ROPE, trade_buf[at, QK_NOPE:], key_rope)
        pair_buf[at, :QK_NOPE] = key_sum[later, :QK_NOPE].astype(low)
        pair_buf[at, QK_NOPE:] = value_sum[later, :].astype(low)
        part = matmul_nt(pair_buf[at, :], up_head[...]).astype(low)
        per = QUERIES // local
        part_buf[pl.ds(index * per, per)] = part.reshape((per,) + part_buf.shape[1:])
        return 0

    for index in range(blocks):
        key_tile(jnp.int32(index), 0)

    def token_trade(step, member, source):
        spot = pl.ds(pl.multiple_of(member * local, local), local)
        return remote(trade_buf.at[spot, :], trade_got.at[source], trade_send.at[1, step], trade_recv.at[1, source],
                      {"expert": place.base + member})

    reduce_run = reduce_steps(place, part_buf, key_got, reduce_scratch_refs, sender)
    next(reduce_run)
    keep_token = pltpu.make_async_copy(trade_buf.at[own_at, :], trade_got.at[place.local], load_sem.at[next(numbers)])
    keep_token.start()
    for step, member in enumerate(members):
        sender.start(place.always, token_trade(step, member, place.local))

    for index, piece in streamed(stream_buf, len(tiles), columns_of(normed_one)):
        term = matmul_tn(trade_buf[...], piece[...].reshape(SEQ, tile))
        per = tile // query_term.shape[1]
        query_term[index * per : (index + 1) * per] = term.T.astype(low).reshape((per,) + query_term.shape[1:])
    up_term[...] = matmul_tn(key_latent[...], pair_buf[...]).astype(low).reshape(up_term.shape)
    next(reduce_run)
    query_trade = everyone(1, lambda target: query_term.at[target], query_got)
    query_trade.start()
    up_trade = everyone(2, lambda target: up_term.at[target], up_got_buf)
    up_trade.start()
    next(reduce_run)
    drain(reduce_run)
    for step, member in enumerate(members):
        token_trade(step, member, member).wait_recv()
    keep_token.wait()

    got_compressed.wait()
    head_dim = QK_NOPE + QK_ROPE
    rope = jnp.zeros((local, 2 * QK_ROPE), jnp.float32)
    for head in range(group):
        own_query[:, head * head_dim : (head + 1) * head_dim] = trade_got[head, :, :head_dim]
        rope = rope + trade_got[head, :, QK_NOPE:].astype(jnp.float32)
    lane = lax.broadcasted_iota(jnp.int32, rope.shape, 1)
    rope = jnp.where(lane < QK_ROPE, pltpu.roll(rope, QK_ROPE, 1), rope)
    rope = rope * turn[own_at, :] - swapped_halves(rope) * sway[own_at, :]
    latent_grad, latent_term = norm_back(own_compressed[...], latent_gain[...], key_got[...].reshape(local, KV_RANK))
    low_grad[0, 0, :, :KV_RANK] = latent_grad.astype(low)
    low_grad[0, 0, :, KV_RANK:] = jnp.where(lane < QK_ROPE, rope, 0.0).astype(low)
    low_run = gather_steps(place, low_grad.at[0], low_all, gather_keep.at[1], gather_send.at[1], gather_recv.at[1], sender)
    next(low_run)
    for copy in got_wd:
        copy.wait()
    for index, piece in streamed(wq_buf, width // row_tile, query_rows):
        rows = slice(index * row_tile, (index + 1) * row_tile)
        shard = index * row_tile // own_rows
        within = slice(rows.start - shard * own_rows, rows.stop - shard * own_rows)
        term = matmul_nt(own_query[...], piece[...])
        input_grad[:, rows] = term + matmul_nt(low_grad[0, 0], wd_buf[shard, within, :])
    next(low_run)
    row_grad, first_term = norm_back(tokens[...].astype(jnp.float32), first_gain[...], input_grad[...])
    input_grad[...] = mid_buf[...] + row_grad
    next(low_run)
    drain(mid_run)
    per_lane = width // 128
    for block in range(per_lane):
        columns = slice(block * 128, (block + 1) * 128)
        small_buf[block, :experts, :] = router_term[:, columns]
        small_buf[block, experts : experts + 1, :] = second_term[:, columns]
        small_buf[block, experts + 1 : experts + 2, :] = first_term[:, columns]
        at = block // (per_lane * 128 // KV_RANK) * 128
        small_buf[block, experts + 2 : experts + 3, :] = latent_term[:, at : at + 128]
        small_buf[block, experts + 3 :, :] = jnp.zeros((small_buf.shape[1] - experts - 3, 128), jnp.float32)
    small_trade = everyone(3, lambda target: small_buf.at[target // (total // per_lane)], small_got)
    small_trade.start()
    drain(low_run)
    got_columns.wait()
    down = matmul_tn(own_columns[...].reshape(SEQ, -1), low_all[...].reshape(SEQ, -1))
    down_rows[...] = down.astype(low).reshape(down_rows.shape)
    down_trade = head_rows(place, plane, shards, down_rows, down_got, rows_keep.at[0], rows_send.at[0], rows_recv.at[0])[0]
    for index, piece in streamed(stream_buf, len(tiles), columns_of(mid_all)):
        term = matmul_tn(head_out[...], piece[...].reshape(SEQ, tile)).astype(low)
        out_rows[:, :, tiles[index]] = term.reshape(out_rows.shape[:2] + (tile,))
    out_trade = head_rows(place, plane, shards, out_rows, out_got, rows_keep.at[1], rows_send.at[1], rows_recv.at[1])[0]

    sequences = total // group
    query_trade.wait()
    up_trade.wait()
    for head in range(group):
        query_sum, up_sum = 0.0, 0.0
        for sequence in range(sequences):
            query_sum = query_sum + query_got[sequence * group + head].astype(jnp.float32)
            up_sum = up_sum + up_got_buf[sequence * group + head].astype(jnp.float32)
        query_out[:, head * head_dim : (head + 1) * head_dim] = query_sum[:, :head_dim]
        both = QK_NOPE + V_HEAD
        up_out[:, head * both : (head + 1) * both] = up_sum
    small_trade.wait()
    small_out[...] = small_got[0]

    def small_sum(source, _):
        small_out[...] += small_got[source]
        return 0

    lax.fori_loop(1, total, small_sum, 0)
    down_trade.wait()
    out_trade.wait()
    down_sum, out_sum = 0.0, 0.0
    for sequence in range(sequences):
        down_sum = down_sum + down_got[sequence].astype(jnp.float32)
        out_sum = out_sum + out_got[sequence].astype(jnp.float32)
    down_out[...] = down_sum[:, : down_out.shape[1]]
    out_out[...] = out_sum
    shared_trade.wait()
    for share in shares:
        share.wait_recv()
    for trade in (shared_trade, query_trade, up_trade, small_trade):
        trade.finish()
    sender.finish()


def backward_pass(scale, last, small, tables, saved, weights, sends):
    shards, plane = lax.axis_size("shard"), lax.axis_size("expert")
    total = shards * plane
    low, shape = jnp.bfloat16, jax.ShapeDtypeStruct
    local, width = small[3].shape
    head_dim = QK_NOPE + QK_ROPE
    vmem, any_space = pl.BlockSpec(memory_space=pltpu.VMEM), pl.BlockSpec(memory_space=pl.ANY)
    inputs = list(small) + list(tables) + list(saved)
    hbm = list(weights) + list(sends)
    gate_send, up_send, narrow_send, shared_term = sends
    experts = small[9].shape[0]
    small_rows = experts + 3 + -(experts + 3) % 8
    own_width = width // total
    out_shape = [
        shape((local, width), jnp.float32),
        shape((own_width, HEADS * head_dim), jnp.float32),
        shape((KV_RANK // total, HEADS * (QK_NOPE + V_HEAD)), jnp.float32),
        shape((own_width, KV_RANK + QK_ROPE), jnp.float32),
        shape((own_width, width), jnp.float32),
        shape((small_rows, 128), jnp.float32),
        shape(gate_send.shape, low),
        shape(up_send.shape, low),
        shape(narrow_send.shape, low),
        shape(shared_term.shape, low),
        shape((SEQ_DEVICES, PIECES, local // PIECES, width), low),
    ]
    hbm_out = 5
    dma, scratch = pltpu.SemaphoreType.DMA, pltpu.VMEM
    pieces = (PIECES, local // PIECES)
    down_width = weights[3].shape[2]
    row_count = 128 // own_width
    sequences = total // SEQ_DEVICES
    wide_head = 2 * QK_NOPE
    return pl.pallas_call(
        functools.partial(backward_kernel, shards, plane, scale, last),
        out_shape=out_shape,
        in_specs=[vmem] * len(inputs) + [any_space] * len(hbm),
        out_specs=[vmem] * (len(out_shape) - hbm_out) + [any_space] * hbm_out,
        scratch_shapes=[
            scratch((2, shards, SEQ_DEVICES // shards) + pieces + (512,), low),
            scratch((2, 256, HEADS * head_dim), low),
            scratch((shards, width // shards, down_width), low),
            scratch((SEQ_DEVICES,) + pieces + (128,), low),
            scratch((local, KV_RANK), jnp.float32),
            scratch((local, width), jnp.float32),
            scratch((local, width), jnp.float32),
            scratch(pieces + (width,), low),
            scratch((local, width), low),
            scratch((SEQ, V_HEAD), low),
            scratch((SEQ + WINDOW, wide_head), jnp.float32),
            scratch((SEQ + WINDOW, V_HEAD), jnp.float32),
            scratch((SEQ_DEVICES,) + pieces + (KV_RANK,), low),
            scratch((SEQ, wide_head), low),
            scratch((SEQ_DEVICES, local, wide_head), low),
            scratch((SEQ, wide_head), low),
            scratch((total, own_width, wide_head), low),
            scratch((total, own_width, wide_head), low),
            scratch((total, KV_RANK // total, wide_head), low),
            scratch((total, KV_RANK // total, wide_head), low),
            scratch((local, HEADS * head_dim), low),
            scratch((1, 1, local, down_width), low),
            scratch((SEQ_DEVICES, 1, local, down_width), low),
            scratch((row_count, own_width, down_width), low),
            scratch((sequences, own_width, down_width), low),
            scratch((row_count, own_width, width), low),
            scratch((sequences, own_width, width), low),
            scratch((width // 128, small_rows, 128), jnp.float32),
            scratch((total, small_rows, 128), jnp.float32),
            scratch(pieces + (KV_RANK,), jnp.float32),
            dma((8,)),
            dma((shards,)),
            dma((2, shards)),
            dma((3, shards)),
            dma((3, shards)),
            dma((2, SEQ_DEVICES)),
            dma((2, SEQ_DEVICES)),
            dma((2, 4, SEQ_DEVICES, PIECES)),
            dma((2, SEQ_DEVICES, PIECES)),
            dma((2,)),
            dma((4, total)),
            dma((4, total)),
            dma((4,)),
            dma((2, max(row_count, sequences))),
            dma((2, max(row_count, sequences))),
            dma((2,)),
        ]
        + reduce_scratch(SEQ_DEVICES, PIECES, local // PIECES, KV_RANK),
        compiler_params=pltpu.CompilerParams(
            collective_id=3, has_side_effects=True, vmem_limit_bytes=62 * 2**20
        ),
        name="backward",
    )(*inputs, *hbm)


def on_device(
    tokens,
    document_lengths,
    routes,
    first_gain,
    query_weight,
    latent_down,
    latent_gain,
    latent_up,
    output_weight,
    second_gain,
    router_weight,
    shared_gate,
    shared_up,
    shared_down,
    expert_gate,
    expert_up,
    expert_down,
    cotangent,
):
    local_rows, width = tokens.shape
    shards = lax.axis_size("shard")
    plane = lax.axis_size("expert")
    everyone = ("shard", "expert")
    all_devices = shards * plane
    shard_at = lax.axis_index("shard")
    plane_at = lax.axis_index("expert")
    head_at = plane_at % SEQ_DEVICES
    sequence_at = (shard_at * plane + plane_at) // SEQ_DEVICES
    capacity = local_rows * TOP * 4 // (3 * plane)
    head_dim = QK_NOPE + QK_ROPE
    scale = 1.0 / math.sqrt(head_dim)
    own_at = head_at * local_rows

    def own_rows(values):
        return lax.dynamic_slice_in_dim(values, own_at, local_rows, 0)

    piece_rows = output_weight.shape[0] // plane
    half = QK_ROPE // 2
    query_columns = lax.dynamic_slice_in_dim(query_weight, head_at * head_dim, head_dim, 1)
    query_turn, key_turn = query_columns[:, QK_NOPE:], latent_down[:, KV_RANK:]
    query_cols = jnp.concatenate(
        [query_columns, query_turn[:, half:], query_turn[:, :half]], axis=1
    )
    down_half = jnp.concatenate(
        [latent_down, key_turn[:, half:], key_turn[:, :half]], axis=1
    )
    units = shared_down.shape[0] // plane
    unit_pad = -units % 16
    padded_units = units + unit_pad
    gate_columns, up_columns = (
        jnp.concatenate(
            [
                jnp.pad(
                    lax.dynamic_slice_in_dim(
                        weight, index * shared_down.shape[0] + plane_at * units, units, 1
                    ),
                    ((0, 0), (0, unit_pad)),
                )
                for index in range(shards)
            ],
            axis=1,
        )
        for weight in (shared_gate, shared_up)
    )
    down_units = lax.dynamic_slice_in_dim(shared_down, plane_at * units, units, 0)
    down_units = jnp.pad(down_units, ((0, unit_pad), (0, 0)))

    def plane_pieces(weight):
        return weight.reshape(plane, 1, -1, weight.shape[1])

    positions = jnp.arange(SEQ, dtype=jnp.int32)
    cosine_part, sine_part = rotary_tables(positions, QK_ROPE)
    sequence_count, entry_count = document_lengths.shape
    ends = jnp.cumsum(document_lengths, axis=1)
    picked = jnp.arange(sequence_count, dtype=jnp.int32)[:, None] == sequence_at
    row_ends = jnp.sum(jnp.where(picked, ends, 0), axis=0)
    documents = jnp.sum((positions[:, None] >= row_ends[None, :]).astype(jnp.int32), axis=1)
    turn = jnp.tile(cosine_part, (1, 4))
    sway = jnp.tile(jnp.concatenate([-sine_part, sine_part], axis=1), (1, 2))
    docs = documents[:, None]
    row_docs = jnp.pad(docs, ((WINDOW, 0), (0, 0)), constant_values=-1).T
    route_rows = jnp.pad(routes.T, ((0, 8 - TOP), (0, 0)), constant_values=-1)
    (
        all_normed,
        all_grads,
        all_routes,
        full_down,
        full_out,
        query_piece,
        gate_single,
        up_single,
        gate_shared,
        up_shared,
        down_shared,
        normed_one,
        query,
        keys,
        value,
        key_latent,
        compressed,
        head_out,
        log_total,
        middle,
        up_head,
    ) = forward_pass(
        scale,
        entry_count - 1,
        tokens,
        cotangent,
        (
            query_cols,
            plane_pieces(down_half),
            lax.dynamic_slice_in_dim(
                latent_up, head_at * (QK_NOPE + V_HEAD), QK_NOPE + V_HEAD, 1
            ),
            plane_pieces(output_weight),
            plane_pieces(query_weight),
            expert_gate[0],
            expert_up[0],
            gate_columns,
            up_columns,
            down_units,
        ),
        route_rows,
        (first_gain[None], latent_gain[None], second_gain[None]),
        (turn, sway, docs, row_docs),
    )
    all_normed = all_normed.reshape(-1, width)
    all_grads = all_grads.reshape(-1, width)
    blocked = (SEQ_DEVICES, PIECES, local_rows // PIECES, width)
    shard_blocked = (shards, SEQ_DEVICES // shards) + blocked[1:]
    (
        slot_rows,
        slot_grad,
        normed_part,
        output_part,
        token_scores,
        hidden,
        gate_pre_grad,
        up_pre_grad,
        shared_hidden,
        shared_gate_back,
        shared_up_back,
        _,
        full_query,
    ) = expert_pass(
        all_routes[:, 0],
        router_weight.T,
        all_normed,
        all_grads,
        (
            gate_columns,
            gate_shared,
            up_columns,
            up_shared,
            down_units,
            down_shared,
            expert_gate[0],
            gate_single,
            expert_up[0],
            up_single,
            expert_down[0],
        ),
        query_piece,
        capacity,
    )
    (
        back,
        output_sum,
        scores,
        down_blocks,
        down_own,
        gate_own,
        up_own,
        gate_send,
        up_send,
        shared_down_own,
        shared_down_send,
        shared_term,
    ) = sums_pass(
        normed_part.reshape(plane, local_rows, width),
        output_part.reshape(plane, local_rows, width),
        token_scores,
        (slot_rows, slot_grad, hidden, gate_pre_grad, up_pre_grad),
        (all_normed, all_grads),
        (shared_hidden, shared_gate_back, shared_up_back),
    )
    activations = (middle + output_sum).astype(jnp.bfloat16)

    def sum_shards(own, blocks):
        for step in range(1, shards):
            own = own + lax.dynamic_index_in_dim(
                blocks, (shard_at + step) % shards, 0, keepdims=False
            ).astype(jnp.float32)
        return own

    (
        input_grad,
        query_weight_grad,
        latent_up_grad,
        latent_down_grad,
        output_weight_grad,
        small_sums,
        gate_blocks,
        up_blocks,
        shared_blocks,
        shared_moved,
        _,
    ) = backward_pass(
        scale,
        entry_count - 1,
        (
            back,
            scores,
            route_rows,
            middle,
            cotangent,
            tokens,
            first_gain[None],
            second_gain[None],
            latent_gain[None],
            router_weight.T,
        ),
        (query, keys, value, docs, row_docs, log_total, turn, sway),
        (key_latent, up_head.reshape(KV_RANK, -1), head_out),
        (
            compressed,
            full_out.reshape(shard_blocked),
            full_query.reshape((shards,) + query_weight.shape),
            full_down.reshape((shards,) + down_half.shape),
            normed_one.reshape(blocked),
            output_weight.reshape(shard_blocked[1:]),
            query_weight,
            down_half,
        ),
        (gate_send, up_send, shared_down_send, shared_term),
    )
    expert_gate_grad = sum_shards(gate_own, gate_blocks)[None]
    expert_up_grad = sum_shards(up_own, up_blocks)[None]
    expert_down_grad = sum_shards(down_own, down_blocks)[None]
    shared_down_grad = sum_shards(shared_down_own, shared_blocks)[:units]
    shared_moved = shared_moved.astype(jnp.float32).reshape(shards, plane, -1, 2, shards, padded_units)
    shared_moved = jnp.sum(shared_moved, axis=0)[..., :units].transpose(2, 1, 3, 0, 4)
    shared_moved = shared_moved.reshape(2, shared_moved.shape[1], -1)
    shared_gate_grad = shared_moved[0]
    shared_up_grad = shared_moved[1]
    own_width = width // all_devices
    number = shard_at * plane + plane_at
    own_small = lax.dynamic_slice_in_dim(small_sums, number * own_width % 128, own_width, 1)
    router_weight_grad = own_small[:plane].T
    second_gain_grad = own_small[plane]
    first_gain_grad = own_small[plane + 1]
    latent_width = KV_RANK // all_devices
    latent_gain_grad = lax.dynamic_slice_in_dim(
        small_sums[plane + 2], number * latent_width % 128, latent_width, 0
    )
    return (
        activations,
        input_grad,
        first_gain_grad,
        query_weight_grad,
        latent_down_grad,
        latent_gain_grad,
        latent_up_grad,
        output_weight_grad,
        second_gain_grad,
        router_weight_grad,
        shared_gate_grad,
        shared_up_grad,
        shared_down_grad,
        expert_gate_grad,
        expert_up_grad,
        expert_down_grad,
    )


def solution(mesh):
    return jax.shard_map(
        on_device,
        mesh=mesh,
        in_specs=(
            P(("shard", "expert"), None),
            P(),
            P(("shard", "expert"), None),
            P(),
            P("shard", None),
            P("shard", None),
            P(),
            P("shard", None),
            P("shard", None),
            P(),
            P(),
            P("shard", None),
            P("shard", None),
            P("shard", None),
            P("expert", "shard", None),
            P("expert", "shard", None),
            P("expert", "shard", None),
            P(("shard", "expert"), None),
        ),
        out_specs=(
            P(("shard", "expert"), None),
            P(("shard", "expert"), None),
            P(("shard", "expert")),
            P(("shard", "expert"), None),
            P(("shard", "expert"), None),
            P(("shard", "expert")),
            P(("shard", "expert"), None),
            P(("shard", "expert"), None),
            P(("shard", "expert")),
            P(("shard", "expert"), None),
            P(("shard", "expert"), None),
            P(("shard", "expert"), None),
            P(("shard", "expert"), None),
            P("expert", "shard", None),
            P("expert", "shard", None),
            P("expert", "shard", None),
        ),
        check_vma=False,
    )
```

```python
import functools
import math

import jax
import jax.numpy as jnp
import numpy as np
from jax import lax
from jax.experimental import pallas as pl
from jax.experimental.pallas import tpu as pltpu
from jax.sharding import PartitionSpec as P

HEADS = 16
QK_NOPE = 128
QK_ROPE = 64
V_HEAD = 128
KV_RANK = 512
TOP = 6
SEQ = 2048
WINDOW = 1024
TOK_DEV = 128
STEP_SENDERS = 4
SEQ_DEVICES = SEQ // TOK_DEV


EPS = 1e-06
THETA = 10000.0
NEG = -1e30
HIGH = lax.Precision.HIGHEST


def matmul(left, right):
    return jnp.dot(left, right, preferred_element_type=jnp.float32)


def matmul_tn(left, right):
    return lax.dot_general(
        left, right, (((0,), (0,)), ((), ())), preferred_element_type=jnp.float32
    )


def matmul_nt(left, right):
    return lax.dot_general(
        left, right, (((1,), (1,)), ((), ())), preferred_element_type=jnp.float32
    )


def norm_scale(values, gain):
    return values * lax.rsqrt(jnp.mean(values * values, axis=-1, keepdims=True) + EPS) * gain


def rotary_tables(positions, width):
    half = width // 2
    freqs = THETA ** (-jnp.arange(half, dtype=jnp.float32) / half)
    angles = positions.astype(jnp.float32)[:, None] * freqs[None, :]
    return (jnp.cos(angles), jnp.sin(angles))


def rotate(values, cosine_part, sine_part):
    half = values.shape[-1] // 2
    first = values[..., :half]
    second = values[..., half:]
    return jnp.concatenate(
        [first * cosine_part - second * sine_part, second * cosine_part + first * sine_part],
        axis=-1,
    )


def unrotate(values, cosine_part, sine_part):
    half = values.shape[-1] // 2
    first = values[..., :half]
    second = values[..., half:]
    return jnp.concatenate(
        [first * cosine_part + second * sine_part, second * cosine_part - first * sine_part],
        axis=-1,
    )


def swish_parts(values):
    sigmoid_part = jax.nn.sigmoid(values)
    return (values * sigmoid_part, sigmoid_part * (1.0 + values * (1.0 - sigmoid_part)))


MESH = pl.DeviceIdType.MESH
INNER = 4
PIECES = 2


class Sender:
    def __init__(self):
        self.started = []

    def start(self, there, copy):
        @pl.when(there)
        def _():
            copy.start()

        self.started.append((there, copy))

    def finish(self):
        for there, copy in self.started:
            @pl.when(there)
            def _():
                copy.wait_send()


def remote(source, target, send_sem, recv_sem, place):
    return pltpu.make_async_remote_copy(
        src_ref=source,
        dst_ref=target,
        send_sem=send_sem,
        recv_sem=recv_sem,
        device_id=place,
        device_id_type=MESH,
    )


class Place:
    def __init__(self, group):
        self.me = lax.axis_index("expert")
        self.shard = lax.axis_index("shard")
        self.group = group
        self.outer = group // INNER
        self.local = lax.rem(self.me, group)
        self.base = self.me - self.local
        self.level = self.local // INNER
        inner = lax.rem(self.local, INNER)
        self.row_step = 2 - 4 * (inner // 2)
        self.twin_step = 1 - 2 * lax.rem(inner, 2)
        self.always = self.me >= 0
        self.upper = self.level < self.outer - 1
        self.lower = self.level > 0

    def neighbours(self):
        return [
            (self.upper, {"expert": self.me + INNER}),
            (self.lower, {"expert": self.me - INNER}),
            (self.always, {"expert": self.me + self.row_step}),
            (self.always, {"expert": self.me + self.twin_step}),
        ]

    def along(self, step):
        below = (self.level >= step, self.local - step * INNER, self.upper, self.me + INNER, 0)
        above = (self.level + step < self.outer, self.local + step * INNER, self.lower, self.me - INNER, 1)
        return (below, above)


def greet(peers):
    barrier = pltpu.get_barrier_semaphore()
    for there, peer in peers:
        @pl.when(there)
        def _():
            pl.semaphore_signal(barrier, inc=1, device_id=peer, device_id_type=MESH)
    pl.semaphore_wait(barrier, sum(there.astype(jnp.int32) for there, _ in peers))


def gather_plan(place, own_ref, out_ref, copy_sem, send_sem, recv_sem):
    local = place.local
    pieces = out_ref.shape[1]
    row_at, twin_at = place.me + place.row_step, place.me + place.twin_step
    segments, sends = [[]], []

    def push(kind, block, piece, target, source=None):
        spot = out_ref.at[block, piece]
        return remote(
            spot if source is None else source.at[piece],
            spot,
            send_sem.at[kind, block, piece],
            recv_sem.at[block, piece],
            {"expert": target},
        )

    def start(there, copy):
        segments[-1].append((there, copy.start))
        sends.append((there, copy))

    def arrive(there, block, piece):
        segments[-1].append((there, push(0, block, piece, place.me).wait_recv))

    if own_ref is None:
        own_ref = out_ref.at[local]
    else:
        keep = pltpu.make_async_copy(own_ref, out_ref.at[local], copy_sem)
        segments[-1].append((place.always, keep.start))
    for piece in range(pieces):
        start(place.upper, push(0, local, piece, place.me + INNER, own_ref))
        start(place.lower, push(1, local, piece, place.me - INNER, own_ref))
        start(place.always, push(2, local, piece, row_at, own_ref))
        start(place.always, push(3, local, piece, twin_at, own_ref))
    for step in range(1, place.outer + 1):
        segments.append([])
        if step < place.outer:
            for piece in range(pieces):
                for there, block, onward, target, kind in place.along(step):
                    arrive(there, block, piece)
                    start(there & onward, push(kind, block, piece, target))
                    start(there, push(2, block, piece, row_at))
                    start(there, push(3, block, piece, twin_at))
        for piece in range(pieces):
            for there, block, *_ in place.along(step - 1)[: 1 if step == 1 else 2]:
                arrive(there, block + place.row_step, piece)
                start(there, push(3, block + place.row_step, piece, twin_at))
    segments.append([])
    for step in range(place.outer):
        for piece in range(pieces):
            for there, block, *_ in place.along(step)[: 1 if step == 0 else 2]:
                arrive(there, block + place.twin_step, piece)
                arrive(there, block + place.twin_step + place.row_step, piece)
    if copy_sem is not None:
        segments[-1].append((place.always, keep.wait))
    return segments, sends


def emit(actions):
    for there, action in actions:
        @pl.when(there)
        def _():
            action()


def gather_steps(place, own_ref, out_ref, copy_sem, send_sem, recv_sem, sender):
    segments, sends = gather_plan(place, own_ref, out_ref, copy_sem, send_sem, recv_sem)
    sender.started += sends
    for actions in segments:
        emit(actions)
        yield


def add_into(target, first, *others):
    rows = target.shape[0]
    chunk = 32

    def body(index, _):
        at = pl.ds(pl.multiple_of(index * chunk, chunk), chunk)
        total = first[at, :].astype(jnp.float32)
        for other in others:
            total = total + other[at, :].astype(jnp.float32)
        target[at, :] = total.astype(target.dtype)
        return 0

    lax.fori_loop(0, rows // chunk, body, 0)


def reduce_steps(place, part_ref, out_ref, scratch, sender, fine=False):
    (own_buf, twin_buf, row_buf, line_buf, load_sem, twin_send, twin_recv, row_send, row_recv, line_send, line_recv,
     out_buf, out_sem) = scratch
    outer, local, level = place.outer, place.local, place.level
    pieces = part_ref.shape[1]
    inner = lax.rem(local, INNER)
    row_bit, core = inner // 2, lax.rem(inner, 2)
    twin_at, row_at = {"expert": place.me + place.twin_step}, {"expert": place.me + place.row_step}
    order = []
    low, high = 0, outer - 1
    while low <= high:
        order += [high] if low == high else [high, low]
        low, high = low + 1, high - 1
    units = [(at, piece) for at in order for piece in range(pieces)]
    bits = (1 - row_bit, row_bit)

    def loading(at, piece, bit):
        where = at * 2 + bit
        return pltpu.make_async_copy(
            part_ref.at[at * INNER + bit * 2 + core, piece], own_buf.at[where, piece], load_sem.at[where, piece]
        )

    def to_twin(at, piece, bit):
        where = at * 2 + bit
        return remote(
            part_ref.at[at * INNER + bit * 2 + 1 - core, piece],
            twin_buf.at[where, piece],
            twin_send.at[where, piece],
            twin_recv.at[where, piece],
            twin_at,
        )

    def to_row(at, piece):
        return remote(
            own_buf.at[at * 2 + bits[0], piece], row_buf.at[at, piece], row_send.at[at, piece], row_recv.at[at, piece], row_at
        )

    def mine(at, piece):
        return own_buf.at[at * 2 + row_bit, piece]

    def to_line(side, at, piece):
        return remote(
            mine(at, piece),
            line_buf.at[side, at, piece],
            line_send.at[side, at, piece],
            line_recv.at[side, at, piece],
            {"expert": place.me + (INNER if side == 0 else -INNER)},
        )

    for at, piece in units:
        for bit in bits:
            sender.start(place.always, to_twin(at, piece, bit))
            loading(at, piece, bit).start()
    yield
    for at, piece in units:
        for bit in bits:
            where = at * 2 + bit
            loading(at, piece, bit).wait()
            to_twin(at, piece, bit).wait_recv()
            add_into(own_buf.at[where, piece], own_buf.at[where, piece], twin_buf.at[where, piece])
            if bit is bits[0]:
                sender.start(place.always, to_row(at, piece))
        if fine:
            yield
    if not fine:
        yield
    for at, piece in units:
        to_row(at, piece).wait_recv()
        spot, row = mine(at, piece), row_buf.at[at, piece]
        for side, there, first in ((0, level < at, level == 0), (1, level > at, level == outer - 1)):
            line = to_line(side, at, piece)

            @pl.when(there & first)
            def _():
                add_into(spot, spot, row)

            @pl.when(there & ~first)
            def _():
                line.wait_recv()
                add_into(spot, spot, row, line_buf.at[side, at, piece])

            sender.start(there, line)
        if fine:
            yield
    if not fine:
        yield
    for at, piece in units:
        @pl.when(level == at)
        def _():
            parts = [mine(at, piece), row_buf.at[at, piece]]
            for side, there in ((0, at > 0), (1, at < outer - 1)):
                if there:
                    to_line(side, at, piece).wait_recv()
                    parts.append(line_buf.at[side, at, piece])
            add_into(out_buf.at[piece], *parts)
    done = pltpu.make_async_copy(out_buf, out_ref, out_sem)
    done.start()
    done.wait()
    yield


def reduce_scratch(group, pieces, rows, columns):
    outer = group // INNER
    bf = jnp.bfloat16
    pair, single, line = (2 * outer, pieces), (outer, pieces), (2, outer, pieces)
    block = (rows, columns)
    return [
        pltpu.VMEM(pair + block, bf),
        pltpu.VMEM(pair + block, bf),
        pltpu.VMEM(single + block, bf),
        pltpu.VMEM(line + block, bf),
        pltpu.SemaphoreType.DMA(pair),
        pltpu.SemaphoreType.DMA(pair),
        pltpu.SemaphoreType.DMA(pair),
        pltpu.SemaphoreType.DMA(single),
        pltpu.SemaphoreType.DMA(single),
        pltpu.SemaphoreType.DMA(line),
        pltpu.SemaphoreType.DMA(line),
        pltpu.VMEM((pieces,) + block, jnp.float32),
        pltpu.SemaphoreType.DMA(()),
    ]


class HeadRows:
    def __init__(self, started, received):
        self.started, self.received = started, received

    def wait(self):
        for there, local, copy, keep in self.started:
            @pl.when(there)
            def _():
                copy.wait_send()

            @pl.when(local)
            def _():
                keep.wait()
        for there, copy in self.received:
            @pl.when(there)
            def _():
                copy.wait_recv()


def head_rows(place, plane, shards, own_ref, out_ref, copy_sem, send_sem, recv_sem):
    count = own_ref.shape[0]
    number = place.shard * plane + place.me
    sequences = plane // place.group
    mine = place.shard * sequences + place.me // place.group
    started, received = [], []
    for index in range(count):
        target = place.local * count + index
        peer = {"shard": target // plane, "expert": lax.rem(target, plane)}
        copy = remote(own_ref.at[index], out_ref.at[mine], send_sem.at[index], recv_sem.at[mine], peer)
        keep = pltpu.make_async_copy(own_ref.at[index], out_ref.at[mine], copy_sem)

        @pl.when(target != number)
        def _():
            copy.start()

        @pl.when(target == number)
        def _():
            keep.start()

        started.append((target != number, target == number, copy, keep))
    for shard in range(shards):
        for sequence in range(sequences):
            source = shard * plane + sequence * place.group + number // count
            slot = shard * sequences + sequence
            peer = {"shard": source // plane, "expert": lax.rem(source, plane)}
            copy = remote(own_ref.at[0], out_ref.at[slot], send_sem.at[0], recv_sem.at[slot], peer)
            received.append((source != number, copy))
    return HeadRows(started, received), []


def bundle_kernel(group, shards, kinds, *refs):
    count = len(kinds)
    ins, outs, rest = refs[:count], refs[count : 2 * count], refs[2 * count :]
    place = Place(group)
    plane = lax.axis_size("expert")
    peers = []
    if "gather" in kinds or "reduce" in kinds:
        peers += place.neighbours()
    members = [{"expert": place.base + lax.rem(place.local + step, group)} for step in range(1, group)]
    if "trade" in kinds:
        peers = [(place.always, member) for member in members]
    across = [{"shard": lax.rem(place.shard + step, shards)} for step in range(1, shards)]
    if "swap" in kinds or "share" in kinds:
        peers += [(place.always, peer) for peer in across]
    everyone = []
    if "owners" in kinds or "rows" in kinds:
        total = shards * plane
        number = place.shard * plane + place.me
        for step in range(1, total):
            target = lax.rem(number + step, total)
            everyone.append((target, {"shard": target // plane, "expert": lax.rem(target, plane)}))
        peers = [(place.always, peer) for _, peer in everyone]
    greet(peers)
    sender = Sender()
    runs, waits = [], []
    for kind, own, out in zip(kinds, ins, outs):
        if kind == "gather":
            copy_sem, send_sem, recv_sem, *rest = rest
            runs.append(gather_steps(place, own, out, copy_sem, send_sem, recv_sem, sender))
        elif kind == "reduce":
            scratch, rest = rest[:13], rest[13:]
            runs.append(reduce_steps(place, own, out, scratch, sender))
        else:
            copy_sem, send_sem, recv_sem, *rest = rest
            if kind == "swap":
                mine, source = place.shard, lambda target: own
                targets = [(lax.rem(place.shard + step, shards), peer) for step, peer in enumerate(across, 1)]
            elif kind == "share":
                mine, source = place.shard, lambda target: own.at[target]
                targets = [(lax.rem(place.shard + step, shards), peer) for step, peer in enumerate(across, 1)]
            elif kind == "trade":
                mine, source = place.local, lambda target: own.at[target]
                targets = [(lax.rem(place.local + step, group), peer) for step, peer in enumerate(members, 1)]
            elif kind == "owners":
                mine, source = place.shard * plane + place.me, lambda target: own.at[target]
                targets = everyone
            else:
                waits.append(head_rows(place, plane, shards, own, out, copy_sem, send_sem, recv_sem))
                continue
            keep = None
            if kind != "share":
                keep = pltpu.make_async_copy(source(mine), out.at[mine], copy_sem)
                keep.start()
            total = len(targets) + 1
            copies = []
            for step, (target, peer) in enumerate(targets, 1):
                copy = remote(source(target), out.at[mine], send_sem.at[step], recv_sem.at[step], peer)
                copy.start()
                copies.append(copy)
            waits.append((keep, copies))
    while runs:
        runs = [run for run in runs if next(run, "end") != "end"]
    for keep, copies in waits:
        if keep is not None:
            keep.wait()
        for copy in copies:
            copy.wait()
    sender.finish()


def bundle(number, group, shards, transfers, limit=48 * 2**20):
    kinds, arrays, shapes, scratch = [], [], [], []
    members = shards * lax.axis_size("expert")
    for kind, array in transfers:
        kinds.append(kind)
        sems = [pltpu.SemaphoreType.DMA(())]
        if kind == "gather":
            pieces = PIECES if array.shape[0] % (16 * PIECES) == 0 else 1
            array = array.reshape((pieces, array.shape[0] // pieces) + array.shape[1:])
            shape = (group,) + array.shape
            sems += [pltpu.SemaphoreType.DMA((4, group, pieces)), pltpu.SemaphoreType.DMA((group, pieces))]
        elif kind == "reduce":
            pieces = 2 * PIECES
            array = array.reshape(group, pieces, array.shape[1] // pieces, array.shape[2])
            shape = array.shape[1:]
            sems = reduce_scratch(group, *shape)
        else:
            total = {"swap": shards, "share": shards, "trade": group, "owners": members}.get(kind)
            shape = ((total,) + array.shape) if kind == "swap" else array.shape
            if kind == "rows":
                total = max(array.shape[0], members // group)
                shape = (members // group,) + array.shape[1:]
            sems += [pltpu.SemaphoreType.DMA((total,)), pltpu.SemaphoreType.DMA((total,))]
        arrays.append(array)
        shapes.append(jax.ShapeDtypeStruct(shape, jnp.float32 if kind == "reduce" else array.dtype))
        scratch += sems
    outs = pl.pallas_call(
        functools.partial(bundle_kernel, group, shards, tuple(kinds)),
        out_shape=shapes,
        in_specs=[pl.BlockSpec(memory_space=pl.ANY)] * len(arrays),
        out_specs=[pl.BlockSpec(memory_space=pl.ANY)] * len(arrays),
        scratch_shapes=scratch,
        compiler_params=pltpu.CompilerParams(
            collective_id=number, has_side_effects=True, vmem_limit_bytes=limit
        ),
        name="bundle_" + "_".join(kinds[:2]),
    )(*arrays)
    done = []
    for (kind, array), out in zip(transfers, outs):
        if kind == "gather":
            out = out.reshape((group,) + array.shape)
        if kind == "reduce":
            out = out.reshape(array.shape[1:])
        done.append(out)
    return done


def pieces_of(size, most):
    return [(at, min(most, size - at)) for at in range(0, size, most)]


def expert_kernel(shards, *refs):
    (routes_ref, router_ref, rows_in, grads_in, shared_gate_own, shared_gate_got, shared_up_own, shared_up_got,
     shared_down_own, shared_down_got, gate_own, gate_got, up_own, up_got, narrow_own, query_piece, all_rows,
     rows_ref, grad_ref, back_ref, out_ref, score_ref, hidden_ref, gate_back_ref, up_back_ref, shared_hidden_ref,
     shared_got, narrow_got, full_query,
     cotangent, hidden, gate_part, up_part, pick_all, gate_all, shared_hidden, shared_gate_back, shared_up_back,
     gate_w, up_w, down_w, shared_gate_w, shared_up_w, shared_down_w,
     wide_buf, shared_term, weight_sem, save_sem, wide_sem, owner_send, owner_recv, owner_keep, swap_send, swap_recv, piece_keep, piece_send, piece_recv) = refs
    low = jnp.bfloat16
    turn, step = pl.program_id(0), pl.program_id(1)
    steps = pl.num_programs(1)
    width, hidden_width = gate_w.shape
    own_width = width // shards
    senders, _, rows = routes_ref.shape
    slots, tokens = pick_all.shape[1:]
    capacity = slots // senders
    experts = router_ref.shape[0]
    plane = full_query.shape[1]
    place = Place(plane)
    me = place.me
    sender = Sender()
    others = [lax.rem(place.shard + other, shards) for other in range(1, shards)]

    def at_step(number, turn_at=0):
        return pl.when((turn == turn_at) & (step == number))

    arrivals = []
    for number, other in enumerate(others, 1):
        push = remote(narrow_own, narrow_got.at[place.shard], swap_send.at[number], swap_recv.at[place.shard], {"shard": other})
        arrivals.append(remote(narrow_own, narrow_got.at[other], swap_send.at[number], swap_recv.at[other], {"shard": other}))
        sender.started.append((place.always, push))
    pushes = [copy for _, copy in sender.started]
    plans = [
        gather_plan(
            place, query_piece.at[other], full_query.at[other], piece_keep.at[number], piece_send.at[number],
            piece_recv.at[number],
        )
        for number, other in enumerate(others)
    ]
    segments = [sum(parts, []) for parts in zip(*[plan[0] for plan in plans])]
    for plan in plans:
        sender.started += plan[1]

    def loading(source, target, index, number):
        return pltpu.make_async_copy(source, target, weight_sem.at[index, number])

    def loads_of(index, own, got, target):
        copies = []
        for number in range(shards):
            at = lax.rem(place.shard + number, shards)
            block = own.shape[0]
            spot = target.at[at] if len(target.shape) == 3 else target.at[pl.ds(pl.multiple_of(at * block, 16), block), :]
            copies.append(loading(own if number == 0 else got.at[at], spot, index, number))
        return copies

    early = (
        loads_of(0, shared_gate_own, shared_gate_got, shared_gate_w)
        + loads_of(1, shared_up_own, shared_up_got, shared_up_w)
        + loads_of(2, shared_down_own, shared_down_got, shared_down_w)
        + loads_of(3, gate_own, gate_got, gate_w)
        + loads_of(4, up_own, up_got, up_w)
    )
    late = loads_of(5, narrow_own, narrow_got, down_w)

    to_owners = Everyone(
        place, plane, shards, lambda target: shared_term.at[target], shared_got, owner_send, owner_recv, owner_keep
    )

    @at_step(0)
    def _():
        greet_everyone(place, plane, shards)
        for push in pushes:
            push.start()
        for load in early:
            load.start()
        emit(segments[0])

    for number in range(1, len(segments)):

        @at_step(number if number < 4 else min(number - 4, 2), number // 4 and 1)
        def _():
            emit(segments[number])

    at_slots = pl.ds(pl.multiple_of(step * slots, slots), slots)
    at_tokens = pl.ds(pl.multiple_of(step * tokens, tokens), tokens)

    @pl.when(turn == 0)
    def _():
        logits = matmul_nt(router_ref[...], rows_in[...])
        names = lax.broadcasted_iota(jnp.int32, (experts, rows), 0)
        earlier = lax.broadcasted_iota(jnp.int32, (rows, rows), 0) <= lax.broadcasted_iota(jnp.int32, (rows, rows), 1)
        earlier = jnp.where(earlier, 1.0, 0.0).astype(low)
        slot_names = lax.broadcasted_iota(jnp.int32, (capacity, rows), 0).astype(jnp.float32)
        pick_buf, gate_buf = pick_all.at[step], gate_all.at[at_slots, :]
        pick_buf[...] = jnp.zeros(pick_buf.shape, low)
        for number in range(senders):
            routed = routes_ref[number]
            chosen = jnp.zeros((experts, rows), jnp.float32)
            for choice in range(TOP):
                chosen = chosen + jnp.where(routed[choice : choice + 1] == names, 1.0, 0.0)
            logit = jnp.where(chosen > 0.0, logits[:, number * rows : (number + 1) * rows], NEG)
            expo = jnp.exp(logit - jnp.max(logit, axis=0, keepdims=True)) * chosen
            dense = expo / jnp.sum(expo, axis=0, keepdims=True)
            gate_row = jnp.sum(jnp.where(names == me, dense, 0.0), axis=0, keepdims=True)
            mark = jnp.sum(jnp.where(routed == me, 1.0, 0.0), axis=0, keepdims=True)
            rank = matmul(jnp.broadcast_to(mark, (8, rows)).astype(low), earlier)[:1] - 1.0
            pick = jnp.where((slot_names == rank) & (mark > 0.0), 1.0, 0.0)
            at = slice(number * capacity, (number + 1) * capacity)
            pick_buf[at, number * rows : (number + 1) * rows] = pick.astype(low)
            gate_buf[at, :] = jnp.sum(pick * gate_row, axis=1, keepdims=True)
        gate = gate_buf[...]

        def pick_step(index, _):
            at = pl.ds(pl.multiple_of(index * 512, 512), 512)
            rows_ref[:, at] = matmul(pick_buf[...], rows_in[:, at]).astype(low)
            picked = matmul(pick_buf[...], grads_in[:, at])
            cotangent[at_slots, at] = picked.astype(low)
            grad_ref[:, at] = (gate * picked).astype(low)
            return 0

        lax.fori_loop(0, width // 512, pick_step, 0)

        @pl.when(step == 0)
        def _():
            for load in early:
                load.wait()

        shared_pre, shared_up = 0.0, 0.0
        for shard in range(shards):
            part = rows_in[:, shard * own_width : (shard + 1) * own_width]
            shared_pre = shared_pre + matmul(part, shared_gate_w[shard])
            shared_up = shared_up + matmul(part, shared_up_w[shard])
        swished, slope = swish_parts(shared_pre)
        shared_hidden[at_tokens, :] = (swished * shared_up).astype(low)
        shared_grad = matmul_nt(grads_in[...], shared_down_w[...])
        shared_gate_back[at_tokens, :] = (shared_grad * shared_up * slope).astype(low)
        shared_up_back[at_tokens, :] = (shared_grad * swished).astype(low)
        for at, size in pieces_of(hidden_width, 512):
            columns = slice(at, at + size)
            gate_pre = matmul(rows_ref[...], gate_w[:, columns])
            up_pre = matmul(rows_ref[...], up_w[:, columns])
            swished, slope = swish_parts(gate_pre)
            hidden[at_slots, columns] = (swished * up_pre).astype(low)
            gate_part[at_slots, columns] = (up_pre * slope).astype(low)
            up_part[at_slots, columns] = swished.astype(low)

    @at_step(0, 1)
    def _():
        tile = wide_buf.shape[2]
        units = shared_hidden.shape[1]
        per = tile // shared_term.shape[1]
        copies = [
            pltpu.make_async_copy(all_rows.at[:, at : at + tile], wide_buf.at[index % 2], wide_sem.at[index % 2])
            for index, at in enumerate(range(0, width, tile))
        ]
        copies[0].start()
        for index, copy in enumerate(copies):
            if index + 1 < len(copies):
                copies[index + 1].start()
            copy.wait()
            spot = slice(index * per, (index + 1) * per)
            shape = (per, shared_term.shape[1], units)
            for part, grads in enumerate((shared_gate_back, shared_up_back)):
                term = matmul_tn(wide_buf[index % 2], grads[...]).astype(low)
                shared_term[spot, :, part * units : (part + 1) * units] = term.reshape(shape)
        for arrival in arrivals:
            arrival.wait_recv()
        to_owners.start()
        for load in late:
            load.start()
        for load in late:
            load.wait()

    @pl.when(turn == 1)
    def _():
        gate = gate_all[at_slots, :]
        pick = pick_all[step]
        slot_grad = (gate * cotangent[at_slots, :].astype(jnp.float32)).astype(low)
        for at, size in pieces_of(hidden_width, 512):
            columns = slice(at, at + size)
            hidden_grad = matmul_nt(slot_grad, down_w[columns, :])
            gate_part[at_slots, columns] = (hidden_grad * gate_part[at_slots, columns].astype(jnp.float32)).astype(low)
            up_part[at_slots, columns] = (hidden_grad * up_part[at_slots, columns].astype(jnp.float32)).astype(low)

        def out_step(index, score):
            at = pl.ds(pl.multiple_of(index * 512, 512), 512)
            shard = index * 512 // own_width
            within = pl.ds(pl.multiple_of(index * 512 - shard * own_width, 512), 512)
            expert_out = matmul(hidden[at_slots, :], down_w[:, at]).astype(low).astype(jnp.float32)
            score = score + jnp.sum(expert_out * cotangent[at_slots, at].astype(jnp.float32), axis=1, keepdims=True)
            out = matmul_tn(pick, (gate * expert_out).astype(low))
            out_ref[:, at] = (out + matmul(shared_hidden[at_tokens, :], shared_down_w[:, at])).astype(low)
            row_back = matmul_nt(gate_part[at_slots, :], gate_w[at, :]) + matmul_nt(up_part[at_slots, :], up_w[at, :])
            back = (
                matmul_tn(pick, row_back.astype(low))
                + matmul_nt(shared_gate_back[at_tokens, :], shared_gate_w[shard, within, :])
                + matmul_nt(shared_up_back[at_tokens, :], shared_up_w[shard, within, :])
            )
            back_ref[:, at] = back.astype(low)
            return score

        score = lax.fori_loop(0, width // 512, out_step, jnp.zeros((slots, 1), jnp.float32))
        for number in range(senders):
            at = slice(number * capacity, (number + 1) * capacity)
            own_pick = pick[at, number * rows : (number + 1) * rows].astype(jnp.float32)
            total = jnp.sum(own_pick * score[at], axis=0, keepdims=True)
            score_ref[number] = jnp.broadcast_to(total, score_ref.shape[1:])

    @pl.when((turn == 1) & (step == steps - 1))
    def _():
        saves = [
            pltpu.make_async_copy(source, target, save_sem.at[index])
            for index, (source, target) in enumerate(
                (
                    (hidden, hidden_ref),
                    (gate_part, gate_back_ref),
                    (up_part, up_back_ref),
                    (shared_hidden, shared_hidden_ref),
                )
            )
        ]
        for save in saves:
            save.start()
        for save in saves:
            save.wait()
        to_owners.wait()
        to_owners.finish()
        sender.finish()


def expert_pass(routes, router, rows, grads, weights, query_piece, capacity):
    plane, _, local = routes.shape
    senders = STEP_SENDERS
    tokens, slots = senders * local, senders * capacity
    steps = plane // senders
    shards = weights[1].shape[0]
    width, hidden_width = rows.shape[1], weights[6].shape[1]
    units = weights[0].shape[1]
    low = jnp.bfloat16
    total = steps * slots
    shape, scratch, dma = jax.ShapeDtypeStruct, pltpu.VMEM, pltpu.SemaphoreType.DMA
    any_space = pl.BlockSpec(memory_space=pl.ANY)

    def first(r, c):
        return pl.BlockSpec((r, c), lambda turn, i: (i + turn * (steps - 1 - i), 0))

    def second(r, c):
        return pl.BlockSpec((r, c), lambda turn, i: (i * turn, 0))

    return pl.pallas_call(
        functools.partial(expert_kernel, shards),
        grid=(2, steps),
        out_shape=[
            shape((total, width), low),
            shape((total, width), low),
            shape((steps * tokens, width), low),
            shape((steps * tokens, width), low),
            shape((plane, 8, local), jnp.float32),
            shape((total, hidden_width), low),
            shape((total, hidden_width), low),
            shape((total, hidden_width), low),
            shape((steps * tokens, units), low),
            shape((shards * plane, width // (shards * plane), 2 * units), low),
            shape((shards,) + weights[10].shape, low),
            shape((shards, plane) + query_piece.shape[1:], low),
        ],
        in_specs=[
            pl.BlockSpec((senders, 8, local), lambda turn, i: (i + turn * (steps - 1 - i), 0, 0)),
            pl.BlockSpec(router.shape, lambda turn, i: (0, 0), pipeline_mode=pl.Buffered(1)),
            first(tokens, width),
            first(tokens, width),
        ]
        + [any_space] * (len(weights) + 2),
        out_specs=[
            first(slots, width),
            first(slots, width),
            second(tokens, width),
            second(tokens, width),
            pl.BlockSpec((senders, 8, local), lambda turn, i: (i * turn, 0, 0)),
        ]
        + [any_space] * 7,
        scratch_shapes=[
            scratch((total, width), low),
            scratch((total, hidden_width), low),
            scratch((total, hidden_width), low),
            scratch((total, hidden_width), low),
            scratch((steps, slots, tokens), low),
            scratch((total, 1), jnp.float32),
            scratch((steps * tokens, units), low),
            scratch((steps * tokens, units), low),
            scratch((steps * tokens, units), low),
            scratch((width, hidden_width), low),
            scratch((width, hidden_width), low),
            scratch((hidden_width, width), low),
            scratch((shards, width // shards, units), low),
            scratch((shards, width // shards, units), low),
            scratch((units, width), low),
            scratch((2, steps * tokens, 128), low),
            scratch((shards * plane, width // (shards * plane), 2 * units), low),
            dma((6, shards)),
            dma((6,)),
            dma((2,)),
            dma((shards * plane,)),
            dma((shards * plane,)),
            dma(()),
            dma((shards,)),
            dma((shards,)),
            dma((shards,)),
            dma((shards, 4, plane, 1)),
            dma((shards, plane, 1)),
        ],
        compiler_params=pltpu.CompilerParams(
            vmem_limit_bytes=63 * 2**20,
            dimension_semantics=("arbitrary", "arbitrary"),
            collective_id=5,
            has_side_effects=True,
        ),
        name="experts",
    )(routes, router, rows, grads, *weights, query_piece, rows)


QUERIES = 256
KEYS = WINDOW + QUERIES


def document_ends(lengths, sequence):
    ends, total = [], 0
    for entry in range(lengths.shape[1]):
        total = total + lengths[sequence, entry]
        ends.append(total)
    return ends


def documents_at(positions, ends):
    inside = sum(jnp.where(positions >= end, 1, 0) for end in ends)
    return jnp.where(positions < 0, -1, inside)


def query_documents(index, ends):
    return documents_at(lax.broadcasted_iota(jnp.int32, (QUERIES, 1), 0) + index * QUERIES, ends)


def score_block(scale, index, ends, query, keys):
    raw = matmul_nt(query, keys) * scale
    query_docs = query_documents(index, ends)
    key_docs = documents_at(lax.broadcasted_iota(jnp.int32, (1, KEYS), 1) + (index * QUERIES - WINDOW), ends)
    row = lax.broadcasted_iota(jnp.int32, raw.shape, 0) + WINDOW
    column = lax.broadcasted_iota(jnp.int32, raw.shape, 1)
    allowed = (query_docs == key_docs) & (column <= row) & (column > row - WINDOW)
    return jnp.where(allowed, raw, NEG)


class Swaps:
    def __init__(self, place, shards, sender):
        self.place, self.shards, self.sender = place, shards, sender

    def start(self, source, target, send_sem, recv_sem, keep=None):
        place, shards = self.place, self.shards
        arrivals = []
        for step in range(1, shards):
            other = lax.rem(place.shard + step, shards)
            self.sender.start(
                place.always,
                remote(source, target(place.shard), send_sem.at[step], recv_sem.at[place.shard], {"shard": other}),
            )
            arrivals.append(
                remote(source, target(other), send_sem.at[step], recv_sem.at[other], {"shard": other})
            )
        if keep is not None:
            copy = pltpu.make_async_copy(source, target(place.shard), keep)
            copy.start()

        def wait():
            for arrival in arrivals:
                arrival.wait_recv()
            if keep is not None:
                copy.wait()

        return wait


def whole_weight(place, others, own_ref, full_ref, buf, sem):
    copies = [pltpu.make_async_copy(own_ref, buf.at[place.shard], sem.at[0])]
    for step, other in enumerate(others, 1):
        copies.append(pltpu.make_async_copy(full_ref.at[other], buf.at[other], sem.at[step]))
    for copy in copies:
        copy.start()
    return copies


def drain(run):
    for _ in run:
        pass


def forward_kernel(shards, plane, scale, last, *refs):
    (tokens, cotangent, query_cols, down_half, up_half, out_half, query_half, gate_half, wide_half,
     shared_gate, shared_up, shared_down, routes, first_gain, latent_gain, second_gain, turn, sway, lengths,
     all_normed, all_grads, all_routes, full_down, full_out, query_piece, full_gate, full_up,
     full_shared_gate, full_shared_up, full_shared_down, normed_one,
     query, keys, value, key_latent, compressed, head_out, log_total, middle, up_buf,
     token_buf, normed_buf, query_buf, down_buf, out_buf, heads_buf, second_buf,
     swap_send, swap_recv, keep_sem, gather_send, gather_recv, gather_keep, piece_send, piece_recv,
     trade_send, trade_recv, load_sem, whole_sem) = refs
    low = jnp.bfloat16
    group = SEQ_DEVICES
    place, wide = Place(group), Place(plane)
    width = tokens.shape[-1]
    rows = middle.shape[0]
    ends = document_ends(lengths, (place.shard * plane + place.me) // group)
    sender = Sender()
    members = [lax.rem(place.local + step, group) for step in range(1, group)]
    peers = [(place.always, {"expert": place.base + member}) for member in members]
    if plane != group:
        peers += [
            (wide.upper & ~place.upper, {"expert": place.me + INNER}),
            (wide.lower & ~place.lower, {"expert": place.me - INNER}),
        ]
    others = [lax.rem(place.shard + step, shards) for step in range(1, shards)]
    peers += [(place.always, {"shard": other}) for other in others]
    greet(peers)

    swaps = Swaps(place, shards, sender)
    numbers = iter(range(16))

    def swap(source, target, keep=False):
        at = next(numbers)
        return swaps.start(
            source, target, swap_send.at[at], swap_recv.at[at], keep_sem.at[at] if keep else None
        )

    at_piece = lambda ref: ref.at[wide.me]
    head_dim = QK_NOPE + QK_ROPE
    start = place.local * head_dim // 128 * 128
    odd = lax.rem(place.local * head_dim, 128) > 0
    query_cols = query_cols.at[:, pl.ds(pl.multiple_of(start, 128), 2 * QK_NOPE)]
    both = QK_NOPE + V_HEAD
    up_half = up_half.at[:, pl.ds(pl.multiple_of(place.local * both, both), both)]
    got_query = swap(query_cols, lambda shard: query_buf.at[shard], True)
    got_down = swap(at_piece(down_half), lambda shard: full_down.at[shard, wide.me])
    got_up = swap(up_half, lambda shard: up_buf.at[shard], True)
    token_run = gather_steps(
        place, tokens, token_buf, gather_keep.at[0], gather_send.at[0], gather_recv.at[0], sender
    )
    next(token_run)
    got_out = swap(at_piece(out_half), lambda shard: full_out.at[shard, wide.me])
    waits = [swap(at_piece(query_half), lambda shard: query_piece.at[shard])]
    def piece_gathers(kind, full):
        return [
            gather_steps(
                wide, None, full.at[other], None, piece_send.at[kind, step], piece_recv.at[kind, step], sender
            )
            for step, other in enumerate(others)
        ]

    next(token_run)
    got_down()
    down_runs = piece_gathers(0, full_down)
    for run in down_runs:
        next(run)
    next(token_run)
    for run in down_runs:
        next(run)
    got_query()
    got_up()
    waits += [
        swap(gate_half, lambda shard: full_gate.at[shard]),
        swap(wide_half, lambda shard: full_up.at[shard]),
    ]
    drain(token_run)
    got_out()
    waits += [
        swap(shared_gate, lambda shard: full_shared_gate.at[shard]),
        swap(shared_up, lambda shard: full_shared_up.at[shard]),
        swap(shared_down, lambda shard: full_shared_down.at[shard]),
    ]
    for run in down_runs:
        drain(run)
    route_run = gather_steps(
        wide, routes, all_routes, gather_keep.at[1], gather_send.at[1], gather_recv.at[1], sender
    )
    next(route_run)
    out_runs = piece_gathers(1, full_out)
    for run in out_runs:
        next(run)
    for copy in whole_weight(place, others, down_half, full_down, down_buf, whole_sem.at[0]):
        copy.wait()

    keys[:WINDOW, :] = jnp.zeros((WINDOW, keys.shape[1]), low)
    value[:WINDOW, :] = jnp.zeros((WINDOW, value.shape[1]), low)
    tile = 2 * rows
    own_width = width // shards

    def whole_dot(at, weight_of):
        total = 0.0
        for shard in range(shards):
            total = total + matmul(normed_buf[at, shard * own_width : (shard + 1) * own_width], weight_of(shard))
        return total

    def front_tile(index, _):
        at = pl.ds(pl.multiple_of(index * tile, tile), tile)
        values = token_buf[pl.ds(index * 2, 2)].reshape(tile, width).astype(jnp.float32)
        root = lax.rsqrt(jnp.mean(values * values, axis=1, keepdims=True) + EPS)
        normed_buf[at, :] = (values * root * first_gain[...]).astype(low)
        first = whole_dot(at, lambda shard: query_buf[shard])
        latent = whole_dot(at, lambda shard: down_buf[shard].reshape(own_width, -1))
        first = jnp.where(odd, pltpu.roll(first, first.shape[1] - QK_ROPE, 1), first)
        turn_at, sway_at = turn[at, :], sway[at, :]
        lane = lax.broadcasted_iota(jnp.int32, turn_at.shape, 1)

        def rotated(values):
            pair = jnp.where(lane < QK_ROPE, values, pltpu.roll(values, QK_ROPE, 1))
            return pair * turn_at + swapped_halves(pair) * sway_at

        query[at, :QK_NOPE] = first[:, :QK_NOPE].astype(low)
        query[at, QK_NOPE:] = jnp.where(lane < QK_ROPE, rotated(first[:, QK_NOPE:]), 0.0).astype(low)
        key_rope = rotated(latent[:, KV_RANK:]).astype(low)
        latent = latent[:, :KV_RANK]

        @pl.when(index == place.local // 2)
        def _():
            compressed[...] = jnp.where(lax.rem(place.local, 2) == 0, latent[:rows], latent[rows:])

        root = lax.rsqrt(jnp.mean(latent * latent, axis=1, keepdims=True) + EPS)
        normed_latent = (latent * root * latent_gain[...]).astype(low)
        key_latent[at, :] = normed_latent
        up_rows = KV_RANK // shards
        both = 0.0
        for shard in range(shards):
            both = both + matmul(normed_latent[:, shard * up_rows : (shard + 1) * up_rows], up_buf[shard])
        both = both.astype(low)
        later = pl.ds(pl.multiple_of(index * tile + WINDOW, tile), tile)
        keys[later, :QK_NOPE] = both[:, :QK_NOPE]
        keys[later, QK_NOPE:] = key_rope
        value[later, :] = both[:, QK_NOPE:]
        return 0

    tiles = group // 2
    grad_run = gather_steps(
        wide, cotangent, all_grads, gather_keep.at[3], gather_send.at[3], gather_recv.at[3], sender
    )
    for part in range(2):
        lax.fori_loop(part * tiles // 2, (part + 1) * tiles // 2, front_tile, 0)
        for run in out_runs + [route_run]:
            next(run, None)
    next(grad_run)
    save = pltpu.make_async_copy(normed_buf, normed_one, load_sem.at[1])
    save.start()
    for run in out_runs + [route_run]:
        next(run, None)

    def attend_tile(index, _):
        at = pl.ds(pl.multiple_of(index * QUERIES, QUERIES), QUERIES)
        window = pl.ds(pl.multiple_of(index * QUERIES, QUERIES), KEYS)
        scores = score_block(scale, index, ends, query[at, :], keys[window, :])
        top = jnp.max(scores, axis=1, keepdims=True)
        expo = jnp.exp(scores - top)
        total = jnp.sum(expo, axis=1, keepdims=True)
        probs = (expo / total).astype(low)
        real = jnp.where(query_documents(index, ends) < last, 1.0, 0.0)
        head_out[at, :] = (matmul(probs, value[window, :]) * real).astype(low)
        log_total[at, :] = jnp.broadcast_to(top + jnp.log(total), (QUERIES, log_total.shape[1]))
        return 0

    blocks = query.shape[0] // QUERIES
    lax.fori_loop(0, blocks // 2, attend_tile, 0)
    for run in out_runs + [route_run]:
        drain(run)
    load_out = whole_weight(place, others, out_half, full_out, out_buf, whole_sem.at[1])
    next(grad_run)
    lax.fori_loop(blocks // 2, blocks, attend_tile, 0)

    def head_at(member):
        return head_out.at[pl.ds(pl.multiple_of(member * rows, rows), rows), :]

    def lands(head):
        return heads_buf.at[:, pl.ds(pl.multiple_of(head * V_HEAD, V_HEAD), V_HEAD)]

    keep = pltpu.make_async_copy(head_at(place.local), lands(place.local), load_sem.at[2])
    keep.start()
    for step, member in enumerate(members):
        sender.start(
            place.always,
            remote(
                head_at(member), lands(place.local), trade_send.at[step], trade_recv.at[place.local],
                {"expert": place.base + member},
            ),
        )
    for step, member in enumerate(members):
        remote(
            head_at(member), lands(member), trade_send.at[step], trade_recv.at[member], {"expert": place.base + member}
        ).wait_recv()
    keep.wait()
    for copy in load_out:
        copy.wait()

    for at, size in pieces_of(width, 512):
        columns = slice(at, at + size)
        total = token_buf[place.local].reshape(rows, width)[:, columns].astype(jnp.float32)
        for shard in range(shards):
            weight = out_buf[shard, :, :, :, columns].reshape(own_width, size)
            total = total + matmul(heads_buf[:, shard * own_width : (shard + 1) * own_width], weight)
        middle[:, columns] = total
    values = middle[...]
    root = lax.rsqrt(jnp.mean(values * values, axis=1, keepdims=True) + EPS)
    second_buf[...] = (values * root * second_gain[...]).astype(low).reshape(second_buf.shape)

    normed_run = gather_steps(
        wide, second_buf, all_normed, gather_keep.at[2], gather_send.at[2], gather_recv.at[2], sender
    )
    runs = [normed_run, grad_run]
    while runs:
        runs = [run for run in runs if next(run, "end") != "end"]
    save.wait()
    for wait in waits:
        wait()
    sender.finish()


def forward_pass(scale, last, tokens, cotangent, blocks, routes, gains, tables):
    shards, plane = lax.axis_size("shard"), lax.axis_size("expert")
    local, width = tokens.shape
    low, shape = jnp.bfloat16, jax.ShapeDtypeStruct
    pieces = (PIECES, local // PIECES, width)
    any_space, vmem = pl.BlockSpec(memory_space=pl.ANY), pl.BlockSpec(memory_space=pltpu.VMEM)
    head_dim = QK_NOPE + QK_ROPE
    query_cols, down_half, up_half, out_half, query_half = blocks[:5]
    out_shape = [
        shape((plane,) + pieces, low),
        shape((plane,) + pieces, low),
        shape((plane, 1) + routes.shape, jnp.int32),
    ]
    stacked = [down_half.shape, out_half.shape, query_half.shape[1:]] + [block.shape for block in blocks[5:]]
    out_shape += [shape((shards,) + block, low) for block in stacked]
    out_shape += [
        shape((SEQ, width), low),
        shape((SEQ, head_dim + QK_ROPE), low),
        shape((SEQ + WINDOW, head_dim + QK_ROPE), low),
        shape((SEQ + WINDOW, V_HEAD), low),
        shape((SEQ, KV_RANK), low),
        shape((local, KV_RANK), jnp.float32),
        shape((SEQ, V_HEAD), low),
        shape((SEQ, 128), jnp.float32),
        shape((local, width), jnp.float32),
        shape((shards, up_half.shape[0], QK_NOPE + V_HEAD), low),
    ]
    hbm_out = 12
    dma = pltpu.SemaphoreType.DMA
    return pl.pallas_call(
        functools.partial(forward_kernel, shards, plane, scale, last),
        out_shape=out_shape,
        in_specs=[any_space] * (3 + len(blocks)) + [vmem] * (len(gains) + len(tables) - 1) + [pl.BlockSpec(memory_space=pltpu.SMEM)],
        out_specs=[any_space] * hbm_out + [vmem] * (len(out_shape) - hbm_out),
        scratch_shapes=[
            pltpu.VMEM((SEQ_DEVICES,) + pieces, low),
            pltpu.VMEM((SEQ, width), low),
            pltpu.VMEM((shards, query_cols.shape[0], 2 * QK_NOPE), low),
            pltpu.VMEM((shards,) + down_half.shape, low),
            pltpu.VMEM((shards,) + out_half.shape, low),
            pltpu.VMEM((local, HEADS * V_HEAD), low),
            pltpu.VMEM(pieces, low),
            dma((12, shards)),
            dma((12, shards)),
            dma((12,)),
            dma((4, 4, plane, PIECES)),
            dma((4, plane, PIECES)),
            dma((4,)),
            dma((3, shards, 4, plane, 1)),
            dma((3, shards, plane, 1)),
            dma((SEQ_DEVICES,)),
            dma((SEQ_DEVICES,)),
            dma((4,)),
            dma((2, shards)),
        ],
        compiler_params=pltpu.CompilerParams(
            collective_id=1, has_side_effects=True, vmem_limit_bytes=60 * 2**20
        ),
        name="forward",
    )(tokens.reshape(pieces), cotangent.reshape(pieces), *blocks, routes[None], *gains, *tables)


def sums_kernel(shards, plane, *refs):
    (normed_part, output_part, token_scores, slot_rows, slot_grad, hidden, gate_back, up_back, all_grads,
     shared_hidden,
     back, output_sum, scores, down_got, down_own, gate_own, up_own, gate_send, up_send, narrow_own, narrow_send,
     down_send, pair_buf, stream_buf, wide_buf, own_stage, send_stage, down_stage,
     load_sem, stream_sem, stage_sem, score_send, score_recv, swap_send, swap_recv, *reduces) = refs
    low = jnp.bfloat16
    place = Place(plane)
    sender = Sender()
    members = [lax.rem(place.me + step, plane) for step in range(1, plane)]
    others = [lax.rem(place.shard + step, shards) for step in range(1, shards)]
    greet([(place.always, {"expert": member}) for member in members] + [(place.always, {"shard": other}) for other in others])
    count = 13
    back_run = reduce_steps(place, normed_part, back, reduces[:count], sender, True)
    output_run = iter(())
    if len(reduces) > count:
        output_run = reduce_steps(place, output_part, output_sum, reduces[count:], sender, True)
    next(back_run)
    keep = pltpu.make_async_copy(token_scores.at[place.me], scores.at[place.me], load_sem.at[0])
    keep.start()

    def score_trade(step, member, source):
        return remote(token_scores.at[member], scores.at[source], score_send.at[step], score_recv.at[source],
                      {"expert": member})

    for step, member in enumerate(members):
        sender.start(place.always, score_trade(step, member, place.me))
    load_hidden = pltpu.make_async_copy(hidden, pair_buf.at[0], load_sem.at[1])
    load_hidden.start()
    load_up = pltpu.make_async_copy(up_back, pair_buf.at[1], load_sem.at[2])
    load_up.start()
    width = slot_rows.shape[1]
    tile = stream_buf.shape[-1]
    tiles = [slice(at, at + tile) for at in range(0, width, tile)]
    hidden_width = hidden.shape[1]
    own_hidden, own_width = hidden_width // shards, width // shards

    def streamed(source, buf, sem):
        copies = [
            pltpu.make_async_copy(source.at[:, columns], buf.at[index % 2], sem.at[index % 2])
            for index, columns in enumerate(tiles)
        ]
        copies[0].start()
        for index, copy in enumerate(copies):
            if index + 1 < len(copies):
                copies[index + 1].start()
            copy.wait()
            yield index, buf.at[index % 2]

    def down_chunks():
        load_hidden.wait()
        before = None
        for index, piece in streamed(slot_grad, stream_buf, stream_sem.at[0]):
            term = matmul_tn(pair_buf[0], piece[...])
            if before is not None:
                before.wait()
            for shard in range(shards):
                part = term[shard * own_hidden : (shard + 1) * own_hidden]

                @pl.when(place.shard == shard)
                def _():
                    down_stage[...] = part

                @pl.when(place.shard != shard)
                def _():
                    down_send[shard, :, tiles[index]] = part.astype(low)

            before = pltpu.make_async_copy(down_stage, down_own.at[:, tiles[index]], stage_sem.at[0])
            before.start()
            yield
        before.wait()
        for step, other in enumerate(others, 1):
            sender.start(
                place.always,
                remote(down_send.at[other], down_got.at[place.shard], swap_send.at[step], swap_recv.at[place.shard],
                       {"shard": other}),
            )

    def gate_chunks():
        load_gate = pltpu.make_async_copy(gate_back, pair_buf.at[0], load_sem.at[1])
        load_gate.start()
        load_gate.wait()
        load_up.wait()
        before = []
        for index, piece in streamed(slot_rows, stream_buf, stream_sem.at[0]):
            shard = index * tile // own_width
            within = pl.ds(index * tile - shard * own_width, tile)
            mine = place.shard == shard
            after = []
            for matrix, (own, send) in enumerate(((gate_own, gate_send), (up_own, up_send))):
                term = matmul_tn(piece[...], pair_buf[matrix])
                for there, copy in before[2 * matrix : 2 * matrix + 2]:
                    @pl.when(there)
                    def _():
                        copy.wait()

                to_own = pltpu.make_async_copy(own_stage.at[matrix], own.at[within], stage_sem.at[1 + matrix])
                to_send = pltpu.make_async_copy(send_stage.at[matrix], send.at[shard, within], stage_sem.at[3 + matrix])

                @pl.when(mine)
                def _():
                    own_stage[matrix] = term
                    to_own.start()

                @pl.when(~mine)
                def _():
                    send_stage[matrix] = term.astype(low)
                    to_send.start()

                after += [(mine, to_own), (~mine, to_send)]
                yield
            before = after
        for there, copy in before:
            @pl.when(there)
            def _():
                copy.wait()

    def shared_chunks():
        units = shared_hidden.shape[1]
        own_units = units // shards
        for index, piece in streamed(all_grads, wide_buf, stream_sem.at[1]):
            term = matmul_tn(shared_hidden[...], piece[...])
            for shard in range(shards):
                part = term[shard * own_units : (shard + 1) * own_units]
                narrow_send[shard, :, tiles[index]] = part.astype(low)

                @pl.when(place.shard == shard)
                def _():
                    narrow_own[:, tiles[index]] = part

            yield

    def chunks():
        yield from down_chunks()
        yield from gate_chunks()
        yield from shared_chunks()

    work = chunks()
    units = plane // INNER * normed_part.shape[1]
    next(work)
    for _ in range(units):
        next(back_run)
    next(output_run, None)
    for index in range(8):
        next(work)
    for index in range(units):
        next(work, None)
        next(back_run)
    for index in range(units):
        next(work, None)
        next(output_run, None)
    drain(back_run)
    drain(work)
    drain(output_run)
    for step, member in enumerate(members):
        score_trade(step, member, member).wait_recv()
    keep.wait()
    for step, other in enumerate(others, 1):
        remote(down_send.at[other], down_got.at[other], swap_send.at[step], swap_recv.at[other], {"shard": other}).wait_recv()
    sender.finish()


def sums_pass(normed_part, output_part, token_scores, expert_terms, plane_terms, shared_terms):
    shards, plane = lax.axis_size("shard"), lax.axis_size("expert")
    low, shape = jnp.bfloat16, jax.ShapeDtypeStruct
    slot_rows, slot_grad, hidden, gate_back, up_back = expert_terms
    local, width = normed_part.shape[1:]
    slots, hidden_width = hidden.shape
    units = shared_terms[0].shape[1]
    count = 2 * PIECES
    pieces = (plane, count, local // count, width)
    own_width, own_hidden = width // shards, hidden_width // shards
    any_space, vmem = pl.BlockSpec(memory_space=pl.ANY), pl.BlockSpec(memory_space=pltpu.VMEM)
    reduces = 2 if plane == SEQ_DEVICES else 1
    out_shape = [
        shape(pieces[1:], jnp.float32),
        shape(pieces[1:], jnp.float32),
        shape(token_scores.shape, jnp.float32),
        shape((shards, own_hidden, width), low),
        shape((own_hidden, width), jnp.float32),
        shape((own_width, hidden_width), jnp.float32),
        shape((own_width, hidden_width), jnp.float32),
        shape((shards, own_width, hidden_width), low),
        shape((shards, own_width, hidden_width), low),
        shape((units // shards, width), jnp.float32),
        shape((shards, units // shards, width), low),
    ]
    dma, scratch = pltpu.SemaphoreType.DMA, pltpu.VMEM
    tile = 256
    outs = pl.pallas_call(
        functools.partial(sums_kernel, shards, plane),
        out_shape=out_shape,
        in_specs=[any_space] * 9 + [vmem],
        out_specs=[any_space] * 9 + [vmem] * 2,
        scratch_shapes=[
            scratch((shards, own_hidden, width), low),
            scratch((2, slots, hidden_width), low),
            scratch((2, slots, tile), low),
            scratch((2, plane * local, tile), low),
            scratch((2, tile, hidden_width), jnp.float32),
            scratch((2, tile, hidden_width), low),
            scratch((own_hidden, tile), jnp.float32),
            dma((3,)),
            dma((2, 2)),
            dma((5,)),
            dma((plane,)),
            dma((plane,)),
            dma((shards,)),
            dma((shards,)),
        ]
        + reduces * reduce_scratch(plane, count, local // count, width),
        compiler_params=pltpu.CompilerParams(
            collective_id=2, has_side_effects=True, vmem_limit_bytes=63 * 2**20
        ),
        name="sums",
    )(
        normed_part.reshape(pieces),
        output_part.reshape(pieces),
        token_scores,
        *expert_terms,
        *plane_terms,
        *shared_terms,
    )
    output_sum = outs[1].reshape(local, width)
    if reduces == 1:
        (output_sum,) = bundle(4, plane, shards, [("reduce", output_part)], 56 * 2**20)
    return (outs[0].reshape(local, width), output_sum) + tuple(outs[2:])


class Everyone:
    def __init__(self, place, plane, shards, source, got, send_sem, recv_sem, keep_sem):
        self.total = shards * plane
        self.plane = plane
        self.number = place.shard * plane + place.me
        self.source, self.got = source, got
        self.send_sem, self.recv_sem = send_sem, recv_sem
        self.keep = pltpu.make_async_copy(source(self.number), got.at[self.number], keep_sem)

    def copy(self, step, arriving):
        other = lax.rem(self.number + step, self.total)
        spot = other if arriving else self.number
        return remote(
            self.source(other),
            self.got.at[spot],
            self.send_sem.at[step],
            self.recv_sem.at[spot],
            {"shard": other // self.plane, "expert": lax.rem(other, self.plane)},
        )

    def start(self):
        self.keep.start()

        def body(step, _):
            self.copy(step, False).start()
            return 0

        lax.fori_loop(1, self.total, body, 0)

    def wait(self):
        self.keep.wait()

        def body(step, _):
            self.copy(step, True).wait_recv()
            return 0

        lax.fori_loop(1, self.total, body, 0)

    def finish(self):
        def body(step, _):
            self.copy(step, False).wait_send()
            return 0

        lax.fori_loop(1, self.total, body, 0)


def greet_everyone(place, plane, shards):
    barrier = pltpu.get_barrier_semaphore()
    total = shards * plane
    number = place.shard * plane + place.me

    def body(step, _):
        other = lax.rem(number + step, total)
        pl.semaphore_signal(
            barrier,
            inc=1,
            device_id={"shard": other // plane, "expert": lax.rem(other, plane)},
            device_id_type=MESH,
        )
        return 0

    lax.fori_loop(1, total, body, 0)
    pl.semaphore_wait(barrier, total - 1)


def norm_back(values, gain, grad):
    root = lax.rsqrt(jnp.mean(values * values, axis=1, keepdims=True) + EPS)
    weighted = grad * gain
    inner = jnp.mean(weighted * values, axis=1, keepdims=True)
    scaled = values * root
    return root * (weighted - scaled * (root * inner)), jnp.sum(grad * scaled, axis=0, keepdims=True)


def two_parts(values):
    high = values.astype(jnp.bfloat16)
    return high, (values - high.astype(jnp.float32)).astype(jnp.bfloat16)


def swapped_halves(pair):
    return pltpu.roll(pair, QK_ROPE // 2, 1)


def backward_kernel(shards, plane, scale, last, *refs):
    (back, scores, routes, middle, cotangent, tokens, first_gain, second_gain, latent_gain, router,
     lengths, query, keys, value, log_total, turn, sway, key_latent, up_head, head_out,
     compressed, full_out, full_query, full_down, normed_one, out_half, query_half, down_half, gate_send, up_send, narrow_send, down_own, down_sum_got,
     shared_moved, input_grad, query_out, up_out, down_out, out_out, small_out, shared_gate_out, shared_up_out,
     gate_got, up_got, narrow_got, mid_all, down_total,
     stream_buf, wq_buf, wd_buf, own_columns, own_compressed, heads_sum, mid_buf, low_buf, heads_buf, grad_buf, key_sum, value_sum,
     part_buf, trade_buf, trade_got, pair_buf, query_term, query_got, up_term, up_got_buf, own_query, low_grad, low_all,
     down_rows, down_got, out_rows, out_got, small_buf, small_got, key_got, total_buf, part_in, *sems) = refs
    (total_sem, part_sem, save_sem, load_sem, whole_sem, stream_sem, swap_send, swap_recv, trade_send, trade_recv, gather_send, gather_recv, gather_keep,
     all_send, all_recv, all_keep, rows_send, rows_recv, rows_keep, *reduce_scratch_refs) = sems
    low = jnp.bfloat16
    group = SEQ_DEVICES
    place = Place(group)
    local, width = middle.shape
    total = shards * plane
    ends = document_ends(lengths, (place.shard * plane + place.me) // group)
    sender = Sender()
    greet_everyone(place, plane, shards)
    members = [lax.rem(place.local + step, group) for step in range(1, group)]
    others = [lax.rem(place.shard + step, shards) for step in range(1, shards)]

    shares = []

    def share(number, source, got):
        for step, other in enumerate(others, 1):
            sender.start(
                place.always,
                remote(source.at[other], got.at[place.shard], swap_send.at[number, step],
                       swap_recv.at[number, place.shard], {"shard": other}),
            )
            shares.append(
                remote(source.at[other], got.at[other], swap_send.at[number, step], swap_recv.at[number, other],
                       {"shard": other})
            )

    share(0, gate_send, gate_got)
    numbers = iter(range(16))

    def load(source, target):
        copy = pltpu.make_async_copy(source, target, load_sem.at[next(numbers)])
        copy.start()
        return copy

    own_lanes = pl.ds(pl.multiple_of(place.local * 128, 128), 128)
    got_wd = whole_weight(place, others, down_half, full_down, wd_buf, whole_sem)
    got_columns = load(normed_one.at[:, :, :, own_lanes], own_columns)
    tile = stream_buf.shape[-1]
    tiles = [slice(at, at + tile) for at in range(0, width, tile)]

    def streamed(buf, count, sources):
        def copies(index):
            half = index % 2
            return [
                (there, pltpu.make_async_copy(source, target, stream_sem.at[half, number]))
                for there, source, target, number in sources(index, buf.at[half])
            ]

        def start(index):
            for there, copy in copies(index):
                @pl.when(there)
                def _():
                    copy.start()

        start(0)
        for index in range(count):
            if index + 1 < count:
                start(index + 1)
            for there, copy in copies(index):
                @pl.when(there)
                def _():
                    copy.wait()
            yield index, buf.at[index % 2]

    own_at = pl.ds(pl.multiple_of(place.local * local, local), local)
    per_shard = group // shards

    def columns_of(array):
        def sources(index, target):
            return [
                (place.always, array.at[pl.ds(shard * per_shard, per_shard), :, :, tiles[index]], target.at[shard], shard)
                for shard in range(shards)
            ]

        return sources

    def out_columns(index, target):
        found = []
        for shard in range(shards):
            mine = place.shard == shard
            found.append((mine, out_half.at[:, :, :, tiles[index]], target.at[shard], shard))
            found.append((~mine, full_out.at[shard, :, :, :, tiles[index]], target.at[shard], shard))
        return found

    row_tile = wq_buf.shape[1]
    own_rows = width // shards

    def query_rows(index, target):
        shard = index * row_tile // own_rows
        rows = slice(index * row_tile - shard * own_rows, (index + 1) * row_tile - shard * own_rows)
        mine = place.shard == shard
        return [(mine, query_half.at[rows], target, 0), (~mine, full_query.at[shard, rows], target, 0)]

    got_compressed = load(compressed, own_compressed)

    def everyone(index, source, got):
        return Everyone(place, plane, shards, source, got, all_send.at[index], all_recv.at[index], all_keep.at[index])

    def add_shards(own, got, result):
        rows, columns = own.shape
        size = 128 if rows % 128 == 0 else 176
        lanes = pl.ds(0, columns)

        def copies(index):
            half, at = index % 2, pl.ds(index * size, size)
            found = [pltpu.make_async_copy(own.at[at], total_buf.at[half, pl.ds(0, size), lanes], total_sem.at[half])]
            for step, other in enumerate(others):
                found.append(
                    pltpu.make_async_copy(
                        got.at[other, at], part_in.at[half, step, pl.ds(0, size), lanes], part_sem.at[half, step]
                    )
                )
            return found, pltpu.make_async_copy(
                total_buf.at[half, pl.ds(0, size), lanes], result.at[at], save_sem.at[half]
            )

        tiles_of = [copies(index) for index in range(rows // size)]
        for copy in tiles_of[0][0]:
            copy.start()
        for index, (loads, save) in enumerate(tiles_of):
            if index + 1 < len(tiles_of):
                if index:
                    tiles_of[index - 1][1].wait()
                for copy in tiles_of[index + 1][0]:
                    copy.start()
            for copy in loads:
                copy.wait()

            def body(chunk, _):
                at = pl.ds(pl.multiple_of(chunk * 16, 16), 16)
                total = total_buf[index % 2, at, lanes]
                for step in range(len(others)):
                    total = total + part_in[index % 2, step, at, lanes].astype(jnp.float32)
                total_buf[index % 2, at, lanes] = total
                return 0

            lax.fori_loop(0, size // 16, body, 0)
            save.start()
        for _, save in tiles_of[-2:]:
            save.wait()

    experts = router.shape[0]
    values = middle[...]
    root = lax.rsqrt(jnp.mean(values * values, axis=1, keepdims=True) + EPS)
    second_normed = (values * root * second_gain[...]).astype(low)
    logits = matmul_nt(router[...], second_normed)
    names = lax.broadcasted_iota(jnp.int32, (experts, local), 0)
    chosen = jnp.zeros((experts, local), jnp.float32)
    for choice in range(TOP):
        chosen = chosen + jnp.where(routes[choice : choice + 1, :] == names, 1.0, 0.0)
    logits = jnp.where(chosen > 0.0, logits, NEG)
    gates = jnp.exp(logits - jnp.max(logits, axis=0, keepdims=True)) * chosen
    gates = gates / jnp.sum(gates, axis=0, keepdims=True)
    gate_grad = jnp.concatenate([scores[index, :1, :] for index in range(experts)], axis=0)
    logit_grad = gates * (gate_grad - jnp.sum(gates * gate_grad, axis=0, keepdims=True))
    high, rest = two_parts(logit_grad)
    router_term = matmul(high, second_normed) + matmul(rest, second_normed)
    grad = back[...] + matmul_tn(high, router[...]) + matmul_tn(rest, router[...])
    row_grad, second_term = norm_back(values, second_gain[...], grad)
    mid_buf[...] = cotangent[...].astype(jnp.float32) + row_grad
    low_buf[...] = mid_buf[...].astype(low).reshape(low_buf.shape)

    for index, piece in streamed(stream_buf, len(tiles), out_columns):
        part = matmul_nt(low_buf[:, :, tiles[index]].reshape(local, tile), piece[...].reshape(-1, tile))
        heads_sum[...] = part if index == 0 else heads_sum[...] + part
    heads_buf[...] = heads_sum[...].astype(low)

    def lands(member):
        return heads_buf.at[:, pl.ds(pl.multiple_of(member * V_HEAD, V_HEAD), V_HEAD)]

    def head_trade(step, member, source):
        spot = pl.ds(pl.multiple_of(source * local, local), local)
        return remote(lands(member), grad_buf.at[spot, :], trade_send.at[0, step], trade_recv.at[0, source],
                      {"expert": place.base + member})

    keep_head = pltpu.make_async_copy(lands(place.local), grad_buf.at[own_at, :], load_sem.at[next(numbers)])
    keep_head.start()
    for step, member in enumerate(members):
        sender.start(place.always, head_trade(step, member, place.local))
    mid_run = gather_steps(place, low_buf, mid_all, gather_keep.at[0], gather_send.at[0], gather_recv.at[0], sender)
    next(mid_run)
    add_shards(down_own, down_sum_got, down_total)
    for step, member in enumerate(members):
        head_trade(step, member, member).wait_recv()
    keep_head.wait()

    key_sum[...] = jnp.zeros_like(key_sum)
    value_sum[...] = jnp.zeros_like(value_sum)

    def attend_tile(index, _):
        at = pl.ds(pl.multiple_of(index * QUERIES, QUERIES), QUERIES)
        window = pl.ds(pl.multiple_of(index * QUERIES, QUERIES), KEYS)
        tile, key_tile = query[at, :], keys[window, :]
        head_grad = jnp.where(query_documents(index, ends) < last, grad_buf[at, :], jnp.zeros((), low))
        scores_at = score_block(scale, index, ends, tile, key_tile)
        probs = jnp.exp(scores_at - log_total[at, :1])
        prob_grad = matmul_nt(head_grad, value[window, :])
        inner = jnp.sum(probs * prob_grad, axis=1, keepdims=True)
        raw_grad = (probs * (prob_grad - inner) * scale).astype(low)
        grads = matmul(raw_grad, key_tile)
        trade_buf[at, :QK_NOPE] = grads[:, :QK_NOPE].astype(low)
        pair = grads[:, QK_NOPE:]
        trade_buf[at, QK_NOPE:] = (pair * turn[at, :] - swapped_halves(pair) * sway[at, :]).astype(low)
        key_sum[window, :] += matmul_tn(raw_grad, tile)
        value_sum[window, :] += matmul_tn(probs.astype(low), head_grad)
        return 0

    blocks = query.shape[0] // QUERIES
    for index in range(blocks // 2):
        attend_tile(jnp.int32(index), 0)
    next(mid_run)
    for index in range(blocks // 2, blocks):
        attend_tile(jnp.int32(index), 0)
    next(mid_run)

    share(1, up_send, up_got)
    share(2, narrow_send, narrow_got)

    lane = lax.broadcasted_iota(jnp.int32, (QUERIES, 2 * QK_ROPE), 1)

    def key_tile(index, _):
        at = pl.ds(pl.multiple_of(index * QUERIES, QUERIES), QUERIES)
        later = pl.ds(pl.multiple_of(index * QUERIES + WINDOW, QUERIES), QUERIES)
        key_rope = pltpu.roll(key_sum[later, QK_NOPE:], QK_ROPE, 1).astype(low)
        trade_buf[at, QK_NOPE:] = jnp.where(lane < QK_ROPE, trade_buf[at, QK_NOPE:], key_rope)
        pair_buf[at, :QK_NOPE] = key_sum[later, :QK_NOPE].astype(low)
        pair_buf[at, QK_NOPE:] = value_sum[later, :].astype(low)
        part = matmul_nt(pair_buf[at, :], up_head[...]).astype(low)
        per = QUERIES // local
        part_buf[pl.ds(index * per, per)] = part.reshape((per,) + part_buf.shape[1:])
        return 0

    for index in range(blocks):
        key_tile(jnp.int32(index), 0)

    def token_trade(step, member, source):
        spot = pl.ds(pl.multiple_of(member * local, local), local)
        return remote(trade_buf.at[spot, :], trade_got.at[source], trade_send.at[1, step], trade_recv.at[1, source],
                      {"expert": place.base + member})

    reduce_run = reduce_steps(place, part_buf, key_got, reduce_scratch_refs, sender)
    next(reduce_run)
    keep_token = pltpu.make_async_copy(trade_buf.at[own_at, :], trade_got.at[place.local], load_sem.at[next(numbers)])
    keep_token.start()
    for step, member in enumerate(members):
        sender.start(place.always, token_trade(step, member, place.local))

    for index, piece in streamed(stream_buf, len(tiles), columns_of(normed_one)):
        term = matmul_tn(trade_buf[...], piece[...].reshape(SEQ, tile))
        per = tile // query_term.shape[1]
        query_term[index * per : (index + 1) * per] = term.T.astype(low).reshape((per,) + query_term.shape[1:])
    up_term[...] = matmul_tn(key_latent[...], pair_buf[...]).astype(low).reshape(up_term.shape)
    next(reduce_run)
    query_trade = everyone(1, lambda target: query_term.at[target], query_got)
    query_trade.start()
    up_trade = everyone(2, lambda target: up_term.at[target], up_got_buf)
    up_trade.start()
    units = shared_gate_out.shape[1] // total
    padded = shared_moved.shape[2] // (2 * shards)
    next(reduce_run)
    for member in range(plane):
        block = 0.0
        for shard in range(shards):
            block = block + shared_moved[shard * plane + member].astype(jnp.float32)
        for part, result in enumerate((shared_gate_out, shared_up_out)):
            for shard in range(shards):
                at = (part * shards + shard) * padded
                spot = (shard * plane + member) * units
                result[:, spot : spot + units] = block[:, at : at + units]
    drain(reduce_run)
    for step, member in enumerate(members):
        token_trade(step, member, member).wait_recv()
    keep_token.wait()

    got_compressed.wait()
    head_dim = QK_NOPE + QK_ROPE
    rope = jnp.zeros((local, 2 * QK_ROPE), jnp.float32)
    for head in range(group):
        own_query[:, head * head_dim : (head + 1) * head_dim] = trade_got[head, :, :head_dim]
        rope = rope + trade_got[head, :, QK_NOPE:].astype(jnp.float32)
    lane = lax.broadcasted_iota(jnp.int32, rope.shape, 1)
    rope = jnp.where(lane < QK_ROPE, pltpu.roll(rope, QK_ROPE, 1), rope)
    rope = rope * turn[own_at, :] - swapped_halves(rope) * sway[own_at, :]
    latent_grad, latent_term = norm_back(own_compressed[...], latent_gain[...], key_got[...].reshape(local, KV_RANK))
    low_grad[0, 0, :, :KV_RANK] = latent_grad.astype(low)
    low_grad[0, 0, :, KV_RANK:] = jnp.where(lane < QK_ROPE, rope, 0.0).astype(low)
    low_run = gather_steps(place, low_grad.at[0], low_all, gather_keep.at[1], gather_send.at[1], gather_recv.at[1], sender)
    next(low_run)
    for copy in got_wd:
        copy.wait()
    for index, piece in streamed(wq_buf, width // row_tile, query_rows):
        rows = slice(index * row_tile, (index + 1) * row_tile)
        shard = index * row_tile // own_rows
        within = slice(rows.start - shard * own_rows, rows.stop - shard * own_rows)
        term = matmul_nt(own_query[...], piece[...])
        input_grad[:, rows] = term + matmul_nt(low_grad[0, 0], wd_buf[shard, within, :])
    next(low_run)
    row_grad, first_term = norm_back(tokens[...].astype(jnp.float32), first_gain[...], input_grad[...])
    input_grad[...] = mid_buf[...] + row_grad
    next(low_run)
    drain(mid_run)
    per_lane = width // 128
    for block in range(per_lane):
        columns = slice(block * 128, (block + 1) * 128)
        small_buf[block, :experts, :] = router_term[:, columns]
        small_buf[block, experts : experts + 1, :] = second_term[:, columns]
        small_buf[block, experts + 1 : experts + 2, :] = first_term[:, columns]
        at = block // (per_lane * 128 // KV_RANK) * 128
        small_buf[block, experts + 2 : experts + 3, :] = latent_term[:, at : at + 128]
        small_buf[block, experts + 3 :, :] = jnp.zeros((small_buf.shape[1] - experts - 3, 128), jnp.float32)
    small_trade = everyone(3, lambda target: small_buf.at[target // (total // per_lane)], small_got)
    small_trade.start()
    drain(low_run)
    got_columns.wait()
    down = matmul_tn(own_columns[...].reshape(SEQ, -1), low_all[...].reshape(SEQ, -1))
    down_rows[...] = down.astype(low).reshape(down_rows.shape)
    down_trade = head_rows(place, plane, shards, down_rows, down_got, rows_keep.at[0], rows_send.at[0], rows_recv.at[0])[0]
    for index, piece in streamed(stream_buf, len(tiles), columns_of(mid_all)):
        term = matmul_tn(head_out[...], piece[...].reshape(SEQ, tile)).astype(low)
        out_rows[:, :, tiles[index]] = term.reshape(out_rows.shape[:2] + (tile,))
    out_trade = head_rows(place, plane, shards, out_rows, out_got, rows_keep.at[1], rows_send.at[1], rows_recv.at[1])[0]

    sequences = total // group
    query_trade.wait()
    up_trade.wait()
    for head in range(group):
        query_sum, up_sum = 0.0, 0.0
        for sequence in range(sequences):
            query_sum = query_sum + query_got[sequence * group + head].astype(jnp.float32)
            up_sum = up_sum + up_got_buf[sequence * group + head].astype(jnp.float32)
        query_out[:, head * head_dim : (head + 1) * head_dim] = query_sum[:, :head_dim]
        both = QK_NOPE + V_HEAD
        up_out[:, head * both : (head + 1) * both] = up_sum
    small_trade.wait()
    small_out[...] = small_got[0]

    def small_sum(source, _):
        small_out[...] += small_got[source]
        return 0

    lax.fori_loop(1, total, small_sum, 0)
    down_trade.wait()
    out_trade.wait()
    down_sum, out_sum = 0.0, 0.0
    for sequence in range(sequences):
        down_sum = down_sum + down_got[sequence].astype(jnp.float32)
        out_sum = out_sum + out_got[sequence].astype(jnp.float32)
    down_out[...] = down_sum[:, : down_out.shape[1]]
    out_out[...] = out_sum
    for arrival in shares:
        arrival.wait_recv()
    for trade in (query_trade, up_trade, small_trade):
        trade.finish()
    sender.finish()


def backward_pass(scale, last, small, tables, saved, weights, sends, owns, shared_moved, shared_width):
    shards, plane = lax.axis_size("shard"), lax.axis_size("expert")
    total = shards * plane
    low, shape = jnp.bfloat16, jax.ShapeDtypeStruct
    local, width = small[3].shape
    head_dim = QK_NOPE + QK_ROPE
    vmem, any_space = pl.BlockSpec(memory_space=pltpu.VMEM), pl.BlockSpec(memory_space=pl.ANY)
    inputs = list(small) + list(tables) + list(saved)
    spaces = [vmem] * len(inputs)
    spaces[len(small)] = pl.BlockSpec(memory_space=pltpu.SMEM)
    hbm = list(weights) + list(sends) + list(owns) + [shared_moved]
    gate_send, up_send, narrow_send = sends
    experts = small[9].shape[0]
    small_rows = experts + 3 + -(experts + 3) % 8
    own_width = width // total
    out_shape = [
        shape((local, width), jnp.float32),
        shape((own_width, HEADS * head_dim), jnp.float32),
        shape((KV_RANK // total, HEADS * (QK_NOPE + V_HEAD)), jnp.float32),
        shape((own_width, KV_RANK + QK_ROPE), jnp.float32),
        shape((own_width, width), jnp.float32),
        shape((small_rows, 128), jnp.float32),
        shape((own_width, shared_width), jnp.float32),
        shape((own_width, shared_width), jnp.float32),
        shape(gate_send.shape, low),
        shape(up_send.shape, low),
        shape(narrow_send.shape, low),
        shape((SEQ_DEVICES, PIECES, local // PIECES, width), low),
        shape(owns[0].shape, jnp.float32),
    ]
    hbm_out = 5
    dma, scratch = pltpu.SemaphoreType.DMA, pltpu.VMEM
    pieces = (PIECES, local // PIECES)
    down_width = weights[3].shape[2]
    row_count = 128 // own_width
    sequences = total // SEQ_DEVICES
    wide_head = 2 * QK_NOPE
    return pl.pallas_call(
        functools.partial(backward_kernel, shards, plane, scale, last),
        out_shape=out_shape,
        in_specs=spaces + [any_space] * (len(hbm) - 1) + [vmem],
        out_specs=[vmem] * (len(out_shape) - hbm_out) + [any_space] * hbm_out,
        scratch_shapes=[
            scratch((2, shards, SEQ_DEVICES // shards) + pieces + (512,), low),
            scratch((2, 256, HEADS * head_dim), low),
            scratch((shards, width // shards, down_width), low),
            scratch((SEQ_DEVICES,) + pieces + (128,), low),
            scratch((local, KV_RANK), jnp.float32),
            scratch((local, width), jnp.float32),
            scratch((local, width), jnp.float32),
            scratch(pieces + (width,), low),
            scratch((local, width), low),
            scratch((SEQ, V_HEAD), low),
            scratch((SEQ + WINDOW, wide_head), jnp.float32),
            scratch((SEQ + WINDOW, V_HEAD), jnp.float32),
            scratch((SEQ_DEVICES,) + pieces + (KV_RANK,), low),
            scratch((SEQ, wide_head), low),
            scratch((SEQ_DEVICES, local, wide_head), low),
            scratch((SEQ, wide_head), low),
            scratch((total, own_width, wide_head), low),
            scratch((total, own_width, wide_head), low),
            scratch((total, KV_RANK // total, wide_head), low),
            scratch((total, KV_RANK // total, wide_head), low),
            scratch((local, HEADS * head_dim), low),
            scratch((1, 1, local, down_width), low),
            scratch((SEQ_DEVICES, 1, local, down_width), low),
            scratch((row_count, own_width, down_width), low),
            scratch((sequences, own_width, down_width), low),
            scratch((row_count, own_width, width), low),
            scratch((sequences, own_width, width), low),
            scratch((width // 128, small_rows, 128), jnp.float32),
            scratch((total, small_rows, 128), jnp.float32),
            scratch(pieces + (KV_RANK,), jnp.float32),
            scratch((2, 176, width), jnp.float32),
            scratch((2, shards - 1, 176, width), low),
            dma((2,)),
            dma((2, shards)),
            dma((2,)),
            dma((8,)),
            dma((shards,)),
            dma((2, shards)),
            dma((3, shards)),
            dma((3, shards)),
            dma((2, SEQ_DEVICES)),
            dma((2, SEQ_DEVICES)),
            dma((2, 4, SEQ_DEVICES, PIECES)),
            dma((2, SEQ_DEVICES, PIECES)),
            dma((2,)),
            dma((4, total)),
            dma((4, total)),
            dma((4,)),
            dma((2, max(row_count, sequences))),
            dma((2, max(row_count, sequences))),
            dma((2,)),
        ]
        + reduce_scratch(SEQ_DEVICES, PIECES, local // PIECES, KV_RANK),
        compiler_params=pltpu.CompilerParams(
            collective_id=3, has_side_effects=True, vmem_limit_bytes=62 * 2**20
        ),
        name="backward",
    )(*inputs, *hbm)


def on_device(
    tokens,
    document_lengths,
    routes,
    first_gain,
    query_weight,
    latent_down,
    latent_gain,
    latent_up,
    output_weight,
    second_gain,
    router_weight,
    shared_gate,
    shared_up,
    shared_down,
    expert_gate,
    expert_up,
    expert_down,
    cotangent,
):
    local_rows, width = tokens.shape
    shards = lax.axis_size("shard")
    plane = lax.axis_size("expert")
    everyone = ("shard", "expert")
    all_devices = shards * plane
    shard_at = lax.axis_index("shard")
    plane_at = lax.axis_index("expert")
    head_at = plane_at % SEQ_DEVICES
    sequence_at = (shard_at * plane + plane_at) // SEQ_DEVICES
    capacity = local_rows * TOP * 4 // (3 * plane)
    head_dim = QK_NOPE + QK_ROPE
    scale = 1.0 / math.sqrt(head_dim)
    own_at = head_at * local_rows

    def own_rows(values):
        return lax.dynamic_slice_in_dim(values, own_at, local_rows, 0)

    piece_rows = output_weight.shape[0] // plane
    down_half = jnp.pad(latent_down, ((0, 0), (0, QK_ROPE)))
    units = shared_down.shape[0] // plane
    unit_pad = -units % 16
    padded_units = units + unit_pad
    gate_columns, up_columns = (
        jnp.concatenate(
            [
                jnp.pad(
                    lax.dynamic_slice_in_dim(
                        weight, index * shared_down.shape[0] + plane_at * units, units, 1
                    ),
                    ((0, 0), (0, unit_pad)),
                )
                for index in range(shards)
            ],
            axis=1,
        )
        for weight in (shared_gate, shared_up)
    )
    down_units = lax.dynamic_slice_in_dim(shared_down, plane_at * units, units, 0)
    down_units = jnp.pad(down_units, ((0, unit_pad), (0, 0)))

    def plane_pieces(weight):
        return weight.reshape(plane, 1, -1, weight.shape[1])

    angles = np.arange(SEQ)[:, None] * THETA ** (-np.arange(QK_ROPE // 2) / (QK_ROPE // 2))
    turn = jnp.asarray(np.tile(np.cos(angles), (1, 4)), jnp.float32)
    sway = jnp.asarray(np.tile(np.sin(angles), (1, 4)) * np.repeat([-1.0, 1.0, -1.0, 1.0], 32), jnp.float32)
    entry_count = document_lengths.shape[1]
    route_rows = jnp.pad(routes.T, ((0, 8 - TOP), (0, 0)), constant_values=-1)
    (
        all_normed,
        all_grads,
        all_routes,
        full_down,
        full_out,
        query_piece,
        gate_single,
        up_single,
        gate_shared,
        up_shared,
        down_shared,
        normed_one,
        query,
        keys,
        value,
        key_latent,
        compressed,
        head_out,
        log_total,
        middle,
        up_head,
    ) = forward_pass(
        scale,
        entry_count - 1,
        tokens,
        cotangent,
        (
            query_weight,
            plane_pieces(down_half),
            latent_up,
            plane_pieces(output_weight),
            plane_pieces(query_weight),
            expert_gate[0],
            expert_up[0],
            gate_columns,
            up_columns,
            down_units,
        ),
        route_rows,
        (first_gain[None], latent_gain[None], second_gain[None]),
        (turn, sway, document_lengths),
    )
    all_normed = all_normed.reshape(-1, width)
    all_grads = all_grads.reshape(-1, width)
    blocked = (SEQ_DEVICES, PIECES, local_rows // PIECES, width)
    shard_blocked = (shards, SEQ_DEVICES // shards) + blocked[1:]
    (
        slot_rows,
        slot_grad,
        normed_part,
        output_part,
        token_scores,
        hidden,
        gate_pre_grad,
        up_pre_grad,
        shared_hidden,
        shared_moved,
        _,
        full_query,
    ) = expert_pass(
        all_routes[:, 0],
        router_weight.T,
        all_normed,
        all_grads,
        (
            gate_columns,
            gate_shared,
            up_columns,
            up_shared,
            down_units,
            down_shared,
            expert_gate[0],
            gate_single,
            expert_up[0],
            up_single,
            expert_down[0],
        ),
        query_piece,
        capacity,
    )
    (
        back,
        output_sum,
        scores,
        down_blocks,
        down_own,
        gate_own,
        up_own,
        gate_send,
        up_send,
        shared_down_own,
        shared_down_send,
    ) = sums_pass(
        normed_part.reshape(plane, local_rows, width),
        output_part.reshape(plane, local_rows, width),
        token_scores,
        (slot_rows, slot_grad, hidden, gate_pre_grad, up_pre_grad),
        (all_grads,),
        (shared_hidden,),
    )
    activations = (middle + output_sum).astype(jnp.bfloat16)

    def sum_shards(own, blocks):
        for step in range(1, shards):
            own = own + lax.dynamic_index_in_dim(
                blocks, (shard_at + step) % shards, 0, keepdims=False
            ).astype(jnp.float32)
        return own

    (
        input_grad,
        query_weight_grad,
        latent_up_grad,
        latent_down_grad,
        output_weight_grad,
        small_sums,
        shared_gate_grad,
        shared_up_grad,
        gate_blocks,
        up_blocks,
        shared_blocks,
        _,
        expert_down_grad,
    ) = backward_pass(
        scale,
        entry_count - 1,
        (
            back,
            scores,
            route_rows,
            middle,
            cotangent,
            tokens,
            first_gain[None],
            second_gain[None],
            latent_gain[None],
            router_weight.T,
        ),
        (document_lengths, query, keys, value, log_total, turn, sway),
        (key_latent, up_head.reshape(KV_RANK, -1), head_out),
        (
            compressed,
            full_out.reshape(shard_blocked),
            full_query.reshape((shards,) + query_weight.shape),
            full_down.reshape((shards,) + down_half.shape),
            normed_one.reshape(blocked),
            output_weight.reshape(shard_blocked[1:]),
            query_weight,
            down_half,
        ),
        (gate_send, up_send, shared_down_send),
        (down_own, down_blocks),
        shared_moved,
        shared_gate.shape[1],
    )
    expert_gate_grad = sum_shards(gate_own, gate_blocks)
    expert_up_grad = sum_shards(up_own, up_blocks)
    shared_down_grad = sum_shards(shared_down_own, shared_blocks)[:units]
    own_width = width // all_devices
    number = shard_at * plane + plane_at
    own_small = lax.dynamic_slice_in_dim(small_sums, number * own_width % 128, own_width, 1)
    router_weight_grad = own_small[:plane].T
    second_gain_grad = own_small[plane]
    first_gain_grad = own_small[plane + 1]
    latent_width = KV_RANK // all_devices
    latent_gain_grad = lax.dynamic_slice_in_dim(
        small_sums[plane + 2], number * latent_width % 128, latent_width, 0
    )
    return (
        activations,
        input_grad,
        first_gain_grad,
        query_weight_grad,
        latent_down_grad,
        latent_gain_grad,
        latent_up_grad,
        output_weight_grad,
        second_gain_grad,
        router_weight_grad,
        shared_gate_grad,
        shared_up_grad,
        shared_down_grad,
        expert_gate_grad[None],
        expert_up_grad[None],
        expert_down_grad[None],
    )


def solution(mesh):
    return jax.shard_map(
        on_device,
        mesh=mesh,
        in_specs=(
            P(("shard", "expert"), None),
            P(),
            P(("shard", "expert"), None),
            P(),
            P("shard", None),
            P("shard", None),
            P(),
            P("shard", None),
            P("shard", None),
            P(),
            P(),
            P("shard", None),
            P("shard", None),
            P("shard", None),
            P("expert", "shard", None),
            P("expert", "shard", None),
            P("expert", "shard", None),
            P(("shard", "expert"), None),
        ),
        out_specs=(
            P(("shard", "expert"), None),
            P(("shard", "expert"), None),
            P(("shard", "expert")),
            P(("shard", "expert"), None),
            P(("shard", "expert"), None),
            P(("shard", "expert")),
            P(("shard", "expert"), None),
            P(("shard", "expert"), None),
            P(("shard", "expert")),
            P(("shard", "expert"), None),
            P(("shard", "expert"), None),
            P(("shard", "expert"), None),
            P(("shard", "expert"), None),
            P("expert", "shard", None),
            P("expert", "shard", None),
            P("expert", "shard", None),
        ),
        check_vma=False,
    )
```

```python
import functools
import math

import jax
import jax.numpy as jnp
import numpy as np
from jax import lax
from jax.experimental import pallas as pl
from jax.experimental.pallas import tpu as pltpu
from jax.sharding import PartitionSpec as P

HEADS = 16
QK_NOPE = 128
QK_ROPE = 64
V_HEAD = 128
KV_RANK = 512
TOP = 6
SEQ = 2048
WINDOW = 1024
TOK_DEV = 128
STEP_SENDERS = 4
SEQ_DEVICES = SEQ // TOK_DEV


EPS = 1e-06
THETA = 10000.0
NEG = -1e30
HIGH = lax.Precision.HIGHEST


def matmul(left, right):
    return jnp.dot(left, right, preferred_element_type=jnp.float32)


def matmul_tn(left, right):
    return lax.dot_general(
        left, right, (((0,), (0,)), ((), ())), preferred_element_type=jnp.float32
    )


def matmul_nt(left, right):
    return lax.dot_general(
        left, right, (((1,), (1,)), ((), ())), preferred_element_type=jnp.float32
    )


def norm_scale(values, gain):
    return values * lax.rsqrt(jnp.mean(values * values, axis=-1, keepdims=True) + EPS) * gain


def rotary_tables(positions, width):
    half = width // 2
    freqs = THETA ** (-jnp.arange(half, dtype=jnp.float32) / half)
    angles = positions.astype(jnp.float32)[:, None] * freqs[None, :]
    return (jnp.cos(angles), jnp.sin(angles))


def rotate(values, cosine_part, sine_part):
    half = values.shape[-1] // 2
    first = values[..., :half]
    second = values[..., half:]
    return jnp.concatenate(
        [first * cosine_part - second * sine_part, second * cosine_part + first * sine_part],
        axis=-1,
    )


def unrotate(values, cosine_part, sine_part):
    half = values.shape[-1] // 2
    first = values[..., :half]
    second = values[..., half:]
    return jnp.concatenate(
        [first * cosine_part + second * sine_part, second * cosine_part - first * sine_part],
        axis=-1,
    )


def swish_parts(values):
    sigmoid_part = jax.nn.sigmoid(values)
    return (values * sigmoid_part, sigmoid_part * (1.0 + values * (1.0 - sigmoid_part)))


MESH = pl.DeviceIdType.MESH
INNER = 4
PIECES = 2


class Sender:
    def __init__(self):
        self.started = []

    def start(self, there, copy):
        @pl.when(there)
        def _():
            copy.start()

        self.started.append((there, copy))

    def finish(self):
        for there, copy in self.started:
            @pl.when(there)
            def _():
                copy.wait_send()


def remote(source, target, send_sem, recv_sem, place):
    return pltpu.make_async_remote_copy(
        src_ref=source,
        dst_ref=target,
        send_sem=send_sem,
        recv_sem=recv_sem,
        device_id=place,
        device_id_type=MESH,
    )


class Place:
    def __init__(self, group):
        self.me = lax.axis_index("expert")
        self.shard = lax.axis_index("shard")
        self.group = group
        self.outer = group // INNER
        self.local = lax.rem(self.me, group)
        self.base = self.me - self.local
        self.level = self.local // INNER
        inner = lax.rem(self.local, INNER)
        self.row_step = 2 - 4 * (inner // 2)
        self.twin_step = 1 - 2 * lax.rem(inner, 2)
        self.always = self.me >= 0
        self.upper = self.level < self.outer - 1
        self.lower = self.level > 0

    def neighbours(self):
        return [
            (self.upper, {"expert": self.me + INNER}),
            (self.lower, {"expert": self.me - INNER}),
            (self.always, {"expert": self.me + self.row_step}),
            (self.always, {"expert": self.me + self.twin_step}),
        ]

    def along(self, step):
        below = (self.level >= step, self.local - step * INNER, self.upper, self.me + INNER, 0)
        above = (self.level + step < self.outer, self.local + step * INNER, self.lower, self.me - INNER, 1)
        return (below, above)


def greet(peers):
    barrier = pltpu.get_barrier_semaphore()
    for there, peer in peers:
        @pl.when(there)
        def _():
            pl.semaphore_signal(barrier, inc=1, device_id=peer, device_id_type=MESH)
    pl.semaphore_wait(barrier, sum(there.astype(jnp.int32) for there, _ in peers))


def gather_plan(place, own_ref, out_ref, copy_sem, send_sem, recv_sem):
    local = place.local
    pieces = out_ref.shape[1]
    row_at, twin_at = place.me + place.row_step, place.me + place.twin_step
    segments, sends = [[]], []

    def push(kind, block, piece, target, source=None):
        spot = out_ref.at[block, piece]
        return remote(
            spot if source is None else source.at[piece],
            spot,
            send_sem.at[kind, block, piece],
            recv_sem.at[block, piece],
            {"expert": target},
        )

    def start(there, copy):
        segments[-1].append((there, copy.start))
        sends.append((there, copy))

    def arrive(there, block, piece):
        segments[-1].append((there, push(0, block, piece, place.me).wait_recv))

    if own_ref is None:
        own_ref = out_ref.at[local]
    else:
        keep = pltpu.make_async_copy(own_ref, out_ref.at[local], copy_sem)
        segments[-1].append((place.always, keep.start))
    for piece in range(pieces):
        start(place.upper, push(0, local, piece, place.me + INNER, own_ref))
        start(place.lower, push(1, local, piece, place.me - INNER, own_ref))
        start(place.always, push(2, local, piece, row_at, own_ref))
        start(place.always, push(3, local, piece, twin_at, own_ref))
    for step in range(1, place.outer + 1):
        segments.append([])
        if step < place.outer:
            for piece in range(pieces):
                for there, block, onward, target, kind in place.along(step):
                    arrive(there, block, piece)
                    start(there & onward, push(kind, block, piece, target))
                    start(there, push(2, block, piece, row_at))
                    start(there, push(3, block, piece, twin_at))
        for piece in range(pieces):
            for there, block, *_ in place.along(step - 1)[: 1 if step == 1 else 2]:
                arrive(there, block + place.row_step, piece)
                start(there, push(3, block + place.row_step, piece, twin_at))
    segments.append([])
    for step in range(place.outer):
        for piece in range(pieces):
            for there, block, *_ in place.along(step)[: 1 if step == 0 else 2]:
                arrive(there, block + place.twin_step, piece)
                arrive(there, block + place.twin_step + place.row_step, piece)
    if copy_sem is not None:
        segments[-1].append((place.always, keep.wait))
    return segments, sends


def emit(actions):
    for there, action in actions:
        @pl.when(there)
        def _():
            action()


def gather_steps(place, own_ref, out_ref, copy_sem, send_sem, recv_sem, sender):
    segments, sends = gather_plan(place, own_ref, out_ref, copy_sem, send_sem, recv_sem)
    sender.started += sends
    for actions in segments:
        emit(actions)
        yield


def add_into(target, first, *others):
    rows = target.shape[0]
    chunk = 32

    def body(index, _):
        at = pl.ds(pl.multiple_of(index * chunk, chunk), chunk)
        total = first[at, :].astype(jnp.float32)
        for other in others:
            total = total + other[at, :].astype(jnp.float32)
        target[at, :] = total.astype(target.dtype)
        return 0

    lax.fori_loop(0, rows // chunk, body, 0)


def reduce_steps(place, part_ref, out_ref, scratch, sender, fine=False):
    (own_buf, twin_buf, row_buf, line_buf, load_sem, twin_send, twin_recv, row_send, row_recv, line_send, line_recv,
     out_buf, out_sem) = scratch
    outer, local, level = place.outer, place.local, place.level
    pieces = part_ref.shape[1]
    inner = lax.rem(local, INNER)
    row_bit, core = inner // 2, lax.rem(inner, 2)
    twin_at, row_at = {"expert": place.me + place.twin_step}, {"expert": place.me + place.row_step}
    order = []
    low, high = 0, outer - 1
    while low <= high:
        order += [high] if low == high else [high, low]
        low, high = low + 1, high - 1
    units = [(at, piece) for at in order for piece in range(pieces)]
    bits = (1 - row_bit, row_bit)

    def loading(at, piece, bit):
        where = at * 2 + bit
        return pltpu.make_async_copy(
            part_ref.at[at * INNER + bit * 2 + core, piece], own_buf.at[where, piece], load_sem.at[where, piece]
        )

    def to_twin(at, piece, bit):
        where = at * 2 + bit
        return remote(
            part_ref.at[at * INNER + bit * 2 + 1 - core, piece],
            twin_buf.at[where, piece],
            twin_send.at[where, piece],
            twin_recv.at[where, piece],
            twin_at,
        )

    def to_row(at, piece):
        return remote(
            own_buf.at[at * 2 + bits[0], piece], row_buf.at[at, piece], row_send.at[at, piece], row_recv.at[at, piece], row_at
        )

    def mine(at, piece):
        return own_buf.at[at * 2 + row_bit, piece]

    def to_line(side, at, piece):
        return remote(
            mine(at, piece),
            line_buf.at[side, at, piece],
            line_send.at[side, at, piece],
            line_recv.at[side, at, piece],
            {"expert": place.me + (INNER if side == 0 else -INNER)},
        )

    for at, piece in units:
        for bit in bits:
            sender.start(place.always, to_twin(at, piece, bit))
            loading(at, piece, bit).start()
    yield
    for at, piece in units:
        for bit in bits:
            where = at * 2 + bit
            loading(at, piece, bit).wait()
            to_twin(at, piece, bit).wait_recv()
            add_into(own_buf.at[where, piece], own_buf.at[where, piece], twin_buf.at[where, piece])
            if bit is bits[0]:
                sender.start(place.always, to_row(at, piece))
        if fine:
            yield
    if not fine:
        yield
    for at, piece in units:
        to_row(at, piece).wait_recv()
        spot, row = mine(at, piece), row_buf.at[at, piece]
        for side, there, first in ((0, level < at, level == 0), (1, level > at, level == outer - 1)):
            line = to_line(side, at, piece)

            @pl.when(there & first)
            def _():
                add_into(spot, spot, row)

            @pl.when(there & ~first)
            def _():
                line.wait_recv()
                add_into(spot, spot, row, line_buf.at[side, at, piece])

            sender.start(there, line)
        if fine:
            yield
    if not fine:
        yield
    for at, piece in units:
        @pl.when(level == at)
        def _():
            parts = [mine(at, piece), row_buf.at[at, piece]]
            for side, there in ((0, at > 0), (1, at < outer - 1)):
                if there:
                    to_line(side, at, piece).wait_recv()
                    parts.append(line_buf.at[side, at, piece])
            add_into(out_buf.at[piece], *parts)
    done = pltpu.make_async_copy(out_buf, out_ref, out_sem)
    done.start()
    done.wait()
    yield


def reduce_scratch(group, pieces, rows, columns):
    outer = group // INNER
    bf = jnp.bfloat16
    pair, single, line = (2 * outer, pieces), (outer, pieces), (2, outer, pieces)
    block = (rows, columns)
    return [
        pltpu.VMEM(pair + block, bf),
        pltpu.VMEM(pair + block, bf),
        pltpu.VMEM(single + block, bf),
        pltpu.VMEM(line + block, bf),
        pltpu.SemaphoreType.DMA(pair),
        pltpu.SemaphoreType.DMA(pair),
        pltpu.SemaphoreType.DMA(pair),
        pltpu.SemaphoreType.DMA(single),
        pltpu.SemaphoreType.DMA(single),
        pltpu.SemaphoreType.DMA(line),
        pltpu.SemaphoreType.DMA(line),
        pltpu.VMEM((pieces,) + block, jnp.float32),
        pltpu.SemaphoreType.DMA(()),
    ]


class HeadRows:
    def __init__(self, started, received):
        self.started, self.received = started, received

    def wait(self):
        for there, local, copy, keep in self.started:
            @pl.when(there)
            def _():
                copy.wait_send()

            @pl.when(local)
            def _():
                keep.wait()
        for there, copy in self.received:
            @pl.when(there)
            def _():
                copy.wait_recv()


def head_rows(place, plane, shards, own_ref, out_ref, copy_sem, send_sem, recv_sem):
    count = own_ref.shape[0]
    number = place.shard * plane + place.me
    sequences = plane // place.group
    mine = place.shard * sequences + place.me // place.group
    started, received = [], []
    for index in range(count):
        target = place.local * count + index
        peer = {"shard": target // plane, "expert": lax.rem(target, plane)}
        copy = remote(own_ref.at[index], out_ref.at[mine], send_sem.at[index], recv_sem.at[mine], peer)
        keep = pltpu.make_async_copy(own_ref.at[index], out_ref.at[mine], copy_sem)

        @pl.when(target != number)
        def _():
            copy.start()

        @pl.when(target == number)
        def _():
            keep.start()

        started.append((target != number, target == number, copy, keep))
    for shard in range(shards):
        for sequence in range(sequences):
            source = shard * plane + sequence * place.group + number // count
            slot = shard * sequences + sequence
            peer = {"shard": source // plane, "expert": lax.rem(source, plane)}
            copy = remote(own_ref.at[0], out_ref.at[slot], send_sem.at[0], recv_sem.at[slot], peer)
            received.append((source != number, copy))
    return HeadRows(started, received), []


def bundle_kernel(group, shards, kinds, *refs):
    count = len(kinds)
    ins, outs, rest = refs[:count], refs[count : 2 * count], refs[2 * count :]
    place = Place(group)
    plane = lax.axis_size("expert")
    peers = []
    if "gather" in kinds or "reduce" in kinds:
        peers += place.neighbours()
    members = [{"expert": place.base + lax.rem(place.local + step, group)} for step in range(1, group)]
    if "trade" in kinds:
        peers = [(place.always, member) for member in members]
    across = [{"shard": lax.rem(place.shard + step, shards)} for step in range(1, shards)]
    if "swap" in kinds or "share" in kinds:
        peers += [(place.always, peer) for peer in across]
    everyone = []
    if "owners" in kinds or "rows" in kinds:
        total = shards * plane
        number = place.shard * plane + place.me
        for step in range(1, total):
            target = lax.rem(number + step, total)
            everyone.append((target, {"shard": target // plane, "expert": lax.rem(target, plane)}))
        peers = [(place.always, peer) for _, peer in everyone]
    greet(peers)
    sender = Sender()
    runs, waits = [], []
    for kind, own, out in zip(kinds, ins, outs):
        if kind == "gather":
            copy_sem, send_sem, recv_sem, *rest = rest
            runs.append(gather_steps(place, own, out, copy_sem, send_sem, recv_sem, sender))
        elif kind == "reduce":
            scratch, rest = rest[:13], rest[13:]
            runs.append(reduce_steps(place, own, out, scratch, sender))
        else:
            copy_sem, send_sem, recv_sem, *rest = rest
            if kind == "swap":
                mine, source = place.shard, lambda target: own
                targets = [(lax.rem(place.shard + step, shards), peer) for step, peer in enumerate(across, 1)]
            elif kind == "share":
                mine, source = place.shard, lambda target: own.at[target]
                targets = [(lax.rem(place.shard + step, shards), peer) for step, peer in enumerate(across, 1)]
            elif kind == "trade":
                mine, source = place.local, lambda target: own.at[target]
                targets = [(lax.rem(place.local + step, group), peer) for step, peer in enumerate(members, 1)]
            elif kind == "owners":
                mine, source = place.shard * plane + place.me, lambda target: own.at[target]
                targets = everyone
            else:
                waits.append(head_rows(place, plane, shards, own, out, copy_sem, send_sem, recv_sem))
                continue
            keep = None
            if kind != "share":
                keep = pltpu.make_async_copy(source(mine), out.at[mine], copy_sem)
                keep.start()
            total = len(targets) + 1
            copies = []
            for step, (target, peer) in enumerate(targets, 1):
                copy = remote(source(target), out.at[mine], send_sem.at[step], recv_sem.at[step], peer)
                copy.start()
                copies.append(copy)
            waits.append((keep, copies))
    while runs:
        runs = [run for run in runs if next(run, "end") != "end"]
    for keep, copies in waits:
        if keep is not None:
            keep.wait()
        for copy in copies:
            copy.wait()
    sender.finish()


def bundle(number, group, shards, transfers, limit=48 * 2**20):
    kinds, arrays, shapes, scratch = [], [], [], []
    members = shards * lax.axis_size("expert")
    for kind, array in transfers:
        kinds.append(kind)
        sems = [pltpu.SemaphoreType.DMA(())]
        if kind == "gather":
            pieces = PIECES if array.shape[0] % (16 * PIECES) == 0 else 1
            array = array.reshape((pieces, array.shape[0] // pieces) + array.shape[1:])
            shape = (group,) + array.shape
            sems += [pltpu.SemaphoreType.DMA((4, group, pieces)), pltpu.SemaphoreType.DMA((group, pieces))]
        elif kind == "reduce":
            pieces = 2 * PIECES
            array = array.reshape(group, pieces, array.shape[1] // pieces, array.shape[2])
            shape = array.shape[1:]
            sems = reduce_scratch(group, *shape)
        else:
            total = {"swap": shards, "share": shards, "trade": group, "owners": members}.get(kind)
            shape = ((total,) + array.shape) if kind == "swap" else array.shape
            if kind == "rows":
                total = max(array.shape[0], members // group)
                shape = (members // group,) + array.shape[1:]
            sems += [pltpu.SemaphoreType.DMA((total,)), pltpu.SemaphoreType.DMA((total,))]
        arrays.append(array)
        shapes.append(jax.ShapeDtypeStruct(shape, jnp.float32 if kind == "reduce" else array.dtype))
        scratch += sems
    outs = pl.pallas_call(
        functools.partial(bundle_kernel, group, shards, tuple(kinds)),
        out_shape=shapes,
        in_specs=[pl.BlockSpec(memory_space=pl.ANY)] * len(arrays),
        out_specs=[pl.BlockSpec(memory_space=pl.ANY)] * len(arrays),
        scratch_shapes=scratch,
        compiler_params=pltpu.CompilerParams(
            collective_id=number, has_side_effects=True, vmem_limit_bytes=limit
        ),
        name="bundle_" + "_".join(kinds[:2]),
    )(*arrays)
    done = []
    for (kind, array), out in zip(transfers, outs):
        if kind == "gather":
            out = out.reshape((group,) + array.shape)
        if kind == "reduce":
            out = out.reshape(array.shape[1:])
        done.append(out)
    return done


def pieces_of(size, most):
    return [(at, min(most, size - at)) for at in range(0, size, most)]


def expert_kernel(shards, *refs):
    (routes_ref, router_ref, rows_in, grads_in, shared_gate_own, shared_gate_got, shared_up_own, shared_up_got,
     shared_down_own, shared_down_got, gate_own, gate_got, up_own, up_got, narrow_own, query_piece, all_rows,
     rows_ref, grad_ref, back_ref, out_ref, score_ref, hidden_ref, gate_back_ref, up_back_ref, shared_hidden_ref,
     shared_got, narrow_got, full_query,
     cotangent, hidden, gate_part, up_part, pick_all, gate_all, shared_hidden, shared_gate_back, shared_up_back,
     gate_w, up_w, down_w, shared_gate_w, shared_up_w, shared_down_w,
     wide_buf, shared_term, weight_sem, save_sem, wide_sem, owner_send, owner_recv, owner_keep, swap_send, swap_recv, piece_keep, piece_send, piece_recv) = refs
    low = jnp.bfloat16
    turn, step = pl.program_id(0), pl.program_id(1)
    steps = pl.num_programs(1)
    width, hidden_width = gate_w.shape
    own_width = width // shards
    senders, _, rows = routes_ref.shape
    slots, tokens = pick_all.shape[1:]
    capacity = slots // senders
    experts = router_ref.shape[0]
    plane = full_query.shape[1]
    place = Place(plane)
    me = place.me
    sender = Sender()
    others = [lax.rem(place.shard + other, shards) for other in range(1, shards)]

    def at_step(number, turn_at=0):
        return pl.when((turn == turn_at) & (step == number))

    arrivals = []
    for number, other in enumerate(others, 1):
        push = remote(narrow_own, narrow_got.at[place.shard], swap_send.at[number], swap_recv.at[place.shard], {"shard": other})
        arrivals.append(remote(narrow_own, narrow_got.at[other], swap_send.at[number], swap_recv.at[other], {"shard": other}))
        sender.started.append((place.always, push))
    pushes = [copy for _, copy in sender.started]
    plans = [
        gather_plan(
            place, query_piece.at[other], full_query.at[other], piece_keep.at[number], piece_send.at[number],
            piece_recv.at[number],
        )
        for number, other in enumerate(others)
    ]
    segments = [sum(parts, []) for parts in zip(*[plan[0] for plan in plans])]
    for plan in plans:
        sender.started += plan[1]

    def loading(source, target, index, number):
        return pltpu.make_async_copy(source, target, weight_sem.at[index, number])

    def loads_of(index, own, got, target):
        copies = []
        for number in range(shards):
            at = lax.rem(place.shard + number, shards)
            block = own.shape[0]
            spot = target.at[at] if len(target.shape) == 3 else target.at[pl.ds(pl.multiple_of(at * block, 16), block), :]
            copies.append(loading(own if number == 0 else got.at[at], spot, index, number))
        return copies

    early = (
        loads_of(0, shared_gate_own, shared_gate_got, shared_gate_w)
        + loads_of(1, shared_up_own, shared_up_got, shared_up_w)
        + loads_of(2, shared_down_own, shared_down_got, shared_down_w)
        + loads_of(3, gate_own, gate_got, gate_w)
        + loads_of(4, up_own, up_got, up_w)
    )
    late = loads_of(5, narrow_own, narrow_got, down_w)

    to_owners = Everyone(
        place, plane, shards, lambda target: shared_term.at[target], shared_got, owner_send, owner_recv, owner_keep
    )

    @at_step(0)
    def _():
        greet_everyone(place, plane, shards)
        for push in pushes:
            push.start()
        for load in early:
            load.start()
        emit(segments[0])

    for number in range(1, len(segments)):

        @at_step(number if number < 4 else min(number - 4, 2), number // 4 and 1)
        def _():
            emit(segments[number])

    at_slots = pl.ds(pl.multiple_of(step * slots, slots), slots)
    at_tokens = pl.ds(pl.multiple_of(step * tokens, tokens), tokens)

    @pl.when(turn == 0)
    def _():
        logits = matmul_nt(router_ref[...], rows_in[...])
        names = lax.broadcasted_iota(jnp.int32, (experts, rows), 0)
        earlier = lax.broadcasted_iota(jnp.int32, (rows, rows), 0) <= lax.broadcasted_iota(jnp.int32, (rows, rows), 1)
        earlier = jnp.where(earlier, 1.0, 0.0).astype(low)
        slot_names = lax.broadcasted_iota(jnp.int32, (capacity, rows), 0).astype(jnp.float32)
        pick_buf, gate_buf = pick_all.at[step], gate_all.at[at_slots, :]
        pick_buf[...] = jnp.zeros(pick_buf.shape, low)
        for number in range(senders):
            routed = routes_ref[number]
            chosen = jnp.zeros((experts, rows), jnp.float32)
            for choice in range(TOP):
                chosen = chosen + jnp.where(routed[choice : choice + 1] == names, 1.0, 0.0)
            logit = jnp.where(chosen > 0.0, logits[:, number * rows : (number + 1) * rows], NEG)
            expo = jnp.exp(logit - jnp.max(logit, axis=0, keepdims=True)) * chosen
            dense = expo / jnp.sum(expo, axis=0, keepdims=True)
            gate_row = jnp.sum(jnp.where(names == me, dense, 0.0), axis=0, keepdims=True)
            mark = jnp.sum(jnp.where(routed == me, 1.0, 0.0), axis=0, keepdims=True)
            rank = matmul(jnp.broadcast_to(mark, (8, rows)).astype(low), earlier)[:1] - 1.0
            pick = jnp.where((slot_names == rank) & (mark > 0.0), 1.0, 0.0)
            at = slice(number * capacity, (number + 1) * capacity)
            pick_buf[at, number * rows : (number + 1) * rows] = pick.astype(low)
            gate_buf[at, :] = jnp.sum(pick * gate_row, axis=1, keepdims=True)
        gate = gate_buf[...]

        def pick_step(index, _):
            at = pl.ds(pl.multiple_of(index * 512, 512), 512)
            rows_ref[:, at] = matmul(pick_buf[...], rows_in[:, at]).astype(low)
            picked = matmul(pick_buf[...], grads_in[:, at])
            cotangent[at_slots, at] = picked.astype(low)
            grad_ref[:, at] = (gate * picked).astype(low)
            return 0

        lax.fori_loop(0, width // 512, pick_step, 0)

        @pl.when(step == 0)
        def _():
            for load in early:
                load.wait()

        shared_pre, shared_up = 0.0, 0.0
        for shard in range(shards):
            part = rows_in[:, shard * own_width : (shard + 1) * own_width]
            shared_pre = shared_pre + matmul(part, shared_gate_w[shard])
            shared_up = shared_up + matmul(part, shared_up_w[shard])
        swished, slope = swish_parts(shared_pre)
        shared_hidden[at_tokens, :] = (swished * shared_up).astype(low)
        shared_grad = matmul_nt(grads_in[...], shared_down_w[...])
        shared_gate_back[at_tokens, :] = (shared_grad * shared_up * slope).astype(low)
        shared_up_back[at_tokens, :] = (shared_grad * swished).astype(low)
        for at, size in pieces_of(hidden_width, 512):
            columns = slice(at, at + size)
            gate_pre = matmul(rows_ref[...], gate_w[:, columns])
            up_pre = matmul(rows_ref[...], up_w[:, columns])
            swished, slope = swish_parts(gate_pre)
            hidden[at_slots, columns] = (swished * up_pre).astype(low)
            gate_part[at_slots, columns] = (up_pre * slope).astype(low)
            up_part[at_slots, columns] = swished.astype(low)

    @at_step(0, 1)
    def _():
        tile = wide_buf.shape[2]
        units = shared_hidden.shape[1]
        per = tile // shared_term.shape[1]
        copies = [
            pltpu.make_async_copy(all_rows.at[:, at : at + tile], wide_buf.at[index % 2], wide_sem.at[index % 2])
            for index, at in enumerate(range(0, width, tile))
        ]
        copies[0].start()
        for index, copy in enumerate(copies):
            if index + 1 < len(copies):
                copies[index + 1].start()
            copy.wait()
            spot = slice(index * per, (index + 1) * per)
            shape = (per, shared_term.shape[1], units)
            for part, grads in enumerate((shared_gate_back, shared_up_back)):
                term = matmul_tn(wide_buf[index % 2], grads[...]).astype(low)
                shared_term[spot, :, part * units : (part + 1) * units] = term.reshape(shape)
        for arrival in arrivals:
            arrival.wait_recv()
        to_owners.start()
        for load in late:
            load.start()
        for load in late:
            load.wait()

    @pl.when(turn == 1)
    def _():
        gate = gate_all[at_slots, :]
        pick = pick_all[step]
        slot_grad = (gate * cotangent[at_slots, :].astype(jnp.float32)).astype(low)
        for at, size in pieces_of(hidden_width, 512):
            columns = slice(at, at + size)
            hidden_grad = matmul_nt(slot_grad, down_w[columns, :])
            gate_part[at_slots, columns] = (hidden_grad * gate_part[at_slots, columns].astype(jnp.float32)).astype(low)
            up_part[at_slots, columns] = (hidden_grad * up_part[at_slots, columns].astype(jnp.float32)).astype(low)

        def out_step(index, score):
            at = pl.ds(pl.multiple_of(index * 512, 512), 512)
            shard = index * 512 // own_width
            within = pl.ds(pl.multiple_of(index * 512 - shard * own_width, 512), 512)
            expert_out = matmul(hidden[at_slots, :], down_w[:, at]).astype(low).astype(jnp.float32)
            score = score + jnp.sum(expert_out * cotangent[at_slots, at].astype(jnp.float32), axis=1, keepdims=True)
            out = matmul_tn(pick, (gate * expert_out).astype(low))
            out_ref[:, at] = (out + matmul(shared_hidden[at_tokens, :], shared_down_w[:, at])).astype(low)
            row_back = matmul_nt(gate_part[at_slots, :], gate_w[at, :]) + matmul_nt(up_part[at_slots, :], up_w[at, :])
            back = (
                matmul_tn(pick, row_back.astype(low))
                + matmul_nt(shared_gate_back[at_tokens, :], shared_gate_w[shard, within, :])
                + matmul_nt(shared_up_back[at_tokens, :], shared_up_w[shard, within, :])
            )
            back_ref[:, at] = back.astype(low)
            return score

        score = lax.fori_loop(0, width // 512, out_step, jnp.zeros((slots, 1), jnp.float32))
        for number in range(senders):
            at = slice(number * capacity, (number + 1) * capacity)
            own_pick = pick[at, number * rows : (number + 1) * rows].astype(jnp.float32)
            total = jnp.sum(own_pick * score[at], axis=0, keepdims=True)
            score_ref[number] = jnp.broadcast_to(total, score_ref.shape[1:])

    @pl.when((turn == 1) & (step == steps - 1))
    def _():
        saves = [
            pltpu.make_async_copy(source, target, save_sem.at[index])
            for index, (source, target) in enumerate(
                (
                    (hidden, hidden_ref),
                    (gate_part, gate_back_ref),
                    (up_part, up_back_ref),
                    (shared_hidden, shared_hidden_ref),
                )
            )
        ]
        for save in saves:
            save.start()
        for save in saves:
            save.wait()
        to_owners.wait()
        to_owners.finish()
        sender.finish()


def expert_pass(routes, router, rows, grads, weights, query_piece, capacity):
    plane, _, local = routes.shape
    senders = STEP_SENDERS
    tokens, slots = senders * local, senders * capacity
    steps = plane // senders
    shards = weights[1].shape[0]
    width, hidden_width = rows.shape[1], weights[6].shape[1]
    units = weights[0].shape[1]
    low = jnp.bfloat16
    total = steps * slots
    shape, scratch, dma = jax.ShapeDtypeStruct, pltpu.VMEM, pltpu.SemaphoreType.DMA
    any_space = pl.BlockSpec(memory_space=pl.ANY)

    def first(r, c):
        return pl.BlockSpec((r, c), lambda turn, i: (i + turn * (steps - 1 - i), 0))

    def second(r, c):
        return pl.BlockSpec((r, c), lambda turn, i: (i * turn, 0))

    return pl.pallas_call(
        functools.partial(expert_kernel, shards),
        grid=(2, steps),
        out_shape=[
            shape((total, width), low),
            shape((total, width), low),
            shape((steps * tokens, width), low),
            shape((steps * tokens, width), low),
            shape((plane, 8, local), jnp.float32),
            shape((total, hidden_width), low),
            shape((total, hidden_width), low),
            shape((total, hidden_width), low),
            shape((steps * tokens, units), low),
            shape((shards * plane, width // (shards * plane), 2 * units), low),
            shape((shards,) + weights[10].shape, low),
            shape((shards, plane) + query_piece.shape[1:], low),
        ],
        in_specs=[
            pl.BlockSpec((senders, 8, local), lambda turn, i: (i + turn * (steps - 1 - i), 0, 0)),
            pl.BlockSpec(router.shape, lambda turn, i: (0, 0), pipeline_mode=pl.Buffered(1)),
            first(tokens, width),
            first(tokens, width),
        ]
        + [any_space] * (len(weights) + 2),
        out_specs=[
            first(slots, width),
            first(slots, width),
            second(tokens, width),
            second(tokens, width),
            pl.BlockSpec((senders, 8, local), lambda turn, i: (i * turn, 0, 0)),
        ]
        + [any_space] * 7,
        scratch_shapes=[
            scratch((total, width), low),
            scratch((total, hidden_width), low),
            scratch((total, hidden_width), low),
            scratch((total, hidden_width), low),
            scratch((steps, slots, tokens), low),
            scratch((total, 1), jnp.float32),
            scratch((steps * tokens, units), low),
            scratch((steps * tokens, units), low),
            scratch((steps * tokens, units), low),
            scratch((width, hidden_width), low),
            scratch((width, hidden_width), low),
            scratch((hidden_width, width), low),
            scratch((shards, width // shards, units), low),
            scratch((shards, width // shards, units), low),
            scratch((units, width), low),
            scratch((2, steps * tokens, 128), low),
            scratch((shards * plane, width // (shards * plane), 2 * units), low),
            dma((6, shards)),
            dma((6,)),
            dma((2,)),
            dma((shards * plane,)),
            dma((shards * plane,)),
            dma(()),
            dma((shards,)),
            dma((shards,)),
            dma((shards,)),
            dma((shards, 4, plane, 1)),
            dma((shards, plane, 1)),
        ],
        compiler_params=pltpu.CompilerParams(
            vmem_limit_bytes=63 * 2**20,
            dimension_semantics=("arbitrary", "arbitrary"),
            collective_id=5,
            has_side_effects=True,
        ),
        name="experts",
    )(routes, router, rows, grads, *weights, query_piece, rows)


QUERIES = 256
KEYS = WINDOW + QUERIES


def document_ends(lengths, sequence):
    ends, total = [], 0
    for entry in range(lengths.shape[1]):
        total = total + lengths[sequence, entry]
        ends.append(total)
    return ends


def documents_at(positions, ends):
    inside = sum(jnp.where(positions >= end, 1, 0) for end in ends)
    return jnp.where(positions < 0, -1, inside)


def query_documents(index, ends):
    return documents_at(lax.broadcasted_iota(jnp.int32, (QUERIES, 1), 0) + index * QUERIES, ends)


def score_block(scale, index, ends, query, keys):
    raw = matmul_nt(query, keys) * scale
    query_docs = query_documents(index, ends)
    key_docs = documents_at(lax.broadcasted_iota(jnp.int32, (1, KEYS), 1) + (index * QUERIES - WINDOW), ends)
    row = lax.broadcasted_iota(jnp.int32, raw.shape, 0) + WINDOW
    column = lax.broadcasted_iota(jnp.int32, raw.shape, 1)
    allowed = (query_docs == key_docs) & (column <= row) & (column > row - WINDOW)
    return jnp.where(allowed, raw, NEG)


class Swaps:
    def __init__(self, place, shards, sender):
        self.place, self.shards, self.sender = place, shards, sender

    def start(self, source, target, send_sem, recv_sem, keep=None):
        place, shards = self.place, self.shards
        arrivals = []
        for step in range(1, shards):
            other = lax.rem(place.shard + step, shards)
            self.sender.start(
                place.always,
                remote(source, target(place.shard), send_sem.at[step], recv_sem.at[place.shard], {"shard": other}),
            )
            arrivals.append(
                remote(source, target(other), send_sem.at[step], recv_sem.at[other], {"shard": other})
            )
        if keep is not None:
            copy = pltpu.make_async_copy(source, target(place.shard), keep)
            copy.start()

        def wait():
            for arrival in arrivals:
                arrival.wait_recv()
            if keep is not None:
                copy.wait()

        return wait


def whole_weight(place, others, own_ref, full_ref, buf, sem):
    copies = [pltpu.make_async_copy(own_ref, buf.at[place.shard], sem.at[0])]
    for step, other in enumerate(others, 1):
        copies.append(pltpu.make_async_copy(full_ref.at[other], buf.at[other], sem.at[step]))
    for copy in copies:
        copy.start()
    return copies


def drain(run):
    for _ in run:
        pass


def forward_kernel(shards, plane, scale, last, *refs):
    (tokens, cotangent, query_cols, down_half, up_half, out_half, query_half, gate_half, wide_half,
     shared_gate, shared_up, shared_down, routes, first_gain, latent_gain, second_gain, turn, sway, lengths,
     all_normed, all_grads, all_routes, full_down, full_out, query_piece, full_gate, full_up,
     full_shared_gate, full_shared_up, full_shared_down, normed_one,
     query, keys, value, key_latent, compressed, head_out, log_total, middle, up_buf,
     token_buf, normed_buf, query_buf, down_buf, out_buf, heads_buf, second_buf,
     swap_send, swap_recv, keep_sem, gather_send, gather_recv, gather_keep, piece_send, piece_recv,
     trade_send, trade_recv, load_sem, whole_sem) = refs
    low = jnp.bfloat16
    group = SEQ_DEVICES
    place, wide = Place(group), Place(plane)
    width = tokens.shape[-1]
    rows = middle.shape[0]
    ends = document_ends(lengths, (place.shard * plane + place.me) // group)
    sender = Sender()
    members = [lax.rem(place.local + step, group) for step in range(1, group)]
    peers = [(place.always, {"expert": place.base + member}) for member in members]
    if plane != group:
        peers += [
            (wide.upper & ~place.upper, {"expert": place.me + INNER}),
            (wide.lower & ~place.lower, {"expert": place.me - INNER}),
        ]
    others = [lax.rem(place.shard + step, shards) for step in range(1, shards)]
    peers += [(place.always, {"shard": other}) for other in others]
    greet(peers)

    swaps = Swaps(place, shards, sender)
    numbers = iter(range(16))

    def swap(source, target, keep=False):
        at = next(numbers)
        return swaps.start(
            source, target, swap_send.at[at], swap_recv.at[at], keep_sem.at[at] if keep else None
        )

    at_piece = lambda ref: ref.at[wide.me]
    head_dim = QK_NOPE + QK_ROPE
    start = place.local * head_dim // 128 * 128
    odd = lax.rem(place.local * head_dim, 128) > 0
    query_cols = query_cols.at[:, pl.ds(pl.multiple_of(start, 128), 2 * QK_NOPE)]
    both = QK_NOPE + V_HEAD
    up_half = up_half.at[:, pl.ds(pl.multiple_of(place.local * both, both), both)]
    got_query = swap(query_cols, lambda shard: query_buf.at[shard], True)
    got_down = swap(at_piece(down_half), lambda shard: full_down.at[shard, wide.me])
    got_up = swap(up_half, lambda shard: up_buf.at[shard], True)
    token_run = gather_steps(
        place, tokens, token_buf, gather_keep.at[0], gather_send.at[0], gather_recv.at[0], sender
    )
    next(token_run)
    got_out = swap(at_piece(out_half), lambda shard: full_out.at[shard, wide.me])
    waits = [swap(at_piece(query_half), lambda shard: query_piece.at[shard])]
    def piece_gathers(kind, full):
        return [
            gather_steps(
                wide, None, full.at[other], None, piece_send.at[kind, step], piece_recv.at[kind, step], sender
            )
            for step, other in enumerate(others)
        ]

    next(token_run)
    got_down()
    down_runs = piece_gathers(0, full_down)
    for run in down_runs:
        next(run)
    next(token_run)
    for run in down_runs:
        next(run)
    got_query()
    got_up()
    waits += [
        swap(gate_half, lambda shard: full_gate.at[shard]),
        swap(wide_half, lambda shard: full_up.at[shard]),
    ]
    drain(token_run)
    got_out()
    waits += [
        swap(shared_gate, lambda shard: full_shared_gate.at[shard]),
        swap(shared_up, lambda shard: full_shared_up.at[shard]),
        swap(shared_down, lambda shard: full_shared_down.at[shard]),
    ]
    for run in down_runs:
        drain(run)
    route_run = gather_steps(
        wide, routes, all_routes, gather_keep.at[1], gather_send.at[1], gather_recv.at[1], sender
    )
    next(route_run)
    out_runs = piece_gathers(1, full_out)
    for run in out_runs:
        next(run)
    for copy in whole_weight(place, others, down_half, full_down, down_buf, whole_sem.at[0]):
        copy.wait()

    keys[:WINDOW, :] = jnp.zeros((WINDOW, keys.shape[1]), low)
    value[:WINDOW, :] = jnp.zeros((WINDOW, value.shape[1]), low)
    tile = 2 * rows
    own_width = width // shards

    def whole_dot(at, weight_of):
        total = 0.0
        for shard in range(shards):
            total = total + matmul(normed_buf[at, shard * own_width : (shard + 1) * own_width], weight_of(shard))
        return total

    def front_tile(index, _):
        at = pl.ds(pl.multiple_of(index * tile, tile), tile)
        values = token_buf[pl.ds(index * 2, 2)].reshape(tile, width).astype(jnp.float32)
        root = lax.rsqrt(jnp.mean(values * values, axis=1, keepdims=True) + EPS)
        normed_buf[at, :] = (values * root * first_gain[...]).astype(low)
        first = whole_dot(at, lambda shard: query_buf[shard])
        latent = whole_dot(at, lambda shard: down_buf[shard].reshape(own_width, -1))
        first = jnp.where(odd, pltpu.roll(first, first.shape[1] - QK_ROPE, 1), first)
        turn_at, sway_at = turn[at, :], sway[at, :]
        lane = lax.broadcasted_iota(jnp.int32, turn_at.shape, 1)

        def rotated(values):
            pair = jnp.where(lane < QK_ROPE, values, pltpu.roll(values, QK_ROPE, 1))
            return pair * turn_at + swapped_halves(pair) * sway_at

        query[at, :QK_NOPE] = first[:, :QK_NOPE].astype(low)
        query[at, QK_NOPE:] = jnp.where(lane < QK_ROPE, rotated(first[:, QK_NOPE:]), 0.0).astype(low)
        key_rope = rotated(latent[:, KV_RANK:]).astype(low)
        latent = latent[:, :KV_RANK]

        @pl.when(index == place.local // 2)
        def _():
            compressed[...] = jnp.where(lax.rem(place.local, 2) == 0, latent[:rows], latent[rows:])

        root = lax.rsqrt(jnp.mean(latent * latent, axis=1, keepdims=True) + EPS)
        normed_latent = (latent * root * latent_gain[...]).astype(low)
        key_latent[at, :] = normed_latent
        up_rows = KV_RANK // shards
        both = 0.0
        for shard in range(shards):
            both = both + matmul(normed_latent[:, shard * up_rows : (shard + 1) * up_rows], up_buf[shard])
        both = both.astype(low)
        later = pl.ds(pl.multiple_of(index * tile + WINDOW, tile), tile)
        keys[later, :QK_NOPE] = both[:, :QK_NOPE]
        keys[later, QK_NOPE:] = key_rope
        value[later, :] = both[:, QK_NOPE:]
        return 0

    tiles = group // 2
    grad_run = gather_steps(
        wide, cotangent, all_grads, gather_keep.at[3], gather_send.at[3], gather_recv.at[3], sender
    )
    for part in range(2):
        lax.fori_loop(part * tiles // 2, (part + 1) * tiles // 2, front_tile, 0)
        for run in out_runs + [route_run]:
            next(run, None)
    next(grad_run)
    save = pltpu.make_async_copy(normed_buf, normed_one, load_sem.at[1])
    save.start()
    for run in out_runs + [route_run]:
        next(run, None)

    def attend_tile(index, _):
        at = pl.ds(pl.multiple_of(index * QUERIES, QUERIES), QUERIES)
        window = pl.ds(pl.multiple_of(index * QUERIES, QUERIES), KEYS)
        scores = score_block(scale, index, ends, query[at, :], keys[window, :])
        top = jnp.max(scores, axis=1, keepdims=True)
        expo = jnp.exp(scores - top)
        total = jnp.sum(expo, axis=1, keepdims=True)
        probs = (expo / total).astype(low)
        real = jnp.where(query_documents(index, ends) < last, 1.0, 0.0)
        head_out[at, :] = (matmul(probs, value[window, :]) * real).astype(low)
        log_total[at, :] = jnp.broadcast_to(top + jnp.log(total), (QUERIES, log_total.shape[1]))
        return 0

    blocks = query.shape[0] // QUERIES
    lax.fori_loop(0, blocks // 2, attend_tile, 0)
    for run in out_runs + [route_run]:
        drain(run)
    load_out = whole_weight(place, others, out_half, full_out, out_buf, whole_sem.at[1])
    next(grad_run)
    lax.fori_loop(blocks // 2, blocks, attend_tile, 0)

    def head_at(member):
        return head_out.at[pl.ds(pl.multiple_of(member * rows, rows), rows), :]

    def lands(head):
        return heads_buf.at[:, pl.ds(pl.multiple_of(head * V_HEAD, V_HEAD), V_HEAD)]

    keep = pltpu.make_async_copy(head_at(place.local), lands(place.local), load_sem.at[2])
    keep.start()
    for step, member in enumerate(members):
        sender.start(
            place.always,
            remote(
                head_at(member), lands(place.local), trade_send.at[step], trade_recv.at[place.local],
                {"expert": place.base + member},
            ),
        )
    for step, member in enumerate(members):
        remote(
            head_at(member), lands(member), trade_send.at[step], trade_recv.at[member], {"expert": place.base + member}
        ).wait_recv()
    keep.wait()
    for copy in load_out:
        copy.wait()

    for at, size in pieces_of(width, 512):
        columns = slice(at, at + size)
        total = token_buf[place.local].reshape(rows, width)[:, columns].astype(jnp.float32)
        for shard in range(shards):
            weight = out_buf[shard, :, :, :, columns].reshape(own_width, size)
            total = total + matmul(heads_buf[:, shard * own_width : (shard + 1) * own_width], weight)
        middle[:, columns] = total
    values = middle[...]
    root = lax.rsqrt(jnp.mean(values * values, axis=1, keepdims=True) + EPS)
    second_buf[...] = (values * root * second_gain[...]).astype(low).reshape(second_buf.shape)

    normed_run = gather_steps(
        wide, second_buf, all_normed, gather_keep.at[2], gather_send.at[2], gather_recv.at[2], sender
    )
    runs = [normed_run, grad_run]
    while runs:
        runs = [run for run in runs if next(run, "end") != "end"]
    save.wait()
    for wait in waits:
        wait()
    sender.finish()


def forward_pass(scale, last, tokens, cotangent, blocks, routes, gains, tables):
    shards, plane = lax.axis_size("shard"), lax.axis_size("expert")
    local, width = tokens.shape
    low, shape = jnp.bfloat16, jax.ShapeDtypeStruct
    pieces = (PIECES, local // PIECES, width)
    any_space, vmem = pl.BlockSpec(memory_space=pl.ANY), pl.BlockSpec(memory_space=pltpu.VMEM)
    head_dim = QK_NOPE + QK_ROPE
    query_cols, down_half, up_half, out_half, query_half = blocks[:5]
    out_shape = [
        shape((plane,) + pieces, low),
        shape((plane,) + pieces, low),
        shape((plane, 1) + routes.shape, jnp.int32),
    ]
    stacked = [down_half.shape, out_half.shape, query_half.shape[1:]] + [block.shape for block in blocks[5:]]
    out_shape += [shape((shards,) + block, low) for block in stacked]
    out_shape += [
        shape((SEQ, width), low),
        shape((SEQ, head_dim + QK_ROPE), low),
        shape((SEQ + WINDOW, head_dim + QK_ROPE), low),
        shape((SEQ + WINDOW, V_HEAD), low),
        shape((SEQ, KV_RANK), low),
        shape((local, KV_RANK), jnp.float32),
        shape((SEQ, V_HEAD), low),
        shape((SEQ, 128), jnp.float32),
        shape((local, width), jnp.float32),
        shape((shards, up_half.shape[0], QK_NOPE + V_HEAD), low),
    ]
    hbm_out = 12
    dma = pltpu.SemaphoreType.DMA
    return pl.pallas_call(
        functools.partial(forward_kernel, shards, plane, scale, last),
        out_shape=out_shape,
        in_specs=[any_space] * (3 + len(blocks)) + [vmem] * (len(gains) + len(tables) - 1) + [pl.BlockSpec(memory_space=pltpu.SMEM)],
        out_specs=[any_space] * hbm_out + [vmem] * (len(out_shape) - hbm_out),
        scratch_shapes=[
            pltpu.VMEM((SEQ_DEVICES,) + pieces, low),
            pltpu.VMEM((SEQ, width), low),
            pltpu.VMEM((shards, query_cols.shape[0], 2 * QK_NOPE), low),
            pltpu.VMEM((shards,) + down_half.shape, low),
            pltpu.VMEM((shards,) + out_half.shape, low),
            pltpu.VMEM((local, HEADS * V_HEAD), low),
            pltpu.VMEM(pieces, low),
            dma((12, shards)),
            dma((12, shards)),
            dma((12,)),
            dma((4, 4, plane, PIECES)),
            dma((4, plane, PIECES)),
            dma((4,)),
            dma((3, shards, 4, plane, 1)),
            dma((3, shards, plane, 1)),
            dma((SEQ_DEVICES,)),
            dma((SEQ_DEVICES,)),
            dma((4,)),
            dma((2, shards)),
        ],
        compiler_params=pltpu.CompilerParams(
            collective_id=1, has_side_effects=True, vmem_limit_bytes=60 * 2**20
        ),
        name="forward",
    )(tokens.reshape(pieces), cotangent.reshape(pieces), *blocks, routes[None], *gains, *tables)


def sums_kernel(shards, plane, *refs):
    (normed_part, output_part, token_scores, slot_rows, slot_grad, hidden, gate_back, up_back, all_grads,
     shared_hidden,
     back, output_sum, scores, down_got, down_own, gate_own, up_own, gate_send, up_send, narrow_own, narrow_send,
     down_send, pair_buf, stream_buf, wide_buf, own_stage, send_stage, down_stage,
     load_sem, stream_sem, stage_sem, score_send, score_recv, swap_send, swap_recv, *reduces) = refs
    low = jnp.bfloat16
    place = Place(plane)
    sender = Sender()
    members = [lax.rem(place.me + step, plane) for step in range(1, plane)]
    others = [lax.rem(place.shard + step, shards) for step in range(1, shards)]
    greet([(place.always, {"expert": member}) for member in members] + [(place.always, {"shard": other}) for other in others])
    count = 13
    back_run = reduce_steps(place, normed_part, back, reduces[:count], sender, True)
    output_run = iter(())
    if len(reduces) > count:
        output_run = reduce_steps(place, output_part, output_sum, reduces[count:], sender, True)
    next(back_run)
    keep = pltpu.make_async_copy(token_scores.at[place.me], scores.at[place.me], load_sem.at[0])
    keep.start()

    def score_trade(step, member, source):
        return remote(token_scores.at[member], scores.at[source], score_send.at[step], score_recv.at[source],
                      {"expert": member})

    for step, member in enumerate(members):
        sender.start(place.always, score_trade(step, member, place.me))
    load_hidden = pltpu.make_async_copy(hidden, pair_buf.at[0], load_sem.at[1])
    load_hidden.start()
    load_up = pltpu.make_async_copy(up_back, pair_buf.at[1], load_sem.at[2])
    load_up.start()
    width = slot_rows.shape[1]
    tile = stream_buf.shape[-1]
    tiles = [slice(at, at + tile) for at in range(0, width, tile)]
    hidden_width = hidden.shape[1]
    own_hidden, own_width = hidden_width // shards, width // shards

    def streamed(source, buf, sem):
        copies = [
            pltpu.make_async_copy(source.at[:, columns], buf.at[index % 2], sem.at[index % 2])
            for index, columns in enumerate(tiles)
        ]
        copies[0].start()
        for index, copy in enumerate(copies):
            if index + 1 < len(copies):
                copies[index + 1].start()
            copy.wait()
            yield index, buf.at[index % 2]

    def down_chunks():
        load_hidden.wait()
        before = None
        for index, piece in streamed(slot_grad, stream_buf, stream_sem.at[0]):
            term = matmul_tn(pair_buf[0], piece[...])
            if before is not None:
                before.wait()
            for shard in range(shards):
                part = term[shard * own_hidden : (shard + 1) * own_hidden]

                @pl.when(place.shard == shard)
                def _():
                    down_stage[...] = part

                @pl.when(place.shard != shard)
                def _():
                    down_send[shard, :, tiles[index]] = part.astype(low)

            before = pltpu.make_async_copy(down_stage, down_own.at[:, tiles[index]], stage_sem.at[0])
            before.start()
            yield
        before.wait()
        for step, other in enumerate(others, 1):
            sender.start(
                place.always,
                remote(down_send.at[other], down_got.at[place.shard], swap_send.at[step], swap_recv.at[place.shard],
                       {"shard": other}),
            )

    def gate_chunks():
        load_gate = pltpu.make_async_copy(gate_back, pair_buf.at[0], load_sem.at[1])
        load_gate.start()
        load_gate.wait()
        load_up.wait()
        before = []
        for index, piece in streamed(slot_rows, stream_buf, stream_sem.at[0]):
            shard = index * tile // own_width
            within = pl.ds(index * tile - shard * own_width, tile)
            mine = place.shard == shard
            after = []
            for matrix, (own, send) in enumerate(((gate_own, gate_send), (up_own, up_send))):
                term = matmul_tn(piece[...], pair_buf[matrix])
                for there, copy in before[2 * matrix : 2 * matrix + 2]:
                    @pl.when(there)
                    def _():
                        copy.wait()

                to_own = pltpu.make_async_copy(own_stage.at[matrix], own.at[within], stage_sem.at[1 + matrix])
                to_send = pltpu.make_async_copy(send_stage.at[matrix], send.at[shard, within], stage_sem.at[3 + matrix])

                @pl.when(mine)
                def _():
                    own_stage[matrix] = term
                    to_own.start()

                @pl.when(~mine)
                def _():
                    send_stage[matrix] = term.astype(low)
                    to_send.start()

                after += [(mine, to_own), (~mine, to_send)]
                yield
            before = after
        for there, copy in before:
            @pl.when(there)
            def _():
                copy.wait()

    def shared_chunks():
        units = shared_hidden.shape[1]
        own_units = units // shards
        for index, piece in streamed(all_grads, wide_buf, stream_sem.at[1]):
            term = matmul_tn(shared_hidden[...], piece[...])
            for shard in range(shards):
                part = term[shard * own_units : (shard + 1) * own_units]
                narrow_send[shard, :, tiles[index]] = part.astype(low)

                @pl.when(place.shard == shard)
                def _():
                    narrow_own[:, tiles[index]] = part

            yield

    def chunks():
        yield from down_chunks()
        yield from gate_chunks()
        yield from shared_chunks()

    work = chunks()
    units = plane // INNER * normed_part.shape[1]
    next(work)
    for _ in range(units):
        next(back_run)
    next(output_run, None)
    for index in range(8):
        next(work)
    for index in range(units):
        next(work, None)
        next(back_run)
        if index >= units // 2:
            next(output_run, None)
            next(output_run, None)
    for index in range(units):
        next(work, None)
        next(output_run, None)
    drain(back_run)
    drain(work)
    drain(output_run)
    for step, member in enumerate(members):
        score_trade(step, member, member).wait_recv()
    keep.wait()
    for step, other in enumerate(others, 1):
        remote(down_send.at[other], down_got.at[other], swap_send.at[step], swap_recv.at[other], {"shard": other}).wait_recv()
    sender.finish()


def sums_pass(normed_part, output_part, token_scores, expert_terms, plane_terms, shared_terms):
    shards, plane = lax.axis_size("shard"), lax.axis_size("expert")
    low, shape = jnp.bfloat16, jax.ShapeDtypeStruct
    slot_rows, slot_grad, hidden, gate_back, up_back = expert_terms
    local, width = normed_part.shape[1:]
    slots, hidden_width = hidden.shape
    units = shared_terms[0].shape[1]
    count = 2 * PIECES
    pieces = (plane, count, local // count, width)
    own_width, own_hidden = width // shards, hidden_width // shards
    any_space, vmem = pl.BlockSpec(memory_space=pl.ANY), pl.BlockSpec(memory_space=pltpu.VMEM)
    reduces = 2 if plane == SEQ_DEVICES else 1
    out_shape = [
        shape(pieces[1:], jnp.float32),
        shape(pieces[1:], jnp.float32),
        shape(token_scores.shape, jnp.float32),
        shape((shards, own_hidden, width), low),
        shape((own_hidden, width), jnp.float32),
        shape((own_width, hidden_width), jnp.float32),
        shape((own_width, hidden_width), jnp.float32),
        shape((shards, own_width, hidden_width), low),
        shape((shards, own_width, hidden_width), low),
        shape((units // shards, width), jnp.float32),
        shape((shards, units // shards, width), low),
    ]
    dma, scratch = pltpu.SemaphoreType.DMA, pltpu.VMEM
    tile = 256
    outs = pl.pallas_call(
        functools.partial(sums_kernel, shards, plane),
        out_shape=out_shape,
        in_specs=[any_space] * 9 + [vmem],
        out_specs=[any_space] * 9 + [vmem] * 2,
        scratch_shapes=[
            scratch((shards, own_hidden, width), low),
            scratch((2, slots, hidden_width), low),
            scratch((2, slots, tile), low),
            scratch((2, plane * local, tile), low),
            scratch((2, tile, hidden_width), jnp.float32),
            scratch((2, tile, hidden_width), low),
            scratch((own_hidden, tile), jnp.float32),
            dma((3,)),
            dma((2, 2)),
            dma((5,)),
            dma((plane,)),
            dma((plane,)),
            dma((shards,)),
            dma((shards,)),
        ]
        + reduces * reduce_scratch(plane, count, local // count, width),
        compiler_params=pltpu.CompilerParams(
            collective_id=2, has_side_effects=True, vmem_limit_bytes=63 * 2**20
        ),
        name="sums",
    )(
        normed_part.reshape(pieces),
        output_part.reshape(pieces),
        token_scores,
        *expert_terms,
        *plane_terms,
        *shared_terms,
    )
    output_sum = outs[1].reshape(local, width)
    if reduces == 1:
        (output_sum,) = bundle(4, plane, shards, [("reduce", output_part)], 56 * 2**20)
    return (outs[0].reshape(local, width), output_sum) + tuple(outs[2:])


class Everyone:
    def __init__(self, place, plane, shards, source, got, send_sem, recv_sem, keep_sem):
        self.total = shards * plane
        self.plane = plane
        self.number = place.shard * plane + place.me
        self.source, self.got = source, got
        self.send_sem, self.recv_sem = send_sem, recv_sem
        self.keep = pltpu.make_async_copy(source(self.number), got.at[self.number], keep_sem)

    def copy(self, step, arriving):
        other = lax.rem(self.number + step, self.total)
        spot = other if arriving else self.number
        return remote(
            self.source(other),
            self.got.at[spot],
            self.send_sem.at[step],
            self.recv_sem.at[spot],
            {"shard": other // self.plane, "expert": lax.rem(other, self.plane)},
        )

    def start(self):
        self.keep.start()

        def body(step, _):
            self.copy(step, False).start()
            return 0

        lax.fori_loop(1, self.total, body, 0)

    def wait(self):
        self.keep.wait()

        def body(step, _):
            self.copy(step, True).wait_recv()
            return 0

        lax.fori_loop(1, self.total, body, 0)

    def finish(self):
        def body(step, _):
            self.copy(step, False).wait_send()
            return 0

        lax.fori_loop(1, self.total, body, 0)


def greet_everyone(place, plane, shards):
    barrier = pltpu.get_barrier_semaphore()
    total = shards * plane
    number = place.shard * plane + place.me

    def body(step, _):
        other = lax.rem(number + step, total)
        pl.semaphore_signal(
            barrier,
            inc=1,
            device_id={"shard": other // plane, "expert": lax.rem(other, plane)},
            device_id_type=MESH,
        )
        return 0

    lax.fori_loop(1, total, body, 0)
    pl.semaphore_wait(barrier, total - 1)


def norm_back(values, gain, grad):
    root = lax.rsqrt(jnp.mean(values * values, axis=1, keepdims=True) + EPS)
    weighted = grad * gain
    inner = jnp.mean(weighted * values, axis=1, keepdims=True)
    scaled = values * root
    return root * (weighted - scaled * (root * inner)), jnp.sum(grad * scaled, axis=0, keepdims=True)


def two_parts(values):
    high = values.astype(jnp.bfloat16)
    return high, (values - high.astype(jnp.float32)).astype(jnp.bfloat16)


def swapped_halves(pair):
    return pltpu.roll(pair, QK_ROPE // 2, 1)


def backward_kernel(shards, plane, scale, last, *refs):
    (back, scores, routes, middle, cotangent, tokens, first_gain, second_gain, latent_gain, router,
     lengths, query, keys, value, log_total, turn, sway, key_latent, up_head, head_out,
     compressed, full_out, full_query, full_down, normed_one, out_half, query_half, down_half, gate_send, up_send, narrow_send, down_own, down_sum_got,
     shared_moved, input_grad, query_out, up_out, down_out, out_out, small_out, shared_gate_out, shared_up_out,
     gate_got, up_got, narrow_got, mid_all, down_total,
     stream_buf, wq_buf, wd_buf, own_columns, own_compressed, heads_sum, mid_buf, low_buf, heads_buf, grad_buf, key_sum, value_sum,
     part_buf, trade_buf, trade_got, pair_buf, query_term, query_got, up_term, up_got_buf, own_query, low_grad, low_all,
     down_rows, down_got, out_rows, out_got, small_buf, small_got, key_got, total_buf, part_in, *sems) = refs
    (total_sem, part_sem, save_sem, load_sem, whole_sem, stream_sem, swap_send, swap_recv, trade_send, trade_recv, gather_send, gather_recv, gather_keep,
     all_send, all_recv, all_keep, rows_send, rows_recv, rows_keep, *reduce_scratch_refs) = sems
    low = jnp.bfloat16
    group = SEQ_DEVICES
    place = Place(group)
    local, width = middle.shape
    total = shards * plane
    ends = document_ends(lengths, (place.shard * plane + place.me) // group)
    sender = Sender()
    greet_everyone(place, plane, shards)
    members = [lax.rem(place.local + step, group) for step in range(1, group)]
    others = [lax.rem(place.shard + step, shards) for step in range(1, shards)]

    shares = []

    def share(number, source, got):
        for step, other in enumerate(others, 1):
            sender.start(
                place.always,
                remote(source.at[other], got.at[place.shard], swap_send.at[number, step],
                       swap_recv.at[number, place.shard], {"shard": other}),
            )
            shares.append(
                remote(source.at[other], got.at[other], swap_send.at[number, step], swap_recv.at[number, other],
                       {"shard": other})
            )

    share(0, gate_send, gate_got)
    numbers = iter(range(16))

    def load(source, target):
        copy = pltpu.make_async_copy(source, target, load_sem.at[next(numbers)])
        copy.start()
        return copy

    own_lanes = pl.ds(pl.multiple_of(place.local * 128, 128), 128)
    got_wd = whole_weight(place, others, down_half, full_down, wd_buf, whole_sem)
    got_columns = load(normed_one.at[:, :, :, own_lanes], own_columns)
    tile = stream_buf.shape[-1]
    tiles = [slice(at, at + tile) for at in range(0, width, tile)]

    def streamed(buf, count, sources):
        def copies(index):
            half = index % 2
            return [
                (there, pltpu.make_async_copy(source, target, stream_sem.at[half, number]))
                for there, source, target, number in sources(index, buf.at[half])
            ]

        def start(index):
            for there, copy in copies(index):
                @pl.when(there)
                def _():
                    copy.start()

        start(0)
        for index in range(count):
            if index + 1 < count:
                start(index + 1)
            for there, copy in copies(index):
                @pl.when(there)
                def _():
                    copy.wait()
            yield index, buf.at[index % 2]

    own_at = pl.ds(pl.multiple_of(place.local * local, local), local)
    per_shard = group // shards

    def columns_of(array):
        def sources(index, target):
            return [
                (place.always, array.at[pl.ds(shard * per_shard, per_shard), :, :, tiles[index]], target.at[shard], shard)
                for shard in range(shards)
            ]

        return sources

    def out_columns(index, target):
        found = []
        for shard in range(shards):
            mine = place.shard == shard
            found.append((mine, out_half.at[:, :, :, tiles[index]], target.at[shard], shard))
            found.append((~mine, full_out.at[shard, :, :, :, tiles[index]], target.at[shard], shard))
        return found

    row_tile = wq_buf.shape[1]
    own_rows = width // shards

    def query_rows(index, target):
        shard = index * row_tile // own_rows
        rows = slice(index * row_tile - shard * own_rows, (index + 1) * row_tile - shard * own_rows)
        mine = place.shard == shard
        return [(mine, query_half.at[rows], target, 0), (~mine, full_query.at[shard, rows], target, 0)]

    got_compressed = load(compressed, own_compressed)

    def everyone(index, source, got):
        return Everyone(place, plane, shards, source, got, all_send.at[index], all_recv.at[index], all_keep.at[index])

    def add_shards(own, got, result):
        rows, columns = own.shape
        size = 128 if rows % 128 == 0 else 176
        lanes = pl.ds(0, columns)

        def copies(index):
            half, at = index % 2, pl.ds(index * size, size)
            found = [pltpu.make_async_copy(own.at[at], total_buf.at[half, pl.ds(0, size), lanes], total_sem.at[half])]
            for step, other in enumerate(others):
                found.append(
                    pltpu.make_async_copy(
                        got.at[other, at], part_in.at[half, step, pl.ds(0, size), lanes], part_sem.at[half, step]
                    )
                )
            return found, pltpu.make_async_copy(
                total_buf.at[half, pl.ds(0, size), lanes], result.at[at], save_sem.at[half]
            )

        tiles_of = [copies(index) for index in range(rows // size)]
        for copy in tiles_of[0][0]:
            copy.start()
        for index, (loads, save) in enumerate(tiles_of):
            if index + 1 < len(tiles_of):
                if index:
                    tiles_of[index - 1][1].wait()
                for copy in tiles_of[index + 1][0]:
                    copy.start()
            for copy in loads:
                copy.wait()

            def body(chunk, _):
                at = pl.ds(pl.multiple_of(chunk * 16, 16), 16)
                total = total_buf[index % 2, at, lanes]
                for step in range(len(others)):
                    total = total + part_in[index % 2, step, at, lanes].astype(jnp.float32)
                total_buf[index % 2, at, lanes] = total
                return 0

            lax.fori_loop(0, size // 16, body, 0)
            save.start()
        for _, save in tiles_of[-2:]:
            save.wait()

    experts = router.shape[0]
    values = middle[...]
    root = lax.rsqrt(jnp.mean(values * values, axis=1, keepdims=True) + EPS)
    second_normed = (values * root * second_gain[...]).astype(low)
    logits = matmul_nt(router[...], second_normed)
    names = lax.broadcasted_iota(jnp.int32, (experts, local), 0)
    chosen = jnp.zeros((experts, local), jnp.float32)
    for choice in range(TOP):
        chosen = chosen + jnp.where(routes[choice : choice + 1, :] == names, 1.0, 0.0)
    logits = jnp.where(chosen > 0.0, logits, NEG)
    gates = jnp.exp(logits - jnp.max(logits, axis=0, keepdims=True)) * chosen
    gates = gates / jnp.sum(gates, axis=0, keepdims=True)
    gate_grad = jnp.concatenate([scores[index, :1, :] for index in range(experts)], axis=0)
    logit_grad = gates * (gate_grad - jnp.sum(gates * gate_grad, axis=0, keepdims=True))
    high, rest = two_parts(logit_grad)
    router_term = matmul(high, second_normed) + matmul(rest, second_normed)
    grad = back[...] + matmul_tn(high, router[...]) + matmul_tn(rest, router[...])
    row_grad, second_term = norm_back(values, second_gain[...], grad)
    mid_buf[...] = cotangent[...].astype(jnp.float32) + row_grad
    low_buf[...] = mid_buf[...].astype(low).reshape(low_buf.shape)

    for index, piece in streamed(stream_buf, len(tiles), out_columns):
        part = matmul_nt(low_buf[:, :, tiles[index]].reshape(local, tile), piece[...].reshape(-1, tile))
        heads_sum[...] = part if index == 0 else heads_sum[...] + part
    heads_buf[...] = heads_sum[...].astype(low)

    def lands(member):
        return heads_buf.at[:, pl.ds(pl.multiple_of(member * V_HEAD, V_HEAD), V_HEAD)]

    def head_trade(step, member, source):
        spot = pl.ds(pl.multiple_of(source * local, local), local)
        return remote(lands(member), grad_buf.at[spot, :], trade_send.at[0, step], trade_recv.at[0, source],
                      {"expert": place.base + member})

    keep_head = pltpu.make_async_copy(lands(place.local), grad_buf.at[own_at, :], load_sem.at[next(numbers)])
    keep_head.start()
    for step, member in enumerate(members):
        sender.start(place.always, head_trade(step, member, place.local))
    mid_run = gather_steps(place, low_buf, mid_all, gather_keep.at[0], gather_send.at[0], gather_recv.at[0], sender)
    next(mid_run)
    add_shards(down_own, down_sum_got, down_total)
    for step, member in enumerate(members):
        head_trade(step, member, member).wait_recv()
    keep_head.wait()

    key_sum[...] = jnp.zeros_like(key_sum)
    value_sum[...] = jnp.zeros_like(value_sum)

    def attend_tile(index, _):
        at = pl.ds(pl.multiple_of(index * QUERIES, QUERIES), QUERIES)
        window = pl.ds(pl.multiple_of(index * QUERIES, QUERIES), KEYS)
        tile, key_tile = query[at, :], keys[window, :]
        head_grad = jnp.where(query_documents(index, ends) < last, grad_buf[at, :], jnp.zeros((), low))
        scores_at = score_block(scale, index, ends, tile, key_tile)
        probs = jnp.exp(scores_at - log_total[at, :1])
        prob_grad = matmul_nt(head_grad, value[window, :])
        inner = jnp.sum(probs * prob_grad, axis=1, keepdims=True)
        raw_grad = (probs * (prob_grad - inner) * scale).astype(low)
        grads = matmul(raw_grad, key_tile)
        trade_buf[at, :QK_NOPE] = grads[:, :QK_NOPE].astype(low)
        pair = grads[:, QK_NOPE:]
        trade_buf[at, QK_NOPE:] = (pair * turn[at, :] - swapped_halves(pair) * sway[at, :]).astype(low)
        key_sum[window, :] += matmul_tn(raw_grad, tile)
        value_sum[window, :] += matmul_tn(probs.astype(low), head_grad)
        return 0

    blocks = query.shape[0] // QUERIES
    for index in range(blocks // 2):
        attend_tile(jnp.int32(index), 0)
    next(mid_run)
    for index in range(blocks // 2, blocks):
        attend_tile(jnp.int32(index), 0)
    next(mid_run)

    share(1, up_send, up_got)
    share(2, narrow_send, narrow_got)

    lane = lax.broadcasted_iota(jnp.int32, (QUERIES, 2 * QK_ROPE), 1)

    def key_tile(index, _):
        at = pl.ds(pl.multiple_of(index * QUERIES, QUERIES), QUERIES)
        later = pl.ds(pl.multiple_of(index * QUERIES + WINDOW, QUERIES), QUERIES)
        key_rope = pltpu.roll(key_sum[later, QK_NOPE:], QK_ROPE, 1).astype(low)
        trade_buf[at, QK_NOPE:] = jnp.where(lane < QK_ROPE, trade_buf[at, QK_NOPE:], key_rope)
        pair_buf[at, :QK_NOPE] = key_sum[later, :QK_NOPE].astype(low)
        pair_buf[at, QK_NOPE:] = value_sum[later, :].astype(low)
        part = matmul_nt(pair_buf[at, :], up_head[...]).astype(low)
        per = QUERIES // local
        part_buf[pl.ds(index * per, per)] = part.reshape((per,) + part_buf.shape[1:])
        return 0

    for index in range(blocks):
        key_tile(jnp.int32(index), 0)

    def token_trade(step, member, source):
        spot = pl.ds(pl.multiple_of(member * local, local), local)
        return remote(trade_buf.at[spot, :], trade_got.at[source], trade_send.at[1, step], trade_recv.at[1, source],
                      {"expert": place.base + member})

    reduce_run = reduce_steps(place, part_buf, key_got, reduce_scratch_refs, sender)
    next(reduce_run)
    keep_token = pltpu.make_async_copy(trade_buf.at[own_at, :], trade_got.at[place.local], load_sem.at[next(numbers)])
    keep_token.start()
    for step, member in enumerate(members):
        sender.start(place.always, token_trade(step, member, place.local))

    for index, piece in streamed(stream_buf, len(tiles), columns_of(normed_one)):
        term = matmul_tn(trade_buf[...], piece[...].reshape(SEQ, tile))
        per = tile // query_term.shape[1]
        query_term[index * per : (index + 1) * per] = term.T.astype(low).reshape((per,) + query_term.shape[1:])
    up_term[...] = matmul_tn(key_latent[...], pair_buf[...]).astype(low).reshape(up_term.shape)
    next(reduce_run)
    query_trade = everyone(1, lambda target: query_term.at[target], query_got)
    query_trade.start()
    up_trade = everyone(2, lambda target: up_term.at[target], up_got_buf)
    up_trade.start()
    units = shared_gate_out.shape[1] // total
    padded = shared_moved.shape[2] // (2 * shards)
    next(reduce_run)
    for member in range(plane):
        block = 0.0
        for shard in range(shards):
            block = block + shared_moved[shard * plane + member].astype(jnp.float32)
        for part, result in enumerate((shared_gate_out, shared_up_out)):
            for shard in range(shards):
                at = (part * shards + shard) * padded
                spot = (shard * plane + member) * units
                result[:, spot : spot + units] = block[:, at : at + units]
    drain(reduce_run)
    for step, member in enumerate(members):
        token_trade(step, member, member).wait_recv()
    keep_token.wait()

    got_compressed.wait()
    head_dim = QK_NOPE + QK_ROPE
    rope = jnp.zeros((local, 2 * QK_ROPE), jnp.float32)
    for head in range(group):
        own_query[:, head * head_dim : (head + 1) * head_dim] = trade_got[head, :, :head_dim]
        rope = rope + trade_got[head, :, QK_NOPE:].astype(jnp.float32)
    lane = lax.broadcasted_iota(jnp.int32, rope.shape, 1)
    rope = jnp.where(lane < QK_ROPE, pltpu.roll(rope, QK_ROPE, 1), rope)
    rope = rope * turn[own_at, :] - swapped_halves(rope) * sway[own_at, :]
    latent_grad, latent_term = norm_back(own_compressed[...], latent_gain[...], key_got[...].reshape(local, KV_RANK))
    low_grad[0, 0, :, :KV_RANK] = latent_grad.astype(low)
    low_grad[0, 0, :, KV_RANK:] = jnp.where(lane < QK_ROPE, rope, 0.0).astype(low)
    low_run = gather_steps(place, low_grad.at[0], low_all, gather_keep.at[1], gather_send.at[1], gather_recv.at[1], sender)
    next(low_run)
    for copy in got_wd:
        copy.wait()
    for index, piece in streamed(wq_buf, width // row_tile, query_rows):
        rows = slice(index * row_tile, (index + 1) * row_tile)
        shard = index * row_tile // own_rows
        within = slice(rows.start - shard * own_rows, rows.stop - shard * own_rows)
        term = matmul_nt(own_query[...], piece[...])
        input_grad[:, rows] = term + matmul_nt(low_grad[0, 0], wd_buf[shard, within, :])
    next(low_run)
    row_grad, first_term = norm_back(tokens[...].astype(jnp.float32), first_gain[...], input_grad[...])
    input_grad[...] = mid_buf[...] + row_grad
    next(low_run)
    drain(mid_run)
    per_lane = width // 128
    for block in range(per_lane):
        columns = slice(block * 128, (block + 1) * 128)
        small_buf[block, :experts, :] = router_term[:, columns]
        small_buf[block, experts : experts + 1, :] = second_term[:, columns]
        small_buf[block, experts + 1 : experts + 2, :] = first_term[:, columns]
        at = block // (per_lane * 128 // KV_RANK) * 128
        small_buf[block, experts + 2 : experts + 3, :] = latent_term[:, at : at + 128]
        small_buf[block, experts + 3 :, :] = jnp.zeros((small_buf.shape[1] - experts - 3, 128), jnp.float32)
    small_trade = everyone(3, lambda target: small_buf.at[target // (total // per_lane)], small_got)
    small_trade.start()
    drain(low_run)
    got_columns.wait()
    down = matmul_tn(own_columns[...].reshape(SEQ, -1), low_all[...].reshape(SEQ, -1))
    down_rows[...] = down.astype(low).reshape(down_rows.shape)
    down_trade = head_rows(place, plane, shards, down_rows, down_got, rows_keep.at[0], rows_send.at[0], rows_recv.at[0])[0]
    for index, piece in streamed(stream_buf, len(tiles), columns_of(mid_all)):
        term = matmul_tn(head_out[...], piece[...].reshape(SEQ, tile)).astype(low)
        out_rows[:, :, tiles[index]] = term.reshape(out_rows.shape[:2] + (tile,))
    out_trade = head_rows(place, plane, shards, out_rows, out_got, rows_keep.at[1], rows_send.at[1], rows_recv.at[1])[0]

    sequences = total // group
    query_trade.wait()
    up_trade.wait()
    for head in range(group):
        query_sum, up_sum = 0.0, 0.0
        for sequence in range(sequences):
            query_sum = query_sum + query_got[sequence * group + head].astype(jnp.float32)
            up_sum = up_sum + up_got_buf[sequence * group + head].astype(jnp.float32)
        query_out[:, head * head_dim : (head + 1) * head_dim] = query_sum[:, :head_dim]
        both = QK_NOPE + V_HEAD
        up_out[:, head * both : (head + 1) * both] = up_sum
    small_trade.wait()
    small_out[...] = small_got[0]

    def small_sum(source, _):
        small_out[...] += small_got[source]
        return 0

    lax.fori_loop(1, total, small_sum, 0)
    down_trade.wait()
    out_trade.wait()
    down_sum, out_sum = 0.0, 0.0
    for sequence in range(sequences):
        down_sum = down_sum + down_got[sequence].astype(jnp.float32)
        out_sum = out_sum + out_got[sequence].astype(jnp.float32)
    down_out[...] = down_sum[:, : down_out.shape[1]]
    out_out[...] = out_sum
    for arrival in shares:
        arrival.wait_recv()
    for trade in (query_trade, up_trade, small_trade):
        trade.finish()
    sender.finish()


def backward_pass(scale, last, small, tables, saved, weights, sends, owns, shared_moved, shared_width):
    shards, plane = lax.axis_size("shard"), lax.axis_size("expert")
    total = shards * plane
    low, shape = jnp.bfloat16, jax.ShapeDtypeStruct
    local, width = small[3].shape
    head_dim = QK_NOPE + QK_ROPE
    vmem, any_space = pl.BlockSpec(memory_space=pltpu.VMEM), pl.BlockSpec(memory_space=pl.ANY)
    inputs = list(small) + list(tables) + list(saved)
    spaces = [vmem] * len(inputs)
    spaces[len(small)] = pl.BlockSpec(memory_space=pltpu.SMEM)
    hbm = list(weights) + list(sends) + list(owns) + [shared_moved]
    gate_send, up_send, narrow_send = sends
    experts = small[9].shape[0]
    small_rows = experts + 3 + -(experts + 3) % 8
    own_width = width // total
    out_shape = [
        shape((local, width), jnp.float32),
        shape((own_width, HEADS * head_dim), jnp.float32),
        shape((KV_RANK // total, HEADS * (QK_NOPE + V_HEAD)), jnp.float32),
        shape((own_width, KV_RANK + QK_ROPE), jnp.float32),
        shape((own_width, width), jnp.float32),
        shape((small_rows, 128), jnp.float32),
        shape((own_width, shared_width), jnp.float32),
        shape((own_width, shared_width), jnp.float32),
        shape(gate_send.shape, low),
        shape(up_send.shape, low),
        shape(narrow_send.shape, low),
        shape((SEQ_DEVICES, PIECES, local // PIECES, width), low),
        shape(owns[0].shape, jnp.float32),
    ]
    hbm_out = 5
    dma, scratch = pltpu.SemaphoreType.DMA, pltpu.VMEM
    pieces = (PIECES, local // PIECES)
    down_width = weights[3].shape[2]
    row_count = 128 // own_width
    sequences = total // SEQ_DEVICES
    wide_head = 2 * QK_NOPE
    return pl.pallas_call(
        functools.partial(backward_kernel, shards, plane, scale, last),
        out_shape=out_shape,
        in_specs=spaces + [any_space] * (len(hbm) - 1) + [vmem],
        out_specs=[vmem] * (len(out_shape) - hbm_out) + [any_space] * hbm_out,
        scratch_shapes=[
            scratch((2, shards, SEQ_DEVICES // shards) + pieces + (512,), low),
            scratch((2, 256, HEADS * head_dim), low),
            scratch((shards, width // shards, down_width), low),
            scratch((SEQ_DEVICES,) + pieces + (128,), low),
            scratch((local, KV_RANK), jnp.float32),
            scratch((local, width), jnp.float32),
            scratch((local, width), jnp.float32),
            scratch(pieces + (width,), low),
            scratch((local, width), low),
            scratch((SEQ, V_HEAD), low),
            scratch((SEQ + WINDOW, wide_head), jnp.float32),
            scratch((SEQ + WINDOW, V_HEAD), jnp.float32),
            scratch((SEQ_DEVICES,) + pieces + (KV_RANK,), low),
            scratch((SEQ, wide_head), low),
            scratch((SEQ_DEVICES, local, wide_head), low),
            scratch((SEQ, wide_head), low),
            scratch((total, own_width, wide_head), low),
            scratch((total, own_width, wide_head), low),
            scratch((total, KV_RANK // total, wide_head), low),
            scratch((total, KV_RANK // total, wide_head), low),
            scratch((local, HEADS * head_dim), low),
            scratch((1, 1, local, down_width), low),
            scratch((SEQ_DEVICES, 1, local, down_width), low),
            scratch((row_count, own_width, down_width), low),
            scratch((sequences, own_width, down_width), low),
            scratch((row_count, own_width, width), low),
            scratch((sequences, own_width, width), low),
            scratch((width // 128, small_rows, 128), jnp.float32),
            scratch((total, small_rows, 128), jnp.float32),
            scratch(pieces + (KV_RANK,), jnp.float32),
            scratch((2, 176, width), jnp.float32),
            scratch((2, shards - 1, 176, width), low),
            dma((2,)),
            dma((2, shards)),
            dma((2,)),
            dma((8,)),
            dma((shards,)),
            dma((2, shards)),
            dma((3, shards)),
            dma((3, shards)),
            dma((2, SEQ_DEVICES)),
            dma((2, SEQ_DEVICES)),
            dma((2, 4, SEQ_DEVICES, PIECES)),
            dma((2, SEQ_DEVICES, PIECES)),
            dma((2,)),
            dma((4, total)),
            dma((4, total)),
            dma((4,)),
            dma((2, max(row_count, sequences))),
            dma((2, max(row_count, sequences))),
            dma((2,)),
        ]
        + reduce_scratch(SEQ_DEVICES, PIECES, local // PIECES, KV_RANK),
        compiler_params=pltpu.CompilerParams(
            collective_id=3, has_side_effects=True, vmem_limit_bytes=62 * 2**20
        ),
        name="backward",
    )(*inputs, *hbm)


def on_device(
    tokens,
    document_lengths,
    routes,
    first_gain,
    query_weight,
    latent_down,
    latent_gain,
    latent_up,
    output_weight,
    second_gain,
    router_weight,
    shared_gate,
    shared_up,
    shared_down,
    expert_gate,
    expert_up,
    expert_down,
    cotangent,
):
    local_rows, width = tokens.shape
    shards = lax.axis_size("shard")
    plane = lax.axis_size("expert")
    everyone = ("shard", "expert")
    all_devices = shards * plane
    shard_at = lax.axis_index("shard")
    plane_at = lax.axis_index("expert")
    head_at = plane_at % SEQ_DEVICES
    sequence_at = (shard_at * plane + plane_at) // SEQ_DEVICES
    capacity = local_rows * TOP * 4 // (3 * plane)
    head_dim = QK_NOPE + QK_ROPE
    scale = 1.0 / math.sqrt(head_dim)
    own_at = head_at * local_rows

    def own_rows(values):
        return lax.dynamic_slice_in_dim(values, own_at, local_rows, 0)

    piece_rows = output_weight.shape[0] // plane
    down_half = jnp.pad(latent_down, ((0, 0), (0, QK_ROPE)))
    units = shared_down.shape[0] // plane
    unit_pad = -units % 16
    padded_units = units + unit_pad
    gate_columns, up_columns = (
        jnp.concatenate(
            [
                jnp.pad(
                    lax.dynamic_slice_in_dim(
                        weight, index * shared_down.shape[0] + plane_at * units, units, 1
                    ),
                    ((0, 0), (0, unit_pad)),
                )
                for index in range(shards)
            ],
            axis=1,
        )
        for weight in (shared_gate, shared_up)
    )
    down_units = lax.dynamic_slice_in_dim(shared_down, plane_at * units, units, 0)
    down_units = jnp.pad(down_units, ((0, unit_pad), (0, 0)))

    def plane_pieces(weight):
        return weight.reshape(plane, 1, -1, weight.shape[1])

    angles = np.arange(SEQ)[:, None] * THETA ** (-np.arange(QK_ROPE // 2) / (QK_ROPE // 2))
    turn = jnp.asarray(np.tile(np.cos(angles), (1, 4)), jnp.float32)
    sway = jnp.asarray(np.tile(np.sin(angles), (1, 4)) * np.repeat([-1.0, 1.0, -1.0, 1.0], 32), jnp.float32)
    entry_count = document_lengths.shape[1]
    route_rows = jnp.pad(routes.T, ((0, 8 - TOP), (0, 0)), constant_values=-1)
    (
        all_normed,
        all_grads,
        all_routes,
        full_down,
        full_out,
        query_piece,
        gate_single,
        up_single,
        gate_shared,
        up_shared,
        down_shared,
        normed_one,
        query,
        keys,
        value,
        key_latent,
        compressed,
        head_out,
        log_total,
        middle,
        up_head,
    ) = forward_pass(
        scale,
        entry_count - 1,
        tokens,
        cotangent,
        (
            query_weight,
            plane_pieces(down_half),
            latent_up,
            plane_pieces(output_weight),
            plane_pieces(query_weight),
            expert_gate[0],
            expert_up[0],
            gate_columns,
            up_columns,
            down_units,
        ),
        route_rows,
        (first_gain[None], latent_gain[None], second_gain[None]),
        (turn, sway, document_lengths),
    )
    all_normed = all_normed.reshape(-1, width)
    all_grads = all_grads.reshape(-1, width)
    blocked = (SEQ_DEVICES, PIECES, local_rows // PIECES, width)
    shard_blocked = (shards, SEQ_DEVICES // shards) + blocked[1:]
    (
        slot_rows,
        slot_grad,
        normed_part,
        output_part,
        token_scores,
        hidden,
        gate_pre_grad,
        up_pre_grad,
        shared_hidden,
        shared_moved,
        _,
        full_query,
    ) = expert_pass(
        all_routes[:, 0],
        router_weight.T,
        all_normed,
        all_grads,
        (
            gate_columns,
            gate_shared,
            up_columns,
            up_shared,
            down_units,
            down_shared,
            expert_gate[0],
            gate_single,
            expert_up[0],
            up_single,
            expert_down[0],
        ),
        query_piece,
        capacity,
    )
    (
        back,
        output_sum,
        scores,
        down_blocks,
        down_own,
        gate_own,
        up_own,
        gate_send,
        up_send,
        shared_down_own,
        shared_down_send,
    ) = sums_pass(
        normed_part.reshape(plane, local_rows, width),
        output_part.reshape(plane, local_rows, width),
        token_scores,
        (slot_rows, slot_grad, hidden, gate_pre_grad, up_pre_grad),
        (all_grads,),
        (shared_hidden,),
    )
    activations = (middle + output_sum).astype(jnp.bfloat16)

    def sum_shards(own, blocks):
        for step in range(1, shards):
            own = own + lax.dynamic_index_in_dim(
                blocks, (shard_at + step) % shards, 0, keepdims=False
            ).astype(jnp.float32)
        return own

    (
        input_grad,
        query_weight_grad,
        latent_up_grad,
        latent_down_grad,
        output_weight_grad,
        small_sums,
        shared_gate_grad,
        shared_up_grad,
        gate_blocks,
        up_blocks,
        shared_blocks,
        _,
        expert_down_grad,
    ) = backward_pass(
        scale,
        entry_count - 1,
        (
            back,
            scores,
            route_rows,
            middle,
            cotangent,
            tokens,
            first_gain[None],
            second_gain[None],
            latent_gain[None],
            router_weight.T,
        ),
        (document_lengths, query, keys, value, log_total, turn, sway),
        (key_latent, up_head.reshape(KV_RANK, -1), head_out),
        (
            compressed,
            full_out.reshape(shard_blocked),
            full_query.reshape((shards,) + query_weight.shape),
            full_down.reshape((shards,) + down_half.shape),
            normed_one.reshape(blocked),
            output_weight.reshape(shard_blocked[1:]),
            query_weight,
            down_half,
        ),
        (gate_send, up_send, shared_down_send),
        (down_own, down_blocks),
        shared_moved,
        shared_gate.shape[1],
    )
    expert_gate_grad = sum_shards(gate_own, gate_blocks)
    expert_up_grad = sum_shards(up_own, up_blocks)
    shared_down_grad = sum_shards(shared_down_own, shared_blocks)[:units]
    own_width = width // all_devices
    number = shard_at * plane + plane_at
    own_small = lax.dynamic_slice_in_dim(small_sums, number * own_width % 128, own_width, 1)
    router_weight_grad = own_small[:plane].T
    second_gain_grad = own_small[plane]
    first_gain_grad = own_small[plane + 1]
    latent_width = KV_RANK // all_devices
    latent_gain_grad = lax.dynamic_slice_in_dim(
        small_sums[plane + 2], number * latent_width % 128, latent_width, 0
    )
    return (
        activations,
        input_grad,
        first_gain_grad,
        query_weight_grad,
        latent_down_grad,
        latent_gain_grad,
        latent_up_grad,
        output_weight_grad,
        second_gain_grad,
        router_weight_grad,
        shared_gate_grad,
        shared_up_grad,
        shared_down_grad,
        expert_gate_grad[None],
        expert_up_grad[None],
        expert_down_grad[None],
    )


def solution(mesh):
    return jax.shard_map(
        on_device,
        mesh=mesh,
        in_specs=(
            P(("shard", "expert"), None),
            P(),
            P(("shard", "expert"), None),
            P(),
            P("shard", None),
            P("shard", None),
            P(),
            P("shard", None),
            P("shard", None),
            P(),
            P(),
            P("shard", None),
            P("shard", None),
            P("shard", None),
            P("expert", "shard", None),
            P("expert", "shard", None),
            P("expert", "shard", None),
            P(("shard", "expert"), None),
        ),
        out_specs=(
            P(("shard", "expert"), None),
            P(("shard", "expert"), None),
            P(("shard", "expert")),
            P(("shard", "expert"), None),
            P(("shard", "expert"), None),
            P(("shard", "expert")),
            P(("shard", "expert"), None),
            P(("shard", "expert"), None),
            P(("shard", "expert")),
            P(("shard", "expert"), None),
            P(("shard", "expert"), None),
            P(("shard", "expert"), None),
            P(("shard", "expert"), None),
            P("expert", "shard", None),
            P("expert", "shard", None),
            P("expert", "shard", None),
        ),
        check_vma=False,
    )
```
